32 devices in a mesh: dp: 8 (over z, x), seq: 4 (over y, core).
Axes of the slice: x: 2, y: 2, z: 4, core: 2. Of those that a mesh axis runs over, the one named last changes fastest.
Arguments:
- doc_tokens: bfloat16 [32, 1024, 768], P('dp', 'seq'), may hold values from -6 to 6
- queries: bfloat16 [512, 32, 768], P(('dp', 'seq')), may hold values from -6 to 6
- doc_cot: bfloat16 [32, 1024, 768], P('dp', 'seq'), may hold values from -6 to 6
- query_cot: bfloat16 [512, 32, 768], P(('dp', 'seq')), may hold values from -6 to 6
- q_weight: bfloat16 [768, 768], P(('dp', 'seq')), may hold values from -0.0546875 to 0.0546875
- kv_weight: bfloat16 [768, 1536], P(('dp', 'seq')), may hold values from -0.21875 to 0.21875
- out_weight: bfloat16 [768, 768], P(('dp', 'seq')), may hold values from -1.5 to 1.5
- up_weight: bfloat16 [768, 3072], P(('dp', 'seq')), may hold values from -0.21875 to 0.21875
- down_weight: bfloat16 [3072, 768], P(('dp', 'seq')), may hold values from -0.109375 to 0.109375
- attn_gain: float32 [768], replicated, may hold values from 0.5 to 1.5
- ff_gain: float32 [768], replicated, may hold values from 0.5 to 1.5
- rel_bias: float32 [32, 12], replicated, may hold values from -4 to 4
- doc_buckets: int32 [1024, 1024], P('seq'), may hold values from 0 to 31
- query_buckets: int32 [32, 32], replicated, may hold values from 0 to 31
- topk_mask: int32 [512, 1024], P(('dp', 'seq')), may hold values 0 or 1
- positives: int32 [512, 4], P(('dp', 'seq')), may hold values from 0 to 1023
- pos_count: int32 [512], P(('dp', 'seq')), may hold values from 1 to 4
Outputs:
- doc_out: bfloat16 [32, 1024, 768], P('dp', 'seq')
- query_out: bfloat16 [512, 32, 768], P(('dp', 'seq'))
- doc_dx: float32 [32, 1024, 768], P('dp', 'seq')
- query_dx: float32 [512, 32, 768], P(('dp', 'seq'))
- grad_q_weight: float32 [768, 768], P(('dp', 'seq'))
- grad_kv_weight: float32 [768, 1536], P(('dp', 'seq'))
- grad_out_weight: float32 [768, 768], P(('dp', 'seq'))
- grad_up_weight: float32 [768, 3072], P(('dp', 'seq'))
- grad_down_weight: float32 [3072, 768], P(('dp', 'seq'))
- grad_attn_gain: float32 [768], replicated
- grad_ff_gain: float32 [768], replicated
- grad_rel_bias: float32 [32, 12], replicated
- retrieved_fraction: float32 [], replicated
The draws below stay inside these ranges and needn't reach their ends.
All inputs are finite; a program needn't handle non-finite values. No bound on the sum of `topk_mask` on one device may be relied on, other than what follows from the above.
Results may differ from the reference program's by a relative error of at most 0.014.
The reference program's roundings to bfloat16 on the way count: a program that leaves them out, or rounds other values in their place, can miss the bound.
Values may be sent and summed in bfloat16 or wider, within the bound.
A program may use at most 256 MiB of HBM per device.

```python
import math
import jax
import jax.numpy as jnp
from jax import lax

D = 768
HEADS = 12
FF = 3072
BUCKETS = 32
DOC_LEN = 1024
QLEN = 32
POS = 4
DOCS = 32
QUERIES = 512


def plant(entries, own_key, smallest, largest):
    longest = entries.shape.index(max(entries.shape))
    spots = []
    for shift in (0, 1):
        where = [jax.random.randint(jax.random.fold_in(own_key, axis), (), 0, length) for axis, length in enumerate(entries.shape)]
        where[longest] = (where[longest] + shift) % entries.shape[longest]
        spots.append(tuple(where))
    return entries.at[spots[0]].set(smallest).at[spots[1]].set(largest)


def steps_of(own_key, extent, pieces, least, top_value):
    def one(axis_at, blocks):
        draws = jax.random.uniform(jax.random.fold_in(jax.random.fold_in(own_key, 6), axis_at), (blocks,), jnp.float32, least / len(pieces), top_value / len(pieces))
        return jnp.repeat(jnp.exp(draws), extent[axis_at] // blocks).reshape((-1,) + (1,) * (len(extent) - axis_at - 1))

    level = one(*pieces[0])
    for cut in pieces[1:]:
        level = level * one(*cut)
    return level


def noise(own_key, extent, deviation, reach, pieces=(), held_as=jnp.bfloat16):
    result = jax.random.normal(own_key, extent, jnp.float32) * deviation
    if len(pieces) > 0:
        result = steps_of(own_key, extent, pieces, -0.22, 0.18) * result
    return jnp.clip(result, min=-reach, max=reach).astype(held_as)


def setup_inputs(seed: int = 0) -> dict:
    splits = jax.random.split(jax.random.key(seed), 18)
    return {
        "doc_tokens": noise(splits[0], (DOCS, DOC_LEN, D), 1.0, 6.0, ((0, 8), (1, 4))),
        "queries": noise(splits[1], (QUERIES, QLEN, D), 1.0, 6.0, ((0, 32),)),
        "doc_cot": noise(splits[2], (DOCS, DOC_LEN, D), 1.0, 6.0, ((0, 8), (1, 4))),
        "query_cot": noise(splits[3], (QUERIES, QLEN, D), 1.0, 6.0, ((0, 32),)),
        "q_weight": noise(splits[4], (D, D), (16 * D) ** -0.5, 0.0546875, ((0, 32),)),
        "kv_weight": noise(splits[5], (D, 2 * D), D ** -0.5, 0.21875, ((0, 32),)),
        "out_weight": noise(splits[6], (D, D), 16 ** -0.5, 1.5, ((0, 32),)),
        "up_weight": noise(splits[7], (D, FF), D ** -0.5, 0.21875, ((0, 32),)),
        "down_weight": noise(splits[8], (FF, D), FF ** -0.5, 0.109375, ((0, 32),)),
        "attn_gain": jnp.clip(1.0 + 0.1 * jax.random.normal(splits[9], (D,), jnp.float32), 0.5, 1.5),
        "ff_gain": jnp.clip(1.0 + 0.1 * jax.random.normal(splits[10], (D,), jnp.float32), 0.5, 1.5),
        "rel_bias": noise(splits[11], (BUCKETS, HEADS), 1.0, 4.0, (), jnp.float32),
        "doc_buckets": plant(jax.random.randint(splits[12], (DOC_LEN, DOC_LEN), 0, BUCKETS), jax.random.fold_in(splits[12], 1), 0, BUCKETS - 1).astype(jnp.int32),
        "query_buckets": plant(jax.random.randint(splits[13], (QLEN, QLEN), 0, BUCKETS), jax.random.fold_in(splits[13], 1), 0, BUCKETS - 1).astype(jnp.int32),
        "topk_mask": plant((jax.random.randint(splits[14], (QUERIES, DOC_LEN), 0, 2) < 1).astype(jnp.int32), jax.random.fold_in(splits[14], 1), 0, 1),
        "positives": plant(jax.random.randint(splits[15], (QUERIES, POS), 0, DOC_LEN), jax.random.fold_in(splits[15], 1), 0, DOC_LEN - 1).astype(jnp.int32),
        "pos_count": plant(jax.random.randint(splits[16], (QUERIES,), 1, POS + 1), jax.random.fold_in(splits[16], 1), 1, POS).astype(jnp.int32),
    }


@jax.custom_vjp
def low(v):
    return lax.optimization_barrier(v.astype(jnp.bfloat16)).astype(jnp.float32)

@jax.custom_vjp
def low_back(v):
    return v

def low_keep(v):
    return (low(v), None)

def low_pass(kept, grad):
    return (grad,)

def back_keep(v):
    return (v, None)

def back_low(kept, grad):
    return (low(grad),)
low.defvjp(low_keep, low_pass)
low_back.defvjp(back_keep, back_low)
EPSILON = 1e-06
PRECISE = lax.Precision.HIGHEST

def normed(values, gain):
    return values * lax.rsqrt(lax.optimization_barrier(jnp.mean(values * values, axis=-1, keepdims=True)) + EPSILON) * gain

def attend(query_h, key_h, value_h, rel_terms):
    scores = jnp.einsum('bihe,bjhe->bhij', query_h, key_h, precision=PRECISE) + rel_terms
    softened = low(jax.nn.softmax(low_back(scores), axis=-1))
    return jnp.einsum('bhij,bjhe->bihe', softened, value_h, precision=PRECISE)

def layer_block(tokens, weights, gain_pair, rel_terms):
    w_query, w_keyval, w_out, w_up, w_down = weights
    batch_rows, seq_len, model_width = tokens.shape
    head_count = rel_terms.shape[0]
    head_shape = (batch_rows, seq_len, head_count, model_width // head_count)
    first_norm = low(normed(tokens, gain_pair[0]))
    query_h = low(low_back(jnp.einsum('bsd,de->bse', first_norm, w_query, precision=PRECISE)))
    keyval = low(low_back(jnp.einsum('bsd,de->bse', first_norm, w_keyval, precision=PRECISE)))
    mixture = attend(query_h.reshape(head_shape), keyval[..., :model_width].reshape(head_shape), keyval[..., model_width:].reshape(head_shape), rel_terms)
    mixture = low(low_back(mixture.reshape(batch_rows, seq_len, model_width)))
    residual = tokens + low_back(jnp.einsum('bsd,de->bse', mixture, w_out, precision=PRECISE))
    second = low(normed(residual, gain_pair[1]))
    pre_act = low_back(jnp.einsum('bsd,df->bsf', second, w_up, precision=PRECISE))
    hidden = low(jax.nn.gelu(pre_act, approximate=True))
    return residual + low_back(jnp.einsum('bsf,fd->bsd', hidden, w_down, precision=PRECISE))

def reference(doc_tokens, queries, doc_cot, query_cot, q_weight, kv_weight, out_weight, up_weight, down_weight, attn_gain, ff_gain, rel_bias, doc_buckets, query_buckets, topk_mask, positives, pos_count):

    def forward(doc_x, query_x, w_query, w_keyval, w_out, w_up, w_down, gain_one, gain_two, bias_table):
        weights = (w_query, w_keyval, w_out, w_up, w_down)
        gain_pair = (gain_one, gain_two)
        doc_terms = jnp.transpose(bias_table[doc_buckets], (2, 0, 1))
        query_terms = jnp.transpose(bias_table[query_buckets], (2, 0, 1))
        doc_step = jax.checkpoint(lambda single: layer_block(single[None], weights, gain_pair, doc_terms)[0])
        doc_y = lax.map(doc_step, doc_x)
        group_size = math.gcd(QUERIES, max(1, 4096 // QLEN))
        grouped = query_x.reshape(QUERIES // group_size, group_size, QLEN, D)
        query_step = jax.checkpoint(lambda member: layer_block(member, weights, gain_pair, query_terms))
        query_y = lax.map(query_step, grouped).reshape(QUERIES, QLEN, D)
        return (doc_y, query_y)
    primals = (doc_tokens.astype(jnp.float32), queries.astype(jnp.float32), q_weight.astype(jnp.float32), kv_weight.astype(jnp.float32), out_weight.astype(jnp.float32), up_weight.astype(jnp.float32), down_weight.astype(jnp.float32), attn_gain, ff_gain, rel_bias)
    (doc_y, query_y), pullback = jax.vjp(forward, *primals)
    gradients = pullback((doc_cot.astype(jnp.float32), query_cot.astype(jnp.float32)))
    matches = positives[:, :, None] == jnp.arange(DOC_LEN, dtype=jnp.int32)[None, None, :]
    counted = jnp.arange(POS, dtype=jnp.int32)[None, :] < pos_count[:, None]
    retrieved = jnp.sum(jnp.where(matches & counted[:, :, None], topk_mask[:, None, :].astype(jnp.float32), 0.0))
    fraction = retrieved / float(QUERIES * POS)
    return (doc_y.astype(jnp.bfloat16), query_y.astype(jnp.bfloat16), gradients[0], gradients[1], gradients[2], gradients[3], gradients[4], gradients[5], gradients[6], gradients[7], gradients[8], gradients[9], fraction)
```

```python
import functools
import math

import jax
import jax.numpy as jnp
from jax import lax
from jax.experimental import pallas as pl
from jax.experimental.pallas import tpu as pltpu
from jax.sharding import PartitionSpec as P

EPSILON = 1e-06
BFLOAT = jnp.bfloat16
SINGLE = jnp.float32
FIXED = 8191.0
GELU_A = math.sqrt(2.0 / math.pi)
GELU_B = 0.044715
VMEM_LIMIT = 60 << 20


def nn(left, right):
    return jnp.dot(left, right, preferred_element_type=SINGLE)


def nt(left, right):
    return lax.dot_general(left, right, (((1,), (1,)), ((), ())), preferred_element_type=SINGLE)


def tn(left, right):
    return lax.dot_general(left, right, (((0,), (0,)), ((), ())), preferred_element_type=SINGLE)


def whole(shape):
    zeros = (0,) * len(shape)
    return pl.BlockSpec(shape, lambda *_: zeros, pipeline_mode=pl.Buffered(1))


def params():
    return pltpu.CompilerParams(vmem_limit_bytes=VMEM_LIMIT)


def cost(flops, moved):
    return pl.CostEstimate(flops=int(flops), bytes_accessed=int(moved), transcendentals=0)


def scale_of(values):
    return lax.rsqrt(jnp.mean(values * values, axis=-1, keepdims=True) + EPSILON)


def norm_back(values, scale, scaled_grad):
    dot = jnp.mean(values * scaled_grad, axis=-1, keepdims=True)
    return scale * (scaled_grad - values * (scale * scale * dot))


def first_lanes(shape, head_dim):
    return lax.broadcasted_iota(jnp.int32, shape, 1) < head_dim


def project_kernel(x_ref, gain_ref, wq_ref, wkv_ref, q_ref, kv_ref):
    values = x_ref[...].astype(SINGLE)
    normed = (values * scale_of(values) * gain_ref[...]).astype(BFLOAT)
    q_ref[...] = nn(normed, wq_ref[...]).astype(BFLOAT)
    kv_ref[...] = nn(normed, wkv_ref[...]).astype(BFLOAT)


def project(tokens, gain, w_query, w_keyval):
    rows, width = tokens.shape
    block = math.gcd(rows, 256)
    return pl.pallas_call(
        project_kernel,
        grid=(rows // block,),
        in_specs=[
            pl.BlockSpec((block, width), lambda i: (i, 0)),
            whole((1, width)),
            whole(w_query.shape),
            whole(w_keyval.shape),
        ],
        out_specs=[
            pl.BlockSpec((block, width), lambda i: (i, 0)),
            pl.BlockSpec((block, 2 * width), lambda i: (i, 0)),
        ],
        out_shape=[
            jax.ShapeDtypeStruct((rows, width), BFLOAT),
            jax.ShapeDtypeStruct((rows, 2 * width), BFLOAT),
        ],
        compiler_params=params(),
        cost_estimate=cost(6 * rows * width * width, 12 * rows * width),
    )(tokens, gain.reshape(1, width), w_query, w_keyval)


def doc_forward_kernel(q_ref, k_ref, v_ref, table_ref, bucket_ref, mix_ref, prob_ref):
    rows, width = q_ref.shape
    keys = k_ref.shape[0]
    heads = prob_ref.shape[0]
    head_dim = width // heads

    def pair(step, carry):
        lanes = pl.ds(pl.multiple_of(step * 2 * head_dim, 128), 2 * head_dim)
        q_pair = q_ref[:, lanes]
        k_pair = k_ref[:, lanes]
        v_pair = v_ref[:, lanes]
        wide = first_lanes(q_pair.shape, head_dim)
        tall = first_lanes(v_pair.shape, head_dim)
        table = jnp.broadcast_to(table_ref[pl.ds(step, 1), :], (rows, 128))
        packed = jnp.concatenate(
            [
                jnp.take_along_axis(
                    table,
                    bucket_ref[:, part * 128 : part * 128 + 128].astype(jnp.int32),
                    axis=1,
                    mode="promise_in_bounds",
                )
                for part in range(keys // 128)
            ],
            1,
        )
        total = None
        for side in range(2):
            mine = wide if side == 0 else ~wide
            mine_tall = tall if side == 0 else ~tall
            coded = (packed >> 16) if side == 0 else ((packed << 16) >> 16)
            scores = nt(jnp.where(mine, q_pair, 0), k_pair)
            scores = scores + coded.astype(SINGLE) * (1.0 / FIXED)
            shifted = jnp.exp(scores - jnp.max(scores, axis=-1, keepdims=True))
            inverse = 1.0 / jnp.sum(shifted, axis=-1, keepdims=True)
            soft = (shifted * inverse).astype(BFLOAT)
            prob_ref[2 * step + side] = soft
            term = nn(soft, jnp.where(mine_tall, v_pair, 0))
            total = term if total is None else total + term
        mix_ref[:, lanes] = total.astype(BFLOAT)
        return carry

    lax.fori_loop(0, heads // 2, pair, 0)


def doc_forward(q_rows, kv_rows, table, buckets, n_docs, rows, heads):
    width = q_rows.shape[1]
    keys = buckets.shape[1]
    block = math.gcd(rows, 256)
    steps = rows // block
    return pl.pallas_call(
        doc_forward_kernel,
        grid=(n_docs, steps),
        in_specs=[
            pl.BlockSpec((block, width), lambda d, i: (d * steps + i, 0)),
            pl.BlockSpec((keys, width), lambda d, i: (d, 0)),
            pl.BlockSpec((keys, width), lambda d, i: (d, 1)),
            whole(table.shape),
            pl.BlockSpec((block, keys), lambda d, i: (i, 0)),
        ],
        out_specs=[
            pl.BlockSpec((block, width), lambda d, i: (d * steps + i, 0)),
            pl.BlockSpec((heads, block, keys), lambda d, i: (0, d * steps + i, 0)),
        ],
        out_shape=[
            jax.ShapeDtypeStruct((n_docs * rows, width), BFLOAT),
            jax.ShapeDtypeStruct((heads, n_docs * rows, keys), BFLOAT),
        ],
        compiler_params=params(),
        cost_estimate=cost(30 * n_docs * rows * keys * width, 2 * heads * n_docs * rows * keys),
    )(q_rows, kv_rows, kv_rows, table, buckets)


def bucket_products(bucket_rows, grad_rows, labels):
    rows, keys = bucket_rows.shape
    numbers = bucket_rows.astype(jnp.int32)
    names = lax.broadcasted_iota(jnp.int32, (labels, keys), 0)
    parts = [
        jnp.where(jnp.broadcast_to(numbers[r : r + 1, :], (labels, keys)) == names, 1.0, 0.0).astype(
            BFLOAT
        )
        for r in range(rows)
    ]
    onehot = jnp.concatenate(parts, 0)
    return nt(onehot, grad_rows)


def attend_back(q_pair, k_pair, v_pair, da_pair, mix_pair, probs, head_dim):
    wide = first_lanes(q_pair.shape, head_dim)
    tall = first_lanes(k_pair.shape, head_dim)
    product = da_pair.astype(SINGLE) * mix_pair.astype(SINGLE)
    dq = dk = dv = None
    kept = []
    for side in range(2):
        mine = wide if side == 0 else ~wide
        mine_tall = tall if side == 0 else ~tall
        da_mine = jnp.where(mine, da_pair, 0)
        correction = jnp.sum(jnp.where(mine, product, 0.0), axis=-1, keepdims=True)
        grad_soft = nt(da_mine, v_pair)
        soft = probs[side]
        grad_scores = (soft.astype(SINGLE) * (grad_soft - correction)).astype(BFLOAT)
        kept.append(grad_scores)
        dq_term = nn(grad_scores, jnp.where(mine_tall, k_pair, 0))
        dk_term = tn(grad_scores, jnp.where(mine, q_pair, 0))
        dv_term = tn(soft, da_mine)
        dq = dq_term if dq is None else dq + dq_term
        dk = dk_term if dk is None else dk + dk_term
        dv = dv_term if dv is None else dv + dv_term
    return dq, dk, dv, kept


def doc_backward_kernel(
    labels,
    q_ref,
    k_ref,
    v_ref,
    da_ref,
    mix_ref,
    prob_ref,
    bucket_ref,
    dq_ref,
    dk_ref,
    dv_ref,
    sums_ref,
    dk_acc,
    dv_acc,
    ds_keep,
):
    rows, width = q_ref.shape
    heads = prob_ref.shape[0]
    keys = k_ref.shape[0]
    head_dim = width // heads
    doc, step_i = pl.program_id(0), pl.program_id(1)

    @pl.when(step_i == 0)
    def _():
        dk_acc[...] = jnp.zeros_like(dk_acc)
        dv_acc[...] = jnp.zeros_like(dv_acc)

    @pl.when((step_i == 0) & (doc == 0))
    def _():
        sums_ref[...] = jnp.zeros_like(sums_ref)

    def pair(step, carry):
        lanes = pl.ds(pl.multiple_of(step * 2 * head_dim, 128), 2 * head_dim)
        dq, dk, dv, kept = attend_back(
            q_ref[:, lanes],
            k_ref[:, lanes],
            v_ref[:, lanes],
            da_ref[:, lanes],
            mix_ref[:, lanes],
            [prob_ref[2 * step], prob_ref[2 * step + 1]],
            head_dim,
        )
        ds_keep[2 * step] = kept[0]
        ds_keep[2 * step + 1] = kept[1]
        dq_ref[:, lanes] = dq.astype(BFLOAT)
        dk_acc[:, lanes] += dk
        dv_acc[:, lanes] += dv
        return carry

    lax.fori_loop(0, heads // 2, pair, 0)

    def group(number, carry):
        span = pl.ds(pl.multiple_of(number * 16, 16), 16)
        sums_ref[...] += bucket_products(
            bucket_ref[span, :], ds_keep[:, span, :].reshape(heads * 16, keys), labels
        )
        return carry

    lax.fori_loop(0, rows // 16, group, 0)

    @pl.when(step_i == pl.num_programs(1) - 1)
    def _():
        dk_ref[...] = dk_acc[...].astype(BFLOAT)
        dv_ref[...] = dv_acc[...].astype(BFLOAT)


def doc_backward(q_rows, kv_rows, da_rows, mixture, probs, buckets, n_docs, rows, labels):
    width = q_rows.shape[1]
    heads = probs.shape[0]
    keys = buckets.shape[1]
    block = math.gcd(rows, 256)
    steps = rows // block
    along = pl.BlockSpec((block, width), lambda d, i: (d * steps + i, 0))
    per_doc = pl.BlockSpec((keys, width), lambda d, i: (d, 0))
    return pl.pallas_call(
        functools.partial(doc_backward_kernel, labels),
        grid=(n_docs, steps),
        in_specs=[
            along,
            per_doc,
            pl.BlockSpec((keys, width), lambda d, i: (d, 1)),
            along,
            along,
            pl.BlockSpec((heads, block, keys), lambda d, i: (0, d * steps + i, 0)),
            pl.BlockSpec((block, keys), lambda d, i: (i, 0)),
        ],
        out_specs=[along, per_doc, per_doc, whole((16 * labels, heads * 16))],
        out_shape=[
            jax.ShapeDtypeStruct((n_docs * rows, width), BFLOAT),
            jax.ShapeDtypeStruct((n_docs * keys, width), BFLOAT),
            jax.ShapeDtypeStruct((n_docs * keys, width), BFLOAT),
            jax.ShapeDtypeStruct((16 * labels, heads * 16), SINGLE),
        ],
        scratch_shapes=[
            pltpu.VMEM((keys, width), SINGLE),
            pltpu.VMEM((keys, width), SINGLE),
            pltpu.VMEM((heads, block, keys), BFLOAT),
        ],
        compiler_params=params(),
        cost_estimate=cost(70 * n_docs * rows * keys * width, 2 * heads * n_docs * rows * keys),
    )(q_rows, kv_rows, kv_rows, da_rows, mixture, probs, buckets)


def query_forward_kernel(q_ref, kv_ref, table_ref, bucket_ref, mix_ref, prob_ref):
    rows, width = q_ref.shape
    heads = prob_ref.shape[0]
    head_dim = width // heads
    index = bucket_ref[...]
    for step in range(heads // 2):
        lanes = slice(step * 2 * head_dim, (step + 1) * 2 * head_dim)
        q_pair = q_ref[:, lanes]
        k_pair = kv_ref[:, lanes]
        v_pair = kv_ref[:, width + lanes.start : width + lanes.stop]
        wide = first_lanes(q_pair.shape, head_dim)
        total = None
        for side in range(2):
            head = 2 * step + side
            mine = wide if side == 0 else ~wide
            table = jnp.broadcast_to(table_ref[head : head + 1, :], (rows, 128))
            bias = jnp.take_along_axis(table, index, axis=1, mode="promise_in_bounds")
            scores = nt(jnp.where(mine, q_pair, 0), k_pair) + bias
            shifted = jnp.exp(scores - jnp.max(scores, axis=-1, keepdims=True))
            inverse = 1.0 / jnp.sum(shifted, axis=-1, keepdims=True)
            soft = (shifted * inverse).astype(BFLOAT)
            prob_ref[head] = soft
            term = nn(soft, jnp.where(mine, v_pair, 0))
            total = term if total is None else total + term
        mix_ref[:, lanes] = total.astype(BFLOAT)


def query_forward(q_rows, kv_rows, table, buckets, start, count, heads):
    width = q_rows.shape[1]
    offset = start // 128
    return pl.pallas_call(
        query_forward_kernel,
        grid=(count // 128,),
        in_specs=[
            pl.BlockSpec((128, width), lambda i: (offset + i, 0)),
            pl.BlockSpec((128, 2 * width), lambda i: (offset + i, 0)),
            whole(table.shape),
            whole(buckets.shape),
        ],
        out_specs=[
            pl.BlockSpec((128, width), lambda i: (i, 0)),
            pl.BlockSpec((heads, 128, 128), lambda i: (0, i, 0)),
        ],
        out_shape=[
            jax.ShapeDtypeStruct((count, width), BFLOAT),
            jax.ShapeDtypeStruct((heads, count, 128), BFLOAT),
        ],
        compiler_params=params(),
        cost_estimate=cost(4 * count * 128 * width * 4, 10 * count * width),
    )(q_rows, kv_rows, table, buckets)


def query_backward_kernel(
    labels, q_ref, kv_ref, da_ref, mix_ref, prob_ref, bucket_ref, dq_ref, dkv_ref, sums_ref, ds_keep
):
    rows, width = q_ref.shape
    heads = prob_ref.shape[0]
    head_dim = width // heads

    @pl.when(pl.program_id(0) == 0)
    def _():
        sums_ref[...] = jnp.zeros_like(sums_ref)

    for step in range(heads // 2):
        lanes = slice(step * 2 * head_dim, (step + 1) * 2 * head_dim)
        right = slice(width + lanes.start, width + lanes.stop)
        dq, dk, dv, kept = attend_back(
            q_ref[:, lanes],
            kv_ref[:, lanes],
            kv_ref[:, right],
            da_ref[:, lanes],
            mix_ref[:, lanes],
            [prob_ref[2 * step], prob_ref[2 * step + 1]],
            head_dim,
        )
        ds_keep[2 * step] = kept[0]
        ds_keep[2 * step + 1] = kept[1]
        dq_ref[:, lanes] = dq.astype(BFLOAT)
        dkv_ref[:, lanes] = dk.astype(BFLOAT)
        dkv_ref[:, right] = dv.astype(BFLOAT)

    def group(number, carry):
        span = pl.ds(pl.multiple_of(number * 16, 16), 16)
        sums_ref[...] += bucket_products(
            bucket_ref[span, :], ds_keep[:, span, :].reshape(heads * 16, rows), labels
        )
        return carry

    lax.fori_loop(0, rows // 16, group, 0)


def query_backward(q_rows, kv_rows, da_rows, mixture, probs, buckets, start, labels):
    width = q_rows.shape[1]
    heads, count, _ = probs.shape
    offset = start // 128
    return pl.pallas_call(
        functools.partial(query_backward_kernel, labels),
        grid=(count // 128,),
        in_specs=[
            pl.BlockSpec((128, width), lambda i: (offset + i, 0)),
            pl.BlockSpec((128, 2 * width), lambda i: (offset + i, 0)),
            pl.BlockSpec((128, width), lambda i: (offset + i, 0)),
            pl.BlockSpec((128, width), lambda i: (offset + i, 0)),
            pl.BlockSpec((heads, 128, 128), lambda i: (0, i, 0)),
            whole(buckets.shape),
        ],
        out_specs=[
            pl.BlockSpec((128, width), lambda i: (i, 0)),
            pl.BlockSpec((128, 2 * width), lambda i: (i, 0)),
            whole((16 * labels, heads * 16)),
        ],
        out_shape=[
            jax.ShapeDtypeStruct((count, width), BFLOAT),
            jax.ShapeDtypeStruct((count, 2 * width), BFLOAT),
            jax.ShapeDtypeStruct((16 * labels, heads * 16), SINGLE),
        ],
        scratch_shapes=[pltpu.VMEM((heads, 128, 128), BFLOAT)],
        compiler_params=params(),
        cost_estimate=cost(8 * count * 128 * width * 4, 14 * count * width),
    )(q_rows, kv_rows, da_rows, mixture, probs, buckets)


def feed_kernel(
    chunk,
    x_ref,
    mix_ref,
    dy_ref,
    gain_ref,
    wo_ref,
    wu_ref,
    wd_ref,
    y_ref,
    dh_ref,
    da_ref,
    go_ref,
    gu_ref,
    gd_ref,
    gg_ref,
    go_acc,
    gu_acc,
    gd_acc,
    stage,
    sems,
):
    step = pl.program_id(0)
    hidden = wu_ref.shape[1]
    width = wu_ref.shape[0]

    @pl.when(step == 0)
    def _():
        go_acc[...] = jnp.zeros_like(go_acc)
        gu_acc[...] = jnp.zeros_like(gu_acc)
        gd_acc[...] = jnp.zeros_like(gd_acc)
        gg_ref[...] = jnp.zeros_like(gg_ref)

    mixture = mix_ref[...]
    dy = dy_ref[...]
    gain = gain_ref[...]
    residual = x_ref[...].astype(SINGLE) + nn(mixture, wo_ref[...])
    scale = scale_of(residual)
    second = (residual * scale * gain).astype(BFLOAT)
    y = residual
    grad_second = jnp.zeros_like(residual)
    for part in range(hidden // chunk):
        span = slice(part * chunk, (part + 1) * chunk)
        pre = nn(second, wu_ref[:, span])
        grad_hidden = nt(dy, wd_ref[span, :])
        square = pre * pre
        tanh = jnp.tanh(pre * (GELU_A + (GELU_A * GELU_B) * square))
        half = 0.5 + 0.5 * tanh
        act = pre * half
        slope = half + act * (1.0 - tanh) * (GELU_A + (3.0 * GELU_A * GELU_B) * square)
        act_low = act.astype(BFLOAT)
        grad_pre = (grad_hidden * slope).astype(BFLOAT)
        y = y + nn(act_low, wd_ref[span, :])
        grad_second = grad_second + nt(grad_pre, wu_ref[:, span])
        gd_acc[span, :] += tn(act_low, dy)
        gu_acc[:, span] += tn(second, grad_pre)
    y_ref[...] = y.astype(BFLOAT)
    gg_ref[...] += jnp.sum(grad_second * residual * scale, axis=0, keepdims=True)
    grad_res = dy.astype(SINGLE) + norm_back(residual, scale, grad_second * gain)
    dh_ref[...] = grad_res
    grad_low = grad_res.astype(BFLOAT)
    da_ref[...] = nt(grad_low, wo_ref[...]).astype(BFLOAT)
    go_acc[...] += tn(mixture, grad_low)

    @pl.when(step == pl.num_programs(0) - 1)
    def _():
        pieces = []
        rows, columns = stage.shape[1:]
        for acc, out in ((gd_acc, gd_ref), (gu_acc, gu_ref), (go_acc, go_ref)):
            for r in range(acc.shape[0] // rows):
                for c in range(acc.shape[1] // columns):
                    spot = (pl.ds(r * rows, rows), pl.ds(c * columns, columns))
                    pieces.append((acc, out, spot))
        flying = [None, None]
        for number, (acc, out, spot) in enumerate(pieces):
            slot = number % 2
            if flying[slot] is not None:
                flying[slot].wait()
            stage[slot] = acc[spot].astype(BFLOAT)
            flying[slot] = pltpu.make_async_copy(stage.at[slot], out.at[spot], sems.at[slot])
            flying[slot].start()
        for copy in flying:
            if copy is not None:
                copy.wait()


def feed(tokens, mixture, cotangent, gain, w_out, w_up, w_down):
    rows, width = tokens.shape
    hidden = w_up.shape[1]
    block = math.gcd(rows, 256)
    along = pl.BlockSpec((block, width), lambda i: (i, 0))
    anywhere = pl.BlockSpec(memory_space=pl.ANY)
    return pl.pallas_call(
        functools.partial(feed_kernel, math.gcd(hidden, 768)),
        grid=(rows // block,),
        in_specs=[
            along,
            along,
            along,
            whole((1, width)),
            whole(w_out.shape),
            whole(w_up.shape),
            whole(w_down.shape),
        ],
        out_specs=[along, along, along, anywhere, anywhere, anywhere, whole((1, width))],
        out_shape=[
            jax.ShapeDtypeStruct((rows, width), BFLOAT),
            jax.ShapeDtypeStruct((rows, width), SINGLE),
            jax.ShapeDtypeStruct((rows, width), BFLOAT),
            jax.ShapeDtypeStruct(w_out.shape, BFLOAT),
            jax.ShapeDtypeStruct(w_up.shape, BFLOAT),
            jax.ShapeDtypeStruct(w_down.shape, BFLOAT),
            jax.ShapeDtypeStruct((1, width), SINGLE),
        ],
        scratch_shapes=[
            pltpu.VMEM(w_out.shape, SINGLE),
            pltpu.VMEM(w_up.shape, SINGLE),
            pltpu.VMEM(w_down.shape, SINGLE),
            pltpu.VMEM((2, width, width), BFLOAT),
            pltpu.SemaphoreType.DMA((2,)),
        ],
        compiler_params=params(),
        cost_estimate=cost(2 * rows * width * (6 * hidden + 3 * width), 14 * rows * width),
    )(tokens, mixture, cotangent, gain.reshape(1, width), w_out, w_up, w_down)


def unproject_kernel(
    x_ref, gain_ref, dq_ref, dk_ref, dv_ref, dh_ref, wq_ref, wkv_ref, dx_ref, gq_ref, gkv_ref, gg_ref, gq_acc, gkv_acc
):
    step = pl.program_id(0)
    width = wq_ref.shape[0]

    @pl.when(step == 0)
    def _():
        gq_acc[...] = jnp.zeros_like(gq_acc)
        gkv_acc[...] = jnp.zeros_like(gkv_acc)
        gg_ref[...] = jnp.zeros_like(gg_ref)

    values = x_ref[...].astype(SINGLE)
    gain = gain_ref[...]
    scale = scale_of(values)
    normed = (values * scale * gain).astype(BFLOAT)
    dq, dk, dv = dq_ref[...], dk_ref[...], dv_ref[...]
    gq_acc[...] += tn(normed, dq)
    gkv_acc[:, :width] += tn(normed, dk)
    gkv_acc[:, width:] += tn(normed, dv)
    grad = nt(dq, wq_ref[...]) + nt(dk, wkv_ref[:, :width]) + nt(dv, wkv_ref[:, width:])
    gg_ref[...] += jnp.sum(grad * values * scale, axis=0, keepdims=True)
    dx_ref[...] = dh_ref[...] + norm_back(values, scale, grad * gain)

    @pl.when(step == pl.num_programs(0) - 1)
    def _():
        gq_ref[...] = gq_acc[...].astype(BFLOAT)
        gkv_ref[...] = gkv_acc[...].astype(BFLOAT)


def unproject(tokens, gain, dq, dk, dv, grad_res, w_query, w_keyval):
    rows, width = tokens.shape
    block = math.gcd(rows, 256)
    along = pl.BlockSpec((block, width), lambda i: (i, 0))
    return pl.pallas_call(
        unproject_kernel,
        grid=(rows // block,),
        in_specs=[
            along,
            whole((1, width)),
            along,
            along,
            along,
            along,
            whole(w_query.shape),
            whole(w_keyval.shape),
        ],
        out_specs=[along, whole(w_query.shape), whole(w_keyval.shape), whole((1, width))],
        out_shape=[
            jax.ShapeDtypeStruct((rows, width), SINGLE),
            jax.ShapeDtypeStruct(w_query.shape, BFLOAT),
            jax.ShapeDtypeStruct(w_keyval.shape, BFLOAT),
            jax.ShapeDtypeStruct((1, width), SINGLE),
        ],
        scratch_shapes=[pltpu.VMEM(w_query.shape, SINGLE), pltpu.VMEM(w_keyval.shape, SINGLE)],
        compiler_params=params(),
        cost_estimate=cost(12 * rows * width * width, 18 * rows * width),
    )(tokens, gain.reshape(1, width), dq, dk, dv, grad_res, w_query, w_keyval)


def bits_of(count):
    return [1 << place for place in reversed(range(count.bit_length() - 1))]


def axis_bits():
    dp_bits = [("dp", bit) for bit in bits_of(lax.axis_size("dp"))]
    seq_bits = [("seq", bit) for bit in bits_of(lax.axis_size("seq"))]
    return dp_bits, seq_bits


def gather_orders():
    dp_bits, seq_bits = axis_bits()
    far = (len(dp_bits) + 1) // 2
    z_bits, x_bits = dp_bits[:far], dp_bits[far:]
    y_bits, core_bits = seq_bits[:-1], seq_bits[-1:]
    return [z_bits + y_bits + x_bits + core_bits, z_bits + x_bits + y_bits + core_bits]


def swap(values, name, bit):
    count = lax.axis_size(name)
    return lax.ppermute(values, name, [(i, i ^ bit) for i in range(count)])


def is_high(name, bit):
    return (lax.axis_index(name) & bit) != 0


def gather_rows(shard, order):
    dp_bits, seq_bits = axis_bits()
    everything = dp_bits + seq_bits
    done = []
    held = shard
    for item in order:
        other = swap(held, *item)
        done.append(item)
        place = sorted(everything.index(one) for one in done).index(everything.index(item))
        high = is_high(*item)
        held = jnp.where(
            high, jnp.stack([other, held], place), jnp.stack([held, other], place)
        )
    return held.reshape(-1, shard.shape[1])


def gather_weights(shards, orders):
    pieces = []
    for shard, order in zip(shards, orders):
        pieces.append(gather_rows(shard, order))
    return pieces


def scatter_rows(values, order):
    dp_bits, seq_bits = axis_bits()
    left = dp_bits + seq_bits
    rows = values.shape[0] >> len(left)
    held = values.reshape((2,) * len(left) + (rows, values.shape[1]))
    for item in order:
        place = left.index(item)
        mine = is_high(*item).astype(jnp.int32)
        away = lax.dynamic_index_in_dim(held, 1 - mine, place, keepdims=False)
        kept = lax.dynamic_index_in_dim(held, mine, place, keepdims=False)
        other = swap(away, *item)
        held = kept.astype(SINGLE) + other.astype(SINGLE)
        left.remove(item)
        if left:
            held = held.astype(BFLOAT)
    return held


def scatter_columns(values, parts):
    orders = [order[::-1] for order in gather_orders()]
    columns = values.shape[1] // parts
    return jnp.concatenate(
        [
            scatter_rows(values[:, p * columns : (p + 1) * columns], orders[p % len(orders)])
            for p in range(parts)
        ],
        1,
    )


def sum_all(values):
    dp_bits, seq_bits = axis_bits()
    for item in seq_bits[::-1] + dp_bits[::-1]:
        values = values + swap(values, *item)
    return values


def own_document(shard):
    count = lax.axis_size("seq")
    n_docs = shard.shape[0]
    me = lax.axis_index("seq")
    if n_docs >= count:
        per = n_docs // count
        blocks = shard.reshape((count, per) + shard.shape[1:])
        sets, group = count, 1
    else:
        blocks = shard[:, None]
        sets, group = n_docs, count // n_docs
    got = []
    for r in range(sets):
        piece = lax.dynamic_index_in_dim(blocks, (me % sets) ^ r, 0, keepdims=False)
        route = [
            (u * sets + i, (i ^ r) * group + u) for u in range(group) for i in range(sets)
        ]
        if any(a != b for a, b in route):
            piece = lax.ppermute(piece, "seq", route)
        got.append(piece)
    stacked = jnp.stack(got, 0)
    mine = me // group
    ordered = [lax.dynamic_index_in_dim(stacked, mine ^ i, 0, keepdims=False) for i in range(sets)]
    return jnp.concatenate(ordered, 1).reshape(-1, shard.shape[-1])


def spread_document(rows, like):
    count = lax.axis_size("seq")
    n_docs, shard_rows, width = like.shape
    me = lax.axis_index("seq")
    if n_docs >= count:
        per = n_docs // count
        sets, group = count, 1
    else:
        per = 1
        sets, group = n_docs, count // n_docs
    blocks = rows.reshape(per, sets, shard_rows, width)
    mine = me // group
    got = []
    for r in range(sets):
        piece = lax.dynamic_index_in_dim(blocks, mine ^ r, 1, keepdims=False)
        route = [
            ((i ^ r) * group + u, u * sets + i) for u in range(group) for i in range(sets)
        ]
        if any(a != b for a, b in route):
            piece = lax.ppermute(piece, "seq", route)
        got.append(piece)
    stacked = jnp.stack(got, 0)
    ordered = [
        lax.dynamic_index_in_dim(stacked, (me % sets) ^ i, 0, keepdims=False) for i in range(sets)
    ]
    return jnp.concatenate(ordered, 0)


def gather_positions(shard):
    seq_bits = axis_bits()[1]
    done = []
    held = shard
    for item in seq_bits:
        other = swap(held, *item)
        high = is_high(*item)
        place = len(done)
        held = jnp.where(
            high, jnp.stack([other, held], place), jnp.stack([held, other], place)
        )
        done.append(item)
    return held.reshape(-1, shard.shape[1])


def on_device(
    doc_tokens,
    queries,
    doc_cot,
    query_cot,
    q_weight,
    kv_weight,
    out_weight,
    up_weight,
    down_weight,
    attn_gain,
    ff_gain,
    rel_bias,
    doc_buckets,
    query_buckets,
    topk_mask,
    positives,
    pos_count,
):
    n_docs, shard_rows, width = doc_tokens.shape
    n_query, query_len, _ = queries.shape
    bucket_count, heads = rel_bias.shape
    doc_len = doc_buckets.shape[1]
    doc_rows = n_docs * shard_rows
    query_total = n_query * query_len
    seq_size = lax.axis_size("seq")
    group = max(1, seq_size // n_docs)
    local_docs = max(1, n_docs // seq_size)
    local_rows = doc_len // group
    orders = gather_orders()

    tokens = jnp.concatenate(
        [own_document(doc_tokens), queries.reshape(query_total, width)], 0
    )
    w_query, w_key, w_value = gather_weights(
        [q_weight, kv_weight[:, :width], kv_weight[:, width:]], [orders[0], orders[1], orders[0]]
    )
    w_keyval = jnp.concatenate([w_key, w_value], 1)
    buckets = gather_positions(doc_buckets.astype(jnp.int16))
    if group > 1:
        part = lax.axis_index("seq") % group
        buckets = lax.dynamic_slice_in_dim(buckets, part * local_rows, local_rows, 0)

    fixed = jnp.round(rel_bias.T * FIXED).astype(jnp.int32)
    packed = (fixed[0::2] << 16) | (fixed[1::2] & 0xFFFF)
    doc_table = jnp.zeros((8, 128), jnp.int32).at[: heads // 2, :bucket_count].set(packed)
    query_table = jnp.zeros((16, 128), SINGLE).at[:heads, :bucket_count].set(rel_bias.T)
    query_table = query_table.at[:, bucket_count].set(-1e30)
    repeats = 128 // query_len
    same = jnp.kron(jnp.eye(repeats, dtype=jnp.int32), jnp.ones_like(query_buckets))
    tiled = jnp.where(same == 1, jnp.tile(query_buckets, (repeats, repeats)), bucket_count)

    q_rows, kv_rows = project(tokens, attn_gain, w_query, w_keyval)
    if group > 1:
        teams = [list(range(t * group, (t + 1) * group)) for t in range(seq_size // group)]
        kv_docs = lax.all_gather(
            kv_rows[:doc_rows], "seq", axis=0, tiled=True, axis_index_groups=teams
        )
    else:
        kv_docs = kv_rows
    doc_mix, doc_probs = doc_forward(
        q_rows, kv_docs, doc_table, buckets, local_docs, local_rows, heads
    )
    query_mix, query_probs = query_forward(
        q_rows, kv_rows, query_table, tiled, doc_rows, query_total, heads
    )
    mixture = jnp.concatenate([doc_mix, query_mix], 0)
    half = out_weight.shape[1] // 2
    half_up = up_weight.shape[1] // 2
    o1, o2, u1, u2, d1, d2 = gather_weights(
        [
            out_weight[:, :half],
            out_weight[:, half:],
            up_weight[:, :half_up],
            up_weight[:, half_up:],
            down_weight[:, :half],
            down_weight[:, half:],
        ],
        [orders[0], orders[1]] * 3,
    )
    w_out = jnp.concatenate([o1, o2], 1)
    w_up = jnp.concatenate([u1, u2], 1)
    w_down = jnp.concatenate([d1, d2], 1)
    cotangent = jnp.concatenate(
        [own_document(doc_cot), query_cot.reshape(query_total, width)], 0
    )
    outputs, grad_res, grad_mix, grad_out, grad_up, grad_down, grad_ff = feed(
        tokens, mixture, cotangent, ff_gain, w_out, w_up, w_down
    )
    grad_down_shard = scatter_columns(grad_down, 2)
    grad_up_shard = scatter_columns(grad_up, 2)
    grad_out_shard = scatter_columns(grad_out, 2)
    doc_out = spread_document(outputs[:doc_rows], doc_tokens)
    query_out = outputs[doc_rows:].reshape(queries.shape)

    doc_dq, doc_dk, doc_dv, doc_sums = doc_backward(
        q_rows, kv_docs, grad_mix, doc_mix, doc_probs, buckets, local_docs, local_rows, bucket_count
    )
    if group > 1:
        both = jnp.concatenate([doc_dk, doc_dv], 1)
        both = lax.psum_scatter(
            both, "seq", scatter_dimension=0, tiled=True, axis_index_groups=teams
        )
        doc_dk, doc_dv = both[:, :width], both[:, width:]
    query_dq, query_dkv, query_sums = query_backward(
        q_rows, kv_rows, grad_mix, mixture, query_probs, tiled, doc_rows, bucket_count
    )
    dq = jnp.concatenate([doc_dq, query_dq], 0)
    dk = jnp.concatenate([doc_dk, query_dkv[:, :width]], 0)
    dv = jnp.concatenate([doc_dv, query_dkv[:, width:]], 0)
    grad_tokens, grad_q, grad_kv, grad_attn = unproject(
        tokens, attn_gain, dq, dk, dv, grad_res, w_query, w_keyval
    )
    grad_q_shard = scatter_columns(grad_q, 2)
    grad_kv_shard = scatter_columns(grad_kv, 2)
    doc_dx = spread_document(grad_tokens[:doc_rows].astype(BFLOAT), doc_tokens).astype(SINGLE)
    query_dx = grad_tokens[doc_rows:].reshape(queries.shape)

    sums = (doc_sums + query_sums).reshape(16, bucket_count, heads, 16)
    keep = jnp.eye(16, dtype=SINGLE)[:, None, None, :]
    bias_local = jnp.sum(sums * keep, axis=(0, 3))
    matches = positives[:, :, None] == jnp.arange(doc_len, dtype=jnp.int32)[None, None, :]
    counted = jnp.arange(positives.shape[1], dtype=jnp.int32)[None, :] < pos_count[:, None]
    retrieved = jnp.sum(
        jnp.where(matches & counted[:, :, None], topk_mask[:, None, :].astype(SINGLE), 0.0)
    )
    flat = jnp.concatenate(
        [grad_attn[0], grad_ff[0], bias_local.reshape(-1), jnp.full((128,), retrieved)]
    )
    total = sum_all(flat)
    slots = float(n_query * lax.axis_size("dp") * seq_size * positives.shape[1])
    return (
        doc_out,
        query_out,
        doc_dx,
        query_dx,
        grad_q_shard,
        grad_kv_shard,
        grad_out_shard,
        grad_up_shard,
        grad_down_shard,
        total[:width],
        total[width : 2 * width],
        total[2 * width : 2 * width + bucket_count * heads].reshape(bucket_count, heads),
        total[-1] / slots,
    )


def solution(mesh):
    rows_all = P(("dp", "seq"), None)
    return jax.shard_map(
        on_device,
        mesh=mesh,
        in_specs=(
            P("dp", "seq", None),
            P(("dp", "seq"), None, None),
            P("dp", "seq", None),
            P(("dp", "seq"), None, None),
            rows_all,
            rows_all,
            rows_all,
            rows_all,
            rows_all,
            P(),
            P(),
            P(),
            P("seq", None),
            P(),
            rows_all,
            rows_all,
            P(("dp", "seq")),
        ),
        out_specs=(
            P("dp", "seq", None),
            P(("dp", "seq"), None, None),
            P("dp", "seq", None),
            P(("dp", "seq"), None, None),
            rows_all,
            rows_all,
            rows_all,
            rows_all,
            rows_all,
            P(),
            P(),
            P(),
            P(),
        ),
        check_vma=False,
    )
```

```python
import functools
import math

import jax
import jax.numpy as jnp
from jax import lax
from jax.experimental import pallas as pl
from jax.experimental.pallas import tpu as pltpu
from jax.sharding import PartitionSpec as P

EPSILON = 1e-06
BFLOAT = jnp.bfloat16
SINGLE = jnp.float32
FIXED = 8191.0
GELU_A = math.sqrt(2.0 / math.pi)
GELU_B = 0.044715
VMEM_LIMIT = 60 << 20


def nn(left, right):
    return jnp.dot(left, right, preferred_element_type=SINGLE)


def nt(left, right):
    return lax.dot_general(left, right, (((1,), (1,)), ((), ())), preferred_element_type=SINGLE)


def tn(left, right):
    return lax.dot_general(left, right, (((0,), (0,)), ((), ())), preferred_element_type=SINGLE)


def whole(shape):
    zeros = (0,) * len(shape)
    return pl.BlockSpec(shape, lambda *_: zeros, pipeline_mode=pl.Buffered(1))


def params():
    return pltpu.CompilerParams(vmem_limit_bytes=VMEM_LIMIT)


def cost(flops, moved):
    return pl.CostEstimate(flops=int(flops), bytes_accessed=int(moved), transcendentals=0)


def scale_of(values):
    return lax.rsqrt(jnp.mean(values * values, axis=-1, keepdims=True) + EPSILON)


def norm_back(values, scale, scaled_grad):
    dot = jnp.mean(values * scaled_grad, axis=-1, keepdims=True)
    return scale * (scaled_grad - values * (scale * scale * dot))


def first_lanes(shape, head_dim):
    return lax.broadcasted_iota(jnp.int32, shape, 1) < head_dim


def project_kernel(x_ref, gain_ref, w_ref, q_ref, kv_ref):
    values = x_ref[...].astype(SINGLE)
    normed = (values * scale_of(values) * gain_ref[...]).astype(BFLOAT)
    width = values.shape[1]
    q_ref[...] = nn(normed, w_ref[:, :width]).astype(BFLOAT)
    kv_ref[...] = nn(normed, w_ref[:, width:]).astype(BFLOAT)


def project(tokens, gain, w_qkv):
    rows, width = tokens.shape
    block = math.gcd(rows, 256)
    return pl.pallas_call(
        project_kernel,
        grid=(rows // block,),
        in_specs=[
            pl.BlockSpec((block, width), lambda i: (i, 0)),
            whole((1, width)),
            whole(w_qkv.shape),
        ],
        out_specs=[
            pl.BlockSpec((block, width), lambda i: (i, 0)),
            pl.BlockSpec((block, 2 * width), lambda i: (i, 0)),
        ],
        out_shape=[
            jax.ShapeDtypeStruct((rows, width), BFLOAT),
            jax.ShapeDtypeStruct((rows, 2 * width), BFLOAT),
        ],
        compiler_params=params(),
        cost_estimate=cost(6 * rows * width * width, 12 * rows * width),
    )(tokens, gain.reshape(1, width), w_qkv)


def doc_forward_kernel(q_ref, k_ref, v_ref, table_ref, bucket_ref, mix_ref, prob_ref):
    rows, width = q_ref.shape
    keys = k_ref.shape[0]
    heads = prob_ref.shape[0]
    head_dim = width // heads

    def pair(step, carry):
        lanes = pl.ds(pl.multiple_of(step * 2 * head_dim, 128), 2 * head_dim)
        q_pair = q_ref[:, lanes]
        k_pair = k_ref[:, lanes]
        v_pair = v_ref[:, lanes]
        wide = first_lanes(q_pair.shape, head_dim)
        tall = first_lanes(v_pair.shape, head_dim)
        table = jnp.broadcast_to(table_ref[pl.ds(step, 1), :], (rows, 128))
        packed = jnp.concatenate(
            [
                jnp.take_along_axis(
                    table,
                    bucket_ref[:, part * 128 : part * 128 + 128].astype(jnp.int32),
                    axis=1,
                    mode="promise_in_bounds",
                )
                for part in range(keys // 128)
            ],
            1,
        )
        total = None
        for side in range(2):
            mine = wide if side == 0 else ~wide
            mine_tall = tall if side == 0 else ~tall
            coded = (packed >> 16) if side == 0 else ((packed << 16) >> 16)
            scores = nt(jnp.where(mine, q_pair, 0), k_pair)
            scores = scores + coded.astype(SINGLE) * (1.0 / FIXED)
            shifted = jnp.exp(scores - jnp.max(scores, axis=-1, keepdims=True))
            inverse = 1.0 / jnp.sum(shifted, axis=-1, keepdims=True)
            soft = (shifted * inverse).astype(BFLOAT)
            prob_ref[2 * step + side] = soft
            term = nn(soft, jnp.where(mine_tall, v_pair, 0))
            total = term if total is None else total + term
        mix_ref[:, lanes] = total.astype(BFLOAT)
        return carry

    lax.fori_loop(0, heads // 2, pair, 0)


def doc_forward(q_rows, kv_rows, table, buckets, n_docs, rows, heads):
    width = q_rows.shape[1]
    keys = buckets.shape[1]
    block = math.gcd(rows, 256)
    steps = rows // block
    return pl.pallas_call(
        doc_forward_kernel,
        grid=(n_docs, steps),
        in_specs=[
            pl.BlockSpec((block, width), lambda d, i: (d * steps + i, 0)),
            pl.BlockSpec((keys, width), lambda d, i: (d, 0)),
            pl.BlockSpec((keys, width), lambda d, i: (d, 1)),
            whole(table.shape),
            pl.BlockSpec((block, keys), lambda d, i: (i, 0)),
        ],
        out_specs=[
            pl.BlockSpec((block, width), lambda d, i: (d * steps + i, 0)),
            pl.BlockSpec((heads, block, keys), lambda d, i: (0, d * steps + i, 0)),
        ],
        out_shape=[
            jax.ShapeDtypeStruct((n_docs * rows, width), BFLOAT),
            jax.ShapeDtypeStruct((heads, n_docs * rows, keys), BFLOAT),
        ],
        compiler_params=params(),
        cost_estimate=cost(30 * n_docs * rows * keys * width, 2 * heads * n_docs * rows * keys),
    )(q_rows, kv_rows, kv_rows, table, buckets)


def bucket_products(bucket_rows, grad_rows, labels):
    rows, keys = bucket_rows.shape
    numbers = bucket_rows.astype(jnp.int32)
    names = lax.broadcasted_iota(jnp.int32, (labels, keys), 0)
    parts = [
        jnp.where(jnp.broadcast_to(numbers[r : r + 1, :], (labels, keys)) == names, 1.0, 0.0).astype(
            BFLOAT
        )
        for r in range(rows)
    ]
    onehot = jnp.concatenate(parts, 0)
    return nt(onehot, grad_rows)


def attend_back(q_pair, k_pair, v_pair, da_pair, mix_pair, probs, head_dim):
    wide = first_lanes(q_pair.shape, head_dim)
    tall = first_lanes(k_pair.shape, head_dim)
    product = da_pair.astype(SINGLE) * mix_pair.astype(SINGLE)
    dq = dk = dv = None
    kept = []
    for side in range(2):
        mine = wide if side == 0 else ~wide
        mine_tall = tall if side == 0 else ~tall
        da_mine = jnp.where(mine, da_pair, 0)
        correction = jnp.sum(jnp.where(mine, product, 0.0), axis=-1, keepdims=True)
        grad_soft = nt(da_mine, v_pair)
        soft = probs[side]
        grad_scores = (soft.astype(SINGLE) * (grad_soft - correction)).astype(BFLOAT)
        kept.append(grad_scores)
        dq_term = nn(grad_scores, jnp.where(mine_tall, k_pair, 0))
        dk_term = tn(grad_scores, jnp.where(mine, q_pair, 0))
        dv_term = tn(soft, da_mine)
        dq = dq_term if dq is None else dq + dq_term
        dk = dk_term if dk is None else dk + dk_term
        dv = dv_term if dv is None else dv + dv_term
    return dq, dk, dv, kept


def doc_backward_kernel(
    labels,
    q_ref,
    k_ref,
    v_ref,
    da_ref,
    mix_ref,
    prob_ref,
    bucket_ref,
    dq_ref,
    dk_ref,
    dv_ref,
    sums_ref,
    dk_acc,
    dv_acc,
    ds_keep,
):
    rows, width = q_ref.shape
    heads = prob_ref.shape[0]
    keys = k_ref.shape[0]
    head_dim = width // heads
    doc, step_i = pl.program_id(0), pl.program_id(1)

    @pl.when(step_i == 0)
    def _():
        dk_acc[...] = jnp.zeros_like(dk_acc)
        dv_acc[...] = jnp.zeros_like(dv_acc)

    @pl.when((step_i == 0) & (doc == 0))
    def _():
        sums_ref[...] = jnp.zeros_like(sums_ref)

    def pair(step, carry):
        lanes = pl.ds(pl.multiple_of(step * 2 * head_dim, 128), 2 * head_dim)
        dq, dk, dv, kept = attend_back(
            q_ref[:, lanes],
            k_ref[:, lanes],
            v_ref[:, lanes],
            da_ref[:, lanes],
            mix_ref[:, lanes],
            [prob_ref[2 * step], prob_ref[2 * step + 1]],
            head_dim,
        )
        ds_keep[2 * step] = kept[0]
        ds_keep[2 * step + 1] = kept[1]
        dq_ref[:, lanes] = dq.astype(BFLOAT)
        dk_acc[:, lanes] += dk
        dv_acc[:, lanes] += dv
        return carry

    lax.fori_loop(0, heads // 2, pair, 0)

    def group(number, carry):
        span = pl.ds(pl.multiple_of(number * 16, 16), 16)
        sums_ref[...] += bucket_products(
            bucket_ref[span, :], ds_keep[:, span, :].reshape(heads * 16, keys), labels
        )
        return carry

    lax.fori_loop(0, rows // 16, group, 0)

    @pl.when(step_i == pl.num_programs(1) - 1)
    def _():
        dk_ref[...] = dk_acc[...].astype(BFLOAT)
        dv_ref[...] = dv_acc[...].astype(BFLOAT)


def doc_backward(q_rows, kv_rows, da_rows, mixture, probs, buckets, n_docs, rows, labels):
    width = q_rows.shape[1]
    heads = probs.shape[0]
    keys = buckets.shape[1]
    block = math.gcd(rows, 256)
    steps = rows // block
    along = pl.BlockSpec((block, width), lambda d, i: (d * steps + i, 0))
    per_doc = pl.BlockSpec((keys, width), lambda d, i: (d, 0))
    return pl.pallas_call(
        functools.partial(doc_backward_kernel, labels),
        grid=(n_docs, steps),
        in_specs=[
            along,
            per_doc,
            pl.BlockSpec((keys, width), lambda d, i: (d, 1)),
            along,
            along,
            pl.BlockSpec((heads, block, keys), lambda d, i: (0, d * steps + i, 0)),
            pl.BlockSpec((block, keys), lambda d, i: (i, 0)),
        ],
        out_specs=[along, per_doc, per_doc, whole((16 * labels, heads * 16))],
        out_shape=[
            jax.ShapeDtypeStruct((n_docs * rows, width), BFLOAT),
            jax.ShapeDtypeStruct((n_docs * keys, width), BFLOAT),
            jax.ShapeDtypeStruct((n_docs * keys, width), BFLOAT),
            jax.ShapeDtypeStruct((16 * labels, heads * 16), SINGLE),
        ],
        scratch_shapes=[
            pltpu.VMEM((keys, width), SINGLE),
            pltpu.VMEM((keys, width), SINGLE),
            pltpu.VMEM((heads, block, keys), BFLOAT),
        ],
        compiler_params=params(),
        cost_estimate=cost(70 * n_docs * rows * keys * width, 2 * heads * n_docs * rows * keys),
    )(q_rows, kv_rows, kv_rows, da_rows, mixture, probs, buckets)


def query_forward_kernel(q_ref, kv_ref, table_ref, bucket_ref, mix_ref, prob_ref):
    rows, width = q_ref.shape
    heads = prob_ref.shape[0]
    head_dim = width // heads
    index = bucket_ref[...]
    for step in range(heads // 2):
        lanes = slice(step * 2 * head_dim, (step + 1) * 2 * head_dim)
        q_pair = q_ref[:, lanes]
        k_pair = kv_ref[:, lanes]
        v_pair = kv_ref[:, width + lanes.start : width + lanes.stop]
        wide = first_lanes(q_pair.shape, head_dim)
        total = None
        for side in range(2):
            head = 2 * step + side
            mine = wide if side == 0 else ~wide
            table = jnp.broadcast_to(table_ref[head : head + 1, :], (rows, 128))
            bias = jnp.take_along_axis(table, index, axis=1, mode="promise_in_bounds")
            scores = nt(jnp.where(mine, q_pair, 0), k_pair) + bias
            shifted = jnp.exp(scores - jnp.max(scores, axis=-1, keepdims=True))
            inverse = 1.0 / jnp.sum(shifted, axis=-1, keepdims=True)
            soft = (shifted * inverse).astype(BFLOAT)
            prob_ref[head] = soft
            term = nn(soft, jnp.where(mine, v_pair, 0))
            total = term if total is None else total + term
        mix_ref[:, lanes] = total.astype(BFLOAT)


def query_forward(q_rows, kv_rows, table, buckets, start, count, heads):
    width = q_rows.shape[1]
    offset = start // 128
    return pl.pallas_call(
        query_forward_kernel,
        grid=(count // 128,),
        in_specs=[
            pl.BlockSpec((128, width), lambda i: (offset + i, 0)),
            pl.BlockSpec((128, 2 * width), lambda i: (offset + i, 0)),
            whole(table.shape),
            whole(buckets.shape),
        ],
        out_specs=[
            pl.BlockSpec((128, width), lambda i: (i, 0)),
            pl.BlockSpec((heads, 128, 128), lambda i: (0, i, 0)),
        ],
        out_shape=[
            jax.ShapeDtypeStruct((count, width), BFLOAT),
            jax.ShapeDtypeStruct((heads, count, 128), BFLOAT),
        ],
        compiler_params=params(),
        cost_estimate=cost(4 * count * 128 * width * 4, 10 * count * width),
    )(q_rows, kv_rows, table, buckets)


def query_backward_kernel(
    labels, q_ref, kv_ref, da_ref, mix_ref, prob_ref, bucket_ref, dq_ref, dkv_ref, sums_ref, ds_keep
):
    rows, width = q_ref.shape
    heads = prob_ref.shape[0]
    head_dim = width // heads

    @pl.when(pl.program_id(0) == 0)
    def _():
        sums_ref[...] = jnp.zeros_like(sums_ref)

    for step in range(heads // 2):
        lanes = slice(step * 2 * head_dim, (step + 1) * 2 * head_dim)
        right = slice(width + lanes.start, width + lanes.stop)
        dq, dk, dv, kept = attend_back(
            q_ref[:, lanes],
            kv_ref[:, lanes],
            kv_ref[:, right],
            da_ref[:, lanes],
            mix_ref[:, lanes],
            [prob_ref[2 * step], prob_ref[2 * step + 1]],
            head_dim,
        )
        ds_keep[2 * step] = kept[0]
        ds_keep[2 * step + 1] = kept[1]
        dq_ref[:, lanes] = dq.astype(BFLOAT)
        dkv_ref[:, lanes] = dk.astype(BFLOAT)
        dkv_ref[:, right] = dv.astype(BFLOAT)

    def group(number, carry):
        span = pl.ds(pl.multiple_of(number * 16, 16), 16)
        sums_ref[...] += bucket_products(
            bucket_ref[span, :], ds_keep[:, span, :].reshape(heads * 16, rows), labels
        )
        return carry

    lax.fori_loop(0, rows // 16, group, 0)


def query_backward(q_rows, kv_rows, da_rows, mixture, probs, buckets, start, labels):
    width = q_rows.shape[1]
    heads, count, _ = probs.shape
    offset = start // 128
    return pl.pallas_call(
        functools.partial(query_backward_kernel, labels),
        grid=(count // 128,),
        in_specs=[
            pl.BlockSpec((128, width), lambda i: (offset + i, 0)),
            pl.BlockSpec((128, 2 * width), lambda i: (offset + i, 0)),
            pl.BlockSpec((128, width), lambda i: (offset + i, 0)),
            pl.BlockSpec((128, width), lambda i: (offset + i, 0)),
            pl.BlockSpec((heads, 128, 128), lambda i: (0, i, 0)),
            whole(buckets.shape),
        ],
        out_specs=[
            pl.BlockSpec((128, width), lambda i: (i, 0)),
            pl.BlockSpec((128, 2 * width), lambda i: (i, 0)),
            whole((16 * labels, heads * 16)),
        ],
        out_shape=[
            jax.ShapeDtypeStruct((count, width), BFLOAT),
            jax.ShapeDtypeStruct((count, 2 * width), BFLOAT),
            jax.ShapeDtypeStruct((16 * labels, heads * 16), SINGLE),
        ],
        scratch_shapes=[pltpu.VMEM((heads, 128, 128), BFLOAT)],
        compiler_params=params(),
        cost_estimate=cost(8 * count * 128 * width * 4, 14 * count * width),
    )(q_rows, kv_rows, da_rows, mixture, probs, buckets)


def feed_kernel(
    chunk,
    x_ref,
    mix_ref,
    dy_ref,
    gain_ref,
    wou_ref,
    wd_ref,
    y_ref,
    dh_ref,
    da_ref,
    gou_ref,
    gd_ref,
    gg_ref,
    gou_acc,
    gd_acc,
    stage,
    sems,
):
    step = pl.program_id(0)
    hidden, width = wd_ref.shape

    @pl.when(step == 0)
    def _():
        gou_acc[...] = jnp.zeros_like(gou_acc)
        gd_acc[...] = jnp.zeros_like(gd_acc)
        gg_ref[...] = jnp.zeros_like(gg_ref)

    mixture = mix_ref[...]
    dy = dy_ref[...]
    gain = gain_ref[...]
    residual = x_ref[...].astype(SINGLE) + nn(mixture, wou_ref[:, :width])
    scale = scale_of(residual)
    second = (residual * scale * gain).astype(BFLOAT)
    y = residual
    grad_second = jnp.zeros_like(residual)
    for part in range(hidden // chunk):
        span = slice(part * chunk, (part + 1) * chunk)
        past = slice(width + part * chunk, width + (part + 1) * chunk)
        pre = nn(second, wou_ref[:, past])
        grad_hidden = nt(dy, wd_ref[span, :])
        square = pre * pre
        tanh = jnp.tanh(pre * (GELU_A + (GELU_A * GELU_B) * square))
        half = 0.5 + 0.5 * tanh
        act = pre * half
        slope = half + act * (1.0 - tanh) * (GELU_A + (3.0 * GELU_A * GELU_B) * square)
        act_low = act.astype(BFLOAT)
        grad_pre = (grad_hidden * slope).astype(BFLOAT)
        y = y + nn(act_low, wd_ref[span, :])
        grad_second = grad_second + nt(grad_pre, wou_ref[:, past])
        gd_acc[span, :] += tn(act_low, dy)
        gou_acc[:, past] += tn(second, grad_pre)
    y_ref[...] = y.astype(BFLOAT)
    gg_ref[...] += jnp.sum(grad_second * residual * scale, axis=0, keepdims=True)
    grad_res = dy.astype(SINGLE) + norm_back(residual, scale, grad_second * gain)
    dh_ref[...] = grad_res
    grad_low = grad_res.astype(BFLOAT)
    da_ref[...] = nt(grad_low, wou_ref[:, :width]).astype(BFLOAT)
    gou_acc[:, :width] += tn(mixture, grad_low)

    @pl.when(step == pl.num_programs(0) - 1)
    def _():
        pieces = []
        rows, columns = stage.shape[1:]
        for acc, out in ((gd_acc, gd_ref), (gou_acc, gou_ref)):
            for r in range(acc.shape[0] // rows):
                for c in range(acc.shape[1] // columns):
                    spot = (pl.ds(r * rows, rows), pl.ds(c * columns, columns))
                    pieces.append((acc, out, spot))
        flying = [None, None]
        for number, (acc, out, spot) in enumerate(pieces):
            slot = number % 2
            if flying[slot] is not None:
                flying[slot].wait()
            stage[slot] = acc[spot].astype(BFLOAT)
            flying[slot] = pltpu.make_async_copy(stage.at[slot], out.at[spot], sems.at[slot])
            flying[slot].start()
        for copy in flying:
            if copy is not None:
                copy.wait()


def feed(tokens, mixture, cotangent, gain, w_out_up, w_down):
    rows, width = tokens.shape
    hidden = w_down.shape[0]
    block = math.gcd(rows, 256)
    along = pl.BlockSpec((block, width), lambda i: (i, 0))
    anywhere = pl.BlockSpec(memory_space=pl.ANY)
    return pl.pallas_call(
        functools.partial(feed_kernel, math.gcd(hidden, 768)),
        grid=(rows // block,),
        in_specs=[
            along,
            along,
            along,
            whole((1, width)),
            whole(w_out_up.shape),
            whole(w_down.shape),
        ],
        out_specs=[along, along, along, anywhere, anywhere, whole((1, width))],
        out_shape=[
            jax.ShapeDtypeStruct((rows, width), BFLOAT),
            jax.ShapeDtypeStruct((rows, width), SINGLE),
            jax.ShapeDtypeStruct((rows, width), BFLOAT),
            jax.ShapeDtypeStruct(w_out_up.shape, BFLOAT),
            jax.ShapeDtypeStruct(w_down.shape, BFLOAT),
            jax.ShapeDtypeStruct((1, width), SINGLE),
        ],
        scratch_shapes=[
            pltpu.VMEM(w_out_up.shape, SINGLE),
            pltpu.VMEM(w_down.shape, SINGLE),
            pltpu.VMEM((2, width, width), BFLOAT),
            pltpu.SemaphoreType.DMA((2,)),
        ],
        compiler_params=params(),
        cost_estimate=cost(2 * rows * width * (6 * hidden + 3 * width), 14 * rows * width),
    )(tokens, mixture, cotangent, gain.reshape(1, width), w_out_up, w_down)


def unproject_kernel(
    x_ref, gain_ref, dq_ref, dk_ref, dv_ref, dh_ref, w_ref, dx_ref, low_ref, gw_ref, gg_ref, acc
):
    step = pl.program_id(0)
    width = w_ref.shape[0]

    @pl.when(step == 0)
    def _():
        acc[...] = jnp.zeros_like(acc)
        gg_ref[...] = jnp.zeros_like(gg_ref)

    values = x_ref[...].astype(SINGLE)
    gain = gain_ref[...]
    scale = scale_of(values)
    normed = (values * scale * gain).astype(BFLOAT)
    grad = jnp.zeros_like(values)
    for number, ref in enumerate((dq_ref, dk_ref, dv_ref)):
        span = slice(number * width, (number + 1) * width)
        part = ref[...]
        acc[:, span] += tn(normed, part)
        grad = grad + nt(part, w_ref[:, span])
    gg_ref[...] += jnp.sum(grad * values * scale, axis=0, keepdims=True)
    dx = dh_ref[...] + norm_back(values, scale, grad * gain)
    dx_ref[...] = dx
    low_ref[...] = dx.astype(BFLOAT)

    @pl.when(step == pl.num_programs(0) - 1)
    def _():
        gw_ref[...] = acc[...].astype(BFLOAT)


def unproject(tokens, gain, dq, dk, dv, grad_res, w_qkv):
    rows, width = tokens.shape
    block = math.gcd(rows, 256)
    along = pl.BlockSpec((block, width), lambda i: (i, 0))
    return pl.pallas_call(
        unproject_kernel,
        grid=(rows // block,),
        in_specs=[along, whole((1, width)), along, along, along, along, whole(w_qkv.shape)],
        out_specs=[along, along, whole(w_qkv.shape), whole((1, width))],
        out_shape=[
            jax.ShapeDtypeStruct((rows, width), SINGLE),
            jax.ShapeDtypeStruct((rows, width), BFLOAT),
            jax.ShapeDtypeStruct(w_qkv.shape, BFLOAT),
            jax.ShapeDtypeStruct((1, width), SINGLE),
        ],
        scratch_shapes=[pltpu.VMEM(w_qkv.shape, SINGLE)],
        compiler_params=params(),
        cost_estimate=cost(12 * rows * width * width, 18 * rows * width),
    )(tokens, gain.reshape(1, width), dq, dk, dv, grad_res, w_qkv)


def bits_of(count):
    return [1 << place for place in reversed(range(count.bit_length() - 1))]


def axis_bits():
    dp_bits = [("dp", bit) for bit in bits_of(lax.axis_size("dp"))]
    seq_bits = [("seq", bit) for bit in bits_of(lax.axis_size("seq"))]
    return dp_bits, seq_bits


def gather_orders():
    dp_bits, seq_bits = axis_bits()
    far = (len(dp_bits) + 1) // 2
    z_bits, x_bits = dp_bits[:far], dp_bits[far:]
    y_bits, core_bits = seq_bits[:-1], seq_bits[-1:]
    return [z_bits + y_bits + x_bits + core_bits, z_bits + x_bits + y_bits + core_bits]


def swap(values, name, bit):
    count = lax.axis_size(name)
    return lax.ppermute(values, name, [(i, i ^ bit) for i in range(count)])


def is_high(name, bit):
    return (lax.axis_index(name) & bit) != 0


def gather_rows(shard, order):
    dp_bits, seq_bits = axis_bits()
    everything = dp_bits + seq_bits
    done = []
    held = shard
    for item in order:
        other = swap(held, *item)
        done.append(item)
        place = sorted(everything.index(one) for one in done).index(everything.index(item))
        high = is_high(*item)
        held = jnp.where(
            high, jnp.stack([other, held], place), jnp.stack([held, other], place)
        )
    return held.reshape(-1, shard.shape[1])


def scatter_rows(values, order):
    dp_bits, seq_bits = axis_bits()
    left = dp_bits + seq_bits
    rows = values.shape[0] >> len(left)
    held = values.reshape((2,) * len(left) + (rows, values.shape[1]))
    for item in order:
        place = left.index(item)
        mine = is_high(*item).astype(jnp.int32)
        away = lax.dynamic_index_in_dim(held, 1 - mine, place, keepdims=False)
        kept = lax.dynamic_index_in_dim(held, mine, place, keepdims=False)
        other = swap(away, *item)
        held = kept.astype(SINGLE) + other.astype(SINGLE)
        left.remove(item)
        if left:
            held = held.astype(BFLOAT)
    return held


def scatter_columns(values, parts):
    orders = [order[::-1] for order in gather_orders()]
    columns = values.shape[1] // parts
    return jnp.concatenate(
        [
            scatter_rows(values[:, p * columns : (p + 1) * columns], orders[p % len(orders)])
            for p in range(parts)
        ],
        1,
    )


def sum_all(values):
    dp_bits, seq_bits = axis_bits()
    for item in seq_bits[::-1] + dp_bits[::-1]:
        values = values + swap(values, *item)
    return values


def own_document(shard):
    count = lax.axis_size("seq")
    n_docs = shard.shape[0]
    me = lax.axis_index("seq")
    if n_docs >= count:
        per = n_docs // count
        blocks = shard.reshape((count, per) + shard.shape[1:])
        sets, group = count, 1
    else:
        blocks = shard[:, None]
        sets, group = n_docs, count // n_docs
    got = []
    for r in range(sets):
        piece = lax.dynamic_index_in_dim(blocks, (me % sets) ^ r, 0, keepdims=False)
        route = [
            (u * sets + i, (i ^ r) * group + u) for u in range(group) for i in range(sets)
        ]
        if any(a != b for a, b in route):
            piece = lax.ppermute(piece, "seq", route)
        got.append(piece)
    stacked = jnp.stack(got, 0)
    mine = me // group
    ordered = [lax.dynamic_index_in_dim(stacked, mine ^ i, 0, keepdims=False) for i in range(sets)]
    return jnp.concatenate(ordered, 1).reshape(-1, shard.shape[-1])


def spread_document(rows, like):
    count = lax.axis_size("seq")
    n_docs, shard_rows, width = like.shape
    me = lax.axis_index("seq")
    if n_docs >= count:
        per = n_docs // count
        sets, group = count, 1
    else:
        per = 1
        sets, group = n_docs, count // n_docs
    blocks = rows.reshape(per, sets, shard_rows, width)
    mine = me // group
    got = []
    for r in range(sets):
        piece = lax.dynamic_index_in_dim(blocks, mine ^ r, 1, keepdims=False)
        route = [
            ((i ^ r) * group + u, u * sets + i) for u in range(group) for i in range(sets)
        ]
        if any(a != b for a, b in route):
            piece = lax.ppermute(piece, "seq", route)
        got.append(piece)
    stacked = jnp.stack(got, 0)
    ordered = [
        lax.dynamic_index_in_dim(stacked, (me % sets) ^ i, 0, keepdims=False) for i in range(sets)
    ]
    return jnp.concatenate(ordered, 0)


def gather_positions(shard):
    seq_bits = axis_bits()[1]
    done = []
    held = shard
    for item in seq_bits:
        other = swap(held, *item)
        high = is_high(*item)
        place = len(done)
        held = jnp.where(
            high, jnp.stack([other, held], place), jnp.stack([held, other], place)
        )
        done.append(item)
    return held.reshape(-1, shard.shape[1])


class Spot:
    def __init__(self):
        self.dp = lax.axis_index("dp")
        self.seq = lax.axis_index("seq")
        self.core = self.seq % 2
        self.y = self.seq // 2
        self.x = self.dp % 2
        self.z = self.dp // 2

    def partner(self, z=0, x=0, y=0, core=0):
        dp = self.flip(self.z, z) * 2 + self.flip(self.x, x)
        seq = self.flip(self.y, y) * 2 + self.flip(self.core, core)
        return (dp, seq)

    @staticmethod
    def flip(value, bits):
        if bits == 0:
            return value
        if bits == 1:
            return value + 1 - 2 * (value % 2)
        if bits == 2:
            return (value + 2) % 4
        return 3 - value

    def chip(self, z=0, x=0, y=0):
        return (self.flip(self.z, z) * 2 + self.flip(self.x, x)) * 2 + self.flip(self.y, y)


def send(source, target, sems, number, device):
    return pltpu.make_async_remote_copy(
        src_ref=source,
        dst_ref=target,
        send_sem=sems.at[0, number],
        recv_sem=sems.at[1, number],
        device_id=device,
        device_id_type=pl.DeviceIdType.MESH,
    )


def greet(partners):
    barrier = pltpu.get_barrier_semaphore()
    for device in partners:
        pl.semaphore_signal(barrier, inc=1, device_id=device, device_id_type=pl.DeviceIdType.MESH)
    pl.semaphore_wait(barrier, len(partners))


GATHER_COPIES = 1 + 3 + 4 + 8 + 1


class Gather:
    def __init__(self, spot, shard, whole_ref, mine, theirs, block, sems, local_sems):
        self.spot, self.shard, self.whole = spot, shard, whole_ref
        self.mine, self.theirs, self.block = mine, theirs, block
        self.sems, self.local = sems, local_sems
        self.rows = block.shape[0]
        self.half = block.shape[1]
        self.sent = []
        self.here = None

    def columns(self, core):
        return pl.ds(pl.multiple_of(core * self.half, 128), self.half)

    def area(self, chip, core):
        return self.whole.at[pl.ds(pl.multiple_of(chip * self.rows, 16), self.rows), self.columns(core)]

    def go(self, source, target, number, device):
        copy = send(source, target, self.sems, number, device)
        copy.start()
        self.sent.append(copy)
        return copy

    def join_start(self):
        core = self.spot.core
        self.first = self.go(
            self.shard.at[:, self.columns(1 - core)], self.theirs, 0, self.spot.partner(core=1)
        )
        self.load = pltpu.make_async_copy(
            self.shard.at[:, self.columns(core)], self.mine, self.local.at[0]
        )
        self.load.start()

    def join_end(self):
        self.load.wait()
        self.first.wait_recv()
        part = self.rows // 2
        low = self.spot.core == 0
        mine = self.mine[...].astype(SINGLE)[:part]
        theirs = self.theirs[...].astype(SINGLE)[:part]
        self.block[:part, :] = jnp.where(low, mine, theirs).astype(BFLOAT)
        self.block[part:, :] = jnp.where(low, theirs, mine).astype(BFLOAT)

    def z_start(self):
        own = self.area(self.spot.chip(), self.spot.core)
        self.here = pltpu.make_async_copy(self.block, own, self.local.at[1])
        self.here.start()
        self.z_copies = [self.go(self.block, own, k, self.spot.partner(z=k)) for k in (1, 2, 3)]

    def y_own(self):
        spot = self.spot
        own = self.area(spot.chip(), spot.core)
        self.y_copies = [self.go(self.block, own, 4, spot.partner(y=1))]
        self.x_copies = [self.go(self.block, own, 8, spot.partner(x=1))]

    def y_more(self, k):
        spot = self.spot
        self.z_copies[k - 1].wait_recv()
        area = self.area(spot.chip(z=k), spot.core)
        self.y_copies.append(self.go(area, area, 4 + k, spot.partner(y=1)))
        self.x_copies.append(self.go(area, area, 8 + k, spot.partner(x=1)))

    def x_more(self, k):
        spot = self.spot
        self.y_copies[k].wait_recv()
        area = self.area(spot.chip(z=k, y=1), spot.core)
        self.x_copies.append(self.go(area, area, 12 + k, spot.partner(x=1)))

    def core_start(self):
        for copy in self.x_copies:
            copy.wait_recv()
        self.here.wait()
        area = self.whole.at[:, self.columns(self.spot.core)]
        self.last = self.go(area, area, 16, self.spot.partner(core=1))

    def finish(self):
        self.last.wait_recv()
        for copy in self.sent:
            copy.wait_send()


def arrive_kernel(
    docs_ref, qkv_ref, x_ref, w_ref, mine, theirs, block, sems, local_sems, doc_sems, doc_local
):
    spot = Spot()
    greet(
        [
            spot.partner(core=1),
            spot.partner(z=1),
            spot.partner(z=2),
            spot.partner(z=3),
            spot.partner(x=1),
            spot.partner(y=1),
            spot.partner(y=1, core=1),
        ]
    )
    gather = Gather(spot, qkv_ref, w_ref, mine, theirs, block, sems, local_sems)
    gather.join_start()
    rows = docs_ref.shape[1]
    space = x_ref.at[pl.ds(pl.multiple_of(spot.seq * rows, 16), rows), :]
    own = pltpu.make_async_copy(docs_ref.at[spot.seq], space, doc_local.at[0])
    own.start()
    moves = []
    gather.join_end()
    gather.z_start()
    gather.y_own()

    def move_document(number, y, core):
        device = spot.partner(y=y, core=core)
        moves.append(send(docs_ref.at[device[1]], space, doc_sems, number, device))
        moves[-1].start()

    move_document(0, 1, 0)
    for k in (1, 2, 3):
        gather.y_more(k)
    move_document(1, 1, 1)
    move_document(2, 0, 1)
    for k in (0, 1, 2, 3):
        gather.x_more(k)
    gather.core_start()
    gather.finish()
    own.wait()
    for move in moves:
        move.wait()


def arrive(docs, qkv_shard):
    n_docs, rows, width = docs.shape
    shard_rows, columns = qkv_shard.shape
    half = columns // 2
    padded = -(-shard_rows // 16) * 16
    qkv_shard = jnp.pad(qkv_shard, ((0, padded - shard_rows), (0, 0)))
    anywhere = pl.BlockSpec(memory_space=pl.ANY)
    return pl.pallas_call(
        arrive_kernel,
        in_specs=[anywhere, anywhere],
        out_specs=[anywhere, anywhere],
        out_shape=[
            jax.ShapeDtypeStruct((n_docs * rows, width), BFLOAT),
            jax.ShapeDtypeStruct((shard_rows * 32, columns), BFLOAT),
        ],
        scratch_shapes=[
            pltpu.VMEM((padded, half), BFLOAT),
            pltpu.VMEM((padded, half), BFLOAT),
            pltpu.VMEM((2 * shard_rows, half), BFLOAT),
            pltpu.SemaphoreType.DMA((2, GATHER_COPIES)),
            pltpu.SemaphoreType.DMA((2,)),
            pltpu.SemaphoreType.DMA((2, 3)),
            pltpu.SemaphoreType.DMA((1,)),
        ],
        compiler_params=pltpu.CompilerParams(
            collective_id=0, has_side_effects=True, vmem_limit_bytes=VMEM_LIMIT
        ),
        cost_estimate=cost(0, 100 << 20),
    )(docs, qkv_shard)


class Scatter:
    def __init__(self, spot, grad, out, held, core_in, x_in, y_in, z_in, tail, tail_in, sems, local):
        self.spot, self.grad, self.out = spot, grad, out
        self.held, self.core_in, self.x_in, self.y_in, self.z_in = held, core_in, x_in, y_in, z_in
        self.tail, self.tail_in, self.sems, self.local = tail, tail_in, sems, local
        self.half = held.shape[1]
        self.rows = held.shape[0] // 16
        self.sent = []

    def go(self, source, target, number, device):
        copy = send(source, target, self.sems, number, device)
        copy.start()
        self.sent.append(copy)
        return copy

    def columns(self, core):
        return pl.ds(pl.multiple_of(core * self.half, 128), self.half)

    def span(self, chip):
        return pl.ds(pl.multiple_of(chip * self.rows, 16), self.rows)

    def core_start(self):
        core = self.spot.core
        self.first = self.go(
            self.grad.at[:, self.columns(1 - core)], self.core_in, 0, self.spot.partner(core=1)
        )
        self.load = pltpu.make_async_copy(
            self.grad.at[:, self.columns(core)], self.held, self.local.at[0]
        )
        self.load.start()

    def core_end(self):
        self.load.wait()
        self.first.wait_recv()

    def add(self, chip, others):
        span = self.span(chip)
        total = self.held[span, :].astype(SINGLE)
        for ref, place in others:
            total = total + ref[place, :].astype(SINGLE)
        return span, total

    def x_start(self):
        spot = self.spot
        self.x_copies = []
        for number, (z, y) in enumerate((z, y) for z in (3, 2, 1, 0) for y in (1, 0)):
            chip = spot.chip(z=z, x=1, y=y)
            span, total = self.add(chip, [(self.core_in, self.span(chip))])
            self.held[span, :] = total.astype(BFLOAT)
            slot = self.x_in.at[pl.ds(number * self.rows, self.rows), :]
            self.x_copies.append(
                self.go(self.held.at[span, :], slot, 1 + number, spot.partner(x=1))
            )

    def y_start(self):
        spot = self.spot
        self.y_copies = []
        for number, z in enumerate((3, 2, 1, 0)):
            chip = spot.chip(z=z, y=1)
            self.x_copies[2 * number].wait_recv()
            place = pl.ds(2 * number * self.rows, self.rows)
            span, total = self.add(chip, [(self.core_in, self.span(chip)), (self.x_in, place)])
            self.held[span, :] = total.astype(BFLOAT)
            slot = self.y_in.at[pl.ds(number * self.rows, self.rows), :]
            self.y_copies.append(
                self.go(self.held.at[span, :], slot, 9 + number, spot.partner(y=1))
            )

    def sum_here(self, number, z):
        chip = self.spot.chip(z=z)
        self.x_copies[2 * number + 1].wait_recv()
        self.y_copies[number].wait_recv()
        return self.add(
            chip,
            [
                (self.core_in, self.span(chip)),
                (self.x_in, pl.ds((2 * number + 1) * self.rows, self.rows)),
                (self.y_in, pl.ds(number * self.rows, self.rows)),
            ],
        )

    def z_start(self):
        self.z_copies = []
        for number, z in enumerate((3, 2, 1)):
            span, total = self.sum_here(number, z)
            self.held[span, :] = total.astype(BFLOAT)
            slot = self.z_in.at[pl.ds(number * self.rows, self.rows), :]
            self.z_copies.append(
                self.go(self.held.at[span, :], slot, 13 + number, self.spot.partner(z=z))
            )

    def tail_start(self):
        _, total = self.sum_here(3, 0)
        for number in range(3):
            self.z_copies[number].wait_recv()
            total = total + self.z_in[pl.ds(number * self.rows, self.rows), :].astype(SINGLE)
        self.tail[...] = total
        part = self.rows // 2
        core = self.spot.core
        theirs = pl.ds(pl.multiple_of((1 - core) * part, 8), part)
        self.last = self.go(self.tail.at[theirs, :], self.tail_in, 16, self.spot.partner(core=1))

    def finish(self):
        part = self.rows // 2
        low = self.spot.core == 0
        mine = jnp.where(low, self.tail[:part, :], self.tail[part:, :])
        self.last.wait_recv()
        other = self.tail_in[...]
        self.out[:, : self.half] = jnp.where(low, mine, other)
        self.out[:, self.half :] = jnp.where(low, other, mine)
        for copy in self.sent:
            copy.wait_send()


def leave_kernel(
    grad_ref,
    dx_ref,
    out_ref,
    docs_ref,
    held,
    core_in,
    x_in,
    y_in,
    z_in,
    tail,
    tail_in,
    sems,
    local_sems,
    doc_sems,
    doc_local,
):
    spot = Spot()
    greet(
        [
            spot.partner(core=1),
            spot.partner(z=1),
            spot.partner(z=2),
            spot.partner(z=3),
            spot.partner(x=1),
            spot.partner(y=1),
            spot.partner(y=1, core=1),
        ]
    )
    scatter = Scatter(
        spot, grad_ref, out_ref, held, core_in, x_in, y_in, z_in, tail, tail_in, sems, local_sems
    )
    scatter.core_start()
    rows = docs_ref.shape[1]
    own = pltpu.make_async_copy(
        dx_ref.at[pl.ds(pl.multiple_of(spot.seq * rows, 16), rows), :],
        docs_ref.at[spot.seq],
        doc_local.at[0],
    )
    own.start()
    scatter.core_end()
    scatter.x_start()
    moves = []
    for number, (y, core) in enumerate(((1, 0), (1, 1), (0, 1))):
        device = spot.partner(y=y, core=core)
        piece = dx_ref.at[pl.ds(pl.multiple_of(device[1] * rows, 16), rows), :]
        moves.append(send(piece, docs_ref.at[spot.seq], doc_sems, number, device))
        moves[-1].start()
    scatter.y_start()
    scatter.z_start()
    scatter.tail_start()
    scatter.finish()
    own.wait()
    for move in moves:
        move.wait()


def leave(grad, dx_docs, n_docs):
    total_rows, columns = grad.shape
    half = columns // 2
    rows = total_rows // 16
    width = dx_docs.shape[1]
    anywhere = pl.BlockSpec(memory_space=pl.ANY)
    return pl.pallas_call(
        leave_kernel,
        in_specs=[anywhere, anywhere],
        out_specs=[pl.BlockSpec(memory_space=pltpu.VMEM), anywhere],
        out_shape=[
            jax.ShapeDtypeStruct((rows // 2, columns), SINGLE),
            jax.ShapeDtypeStruct((n_docs, dx_docs.shape[0] // n_docs, width), BFLOAT),
        ],
        scratch_shapes=[
            pltpu.VMEM((total_rows, half), BFLOAT),
            pltpu.VMEM((total_rows, half), BFLOAT),
            pltpu.VMEM((8 * rows, half), BFLOAT),
            pltpu.VMEM((4 * rows, half), BFLOAT),
            pltpu.VMEM((3 * rows, half), BFLOAT),
            pltpu.VMEM((rows, half), SINGLE),
            pltpu.VMEM((rows // 2, half), SINGLE),
            pltpu.SemaphoreType.DMA((2, GATHER_COPIES)),
            pltpu.SemaphoreType.DMA((1,)),
            pltpu.SemaphoreType.DMA((2, 3)),
            pltpu.SemaphoreType.DMA((1,)),
        ],
        compiler_params=pltpu.CompilerParams(
            collective_id=1, has_side_effects=True, vmem_limit_bytes=VMEM_LIMIT
        ),
        cost_estimate=cost(0, 100 << 20),
    )(grad, dx_docs)


def on_device(
    doc_tokens,
    queries,
    doc_cot,
    query_cot,
    q_weight,
    kv_weight,
    out_weight,
    up_weight,
    down_weight,
    attn_gain,
    ff_gain,
    rel_bias,
    doc_buckets,
    query_buckets,
    topk_mask,
    positives,
    pos_count,
):
    n_docs, shard_rows, width = doc_tokens.shape
    n_query, query_len, _ = queries.shape
    bucket_count, heads = rel_bias.shape
    doc_len = doc_buckets.shape[1]
    doc_rows = n_docs * shard_rows
    query_total = n_query * query_len
    seq_size = lax.axis_size("seq")
    group = max(1, seq_size // n_docs)
    local_docs = max(1, n_docs // seq_size)
    local_rows = doc_len // group
    dp_size = lax.axis_size("dp")
    small = (dp_size, seq_size, n_docs) == (8, 4, 4) and width % 256 == 0 and shard_rows % 16 == 0

    qkv_shard = jnp.concatenate([q_weight, kv_weight], 1)
    if small:
        own_doc, w_qkv = arrive(doc_tokens, qkv_shard)
    else:
        own_doc, w_qkv = own_document(doc_tokens), gather_rows(qkv_shard, gather_orders()[0])
    tokens = jnp.concatenate([own_doc, queries.reshape(query_total, width)], 0)
    buckets = gather_positions(doc_buckets.astype(jnp.int16))
    if group > 1:
        part = lax.axis_index("seq") % group
        buckets = lax.dynamic_slice_in_dim(buckets, part * local_rows, local_rows, 0)

    fixed = jnp.round(rel_bias.T * FIXED).astype(jnp.int32)
    packed = (fixed[0::2] << 16) | (fixed[1::2] & 0xFFFF)
    doc_table = jnp.zeros((8, 128), jnp.int32).at[: heads // 2, :bucket_count].set(packed)
    query_table = jnp.zeros((16, 128), SINGLE).at[:heads, :bucket_count].set(rel_bias.T)
    query_table = query_table.at[:, bucket_count].set(-1e30)
    repeats = 128 // query_len
    same = jnp.kron(jnp.eye(repeats, dtype=jnp.int32), jnp.ones_like(query_buckets))
    tiled = jnp.where(same == 1, jnp.tile(query_buckets, (repeats, repeats)), bucket_count)

    q_rows, kv_rows = project(tokens, attn_gain, w_qkv)
    if group > 1:
        teams = [list(range(t * group, (t + 1) * group)) for t in range(seq_size // group)]
        kv_docs = lax.all_gather(
            kv_rows[:doc_rows], "seq", axis=0, tiled=True, axis_index_groups=teams
        )
    else:
        kv_docs = kv_rows
    doc_mix, doc_probs = doc_forward(
        q_rows, kv_docs, doc_table, buckets, local_docs, local_rows, heads
    )
    query_mix, query_probs = query_forward(
        q_rows, kv_rows, query_table, tiled, doc_rows, query_total, heads
    )
    mixture = jnp.concatenate([doc_mix, query_mix], 0)
    w_out_up = lax.all_gather(
        jnp.concatenate([out_weight, up_weight], 1), ("dp", "seq"), axis=0, tiled=True
    )
    w_down = lax.all_gather(down_weight, ("dp", "seq"), axis=0, tiled=True)
    cotangent = jnp.concatenate(
        [own_document(doc_cot), query_cot.reshape(query_total, width)], 0
    )
    outputs, grad_res, grad_mix, grad_out_up, grad_down, grad_ff = feed(
        tokens, mixture, cotangent, ff_gain, w_out_up, w_down
    )
    grad_down_shard = lax.psum_scatter(
        grad_down, ("dp", "seq"), scatter_dimension=0, tiled=True
    ).astype(SINGLE)
    grad_out_up_shard = lax.psum_scatter(
        grad_out_up, ("dp", "seq"), scatter_dimension=0, tiled=True
    ).astype(SINGLE)
    grad_out_shard = grad_out_up_shard[:, :width]
    grad_up_shard = grad_out_up_shard[:, width:]
    doc_out = spread_document(outputs[:doc_rows], doc_tokens)
    query_out = outputs[doc_rows:].reshape(queries.shape)

    doc_dq, doc_dk, doc_dv, doc_sums = doc_backward(
        q_rows, kv_docs, grad_mix, doc_mix, doc_probs, buckets, local_docs, local_rows, bucket_count
    )
    if group > 1:
        both = jnp.concatenate([doc_dk, doc_dv], 1)
        both = lax.psum_scatter(
            both, "seq", scatter_dimension=0, tiled=True, axis_index_groups=teams
        )
        doc_dk, doc_dv = both[:, :width], both[:, width:]
    query_dq, query_dkv, query_sums = query_backward(
        q_rows, kv_rows, grad_mix, mixture, query_probs, tiled, doc_rows, bucket_count
    )
    dq = jnp.concatenate([doc_dq, query_dq], 0)
    dk = jnp.concatenate([doc_dk, query_dkv[:, :width]], 0)
    dv = jnp.concatenate([doc_dv, query_dkv[:, width:]], 0)
    grad_tokens, grad_low, grad_qkv, grad_attn = unproject(
        tokens, attn_gain, dq, dk, dv, grad_res, w_qkv
    )
    if small:
        grad_qkv_shard, doc_dx = leave(grad_qkv, grad_low[:doc_rows], n_docs)
    else:
        grad_qkv_shard = scatter_columns(grad_qkv, 2)
        doc_dx = spread_document(grad_low[:doc_rows], doc_tokens)
    doc_dx = doc_dx.astype(SINGLE)
    query_dx = grad_tokens[doc_rows:].reshape(queries.shape)

    sums = (doc_sums + query_sums).reshape(16, bucket_count, heads, 16)
    keep = jnp.eye(16, dtype=SINGLE)[:, None, None, :]
    bias_local = jnp.sum(sums * keep, axis=(0, 3))
    matches = positives[:, :, None] == jnp.arange(doc_len, dtype=jnp.int32)[None, None, :]
    counted = jnp.arange(positives.shape[1], dtype=jnp.int32)[None, :] < pos_count[:, None]
    retrieved = jnp.sum(
        jnp.where(matches & counted[:, :, None], topk_mask[:, None, :].astype(SINGLE), 0.0)
    )
    flat = jnp.concatenate(
        [grad_attn[0], grad_ff[0], bias_local.reshape(-1), jnp.full((128,), retrieved)]
    )
    total = sum_all(flat)
    slots = float(n_query * lax.axis_size("dp") * seq_size * positives.shape[1])
    return (
        doc_out,
        query_out,
        doc_dx,
        query_dx,
        grad_qkv_shard[:, :width],
        grad_qkv_shard[:, width:],
        grad_out_shard,
        grad_up_shard,
        grad_down_shard,
        total[:width],
        total[width : 2 * width],
        total[2 * width : 2 * width + bucket_count * heads].reshape(bucket_count, heads),
        total[-1] / slots,
    )


def solution(mesh):
    rows_all = P(("dp", "seq"), None)
    return jax.shard_map(
        on_device,
        mesh=mesh,
        in_specs=(
            P("dp", "seq", None),
            P(("dp", "seq"), None, None),
            P("dp", "seq", None),
            P(("dp", "seq"), None, None),
            rows_all,
            rows_all,
            rows_all,
            rows_all,
            rows_all,
            P(),
            P(),
            P(),
            P("seq", None),
            P(),
            rows_all,
            rows_all,
            P(("dp", "seq")),
        ),
        out_specs=(
            P("dp", "seq", None),
            P(("dp", "seq"), None, None),
            P("dp", "seq", None),
            P(("dp", "seq"), None, None),
            rows_all,
            rows_all,
            rows_all,
            rows_all,
            rows_all,
            P(),
            P(),
            P(),
            P(),
        ),
        check_vma=False,
    )
```

```python
import functools
import math

import jax
import jax.numpy as jnp
from jax import lax
from jax.experimental import pallas as pl
from jax.experimental.pallas import tpu as pltpu
from jax.sharding import PartitionSpec as P

EPSILON = 1e-06
BFLOAT = jnp.bfloat16
SINGLE = jnp.float32
FIXED = 8191.0
GELU_A = math.sqrt(2.0 / math.pi)
GELU_B = 0.044715
VMEM_LIMIT = 60 << 20


def nn(left, right):
    return jnp.dot(left, right, preferred_element_type=SINGLE)


def nt(left, right):
    return lax.dot_general(left, right, (((1,), (1,)), ((), ())), preferred_element_type=SINGLE)


def tn(left, right):
    return lax.dot_general(left, right, (((0,), (0,)), ((), ())), preferred_element_type=SINGLE)


def whole(shape):
    zeros = (0,) * len(shape)
    return pl.BlockSpec(shape, lambda *_: zeros, pipeline_mode=pl.Buffered(1))


def params():
    return pltpu.CompilerParams(vmem_limit_bytes=VMEM_LIMIT)


def cost(flops, moved):
    return pl.CostEstimate(flops=int(flops), bytes_accessed=int(moved), transcendentals=0)


def scale_of(values):
    return lax.rsqrt(jnp.mean(values * values, axis=-1, keepdims=True) + EPSILON)


def norm_back(values, scale, scaled_grad):
    dot = jnp.mean(values * scaled_grad, axis=-1, keepdims=True)
    return scale * (scaled_grad - values * (scale * scale * dot))


def first_lanes(shape, head_dim):
    return lax.broadcasted_iota(jnp.int32, shape, 1) < head_dim


def project_kernel(x_ref, gain_ref, w_ref, q_ref, kv_ref):
    values = x_ref[...].astype(SINGLE)
    normed = (values * scale_of(values) * gain_ref[...]).astype(BFLOAT)
    width = values.shape[1]
    q_ref[...] = nn(normed, w_ref[:, :width]).astype(BFLOAT)
    kv_ref[...] = nn(normed, w_ref[:, width:]).astype(BFLOAT)


def project(tokens, gain, w_qkv):
    rows, width = tokens.shape
    block = math.gcd(rows, 256)
    return pl.pallas_call(
        project_kernel,
        grid=(rows // block,),
        in_specs=[
            pl.BlockSpec((block, width), lambda i: (i, 0)),
            whole((1, width)),
            whole(w_qkv.shape),
        ],
        out_specs=[
            pl.BlockSpec((block, width), lambda i: (i, 0)),
            pl.BlockSpec((block, 2 * width), lambda i: (i, 0)),
        ],
        out_shape=[
            jax.ShapeDtypeStruct((rows, width), BFLOAT),
            jax.ShapeDtypeStruct((rows, 2 * width), BFLOAT),
        ],
        compiler_params=params(),
        cost_estimate=cost(6 * rows * width * width, 12 * rows * width),
    )(tokens, gain.reshape(1, width), w_qkv)


def attend_pair(q_pair, k_pair, v_pair, table_row, bucket_ref, start, prob_ref, step, head_dim):
    rows, keys = q_pair.shape[0], k_pair.shape[0]
    wide = first_lanes(q_pair.shape, head_dim)
    tall = first_lanes(v_pair.shape, head_dim)
    table = jnp.broadcast_to(table_row, (rows, 128))
    span = pl.ds(start, rows)
    packed = jnp.concatenate(
        [
            jnp.take_along_axis(
                table,
                bucket_ref[span, part * 128 : part * 128 + 128].astype(jnp.int32),
                axis=1,
                mode="promise_in_bounds",
            )
            for part in range(keys // 128)
        ],
        1,
    )
    total = None
    for side in range(2):
        mine = wide if side == 0 else ~wide
        mine_tall = tall if side == 0 else ~tall
        coded = (packed >> 16) if side == 0 else ((packed << 16) >> 16)
        scores = nt(jnp.where(mine, q_pair, 0), k_pair)
        scores = scores + coded.astype(SINGLE) * (1.0 / FIXED)
        shifted = jnp.exp(scores - jnp.max(scores, axis=-1, keepdims=True))
        inverse = 1.0 / jnp.sum(shifted, axis=-1, keepdims=True)
        soft = (shifted * inverse).astype(BFLOAT)
        prob_ref[2 * step + side] = soft
        term = nn(soft, jnp.where(mine_tall, v_pair, 0))
        total = term if total is None else total + term
    return total.astype(BFLOAT)


def pair_lanes(step, head_dim, offset=0):
    return pl.ds(pl.multiple_of(offset + step * 2 * head_dim, 128), 2 * head_dim)


def doc_forward_kernel(q_ref, k_ref, v_ref, table_ref, bucket_ref, mix_ref, prob_ref):
    heads = prob_ref.shape[0]
    head_dim = q_ref.shape[1] // heads

    def pair(step, carry):
        lanes = pair_lanes(step, head_dim)
        mix_ref[:, lanes] = attend_pair(
            q_ref[:, lanes],
            k_ref[:, lanes],
            v_ref[:, lanes],
            table_ref[pl.ds(step, 1), :],
            bucket_ref,
            0,
            prob_ref,
            step,
            head_dim,
        )
        return carry

    lax.fori_loop(0, heads // 2, pair, 0)


def doc_forward(q_rows, kv_rows, table, buckets, n_docs, rows, heads):
    width = q_rows.shape[1]
    keys = buckets.shape[1]
    block = math.gcd(rows, 256)
    steps = rows // block
    return pl.pallas_call(
        doc_forward_kernel,
        grid=(n_docs, steps),
        in_specs=[
            pl.BlockSpec((block, width), lambda d, i: (d * steps + i, 0)),
            pl.BlockSpec((keys, width), lambda d, i: (d, 0)),
            pl.BlockSpec((keys, width), lambda d, i: (d, 1)),
            whole(table.shape),
            pl.BlockSpec((block, keys), lambda d, i: (i, 0)),
        ],
        out_specs=[
            pl.BlockSpec((block, width), lambda d, i: (d * steps + i, 0)),
            pl.BlockSpec((heads, block, keys), lambda d, i: (0, d * steps + i, 0)),
        ],
        out_shape=[
            jax.ShapeDtypeStruct((n_docs * rows, width), BFLOAT),
            jax.ShapeDtypeStruct((heads, n_docs * rows, keys), BFLOAT),
        ],
        compiler_params=params(),
        cost_estimate=cost(30 * n_docs * rows * keys * width, 2 * heads * n_docs * rows * keys),
    )(q_rows, kv_rows, kv_rows, table, buckets)


def bucket_products(bucket_rows, grad_rows, labels):
    rows, keys = bucket_rows.shape
    numbers = bucket_rows.astype(jnp.int32)
    names = lax.broadcasted_iota(jnp.int32, (labels, keys), 0)
    parts = [
        jnp.where(jnp.broadcast_to(numbers[r : r + 1, :], (labels, keys)) == names, 1.0, 0.0).astype(
            BFLOAT
        )
        for r in range(rows)
    ]
    onehot = jnp.concatenate(parts, 0)
    return nt(onehot, grad_rows)


def attend_back(q_pair, k_pair, v_pair, da_pair, mix_pair, probs, head_dim):
    wide = first_lanes(q_pair.shape, head_dim)
    tall = first_lanes(k_pair.shape, head_dim)
    product = da_pair.astype(SINGLE) * mix_pair.astype(SINGLE)
    dq = dk = dv = None
    kept = []
    for side in range(2):
        mine = wide if side == 0 else ~wide
        mine_tall = tall if side == 0 else ~tall
        da_mine = jnp.where(mine, da_pair, 0)
        correction = jnp.sum(jnp.where(mine, product, 0.0), axis=-1, keepdims=True)
        grad_soft = nt(da_mine, v_pair)
        soft = probs[side]
        grad_scores = (soft.astype(SINGLE) * (grad_soft - correction)).astype(BFLOAT)
        kept.append(grad_scores)
        dq_term = nn(grad_scores, jnp.where(mine_tall, k_pair, 0))
        dk_term = tn(grad_scores, jnp.where(mine, q_pair, 0))
        dv_term = tn(soft, da_mine)
        dq = dq_term if dq is None else dq + dq_term
        dk = dk_term if dk is None else dk + dk_term
        dv = dv_term if dv is None else dv + dv_term
    return dq, dk, dv, kept


def doc_backward_kernel(
    labels,
    q_ref,
    k_ref,
    v_ref,
    da_ref,
    mix_ref,
    prob_ref,
    bucket_ref,
    dq_ref,
    dk_ref,
    dv_ref,
    sums_ref,
    dk_acc,
    dv_acc,
    ds_keep,
):
    rows, width = q_ref.shape
    heads = prob_ref.shape[0]
    keys = k_ref.shape[0]
    head_dim = width // heads
    doc, step_i = pl.program_id(0), pl.program_id(1)

    @pl.when(step_i == 0)
    def _():
        dk_acc[...] = jnp.zeros_like(dk_acc)
        dv_acc[...] = jnp.zeros_like(dv_acc)

    @pl.when((step_i == 0) & (doc == 0))
    def _():
        sums_ref[...] = jnp.zeros_like(sums_ref)

    def pair(step, carry):
        lanes = pl.ds(pl.multiple_of(step * 2 * head_dim, 128), 2 * head_dim)
        dq, dk, dv, kept = attend_back(
            q_ref[:, lanes],
            k_ref[:, lanes],
            v_ref[:, lanes],
            da_ref[:, lanes],
            mix_ref[:, lanes],
            [prob_ref[2 * step], prob_ref[2 * step + 1]],
            head_dim,
        )
        ds_keep[2 * step] = kept[0]
        ds_keep[2 * step + 1] = kept[1]
        dq_ref[:, lanes] = dq.astype(BFLOAT)
        dk_acc[:, lanes] += dk
        dv_acc[:, lanes] += dv
        return carry

    lax.fori_loop(0, heads // 2, pair, 0)

    def group(number, carry):
        span = pl.ds(pl.multiple_of(number * 16, 16), 16)
        sums_ref[...] += bucket_products(
            bucket_ref[span, :], ds_keep[:, span, :].reshape(heads * 16, keys), labels
        )
        return carry

    lax.fori_loop(0, rows // 16, group, 0)

    @pl.when(step_i == pl.num_programs(1) - 1)
    def _():
        dk_ref[...] = dk_acc[...].astype(BFLOAT)
        dv_ref[...] = dv_acc[...].astype(BFLOAT)


def doc_backward(q_rows, kv_rows, da_rows, mixture, probs, buckets, n_docs, rows, labels):
    width = q_rows.shape[1]
    heads = probs.shape[0]
    keys = buckets.shape[1]
    block = math.gcd(rows, 256)
    steps = rows // block
    along = pl.BlockSpec((block, width), lambda d, i: (d * steps + i, 0))
    per_doc = pl.BlockSpec((keys, width), lambda d, i: (d, 0))
    return pl.pallas_call(
        functools.partial(doc_backward_kernel, labels),
        grid=(n_docs, steps),
        in_specs=[
            along,
            per_doc,
            pl.BlockSpec((keys, width), lambda d, i: (d, 1)),
            along,
            along,
            pl.BlockSpec((heads, block, keys), lambda d, i: (0, d * steps + i, 0)),
            pl.BlockSpec((block, keys), lambda d, i: (i, 0)),
        ],
        out_specs=[along, per_doc, per_doc, whole((16 * labels, heads * 16))],
        out_shape=[
            jax.ShapeDtypeStruct((n_docs * rows, width), BFLOAT),
            jax.ShapeDtypeStruct((n_docs * keys, width), BFLOAT),
            jax.ShapeDtypeStruct((n_docs * keys, width), BFLOAT),
            jax.ShapeDtypeStruct((16 * labels, heads * 16), SINGLE),
        ],
        scratch_shapes=[
            pltpu.VMEM((keys, width), SINGLE),
            pltpu.VMEM((keys, width), SINGLE),
            pltpu.VMEM((heads, block, keys), BFLOAT),
        ],
        compiler_params=params(),
        cost_estimate=cost(70 * n_docs * rows * keys * width, 2 * heads * n_docs * rows * keys),
    )(q_rows, kv_rows, kv_rows, da_rows, mixture, probs, buckets)


def query_block(q_rows, k_rows, v_rows, table_ref, index, heads):
    rows, width = q_rows.shape
    head_dim = width // heads
    softs, outs = [], []
    for step in range(heads // 2):
        lanes = slice(step * 2 * head_dim, (step + 1) * 2 * head_dim)
        q_pair, k_pair, v_pair = q_rows[:, lanes], k_rows[:, lanes], v_rows[:, lanes]
        wide = first_lanes(q_pair.shape, head_dim)
        total = None
        for side in range(2):
            head = 2 * step + side
            mine = wide if side == 0 else ~wide
            table = jnp.broadcast_to(table_ref[head : head + 1, :], (rows, 128))
            bias = jnp.take_along_axis(table, index, axis=1, mode="promise_in_bounds")
            scores = nt(jnp.where(mine, q_pair, 0), k_pair) + bias
            shifted = jnp.exp(scores - jnp.max(scores, axis=-1, keepdims=True))
            inverse = 1.0 / jnp.sum(shifted, axis=-1, keepdims=True)
            soft = (shifted * inverse).astype(BFLOAT)
            softs.append(soft)
            term = nn(soft, jnp.where(mine, v_pair, 0))
            total = term if total is None else total + term
        outs.append(total.astype(BFLOAT))
    return softs, jnp.concatenate(outs, 1)


def query_forward_kernel(q_ref, kv_ref, table_ref, bucket_ref, mix_ref, prob_ref):
    width = q_ref.shape[1]
    softs, mix_ref[...] = query_block(
        q_ref[...], kv_ref[:, :width], kv_ref[:, width:], table_ref, bucket_ref[...], prob_ref.shape[0]
    )
    for head, soft in enumerate(softs):
        prob_ref[head] = soft


def query_forward(q_rows, kv_rows, table, buckets, start, count, heads):
    width = q_rows.shape[1]
    offset = start // 128
    return pl.pallas_call(
        query_forward_kernel,
        grid=(count // 128,),
        in_specs=[
            pl.BlockSpec((128, width), lambda i: (offset + i, 0)),
            pl.BlockSpec((128, 2 * width), lambda i: (offset + i, 0)),
            whole(table.shape),
            whole(buckets.shape),
        ],
        out_specs=[
            pl.BlockSpec((128, width), lambda i: (i, 0)),
            pl.BlockSpec((heads, 128, 128), lambda i: (0, i, 0)),
        ],
        out_shape=[
            jax.ShapeDtypeStruct((count, width), BFLOAT),
            jax.ShapeDtypeStruct((heads, count, 128), BFLOAT),
        ],
        compiler_params=params(),
        cost_estimate=cost(4 * count * 128 * width * 4, 10 * count * width),
    )(q_rows, kv_rows, table, buckets)


def query_backward_kernel(
    labels, q_ref, kv_ref, da_ref, mix_ref, prob_ref, bucket_ref, dq_ref, dkv_ref, sums_ref, ds_keep
):
    rows, width = q_ref.shape
    heads = prob_ref.shape[0]
    head_dim = width // heads

    @pl.when(pl.program_id(0) == 0)
    def _():
        sums_ref[...] = jnp.zeros_like(sums_ref)

    for step in range(heads // 2):
        lanes = slice(step * 2 * head_dim, (step + 1) * 2 * head_dim)
        right = slice(width + lanes.start, width + lanes.stop)
        dq, dk, dv, kept = attend_back(
            q_ref[:, lanes],
            kv_ref[:, lanes],
            kv_ref[:, right],
            da_ref[:, lanes],
            mix_ref[:, lanes],
            [prob_ref[2 * step], prob_ref[2 * step + 1]],
            head_dim,
        )
        ds_keep[2 * step] = kept[0]
        ds_keep[2 * step + 1] = kept[1]
        dq_ref[:, lanes] = dq.astype(BFLOAT)
        dkv_ref[:, lanes] = dk.astype(BFLOAT)
        dkv_ref[:, right] = dv.astype(BFLOAT)

    def group(number, carry):
        span = pl.ds(pl.multiple_of(number * 16, 16), 16)
        sums_ref[...] += bucket_products(
            bucket_ref[span, :], ds_keep[:, span, :].reshape(heads * 16, rows), labels
        )
        return carry

    lax.fori_loop(0, rows // 16, group, 0)


def query_backward(q_rows, kv_rows, da_rows, mixture, probs, buckets, start, labels):
    width = q_rows.shape[1]
    heads, count, _ = probs.shape
    offset = start // 128
    return pl.pallas_call(
        functools.partial(query_backward_kernel, labels),
        grid=(count // 128,),
        in_specs=[
            pl.BlockSpec((128, width), lambda i: (offset + i, 0)),
            pl.BlockSpec((128, 2 * width), lambda i: (offset + i, 0)),
            pl.BlockSpec((128, width), lambda i: (offset + i, 0)),
            pl.BlockSpec((128, width), lambda i: (offset + i, 0)),
            pl.BlockSpec((heads, 128, 128), lambda i: (0, i, 0)),
            whole(buckets.shape),
        ],
        out_specs=[
            pl.BlockSpec((128, width), lambda i: (i, 0)),
            pl.BlockSpec((128, 2 * width), lambda i: (i, 0)),
            whole((16 * labels, heads * 16)),
        ],
        out_shape=[
            jax.ShapeDtypeStruct((count, width), BFLOAT),
            jax.ShapeDtypeStruct((count, 2 * width), BFLOAT),
            jax.ShapeDtypeStruct((16 * labels, heads * 16), SINGLE),
        ],
        scratch_shapes=[pltpu.VMEM((heads, 128, 128), BFLOAT)],
        compiler_params=params(),
        cost_estimate=cost(8 * count * 128 * width * 4, 14 * count * width),
    )(q_rows, kv_rows, da_rows, mixture, probs, buckets)


def feed_kernel(
    chunk,
    x_ref,
    mix_ref,
    dy_ref,
    gain_ref,
    wou_ref,
    wd_ref,
    y_ref,
    dh_ref,
    da_ref,
    gou_ref,
    gd_ref,
    gg_ref,
    gou_acc,
    gd_acc,
    stage,
    sems,
):
    step = pl.program_id(0)
    hidden, width = wd_ref.shape

    @pl.when(step == 0)
    def _():
        gou_acc[...] = jnp.zeros_like(gou_acc)
        gd_acc[...] = jnp.zeros_like(gd_acc)
        gg_ref[...] = jnp.zeros_like(gg_ref)

    mixture = mix_ref[...]
    dy = dy_ref[...]
    gain = gain_ref[...]
    residual = x_ref[...].astype(SINGLE) + nn(mixture, wou_ref[:, :width])
    scale = scale_of(residual)
    second = (residual * scale * gain).astype(BFLOAT)
    y = residual
    grad_second = jnp.zeros_like(residual)
    for part in range(hidden // chunk):
        span = slice(part * chunk, (part + 1) * chunk)
        past = slice(width + part * chunk, width + (part + 1) * chunk)
        pre = nn(second, wou_ref[:, past])
        grad_hidden = nt(dy, wd_ref[span, :])
        square = pre * pre
        tanh = jnp.tanh(pre * (GELU_A + (GELU_A * GELU_B) * square))
        half = 0.5 + 0.5 * tanh
        act = pre * half
        slope = half + act * (1.0 - tanh) * (GELU_A + (3.0 * GELU_A * GELU_B) * square)
        act_low = act.astype(BFLOAT)
        grad_pre = (grad_hidden * slope).astype(BFLOAT)
        y = y + nn(act_low, wd_ref[span, :])
        grad_second = grad_second + nt(grad_pre, wou_ref[:, past])
        gd_acc[span, :] += tn(act_low, dy)
        gou_acc[:, past] += tn(second, grad_pre)
    y_ref[...] = y.astype(BFLOAT)
    gg_ref[...] += jnp.sum(grad_second * residual * scale, axis=0, keepdims=True)
    grad_res = dy.astype(SINGLE) + norm_back(residual, scale, grad_second * gain)
    dh_ref[...] = grad_res
    grad_low = grad_res.astype(BFLOAT)
    da_ref[...] = nt(grad_low, wou_ref[:, :width]).astype(BFLOAT)
    gou_acc[:, :width] += tn(mixture, grad_low)

    @pl.when(step == pl.num_programs(0) - 1)
    def _():
        pieces = []
        rows, columns = stage.shape[1:]
        for acc, out in ((gd_acc, gd_ref), (gou_acc, gou_ref)):
            for r in range(acc.shape[0] // rows):
                for c in range(acc.shape[1] // columns):
                    spot = (pl.ds(r * rows, rows), pl.ds(c * columns, columns))
                    pieces.append((acc, out, spot))
        flying = [None, None]
        for number, (acc, out, spot) in enumerate(pieces):
            slot = number % 2
            if flying[slot] is not None:
                flying[slot].wait()
            stage[slot] = acc[spot].astype(BFLOAT)
            flying[slot] = pltpu.make_async_copy(stage.at[slot], out.at[spot], sems.at[slot])
            flying[slot].start()
        for copy in flying:
            if copy is not None:
                copy.wait()


def feed(tokens, mixture, cotangent, gain, w_out_up, w_down):
    rows, width = tokens.shape
    hidden = w_down.shape[0]
    block = math.gcd(rows, 256)
    along = pl.BlockSpec((block, width), lambda i: (i, 0))
    anywhere = pl.BlockSpec(memory_space=pl.ANY)
    return pl.pallas_call(
        functools.partial(feed_kernel, math.gcd(hidden, 768)),
        grid=(rows // block,),
        in_specs=[
            along,
            along,
            along,
            whole((1, width)),
            whole(w_out_up.shape),
            whole(w_down.shape),
        ],
        out_specs=[along, along, along, anywhere, anywhere, whole((1, width))],
        out_shape=[
            jax.ShapeDtypeStruct((rows, width), BFLOAT),
            jax.ShapeDtypeStruct((rows, width), SINGLE),
            jax.ShapeDtypeStruct((rows, width), BFLOAT),
            jax.ShapeDtypeStruct(w_out_up.shape, BFLOAT),
            jax.ShapeDtypeStruct(w_down.shape, BFLOAT),
            jax.ShapeDtypeStruct((1, width), SINGLE),
        ],
        scratch_shapes=[
            pltpu.VMEM(w_out_up.shape, SINGLE),
            pltpu.VMEM(w_down.shape, SINGLE),
            pltpu.VMEM((2, width, width), BFLOAT),
            pltpu.SemaphoreType.DMA((2,)),
        ],
        compiler_params=params(),
        cost_estimate=cost(2 * rows * width * (6 * hidden + 3 * width), 14 * rows * width),
    )(tokens, mixture, cotangent, gain.reshape(1, width), w_out_up, w_down)


def unproject_kernel(
    x_ref, gain_ref, dq_ref, dk_ref, dv_ref, dh_ref, w_ref, dx_ref, low_ref, gw_ref, gg_ref, acc
):
    step = pl.program_id(0)
    width = w_ref.shape[0]

    @pl.when(step == 0)
    def _():
        acc[...] = jnp.zeros_like(acc)
        gg_ref[...] = jnp.zeros_like(gg_ref)

    values = x_ref[...].astype(SINGLE)
    gain = gain_ref[...]
    scale = scale_of(values)
    normed = (values * scale * gain).astype(BFLOAT)
    grad = jnp.zeros_like(values)
    for number, ref in enumerate((dq_ref, dk_ref, dv_ref)):
        span = slice(number * width, (number + 1) * width)
        part = ref[...]
        acc[:, span] += tn(normed, part)
        grad = grad + nt(part, w_ref[:, span])
    gg_ref[...] += jnp.sum(grad * values * scale, axis=0, keepdims=True)
    dx = dh_ref[...] + norm_back(values, scale, grad * gain)
    dx_ref[...] = dx
    low_ref[...] = dx.astype(BFLOAT)

    @pl.when(step == pl.num_programs(0) - 1)
    def _():
        gw_ref[...] = acc[...].astype(BFLOAT)


def unproject(tokens, gain, dq, dk, dv, grad_res, w_qkv):
    rows, width = tokens.shape
    block = math.gcd(rows, 256)
    along = pl.BlockSpec((block, width), lambda i: (i, 0))
    return pl.pallas_call(
        unproject_kernel,
        grid=(rows // block,),
        in_specs=[along, whole((1, width)), along, along, along, along, whole(w_qkv.shape)],
        out_specs=[along, along, whole(w_qkv.shape), whole((1, width))],
        out_shape=[
            jax.ShapeDtypeStruct((rows, width), SINGLE),
            jax.ShapeDtypeStruct((rows, width), BFLOAT),
            jax.ShapeDtypeStruct(w_qkv.shape, BFLOAT),
            jax.ShapeDtypeStruct((1, width), SINGLE),
        ],
        scratch_shapes=[pltpu.VMEM(w_qkv.shape, SINGLE)],
        compiler_params=params(),
        cost_estimate=cost(12 * rows * width * width, 18 * rows * width),
    )(tokens, gain.reshape(1, width), dq, dk, dv, grad_res, w_qkv)


def bits_of(count):
    return [1 << place for place in reversed(range(count.bit_length() - 1))]


def axis_bits():
    dp_bits = [("dp", bit) for bit in bits_of(lax.axis_size("dp"))]
    seq_bits = [("seq", bit) for bit in bits_of(lax.axis_size("seq"))]
    return dp_bits, seq_bits


def gather_orders():
    dp_bits, seq_bits = axis_bits()
    far = (len(dp_bits) + 1) // 2
    z_bits, x_bits = dp_bits[:far], dp_bits[far:]
    y_bits, core_bits = seq_bits[:-1], seq_bits[-1:]
    return [z_bits + y_bits + x_bits + core_bits, z_bits + x_bits + y_bits + core_bits]


def swap(values, name, bit):
    count = lax.axis_size(name)
    return lax.ppermute(values, name, [(i, i ^ bit) for i in range(count)])


def is_high(name, bit):
    return (lax.axis_index(name) & bit) != 0


def gather_rows(shard, order):
    dp_bits, seq_bits = axis_bits()
    everything = dp_bits + seq_bits
    done = []
    held = shard
    for item in order:
        other = swap(held, *item)
        done.append(item)
        place = sorted(everything.index(one) for one in done).index(everything.index(item))
        high = is_high(*item)
        held = jnp.where(
            high, jnp.stack([other, held], place), jnp.stack([held, other], place)
        )
    return held.reshape(-1, shard.shape[1])


def scatter_rows(values, order):
    dp_bits, seq_bits = axis_bits()
    left = dp_bits + seq_bits
    rows = values.shape[0] >> len(left)
    held = values.reshape((2,) * len(left) + (rows, values.shape[1]))
    for item in order:
        place = left.index(item)
        mine = is_high(*item).astype(jnp.int32)
        away = lax.dynamic_index_in_dim(held, 1 - mine, place, keepdims=False)
        kept = lax.dynamic_index_in_dim(held, mine, place, keepdims=False)
        other = swap(away, *item)
        held = kept.astype(SINGLE) + other.astype(SINGLE)
        left.remove(item)
        if left:
            held = held.astype(BFLOAT)
    return held


def scatter_columns(values, parts):
    orders = [order[::-1] for order in gather_orders()]
    columns = values.shape[1] // parts
    return jnp.concatenate(
        [
            scatter_rows(values[:, p * columns : (p + 1) * columns], orders[p % len(orders)])
            for p in range(parts)
        ],
        1,
    )


def sum_all(values):
    dp_bits, seq_bits = axis_bits()
    for item in seq_bits[::-1] + dp_bits[::-1]:
        values = values + swap(values, *item)
    return values


def own_document(shard):
    count = lax.axis_size("seq")
    n_docs = shard.shape[0]
    me = lax.axis_index("seq")
    if n_docs >= count:
        per = n_docs // count
        blocks = shard.reshape((count, per) + shard.shape[1:])
        sets, group = count, 1
    else:
        blocks = shard[:, None]
        sets, group = n_docs, count // n_docs
    got = []
    for r in range(sets):
        piece = lax.dynamic_index_in_dim(blocks, (me % sets) ^ r, 0, keepdims=False)
        route = [
            (u * sets + i, (i ^ r) * group + u) for u in range(group) for i in range(sets)
        ]
        if any(a != b for a, b in route):
            piece = lax.ppermute(piece, "seq", route)
        got.append(piece)
    stacked = jnp.stack(got, 0)
    mine = me // group
    ordered = [lax.dynamic_index_in_dim(stacked, mine ^ i, 0, keepdims=False) for i in range(sets)]
    return jnp.concatenate(ordered, 1).reshape(-1, shard.shape[-1])


def spread_document(rows, like):
    count = lax.axis_size("seq")
    n_docs, shard_rows, width = like.shape
    me = lax.axis_index("seq")
    if n_docs >= count:
        per = n_docs // count
        sets, group = count, 1
    else:
        per = 1
        sets, group = n_docs, count // n_docs
    blocks = rows.reshape(per, sets, shard_rows, width)
    mine = me // group
    got = []
    for r in range(sets):
        piece = lax.dynamic_index_in_dim(blocks, mine ^ r, 1, keepdims=False)
        route = [
            ((i ^ r) * group + u, u * sets + i) for u in range(group) for i in range(sets)
        ]
        if any(a != b for a, b in route):
            piece = lax.ppermute(piece, "seq", route)
        got.append(piece)
    stacked = jnp.stack(got, 0)
    ordered = [
        lax.dynamic_index_in_dim(stacked, (me % sets) ^ i, 0, keepdims=False) for i in range(sets)
    ]
    return jnp.concatenate(ordered, 0)


def gather_positions(shard):
    seq_bits = axis_bits()[1]
    done = []
    held = shard
    for item in seq_bits:
        other = swap(held, *item)
        high = is_high(*item)
        place = len(done)
        held = jnp.where(
            high, jnp.stack([other, held], place), jnp.stack([held, other], place)
        )
        done.append(item)
    return held.reshape(-1, shard.shape[1])


class Spot:
    def __init__(self):
        self.dp = lax.axis_index("dp")
        self.seq = lax.axis_index("seq")
        self.core = self.seq % 2
        self.y = self.seq // 2
        self.x = self.dp % 2
        self.z = self.dp // 2

    def partner(self, z=0, x=0, y=0, core=0):
        dp = self.flip(self.z, z) * 2 + self.flip(self.x, x)
        seq = self.flip(self.y, y) * 2 + self.flip(self.core, core)
        return (dp, seq)

    @staticmethod
    def flip(value, bits):
        if bits == 0:
            return value
        if bits == 1:
            return value + 1 - 2 * (value % 2)
        if bits == 2:
            return (value + 2) % 4
        return 3 - value

    def chip(self, z=0, x=0, y=0):
        return (self.flip(self.z, z) * 2 + self.flip(self.x, x)) * 2 + self.flip(self.y, y)


def send(source, target, sems, number, device):
    return pltpu.make_async_remote_copy(
        src_ref=source,
        dst_ref=target,
        send_sem=sems.at[0, number],
        recv_sem=sems.at[1, number],
        device_id=device,
        device_id_type=pl.DeviceIdType.MESH,
    )


def greet(partners):
    barrier = pltpu.get_barrier_semaphore()
    for device in partners:
        pl.semaphore_signal(barrier, inc=1, device_id=device, device_id_type=pl.DeviceIdType.MESH)
    pl.semaphore_wait(barrier, len(partners))


COPIES = 17


class Gather:
    def __init__(self, spot, shard, whole_ref, mine, theirs, block, sems, local):
        self.spot, self.shard, self.whole = spot, shard, whole_ref
        self.mine, self.theirs, self.block = mine, theirs, block
        self.sems, self.local = sems, local
        self.rows, self.half = block.shape

    def columns(self, core):
        return pl.ds(pl.multiple_of(core * self.half, 128), self.half)

    def area(self, **bits):
        row = pl.multiple_of(self.spot.chip(**bits) * self.rows, 16)
        return self.whole.at[pl.ds(row, self.rows), self.columns(self.spot.core)]

    def copy(self, number):
        spot = self.spot
        if number == 0:
            source, target = self.shard.at[:, self.columns(1 - spot.core)], self.theirs
            device = spot.partner(core=1)
        elif number < 4:
            source, target, device = self.block, self.area(), spot.partner(z=number)
        elif number < 8:
            target, device = self.area(z=number - 4), spot.partner(y=1)
            source = self.block if number == 4 else target
        elif number < 16:
            target = self.area(z=(number - 8) % 4, y=(number - 8) // 4)
            source, device = self.block if number == 8 else target, spot.partner(x=1)
        else:
            source = target = self.whole.at[:, self.columns(spot.core)]
            device = spot.partner(core=1)
        return send(source, target, self.sems, number, device)

    def load(self):
        return pltpu.make_async_copy(
            self.shard.at[:, self.columns(self.spot.core)], self.mine, self.local.at[0]
        )

    def here(self):
        return pltpu.make_async_copy(self.block, self.area(), self.local.at[1])

    def join_start(self):
        self.copy(0).start()
        self.load().start()

    def join_end(self):
        self.load().wait()
        self.copy(0).wait_recv()
        part = self.rows // 2
        low = self.spot.core == 0
        mine = self.mine[...].astype(SINGLE)[:part]
        theirs = self.theirs[...].astype(SINGLE)[:part]
        self.block[:part, :] = jnp.where(low, mine, theirs).astype(BFLOAT)
        self.block[part:, :] = jnp.where(low, theirs, mine).astype(BFLOAT)
        self.here().start()

    def z_start(self):
        for number in (1, 2, 3):
            self.copy(number).start()

    def y_own(self):
        self.copy(4).start()
        self.copy(8).start()

    def y_more(self):
        for k in (1, 2, 3):
            self.copy(k).wait_recv()
            self.copy(4 + k).start()
            self.copy(8 + k).start()

    def x_more(self):
        for k in (0, 1, 2, 3):
            self.copy(4 + k).wait_recv()
            self.copy(12 + k).start()

    def swap_start(self):
        for number in range(8, 16):
            self.copy(number).wait_recv()
        self.here().wait()
        self.copy(16).start()

    def finish(self):
        self.copy(16).wait_recv()
        for number in range(COPIES):
            self.copy(number).wait_send()


class Move:
    PARTNERS = ((1, 0), (1, 1), (0, 1))

    def __init__(self, spot, source, target, own_target, sems, local):
        self.spot, self.source, self.target = spot, source, target
        self.own_target, self.sems, self.local = own_target, sems, local

    def own(self):
        return pltpu.make_async_copy(
            self.source(self.spot.seq), self.own_target(self.spot.seq), self.local
        )

    def copy(self, number):
        y, core = self.PARTNERS[number]
        device = self.spot.partner(y=y, core=core)
        return send(self.source(device[1]), self.target(self.spot.seq), self.sems, number, device)

    def start(self):
        self.own().start()
        for number in range(3):
            self.copy(number).start()

    def finish(self):
        self.own().wait()
        for number in range(3):
            self.copy(number).wait()


def all_partners(spot):
    return [
        spot.partner(core=1),
        spot.partner(z=1),
        spot.partner(z=2),
        spot.partner(z=3),
        spot.partner(x=1),
        spot.partner(y=1),
        spot.partner(y=1, core=1),
    ]


def row_block(ref, rows):
    return lambda number: ref.at[pl.ds(pl.multiple_of(number * rows, 16), rows), :]


def front_kernel(
    docs_ref,
    queries_ref,
    doc_cot_ref,
    query_cot_ref,
    qkv_shard,
    ou_shard,
    down_shard,
    bucket_shard,
    gain_ref,
    doc_table_ref,
    query_table_ref,
    query_bucket_ref,
    tokens_out,
    cots_out,
    w_out,
    ou_out,
    down_out,
    bucket_out,
    qkv_out,
    mix_ref,
    prob_ref,
    query_prob_ref,
    x_v,
    w_v,
    qkv_v,
    bucket_v,
    qkv_mine,
    qkv_theirs,
    qkv_block,
    ou_mine,
    ou_theirs,
    ou_block,
    down_mine,
    down_theirs,
    down_block,
    gather_sems,
    move_sems,
    local,
):
    step = pl.program_id(0)
    last = pl.num_programs(0) - 1
    spot = Spot()
    n_docs, shard_rows, width = docs_ref.shape
    doc_rows = n_docs * shard_rows
    query_rows = queries_ref.shape[0]
    heads = prob_ref.shape[0]
    head_dim = width // heads
    block = prob_ref.shape[1]

    gathers = []
    for number, parts in enumerate(
        (
            (qkv_shard, w_v, qkv_mine, qkv_theirs, qkv_block),
            (ou_shard, ou_out, ou_mine, ou_theirs, ou_block),
            (down_shard, down_out, down_mine, down_theirs, down_block),
        )
    ):
        gathers.append(
            Gather(spot, *parts, gather_sems.at[number], local.at[pl.ds(2 * number, 2)])
        )
    g_qkv, g_ou, g_down = gathers
    token_move = Move(
        spot,
        lambda number: docs_ref.at[number],
        row_block(x_v, shard_rows),
        row_block(x_v, shard_rows),
        move_sems.at[0],
        local.at[6],
    )
    cot_move = Move(
        spot,
        lambda number: doc_cot_ref.at[number],
        row_block(cots_out, shard_rows),
        row_block(cots_out, shard_rows),
        move_sems.at[1],
        local.at[7],
    )
    query_load = pltpu.make_async_copy(
        queries_ref, x_v.at[pl.ds(doc_rows, query_rows), :], local.at[8]
    )
    cot_copy = pltpu.make_async_copy(
        query_cot_ref, cots_out.at[pl.ds(doc_rows, query_rows), :], local.at[9]
    )
    bucket_rows = row_block(bucket_v, shard_rows)
    bucket_load = pltpu.make_async_copy(bucket_shard, bucket_rows(spot.seq), local.at[10])
    bucket_y = send(
        bucket_shard, bucket_rows(spot.seq), move_sems.at[2], 0, spot.partner(y=1)
    )
    near = bucket_rows(spot.seq)
    far = bucket_rows(spot.partner(y=1)[1])
    bucket_near = send(near, near, move_sems.at[2], 1, spot.partner(core=1))
    bucket_far = send(far, far, move_sems.at[2], 2, spot.partner(core=1))
    saves = [
        pltpu.make_async_copy(x_v, tokens_out, local.at[11]),
        pltpu.make_async_copy(w_v, w_out, local.at[12]),
        pltpu.make_async_copy(qkv_v, qkv_out, local.at[13]),
        pltpu.make_async_copy(bucket_v, bucket_out, local.at[14]),
    ]

    @pl.when(step == 0)
    def _():
        greet(all_partners(spot))
        g_qkv.join_start()
        query_load.start()
        bucket_load.start()
        token_move.own().start()
        g_ou.join_start()
        g_down.join_start()
        g_qkv.join_end()
        g_qkv.z_start()
        g_qkv.y_own()
        token_move.copy(0).start()
        token_move.copy(2).start()
        g_ou.join_end()
        g_down.join_end()
        g_qkv.y_more()
        token_move.copy(1).start()
        g_ou.z_start()
        g_down.z_start()
        g_qkv.x_more()
        bucket_y.start()
        bucket_load.wait()
        bucket_near.start()
        g_qkv.swap_start()
        g_ou.y_own()
        g_down.y_own()
        query_load.wait()
        token_move.finish()
        g_qkv.finish()
        saves[0].start()
        saves[1].start()

        def project_block(number, carry):
            span = pl.ds(pl.multiple_of(number * block, 16), block)
            values = x_v[span, :].astype(SINGLE)
            normed = (values * scale_of(values) * gain_ref[...]).astype(BFLOAT)
            for part in range(3):
                lanes = slice(part * width, (part + 1) * width)
                qkv_v[span, lanes] = nn(normed, w_v[:, lanes]).astype(BFLOAT)
            return carry

        blocks = (doc_rows + query_rows) // block
        lax.fori_loop(0, blocks // 2, project_block, 0)
        g_ou.y_more()
        g_down.y_more()
        lax.fori_loop(blocks // 2, blocks, project_block, 0)
        saves[2].start()
        cot_move.start()
        cot_copy.start()
        bucket_y.wait_recv()
        bucket_far.start()

        def query_step(number, carry):
            span = pl.ds(pl.multiple_of(doc_rows + number * 128, 16), 128)
            softs, mixed = query_block(
                qkv_v[span, :width],
                qkv_v[span, width : 2 * width],
                qkv_v[span, 2 * width :],
                query_table_ref,
                query_bucket_ref[...],
                heads,
            )
            mix_ref[span, :] = mixed
            for head, soft in enumerate(softs):
                query_prob_ref[head, pl.ds(pl.multiple_of(number * 128, 16), 128), :] = soft
            return carry

        lax.fori_loop(0, query_rows // 128, query_step, 0)
        bucket_near.wait()
        bucket_far.wait()
        bucket_y.wait_send()
        saves[3].start()

    @pl.when(step == 1)
    def _():
        g_ou.x_more()
        g_down.x_more()

    @pl.when(step == last - 1)
    def _():
        g_ou.swap_start()

    @pl.when(step == last)
    def _():
        g_down.swap_start()

    @pl.when(step > 0)
    def _():
        span = pl.ds(pl.multiple_of((step - 1) * block, 16), block)

        def pair(number, carry):
            lanes = pair_lanes(number, head_dim)
            mix_ref[span, lanes] = attend_pair(
                qkv_v[span, lanes],
                qkv_v[:doc_rows, pair_lanes(number, head_dim, width)],
                qkv_v[:doc_rows, pair_lanes(number, head_dim, 2 * width)],
                doc_table_ref[pl.ds(number, 1), :],
                bucket_v,
                pl.multiple_of((step - 1) * block, 16),
                prob_ref,
                number,
                head_dim,
            )
            return carry

        lax.fori_loop(0, heads // 2, pair, 0)

    @pl.when(step == last)
    def _():
        g_ou.finish()
        g_down.finish()
        cot_move.finish()
        cot_copy.wait()
        for save in saves:
            save.wait()


def gather_scratch(shard):
    rows, columns = shard.shape
    padded = -(-rows // 16) * 16
    half = columns // 2
    return [
        pltpu.VMEM((padded, half), BFLOAT),
        pltpu.VMEM((padded, half), BFLOAT),
        pltpu.VMEM((2 * rows, half), BFLOAT),
    ]


def pad_rows(shard):
    rows = shard.shape[0]
    return jnp.pad(shard, ((0, -rows % 16), (0, 0)))


def front(
    docs,
    queries,
    doc_cot,
    query_cot,
    shards,
    buckets,
    gain,
    doc_table,
    query_table,
    query_buckets,
    heads,
):
    n_docs, shard_rows, width = docs.shape
    doc_rows = n_docs * shard_rows
    query_rows = queries.shape[0]
    rows = doc_rows + query_rows
    keys = buckets.shape[1]
    block = 256
    steps = doc_rows // block
    anywhere = pl.BlockSpec(memory_space=pl.ANY)
    wholes = [jax.ShapeDtypeStruct((shard.shape[0] * 32, shard.shape[1]), BFLOAT) for shard in shards]
    scratch = []
    for shard in shards:
        scratch += gather_scratch(shard)
    return pl.pallas_call(
        front_kernel,
        grid=(steps + 1,),
        in_specs=[anywhere] * 8
        + [
            whole((1, width)),
            whole(doc_table.shape),
            whole(query_table.shape),
            whole(query_buckets.shape),
        ],
        out_specs=[anywhere] * 7
        + [
            whole((rows, width)),
            pl.BlockSpec((heads, block, keys), lambda i: (0, jnp.maximum(i - 1, 0), 0)),
            whole((heads, query_rows, 128)),
        ],
        out_shape=[
            jax.ShapeDtypeStruct((rows, width), BFLOAT),
            jax.ShapeDtypeStruct((rows, width), BFLOAT),
            *wholes,
            jax.ShapeDtypeStruct((keys, keys), jnp.int16),
            jax.ShapeDtypeStruct((rows, 3 * width), BFLOAT),
            jax.ShapeDtypeStruct((rows, width), BFLOAT),
            jax.ShapeDtypeStruct((heads, doc_rows, keys), BFLOAT),
            jax.ShapeDtypeStruct((heads, query_rows, 128), BFLOAT),
        ],
        scratch_shapes=[
            pltpu.VMEM((rows, width), BFLOAT),
            pltpu.VMEM((width, 3 * width), BFLOAT),
            pltpu.VMEM((rows, 3 * width), BFLOAT),
            pltpu.VMEM((keys, keys), jnp.int16),
            *scratch,
            pltpu.SemaphoreType.DMA((3, 2, COPIES)),
            pltpu.SemaphoreType.DMA((3, 2, 3)),
            pltpu.SemaphoreType.DMA((15,)),
        ],
        compiler_params=pltpu.CompilerParams(
            collective_id=0, has_side_effects=True, vmem_limit_bytes=VMEM_LIMIT
        ),
        cost_estimate=cost(6 * rows * width * width, 100 << 20),
    )(
        docs,
        queries,
        doc_cot,
        query_cot,
        *[pad_rows(shard) for shard in shards],
        buckets,
        gain.reshape(1, width),
        doc_table,
        query_table,
        query_buckets,
    )


class Scatter:
    Z_ORDER = (3, 2, 1, 0)

    def __init__(self, spot, away, buffers, sems):
        self.spot, self.away, self.sems = spot, away, sems
        self.held, self.core_in, self.x_in, self.y_in, self.z_in, self.tail, self.tail_in = buffers
        self.half = self.held.shape[1]
        self.rows = self.held.shape[0] // 16

    def span(self, **bits):
        return pl.ds(pl.multiple_of(self.spot.chip(**bits) * self.rows, 16), self.rows)

    def slot(self, number):
        return pl.ds(number * self.rows, self.rows)

    def copy(self, number):
        spot = self.spot
        if number == 0:
            source, target, device = self.away, self.core_in, spot.partner(core=1)
        elif number < 9:
            index = number - 1
            source = self.held.at[self.span(z=self.Z_ORDER[index // 2], x=1, y=1 - index % 2), :]
            target, device = self.x_in.at[self.slot(index), :], spot.partner(x=1)
        elif number < 13:
            index = number - 9
            source = self.held.at[self.span(z=self.Z_ORDER[index], y=1), :]
            target, device = self.y_in.at[self.slot(index), :], spot.partner(y=1)
        elif number < 16:
            index = number - 13
            source = self.held.at[self.span(z=self.Z_ORDER[index]), :]
            target = self.z_in.at[self.slot(index), :]
            device = spot.partner(z=self.Z_ORDER[index])
        else:
            part = self.rows // 2
            theirs = pl.ds(pl.multiple_of((1 - spot.core) * part, 8), part)
            source, target, device = self.tail.at[theirs, :], self.tail_in, spot.partner(core=1)
        return send(source, target, self.sems, number, device)

    def add(self, span, others):
        total = self.held[span, :].astype(SINGLE) + self.core_in[span, :].astype(SINGLE)
        for ref, place in others:
            total = total + ref[place, :].astype(SINGLE)
        return total

    def core_end(self):
        self.copy(0).wait_recv()

    def x_step(self, index):
        span = self.span(z=self.Z_ORDER[index // 2], x=1, y=1 - index % 2)
        self.held[span, :] = self.add(span, []).astype(BFLOAT)
        self.copy(1 + index).start()

    def y_step(self, index):
        self.copy(1 + 2 * index).wait_recv()
        span = self.span(z=self.Z_ORDER[index], y=1)
        total = self.add(span, [(self.x_in, self.slot(2 * index))])
        self.held[span, :] = total.astype(BFLOAT)
        self.copy(9 + index).start()

    def here(self, index):
        self.copy(2 + 2 * index).wait_recv()
        self.copy(9 + index).wait_recv()
        span = self.span(z=self.Z_ORDER[index])
        others = [(self.x_in, self.slot(2 * index + 1)), (self.y_in, self.slot(index))]
        return span, self.add(span, others)

    def z_step(self, index):
        span, total = self.here(index)
        self.held[span, :] = total.astype(BFLOAT)
        self.copy(13 + index).start()

    def tail_start(self):
        _, total = self.here(3)
        for index in range(3):
            self.copy(13 + index).wait_recv()
            total = total + self.z_in[self.slot(index), :].astype(SINGLE)
        self.tail[...] = total
        self.copy(16).start()

    def finish(self):
        part = self.rows // 2
        low = self.spot.core == 0
        mine = jnp.where(low, self.tail[:part, :], self.tail[part:, :])
        self.copy(16).wait_recv()
        other = self.tail_in[...]
        for number in range(COPIES):
            self.copy(number).wait_send()
        return jnp.where(low, mine, other), jnp.where(low, other, mine)


def scatter_scratch(rows, columns):
    half, part = columns // 2, rows // 16
    return [
        pltpu.VMEM((rows, half), BFLOAT),
        pltpu.VMEM((rows, half), BFLOAT),
        pltpu.VMEM((8 * part, half), BFLOAT),
        pltpu.VMEM((4 * part, half), BFLOAT),
        pltpu.VMEM((3 * part, half), BFLOAT),
        pltpu.VMEM((part, half), SINGLE),
        pltpu.VMEM((part // 2, half), SINGLE),
    ]


def half_of(ref, core):
    half = ref.shape[1] // 2
    return ref.at[:, pl.ds(pl.multiple_of(core * half, 128), half)]


def back_kernel(
    labels,
    doc_steps,
    q_ref,
    k_ref,
    v_ref,
    query_k_ref,
    query_v_ref,
    da_ref,
    mix_ref,
    prob_ref,
    query_prob_ref,
    query_bucket_ref,
    grad_ou_ref,
    grad_down_ref,
    y_ref,
    dq_ref,
    dkv_ref,
    ds_ref,
    sums_ref,
    ou_ref,
    down_ref,
    docs_ref,
    dk_acc,
    dv_acc,
    ds_keep,
    *rest,
):
    ou_buffers, down_buffers, (sems, move_sems, local) = rest[:7], rest[7:14], rest[14:]
    step = pl.program_id(0)
    last = pl.num_programs(0) - 1
    spot = Spot()
    rows, width = q_ref.shape
    pairs = prob_ref.shape[0] // 2
    keys = k_ref.shape[0]
    heads = query_prob_ref.shape[0]
    head_dim = width // heads
    ou = Scatter(spot, half_of(grad_ou_ref, 1 - spot.core), ou_buffers, sems.at[0])
    down = Scatter(spot, half_of(grad_down_ref, 1 - spot.core), down_buffers, sems.at[1])
    both = (ou, down)
    loads = [
        pltpu.make_async_copy(half_of(grad_ou_ref, spot.core), ou.held, local.at[0]),
        pltpu.make_async_copy(half_of(grad_down_ref, spot.core), down.held, local.at[1]),
    ]
    move = Move(
        spot,
        row_block(y_ref, docs_ref.shape[1]),
        lambda number: docs_ref.at[number],
        lambda number: docs_ref.at[number],
        move_sems,
        local.at[2],
    )

    @pl.when(step == 0)
    def _():
        greet(all_partners(spot))
        for scatter, load in zip(both, loads):
            scatter.copy(0).start()
            load.start()
        move.start()
        dk_acc[...] = jnp.zeros_like(dk_acc)
        dv_acc[...] = jnp.zeros_like(dv_acc)
        sums_ref[...] = jnp.zeros_like(sums_ref)

    @pl.when(step == 1)
    def _():
        for scatter, load in zip(both, loads):
            load.wait()
            scatter.core_end()
        for index in range(8):
            for scatter in both:
                scatter.x_step(index)

    def at(when, *actions):
        @pl.when(step == when)
        def _():
            for name, index in actions:
                for scatter in both:
                    getattr(scatter, name)(index)

    at(3, ("y_step", 0))
    at(5, ("z_step", 0), ("y_step", 1))
    at(7, ("z_step", 1), ("y_step", 2))
    at(9, ("z_step", 2), ("y_step", 3))

    @pl.when(step < doc_steps)
    def _():
        def pair(number, carry):
            spread = (step % 2) * pairs + number
            lanes = pair_lanes(spread, head_dim)
            dq, dk, dv, kept = attend_back(
                q_ref[:, lanes],
                k_ref[:, lanes],
                v_ref[:, lanes],
                da_ref[:, lanes],
                mix_ref[:, lanes],
                [prob_ref[2 * number], prob_ref[2 * number + 1]],
                head_dim,
            )
            ds_ref[2 * number] = kept[0]
            ds_ref[2 * number + 1] = kept[1]
            dq_ref[:, lanes] = dq.astype(BFLOAT)
            dk_acc[:, lanes] += dk
            dv_acc[:, lanes] += dv
            return carry

        lax.fori_loop(0, pairs, pair, 0)

    @pl.when(step == doc_steps - 1)
    def _():
        dkv_ref[:keys, :width] = dk_acc[...].astype(BFLOAT)
        dkv_ref[:keys, width:] = dv_acc[...].astype(BFLOAT)

    @pl.when(step >= doc_steps)
    def _():
        def part(number, carry):
            span = pl.ds(pl.multiple_of(number * 128, 128), 128)
            place = pl.ds(pl.multiple_of(keys + (step - doc_steps) * rows + number * 128, 16), 128)
            for pair in range(heads // 2):
                lanes = slice(pair * 2 * head_dim, (pair + 1) * 2 * head_dim)
                dq, dk, dv, kept = attend_back(
                    q_ref[span, lanes],
                    query_k_ref[span, lanes],
                    query_v_ref[span, lanes],
                    da_ref[span, lanes],
                    mix_ref[span, lanes],
                    [query_prob_ref[2 * pair, span, :], query_prob_ref[2 * pair + 1, span, :]],
                    head_dim,
                )
                ds_keep[2 * pair] = kept[0]
                ds_keep[2 * pair + 1] = kept[1]
                dq_ref[span, lanes] = dq.astype(BFLOAT)
                dkv_ref[place, lanes] = dk.astype(BFLOAT)
                dkv_ref[place, width + lanes.start : width + lanes.stop] = dv.astype(BFLOAT)

            def group(index, carry):
                some = pl.ds(pl.multiple_of(index * 16, 16), 16)
                sums_ref[...] += bucket_products(
                    query_bucket_ref[some, :], ds_keep[:, some, :].reshape(heads * 16, 128), labels
                )
                return carry

            lax.fori_loop(0, 8, group, 0)
            return carry

        lax.fori_loop(0, rows // 128, part, 0)

    @pl.when(step == last)
    def _():
        for scatter in both:
            scatter.tail_start()
        for scatter, out in ((ou, ou_ref), (down, down_ref)):
            left, right = scatter.finish()
            out[:, : scatter.half] = left
            out[:, scatter.half :] = right
        move.finish()


def back(qkv, da_rows, mixture, probs, query_probs, query_buckets, grad_ou, grad_down, outputs, n_docs, labels):
    rows, width = da_rows.shape
    heads, doc_rows, keys = probs.shape
    block = 256
    doc_steps = 2 * doc_rows // block
    doc_blocks = doc_rows // block
    steps = doc_steps + (rows - doc_rows) // block
    half = heads // 2

    def row(i):
        return jnp.where(i < doc_steps, i // 2, i - doc_steps + doc_blocks)

    def doc(i):
        clipped = jnp.minimum(i, doc_steps - 1)
        return (clipped % 2, clipped // 2, 0)

    def query(i):
        return jnp.maximum(i, doc_steps) - doc_steps

    anywhere = pl.BlockSpec(memory_space=pl.ANY)
    along = pl.BlockSpec((block, width), lambda i: (row(i), 0))
    once = pl.Buffered(1)
    return pl.pallas_call(
        functools.partial(back_kernel, labels, doc_steps),
        grid=(steps,),
        in_specs=[
            along,
            pl.BlockSpec((keys, width), lambda i: (0, 1), pipeline_mode=once),
            pl.BlockSpec((keys, width), lambda i: (0, 2), pipeline_mode=once),
            pl.BlockSpec((block, width), lambda i: (query(i) + doc_blocks, 1)),
            pl.BlockSpec((block, width), lambda i: (query(i) + doc_blocks, 2)),
            along,
            along,
            pl.BlockSpec((half, block, keys), doc),
            pl.BlockSpec((heads, block, 128), lambda i: (0, query(i), 0)),
            whole(query_buckets.shape),
            anywhere,
            anywhere,
            anywhere,
        ],
        out_specs=[
            along,
            whole((rows, 2 * width)),
            pl.BlockSpec((half, block, keys), doc),
            whole((16 * labels, heads * 16)),
            whole((grad_ou.shape[0] // 32, grad_ou.shape[1])),
            whole((grad_down.shape[0] // 32, grad_down.shape[1])),
            anywhere,
        ],
        out_shape=[
            jax.ShapeDtypeStruct((rows, width), BFLOAT),
            jax.ShapeDtypeStruct((rows, 2 * width), BFLOAT),
            jax.ShapeDtypeStruct(probs.shape, BFLOAT),
            jax.ShapeDtypeStruct((16 * labels, heads * 16), SINGLE),
            jax.ShapeDtypeStruct((grad_ou.shape[0] // 32, grad_ou.shape[1]), SINGLE),
            jax.ShapeDtypeStruct((grad_down.shape[0] // 32, grad_down.shape[1]), SINGLE),
            jax.ShapeDtypeStruct((n_docs, doc_rows // n_docs, width), BFLOAT),
        ],
        scratch_shapes=[
            pltpu.VMEM((keys, width), SINGLE),
            pltpu.VMEM((keys, width), SINGLE),
            pltpu.VMEM((heads, 128, 128), BFLOAT),
            *scatter_scratch(*grad_ou.shape),
            *scatter_scratch(*grad_down.shape),
            pltpu.SemaphoreType.DMA((2, 2, COPIES)),
            pltpu.SemaphoreType.DMA((2, 3)),
            pltpu.SemaphoreType.DMA((3,)),
        ],
        compiler_params=pltpu.CompilerParams(
            collective_id=1, has_side_effects=True, vmem_limit_bytes=VMEM_LIMIT
        ),
        cost_estimate=cost(70 * doc_rows * keys * width, 100 << 20),
    )(
        qkv,
        qkv,
        qkv,
        qkv,
        qkv,
        da_rows,
        mixture,
        probs,
        query_probs,
        query_buckets,
        grad_ou,
        grad_down,
        outputs,
    )


class Total:
    def __init__(self, spot, slots, sems):
        self.spot, self.slots, self.sems = spot, slots, sems

    def rounds(self):
        spot = self.spot
        return (
            (spot.core, 2, [(1, spot.partner(core=1))]),
            (
                spot.x * 2 + spot.y,
                4,
                [(1, spot.partner(y=1)), (2, spot.partner(x=1)), (3, spot.partner(x=1, y=1))],
            ),
            (spot.z, 4, [(k, spot.partner(z=k)) for k in (1, 2, 3)]),
        )

    def run(self, values):
        base = 0
        for index, (place, count, partners) in enumerate(self.rounds()):
            mine = self.slots.at[base + place]
            mine[...] = values
            copies = [send(mine, mine, self.sems.at[index], k - 1, device) for k, device in partners]
            for copy in copies:
                copy.start()
            for copy in copies:
                copy.wait_recv()
            values = self.slots[base]
            for other in range(1, count):
                values = values + self.slots[base + other]
            for copy in copies:
                copy.wait_send()
            base += count
        return values


def leave_kernel(
    labels,
    x_ref,
    gain_ref,
    dq_ref,
    dkv_ref,
    dh_ref,
    w_ref,
    ds_ref,
    bucket_ref,
    query_sums_ref,
    ff_ref,
    found_ref,
    out_ref,
    docs_ref,
    query_dx_ref,
    total_ref,
    normed,
    away,
    low,
    high,
    sums,
    gain_sum,
    slots,
    *rest,
):
    buffers, (sems, move_sems, total_sems, local) = rest[:7], rest[7:]
    step = pl.program_id(0)
    last = pl.num_programs(0) - 1
    spot = Spot()
    rows, width = x_ref.shape
    heads = ds_ref.shape[0]
    doc_rows = low.shape[0]
    block = doc_rows // 4
    scatter = Scatter(spot, away, buffers, sems)
    half = scatter.half
    move = Move(
        spot,
        row_block(low, block),
        lambda number: docs_ref.at[number],
        lambda number: docs_ref.at[number],
        move_sems,
        local.at[0],
    )
    query_copy = pltpu.make_async_copy(high, query_dx_ref, local.at[1])

    @pl.when(step == 0)
    def _():
        greet(all_partners(spot) + [spot.partner(x=1, y=1)])
        gain = gain_ref[...]
        sums[...] = query_sums_ref[...]
        gain_sum[...] = jnp.zeros_like(gain_sum)

        def norm_block(number, carry):
            span = pl.ds(pl.multiple_of(number * block, 16), block)
            values = x_ref[span, :].astype(SINGLE)
            normed[span, :] = (values * scale_of(values) * gain).astype(BFLOAT)
            return carry

        lax.fori_loop(0, rows // block, norm_block, 0)

        def product(core, into):
            part = half // 3

            for number in range(3):
                spot_out = slice(number * part, (number + 1) * part)
                start = core * half + number * part

                def from_q():
                    lanes = pl.ds(pl.multiple_of(start, 128), part)
                    into[:, spot_out] = tn(normed[...], dq_ref[:, lanes]).astype(BFLOAT)

                def from_kv():
                    lanes = pl.ds(pl.multiple_of(start - width, 128), part)
                    into[:, spot_out] = tn(normed[...], dkv_ref[:, lanes]).astype(BFLOAT)

                pl.when(start < width)(from_q)
                pl.when(start >= width)(from_kv)

        product(1 - spot.core, away)
        scatter.copy(0).start()
        product(spot.core, scatter.held)
        scatter.core_end()
        for index in range(8):
            scatter.x_step(index)

        def grad_block(start, into, place):
            span = pl.ds(pl.multiple_of(start, 16), block)
            values = x_ref[span, :].astype(SINGLE)
            scale = scale_of(values)
            grad = nt(dq_ref[span, :], w_ref[:, :width])
            grad = grad + nt(dkv_ref[span, :width], w_ref[:, width : 2 * width])
            grad = grad + nt(dkv_ref[span, width:], w_ref[:, 2 * width :])
            gain_sum[...] += jnp.sum(grad * values * scale, axis=0, keepdims=True)
            dx = dh_ref[span, :] + norm_back(values, scale, grad * gain)
            into[place, :] = dx.astype(into.dtype)

        for number in range(3):
            y, core = Move.PARTNERS[number]
            start = spot.partner(y=y, core=core)[1] * block
            grad_block(start, low, pl.ds(pl.multiple_of(start, 16), block))
            move.copy(number).start()
        start = spot.seq * block
        grad_block(start, low, pl.ds(pl.multiple_of(start, 16), block))
        move.own().start()
        for number in range((rows - doc_rows) // block):
            grad_block(
                doc_rows + number * block, high, pl.ds(number * block, block)
            )
        query_copy.start()

    def at(when, name, index):
        @pl.when(step == when)
        def _():
            getattr(scatter, name)(index)

    at(1, "y_step", 0)
    at(2, "y_step", 1)
    at(3, "z_step", 0)
    at(3, "y_step", 2)
    at(4, "z_step", 1)
    at(4, "y_step", 3)
    at(5, "z_step", 2)

    @pl.when(step == 7)
    def _():
        scatter.tail_start()

    @pl.when(step > 0)
    def _():
        def group(number, carry):
            span = pl.ds(pl.multiple_of(number * 16, 16), 16)
            sums[...] += bucket_products(
                bucket_ref[span, :], ds_ref[:, span, :].reshape(heads * 16, ds_ref.shape[2]), labels
            )
            return carry

        lax.fori_loop(0, ds_ref.shape[1] // 16, group, 0)

    @pl.when(step == last)
    def _():
        shape = sums.shape
        same = (
            lax.broadcasted_iota(jnp.int32, shape, 0) // labels
            == lax.broadcasted_iota(jnp.int32, shape, 1) % 16
        )
        kept = jnp.where(same, sums[...], 0.0)
        folded = kept[:labels]
        for index in range(1, 16):
            folded = folded + kept[index * labels : (index + 1) * labels]
        pick_shape = (heads * 16, 128)
        pick = (
            lax.broadcasted_iota(jnp.int32, pick_shape, 0) // 16
            == lax.broadcasted_iota(jnp.int32, pick_shape, 1)
        )
        bias = jnp.dot(
            folded,
            jnp.where(pick, 1.0, 0.0),
            preferred_element_type=SINGLE,
            precision=lax.Precision.HIGHEST,
        )
        wide = width // 128
        lines = [gain_sum[:, r * 128 : (r + 1) * 128] for r in range(wide)]
        lines += [ff_ref[:, r * 128 : (r + 1) * 128] for r in range(wide)]
        lines += [found_ref[...]] * (slots.shape[1] - labels - 2 * wide)
        total_ref[...] = Total(spot, slots, total_sems).run(jnp.concatenate(lines + [bias], 0))
        left, right = scatter.finish()
        out_ref[:, :half] = left
        out_ref[:, half:] = right
        move.finish()
        query_copy.wait()


def leave(
    tokens, gain, dq, dkv, grad_res, w_qkv, ds, buckets, query_sums, grad_ff, found, n_docs, labels
):
    rows, width = tokens.shape
    heads, doc_rows, keys = ds.shape
    columns = 3 * width
    block = 128
    lines = -(-(2 * width // 128 + 1) // 8) * 8 + labels
    anywhere = pl.BlockSpec(memory_space=pl.ANY)
    return pl.pallas_call(
        functools.partial(leave_kernel, labels),
        grid=(1 + doc_rows // block,),
        in_specs=[
            whole((rows, width)),
            whole((1, width)),
            whole((rows, width)),
            whole((rows, 2 * width)),
            whole((rows, width)),
            whole(w_qkv.shape),
            pl.BlockSpec((heads, block, keys), lambda i: (0, jnp.maximum(i - 1, 0), 0)),
            pl.BlockSpec((block, keys), lambda i: (jnp.maximum(i - 1, 0), 0)),
            whole(query_sums.shape),
            whole((1, width)),
            whole((1, 128)),
        ],
        out_specs=[whole((width // 32, columns)), anywhere, anywhere, whole((lines, 128))],
        out_shape=[
            jax.ShapeDtypeStruct((width // 32, columns), SINGLE),
            jax.ShapeDtypeStruct((n_docs, doc_rows // n_docs, width), BFLOAT),
            jax.ShapeDtypeStruct((rows - doc_rows, width), SINGLE),
            jax.ShapeDtypeStruct((lines, 128), SINGLE),
        ],
        scratch_shapes=[
            pltpu.VMEM((rows, width), BFLOAT),
            pltpu.VMEM((width, columns // 2), BFLOAT),
            pltpu.VMEM((doc_rows, width), BFLOAT),
            pltpu.VMEM((rows - doc_rows, width), SINGLE),
            pltpu.VMEM(query_sums.shape, SINGLE),
            pltpu.VMEM((1, width), SINGLE),
            pltpu.VMEM((10, lines, 128), SINGLE),
            *scatter_scratch(width, columns),
            pltpu.SemaphoreType.DMA((2, COPIES)),
            pltpu.SemaphoreType.DMA((2, 3)),
            pltpu.SemaphoreType.DMA((3, 2, 3)),
            pltpu.SemaphoreType.DMA((2,)),
        ],
        compiler_params=pltpu.CompilerParams(
            collective_id=2, has_side_effects=True, vmem_limit_bytes=VMEM_LIMIT
        ),
        cost_estimate=cost(12 * rows * width * width, 100 << 20),
    )(
        tokens,
        gain.reshape(1, width),
        dq,
        dkv,
        grad_res,
        w_qkv,
        ds,
        buckets,
        query_sums,
        grad_ff,
        found,
    )


def on_device(
    doc_tokens,
    queries,
    doc_cot,
    query_cot,
    q_weight,
    kv_weight,
    out_weight,
    up_weight,
    down_weight,
    attn_gain,
    ff_gain,
    rel_bias,
    doc_buckets,
    query_buckets,
    topk_mask,
    positives,
    pos_count,
):
    n_docs, shard_rows, width = doc_tokens.shape
    n_query, query_len, _ = queries.shape
    bucket_count, heads = rel_bias.shape
    doc_len = doc_buckets.shape[1]
    doc_rows = n_docs * shard_rows
    query_total = n_query * query_len
    seq_size = lax.axis_size("seq")
    group = max(1, seq_size // n_docs)
    local_docs = max(1, n_docs // seq_size)
    local_rows = doc_len // group
    dp_size = lax.axis_size("dp")
    small = (dp_size, seq_size, n_docs) == (8, 4, 4) and width % 256 == 0 and shard_rows % 16 == 0

    qkv_shard = jnp.concatenate([q_weight, kv_weight], 1)
    out_up_shard = jnp.concatenate([out_weight, up_weight], 1)
    low_buckets = doc_buckets.astype(jnp.int16)
    flat_queries = queries.reshape(query_total, width)
    flat_query_cot = query_cot.reshape(query_total, width)

    fixed = jnp.round(rel_bias.T * FIXED).astype(jnp.int32)
    packed = (fixed[0::2] << 16) | (fixed[1::2] & 0xFFFF)
    doc_table = jnp.zeros((8, 128), jnp.int32).at[: heads // 2, :bucket_count].set(packed)
    query_table = jnp.zeros((16, 128), SINGLE).at[:heads, :bucket_count].set(rel_bias.T)
    query_table = query_table.at[:, bucket_count].set(-1e30)
    repeats = 128 // query_len
    same = jnp.kron(jnp.eye(repeats, dtype=jnp.int32), jnp.ones_like(query_buckets))
    tiled = jnp.where(same == 1, jnp.tile(query_buckets, (repeats, repeats)), bucket_count)

    if small:
        tokens, cotangent, w_qkv, w_out_up, w_down, buckets, qkv, mixture, doc_probs, query_probs = front(
            doc_tokens,
            flat_queries,
            doc_cot,
            flat_query_cot,
            (qkv_shard, out_up_shard, down_weight),
            low_buckets,
            attn_gain,
            doc_table,
            query_table,
            tiled,
            heads,
        )
    else:
        order = gather_orders()[0]
        w_qkv = gather_rows(qkv_shard, order)
        w_out_up = gather_rows(out_up_shard, order)
        w_down = gather_rows(down_weight, order)
        tokens = jnp.concatenate([own_document(doc_tokens), flat_queries], 0)
        cotangent = jnp.concatenate([own_document(doc_cot), flat_query_cot], 0)
        buckets = gather_positions(low_buckets)
        if group > 1:
            part = lax.axis_index("seq") % group
            buckets = lax.dynamic_slice_in_dim(buckets, part * local_rows, local_rows, 0)
        q_rows, kv_rows = project(tokens, attn_gain, w_qkv)
        kv_docs = kv_rows
        if group > 1:
            teams = [list(range(t * group, (t + 1) * group)) for t in range(seq_size // group)]
            kv_docs = lax.all_gather(
                kv_rows[:doc_rows], "seq", axis=0, tiled=True, axis_index_groups=teams
            )
        doc_mix, doc_probs = doc_forward(
            q_rows, kv_docs, doc_table, buckets, local_docs, local_rows, heads
        )
        query_mix, query_probs = query_forward(
            q_rows, kv_rows, query_table, tiled, doc_rows, query_total, heads
        )
        mixture = jnp.concatenate([doc_mix, query_mix], 0)
    outputs, grad_res, grad_mix, grad_out_up, grad_down, grad_ff = feed(
        tokens, mixture, cotangent, ff_gain, w_out_up, w_down
    )
    query_out = outputs[doc_rows:].reshape(queries.shape)
    matches = positives[:, :, None] == jnp.arange(doc_len, dtype=jnp.int32)[None, None, :]
    counted = jnp.arange(positives.shape[1], dtype=jnp.int32)[None, :] < pos_count[:, None]
    retrieved = jnp.sum(
        jnp.where(matches & counted[:, :, None], topk_mask[:, None, :].astype(SINGLE), 0.0)
    )

    if small:
        dq, dkv, ds, query_sums, grad_out_up_shard, grad_down_shard, doc_out = back(
            qkv,
            grad_mix,
            mixture,
            doc_probs,
            query_probs,
            tiled,
            grad_out_up,
            grad_down,
            outputs,
            n_docs,
            bucket_count,
        )
        grad_qkv_shard, doc_dx, query_dx, total = leave(
            tokens,
            attn_gain,
            dq,
            dkv,
            grad_res,
            w_qkv,
            ds,
            buckets,
            query_sums,
            grad_ff,
            jnp.full((1, 128), retrieved),
            n_docs,
            bucket_count,
        )
        lines = width // 128
        total_attn = total[:lines].reshape(-1)
        total_ff = total[lines : 2 * lines].reshape(-1)
        total_found = total[2 * lines, 0]
        total_bias = total[-bucket_count:, :heads]
        query_dx = query_dx.reshape(queries.shape)
    else:
        grad_down_shard = scatter_columns(grad_down, 2)
        grad_out_up_shard = scatter_columns(grad_out_up, 2)
        doc_out = spread_document(outputs[:doc_rows], doc_tokens)
        doc_dq, doc_dk, doc_dv, doc_sums = doc_backward(
            q_rows,
            kv_docs,
            grad_mix,
            doc_mix,
            doc_probs,
            buckets,
            local_docs,
            local_rows,
            bucket_count,
        )
        if group > 1:
            both = jnp.concatenate([doc_dk, doc_dv], 1)
            both = lax.psum_scatter(
                both, "seq", scatter_dimension=0, tiled=True, axis_index_groups=teams
            )
            doc_dk, doc_dv = both[:, :width], both[:, width:]
        query_dq, query_dkv, query_sums = query_backward(
            q_rows, kv_rows, grad_mix, mixture, query_probs, tiled, doc_rows, bucket_count
        )
        grad_tokens, grad_low, grad_qkv, grad_attn = unproject(
            tokens,
            attn_gain,
            jnp.concatenate([doc_dq, query_dq], 0),
            jnp.concatenate([doc_dk, query_dkv[:, :width]], 0),
            jnp.concatenate([doc_dv, query_dkv[:, width:]], 0),
            grad_res,
            w_qkv,
        )
        grad_qkv_shard = scatter_columns(grad_qkv, 2)
        doc_dx = spread_document(grad_low[:doc_rows], doc_tokens)
        query_dx = grad_tokens[doc_rows:].reshape(queries.shape)
        sums = (doc_sums + query_sums).reshape(16, bucket_count, heads, 16)
        keep = jnp.eye(16, dtype=SINGLE)[:, None, None, :]
        bias_local = jnp.sum(sums * keep, axis=(0, 3))
        flat = jnp.concatenate(
            [grad_attn[0], grad_ff[0], bias_local.reshape(-1), jnp.full((128,), retrieved)]
        )
        total = sum_all(flat)
        total_attn, total_ff = total[:width], total[width : 2 * width]
        total_bias = total[2 * width : 2 * width + bucket_count * heads]
        total_bias = total_bias.reshape(bucket_count, heads)
        total_found = total[-1]
    slots = float(n_query * dp_size * seq_size * positives.shape[1])
    return (
        doc_out,
        query_out,
        doc_dx.astype(SINGLE),
        query_dx,
        grad_qkv_shard[:, :width],
        grad_qkv_shard[:, width:],
        grad_out_up_shard[:, :width],
        grad_out_up_shard[:, width:],
        grad_down_shard,
        total_attn,
        total_ff,
        total_bias,
        total_found / slots,
    )


def solution(mesh):
    rows_all = P(("dp", "seq"), None)
    return jax.shard_map(
        on_device,
        mesh=mesh,
        in_specs=(
            P("dp", "seq", None),
            P(("dp", "seq"), None, None),
            P("dp", "seq", None),
            P(("dp", "seq"), None, None),
            rows_all,
            rows_all,
            rows_all,
            rows_all,
            rows_all,
            P(),
            P(),
            P(),
            P("seq", None),
            P(),
            rows_all,
            rows_all,
            P(("dp", "seq")),
        ),
        out_specs=(
            P("dp", "seq", None),
            P(("dp", "seq"), None, None),
            P("dp", "seq", None),
            P(("dp", "seq"), None, None),
            rows_all,
            rows_all,
            rows_all,
            rows_all,
            rows_all,
            P(),
            P(),
            P(),
            P(),
        ),
        check_vma=False,
    )
```

```python
import functools
import math

import jax
import jax.numpy as jnp
from jax import lax
from jax.experimental import pallas as pl
from jax.experimental.pallas import tpu as pltpu
from jax.sharding import PartitionSpec as P

EPSILON = 1e-06
BFLOAT = jnp.bfloat16
SINGLE = jnp.float32
FIXED = 8191.0
GELU_A = math.sqrt(2.0 / math.pi)
GELU_B = 0.044715
VMEM_LIMIT = 63 << 20


def nn(left, right):
    return jnp.dot(left, right, preferred_element_type=SINGLE)


def nt(left, right):
    return lax.dot_general(left, right, (((1,), (1,)), ((), ())), preferred_element_type=SINGLE)


def tn(left, right):
    return lax.dot_general(left, right, (((0,), (0,)), ((), ())), preferred_element_type=SINGLE)


def whole(shape):
    zeros = (0,) * len(shape)
    return pl.BlockSpec(shape, lambda *_: zeros, pipeline_mode=pl.Buffered(1))


def params():
    return pltpu.CompilerParams(vmem_limit_bytes=VMEM_LIMIT)


def cost(flops, moved):
    return pl.CostEstimate(flops=int(flops), bytes_accessed=int(moved), transcendentals=0)


def scale_of(values):
    return lax.rsqrt(jnp.mean(values * values, axis=-1, keepdims=True) + EPSILON)


def norm_back(values, scale, scaled_grad):
    dot = jnp.mean(values * scaled_grad, axis=-1, keepdims=True)
    return scale * (scaled_grad - values * (scale * scale * dot))


def first_lanes(shape, head_dim):
    return lax.broadcasted_iota(jnp.int32, shape, 1) < head_dim


def project_kernel(x_ref, gain_ref, w_ref, q_ref, kv_ref):
    values = x_ref[...].astype(SINGLE)
    normed = (values * scale_of(values) * gain_ref[...]).astype(BFLOAT)
    width = values.shape[1]
    q_ref[...] = nn(normed, w_ref[:, :width]).astype(BFLOAT)
    kv_ref[...] = nn(normed, w_ref[:, width:]).astype(BFLOAT)


def project(tokens, gain, w_qkv):
    rows, width = tokens.shape
    block = math.gcd(rows, 256)
    return pl.pallas_call(
        project_kernel,
        grid=(rows // block,),
        in_specs=[
            pl.BlockSpec((block, width), lambda i: (i, 0)),
            whole((1, width)),
            whole(w_qkv.shape),
        ],
        out_specs=[
            pl.BlockSpec((block, width), lambda i: (i, 0)),
            pl.BlockSpec((block, 2 * width), lambda i: (i, 0)),
        ],
        out_shape=[
            jax.ShapeDtypeStruct((rows, width), BFLOAT),
            jax.ShapeDtypeStruct((rows, 2 * width), BFLOAT),
        ],
        compiler_params=params(),
        cost_estimate=cost(6 * rows * width * width, 12 * rows * width),
    )(tokens, gain.reshape(1, width), w_qkv)


def attend_pair(q_pair, k_pair, v_pair, table_ref, bucket_ref, start, prob_ref, step, head_dim):
    rows, keys = q_pair.shape[0], k_pair.shape[0]
    wide = first_lanes(q_pair.shape, head_dim)
    tall = first_lanes(v_pair.shape, head_dim)
    coded_rows = jnp.round(table_ref[pl.ds(2 * step, 2), :] * FIXED).astype(jnp.int32)
    table = (coded_rows[0:1, :] << 16) | (coded_rows[1:2, :] & 0xFFFF)
    table = jnp.broadcast_to(table, (rows, 128))
    span = pl.ds(start, rows)
    packed = jnp.concatenate(
        [
            jnp.take_along_axis(
                table,
                bucket_ref[span, part * 128 : part * 128 + 128].astype(jnp.int32),
                axis=1,
                mode="promise_in_bounds",
            )
            for part in range(keys // 128)
        ],
        1,
    )
    total = None
    for side in range(2):
        mine = wide if side == 0 else ~wide
        mine_tall = tall if side == 0 else ~tall
        coded = (packed >> 16) if side == 0 else ((packed << 16) >> 16)
        scores = nt(jnp.where(mine, q_pair, 0), k_pair)
        scores = scores + coded.astype(SINGLE) * (1.0 / FIXED)
        shifted = jnp.exp(scores - jnp.max(scores, axis=-1, keepdims=True))
        inverse = 1.0 / jnp.sum(shifted, axis=-1, keepdims=True)
        soft = (shifted * inverse).astype(BFLOAT)
        prob_ref[2 * step + side] = soft
        term = nn(soft, jnp.where(mine_tall, v_pair, 0))
        total = term if total is None else total + term
    return total.astype(BFLOAT)


def pair_lanes(step, head_dim, offset=0):
    return pl.ds(pl.multiple_of(offset + step * 2 * head_dim, 128), 2 * head_dim)


def doc_forward_kernel(q_ref, k_ref, v_ref, table_ref, bucket_ref, mix_ref, prob_ref):
    heads = prob_ref.shape[0]
    head_dim = q_ref.shape[1] // heads

    def pair(step, carry):
        lanes = pair_lanes(step, head_dim)
        mix_ref[:, lanes] = attend_pair(
            q_ref[:, lanes],
            k_ref[:, lanes],
            v_ref[:, lanes],
            table_ref,
            bucket_ref,
            0,
            prob_ref,
            step,
            head_dim,
        )
        return carry

    lax.fori_loop(0, heads // 2, pair, 0)


def doc_forward(q_rows, kv_rows, table, buckets, n_docs, rows, heads):
    width = q_rows.shape[1]
    keys = buckets.shape[1]
    block = math.gcd(rows, 256)
    steps = rows // block
    return pl.pallas_call(
        doc_forward_kernel,
        grid=(n_docs, steps),
        in_specs=[
            pl.BlockSpec((block, width), lambda d, i: (d * steps + i, 0)),
            pl.BlockSpec((keys, width), lambda d, i: (d, 0)),
            pl.BlockSpec((keys, width), lambda d, i: (d, 1)),
            whole(table.shape),
            pl.BlockSpec((block, keys), lambda d, i: (i, 0)),
        ],
        out_specs=[
            pl.BlockSpec((block, width), lambda d, i: (d * steps + i, 0)),
            pl.BlockSpec((heads, block, keys), lambda d, i: (0, d * steps + i, 0)),
        ],
        out_shape=[
            jax.ShapeDtypeStruct((n_docs * rows, width), BFLOAT),
            jax.ShapeDtypeStruct((heads, n_docs * rows, keys), BFLOAT),
        ],
        compiler_params=params(),
        cost_estimate=cost(30 * n_docs * rows * keys * width, 2 * heads * n_docs * rows * keys),
    )(q_rows, kv_rows, kv_rows, table, buckets)


def bucket_onehot(bucket_rows, labels):
    rows, keys = bucket_rows.shape
    numbers = bucket_rows.astype(jnp.int32)
    names = lax.broadcasted_iota(jnp.int32, (labels, keys), 0)
    parts = [
        jnp.where(jnp.broadcast_to(numbers[r : r + 1, :], (labels, keys)) == names, 1.0, 0.0).astype(
            BFLOAT
        )
        for r in range(rows)
    ]
    return jnp.concatenate(parts, 0)


def bucket_products(bucket_rows, grad_rows, labels):
    return nt(bucket_onehot(bucket_rows, labels), grad_rows)


def attend_back(q_pair, k_pair, v_pair, da_pair, mix_pair, probs, head_dim):
    wide = first_lanes(q_pair.shape, head_dim)
    tall = first_lanes(k_pair.shape, head_dim)
    product = da_pair.astype(SINGLE) * mix_pair.astype(SINGLE)
    dq = dk = dv = None
    kept = []
    for side in range(2):
        mine = wide if side == 0 else ~wide
        mine_tall = tall if side == 0 else ~tall
        da_mine = jnp.where(mine, da_pair, 0)
        correction = jnp.sum(jnp.where(mine, product, 0.0), axis=-1, keepdims=True)
        grad_soft = nt(da_mine, v_pair)
        soft = probs[side]
        grad_scores = (soft.astype(SINGLE) * (grad_soft - correction)).astype(BFLOAT)
        kept.append(grad_scores)
        dq_term = nn(grad_scores, jnp.where(mine_tall, k_pair, 0))
        dk_term = tn(grad_scores, jnp.where(mine, q_pair, 0))
        dv_term = tn(soft, da_mine)
        dq = dq_term if dq is None else dq + dq_term
        dk = dk_term if dk is None else dk + dk_term
        dv = dv_term if dv is None else dv + dv_term
    return dq, dk, dv, kept


def query_back_block(q_rows, k_rows, v_rows, da_rows, mix_rows, probs, head_dim):
    rows, width = q_rows.shape
    heads = len(probs)
    wide = first_lanes((rows, 2 * head_dim), head_dim)

    def pair(values, step):
        return values[:, step * 2 * head_dim : (step + 1) * 2 * head_dim]

    def halves(values, step):
        return jnp.where(wide, pair(values, step), 0), jnp.where(wide, 0, pair(values, step))

    das, corrections, grads = [], [], []
    for step in range(heads // 2):
        das += halves(da_rows, step)
    for head in range(heads):
        grads.append(nt(das[head], pair(v_rows, head // 2)))
    for head in range(heads):
        product = das[head].astype(SINGLE) * pair(mix_rows, head // 2).astype(SINGLE)
        corrections.append(jnp.sum(product, axis=-1, keepdims=True))
    kept = [
        (prob.astype(SINGLE) * (grad - correction)).astype(BFLOAT)
        for prob, grad, correction in zip(probs, grads, corrections)
    ]
    dq, dk, dv = [], [], []
    for step in range(heads // 2):
        left, right = kept[2 * step], kept[2 * step + 1]
        k_left, k_right = halves(k_rows, step)
        dq.append((nn(left, k_left) + nn(right, k_right)).astype(BFLOAT))
    for step in range(heads // 2):
        left, right = kept[2 * step], kept[2 * step + 1]
        q_left, q_right = halves(q_rows, step)
        dk.append((tn(left, q_left) + tn(right, q_right)).astype(BFLOAT))
    for step in range(heads // 2):
        terms = tn(probs[2 * step], das[2 * step]) + tn(probs[2 * step + 1], das[2 * step + 1])
        dv.append(terms.astype(BFLOAT))
    return dq, dk, dv, kept


def doc_backward_kernel(
    labels,
    q_ref,
    k_ref,
    v_ref,
    da_ref,
    mix_ref,
    prob_ref,
    bucket_ref,
    dq_ref,
    dk_ref,
    dv_ref,
    sums_ref,
    dk_acc,
    dv_acc,
    ds_keep,
):
    rows, width = q_ref.shape
    heads = prob_ref.shape[0]
    keys = k_ref.shape[0]
    head_dim = width // heads
    doc, step_i = pl.program_id(0), pl.program_id(1)

    @pl.when(step_i == 0)
    def _():
        dk_acc[...] = jnp.zeros_like(dk_acc)
        dv_acc[...] = jnp.zeros_like(dv_acc)

    @pl.when((step_i == 0) & (doc == 0))
    def _():
        sums_ref[...] = jnp.zeros_like(sums_ref)

    def pair(step, carry):
        lanes = pl.ds(pl.multiple_of(step * 2 * head_dim, 128), 2 * head_dim)
        dq, dk, dv, kept = attend_back(
            q_ref[:, lanes],
            k_ref[:, lanes],
            v_ref[:, lanes],
            da_ref[:, lanes],
            mix_ref[:, lanes],
            [prob_ref[2 * step], prob_ref[2 * step + 1]],
            head_dim,
        )
        ds_keep[2 * step] = kept[0]
        ds_keep[2 * step + 1] = kept[1]
        dq_ref[:, lanes] = dq.astype(BFLOAT)
        dk_acc[:, lanes] += dk
        dv_acc[:, lanes] += dv
        return carry

    lax.fori_loop(0, heads // 2, pair, 0)

    def group(number, carry):
        span = pl.ds(pl.multiple_of(number * 16, 16), 16)
        sums_ref[...] += bucket_products(
            bucket_ref[span, :], ds_keep[:, span, :].reshape(heads * 16, keys), labels
        )
        return carry

    lax.fori_loop(0, rows // 16, group, 0)

    @pl.when(step_i == pl.num_programs(1) - 1)
    def _():
        dk_ref[...] = dk_acc[...].astype(BFLOAT)
        dv_ref[...] = dv_acc[...].astype(BFLOAT)


def doc_backward(q_rows, kv_rows, da_rows, mixture, probs, buckets, n_docs, rows, labels):
    width = q_rows.shape[1]
    heads = probs.shape[0]
    keys = buckets.shape[1]
    block = math.gcd(rows, 256)
    steps = rows // block
    along = pl.BlockSpec((block, width), lambda d, i: (d * steps + i, 0))
    per_doc = pl.BlockSpec((keys, width), lambda d, i: (d, 0))
    return pl.pallas_call(
        functools.partial(doc_backward_kernel, labels),
        grid=(n_docs, steps),
        in_specs=[
            along,
            per_doc,
            pl.BlockSpec((keys, width), lambda d, i: (d, 1)),
            along,
            along,
            pl.BlockSpec((heads, block, keys), lambda d, i: (0, d * steps + i, 0)),
            pl.BlockSpec((block, keys), lambda d, i: (i, 0)),
        ],
        out_specs=[along, per_doc, per_doc, whole((16 * labels, heads * 16))],
        out_shape=[
            jax.ShapeDtypeStruct((n_docs * rows, width), BFLOAT),
            jax.ShapeDtypeStruct((n_docs * keys, width), BFLOAT),
            jax.ShapeDtypeStruct((n_docs * keys, width), BFLOAT),
            jax.ShapeDtypeStruct((16 * labels, heads * 16), SINGLE),
        ],
        scratch_shapes=[
            pltpu.VMEM((keys, width), SINGLE),
            pltpu.VMEM((keys, width), SINGLE),
            pltpu.VMEM((heads, block, keys), BFLOAT),
        ],
        compiler_params=params(),
        cost_estimate=cost(70 * n_docs * rows * keys * width, 2 * heads * n_docs * rows * keys),
    )(q_rows, kv_rows, kv_rows, da_rows, mixture, probs, buckets)


def query_block(q_rows, k_rows, v_rows, table_ref, index, heads):
    rows, width = q_rows.shape
    head_dim = width // heads
    wide = first_lanes((rows, 2 * head_dim), head_dim)

    def halves(values, step):
        pair = values[:, step * 2 * head_dim : (step + 1) * 2 * head_dim]
        return jnp.where(wide, pair, 0), jnp.where(wide, 0, pair), pair

    scores = []
    for step in range(heads // 2):
        left, right, _ = halves(q_rows, step)
        keys = halves(k_rows, step)[2]
        scores += [nt(left, keys), nt(right, keys)]
    for head in range(heads):
        table = jnp.broadcast_to(table_ref[head : head + 1, :], (rows, 128))
        bias = jnp.take_along_axis(table, index, axis=1, mode="promise_in_bounds")
        scores[head] = scores[head] + bias
    tops = [jnp.max(score, axis=-1, keepdims=True) for score in scores]
    shifted = [jnp.exp(score - top) for score, top in zip(scores, tops)]
    inverse = [1.0 / jnp.sum(shift, axis=-1, keepdims=True) for shift in shifted]
    softs = [(shift * inv).astype(BFLOAT) for shift, inv in zip(shifted, inverse)]
    outs = []
    for step in range(heads // 2):
        left, right, _ = halves(v_rows, step)
        outs.append((nn(softs[2 * step], left) + nn(softs[2 * step + 1], right)).astype(BFLOAT))
    return softs, jnp.concatenate(outs, 1)


def query_forward_kernel(q_ref, kv_ref, table_ref, bucket_ref, mix_ref, prob_ref):
    width = q_ref.shape[1]
    softs, mix_ref[...] = query_block(
        q_ref[...], kv_ref[:, :width], kv_ref[:, width:], table_ref, bucket_ref[...], prob_ref.shape[0]
    )
    for head, soft in enumerate(softs):
        prob_ref[head] = soft


def query_forward(q_rows, kv_rows, table, buckets, start, count, heads):
    width = q_rows.shape[1]
    offset = start // 128
    return pl.pallas_call(
        query_forward_kernel,
        grid=(count // 128,),
        in_specs=[
            pl.BlockSpec((128, width), lambda i: (offset + i, 0)),
            pl.BlockSpec((128, 2 * width), lambda i: (offset + i, 0)),
            whole(table.shape),
            whole(buckets.shape),
        ],
        out_specs=[
            pl.BlockSpec((128, width), lambda i: (i, 0)),
            pl.BlockSpec((heads, 128, 128), lambda i: (0, i, 0)),
        ],
        out_shape=[
            jax.ShapeDtypeStruct((count, width), BFLOAT),
            jax.ShapeDtypeStruct((heads, count, 128), BFLOAT),
        ],
        compiler_params=params(),
        cost_estimate=cost(4 * count * 128 * width * 4, 10 * count * width),
    )(q_rows, kv_rows, table, buckets)


def query_backward_kernel(
    labels, q_ref, kv_ref, da_ref, mix_ref, prob_ref, bucket_ref, dq_ref, dkv_ref, sums_ref, ds_keep
):
    rows, width = q_ref.shape
    heads = prob_ref.shape[0]
    head_dim = width // heads

    @pl.when(pl.program_id(0) == 0)
    def _():
        sums_ref[...] = jnp.zeros_like(sums_ref)

    for step in range(heads // 2):
        lanes = slice(step * 2 * head_dim, (step + 1) * 2 * head_dim)
        right = slice(width + lanes.start, width + lanes.stop)
        dq, dk, dv, kept = attend_back(
            q_ref[:, lanes],
            kv_ref[:, lanes],
            kv_ref[:, right],
            da_ref[:, lanes],
            mix_ref[:, lanes],
            [prob_ref[2 * step], prob_ref[2 * step + 1]],
            head_dim,
        )
        ds_keep[2 * step] = kept[0]
        ds_keep[2 * step + 1] = kept[1]
        dq_ref[:, lanes] = dq.astype(BFLOAT)
        dkv_ref[:, lanes] = dk.astype(BFLOAT)
        dkv_ref[:, right] = dv.astype(BFLOAT)

    def group(number, carry):
        span = pl.ds(pl.multiple_of(number * 16, 16), 16)
        sums_ref[...] += bucket_products(
            bucket_ref[span, :], ds_keep[:, span, :].reshape(heads * 16, rows), labels
        )
        return carry

    lax.fori_loop(0, rows // 16, group, 0)


def query_backward(q_rows, kv_rows, da_rows, mixture, probs, buckets, start, labels):
    width = q_rows.shape[1]
    heads, count, _ = probs.shape
    offset = start // 128
    return pl.pallas_call(
        functools.partial(query_backward_kernel, labels),
        grid=(count // 128,),
        in_specs=[
            pl.BlockSpec((128, width), lambda i: (offset + i, 0)),
            pl.BlockSpec((128, 2 * width), lambda i: (offset + i, 0)),
            pl.BlockSpec((128, width), lambda i: (offset + i, 0)),
            pl.BlockSpec((128, width), lambda i: (offset + i, 0)),
            pl.BlockSpec((heads, 128, 128), lambda i: (0, i, 0)),
            whole(buckets.shape),
        ],
        out_specs=[
            pl.BlockSpec((128, width), lambda i: (i, 0)),
            pl.BlockSpec((128, 2 * width), lambda i: (i, 0)),
            whole((16 * labels, heads * 16)),
        ],
        out_shape=[
            jax.ShapeDtypeStruct((count, width), BFLOAT),
            jax.ShapeDtypeStruct((count, 2 * width), BFLOAT),
            jax.ShapeDtypeStruct((16 * labels, heads * 16), SINGLE),
        ],
        scratch_shapes=[pltpu.VMEM((heads, 128, 128), BFLOAT)],
        compiler_params=params(),
        cost_estimate=cost(8 * count * 128 * width * 4, 14 * count * width),
    )(q_rows, kv_rows, da_rows, mixture, probs, buckets)


def feed_kernel(
    chunk,
    x_ref,
    mix_ref,
    dy_ref,
    gain_ref,
    wou_ref,
    wd_ref,
    y_ref,
    dh_ref,
    da_ref,
    gou_ref,
    gd_ref,
    gg_ref,
    gou_acc,
    gd_acc,
    stage,
    sems,
):
    step = pl.program_id(0)
    hidden, width = wd_ref.shape

    @pl.when(step == 0)
    def _():
        gou_acc[...] = jnp.zeros_like(gou_acc)
        gd_acc[...] = jnp.zeros_like(gd_acc)
        gg_ref[...] = jnp.zeros_like(gg_ref)

    mixture = mix_ref[...]
    dy = dy_ref[...]
    gain = gain_ref[...]
    residual = x_ref[...].astype(SINGLE) + nn(mixture, wou_ref[:, :width])
    scale = scale_of(residual)
    second = (residual * scale * gain).astype(BFLOAT)
    y = residual
    grad_second = jnp.zeros_like(residual)
    for part in range(hidden // chunk):
        span = slice(part * chunk, (part + 1) * chunk)
        past = slice(width + part * chunk, width + (part + 1) * chunk)
        pre = nn(second, wou_ref[:, past])
        grad_hidden = nt(dy, wd_ref[span, :])
        square = pre * pre
        tanh = jnp.tanh(pre * (GELU_A + (GELU_A * GELU_B) * square))
        half = 0.5 + 0.5 * tanh
        act = pre * half
        slope = half + act * (1.0 - tanh) * (GELU_A + (3.0 * GELU_A * GELU_B) * square)
        act_low = act.astype(BFLOAT)
        grad_pre = (grad_hidden * slope).astype(BFLOAT)
        y = y + nn(act_low, wd_ref[span, :])
        grad_second = grad_second + nt(grad_pre, wou_ref[:, past])
        gd_acc[span, :] += tn(act_low, dy)
        gou_acc[:, past] += tn(second, grad_pre)
    y_ref[...] = y.astype(BFLOAT)
    gg_ref[...] += jnp.sum(grad_second * residual * scale, axis=0, keepdims=True)
    grad_res = dy.astype(SINGLE) + norm_back(residual, scale, grad_second * gain)
    dh_ref[...] = grad_res
    grad_low = grad_res.astype(BFLOAT)
    da_ref[...] = nt(grad_low, wou_ref[:, :width]).astype(BFLOAT)
    gou_acc[:, :width] += tn(mixture, grad_low)

    @pl.when(step == pl.num_programs(0) - 1)
    def _():
        pieces = []
        rows, columns = stage.shape[1:]
        for acc, out in ((gd_acc, gd_ref), (gou_acc, gou_ref)):
            for r in range(acc.shape[0] // rows):
                for c in range(acc.shape[1] // columns):
                    spot = (pl.ds(r * rows, rows), pl.ds(c * columns, columns))
                    pieces.append((acc, out, spot))
        flying = [None, None]
        for number, (acc, out, spot) in enumerate(pieces):
            slot = number % 2
            if flying[slot] is not None:
                flying[slot].wait()
            stage[slot] = acc[spot].astype(BFLOAT)
            flying[slot] = pltpu.make_async_copy(stage.at[slot], out.at[spot], sems.at[slot])
            flying[slot].start()
        for copy in flying:
            if copy is not None:
                copy.wait()


def feed(tokens, mixture, cotangent, gain, w_out_up, w_down):
    rows, width = tokens.shape
    hidden = w_down.shape[0]
    block = math.gcd(rows, 256)
    along = pl.BlockSpec((block, width), lambda i: (i, 0))
    anywhere = pl.BlockSpec(memory_space=pl.ANY)
    return pl.pallas_call(
        functools.partial(feed_kernel, math.gcd(hidden, 768)),
        grid=(rows // block,),
        in_specs=[
            along,
            along,
            along,
            whole((1, width)),
            whole(w_out_up.shape),
            whole(w_down.shape),
        ],
        out_specs=[along, along, along, anywhere, anywhere, whole((1, width))],
        out_shape=[
            jax.ShapeDtypeStruct((rows, width), BFLOAT),
            jax.ShapeDtypeStruct((rows, width), SINGLE),
            jax.ShapeDtypeStruct((rows, width), BFLOAT),
            jax.ShapeDtypeStruct(w_out_up.shape, BFLOAT),
            jax.ShapeDtypeStruct(w_down.shape, BFLOAT),
            jax.ShapeDtypeStruct((1, width), SINGLE),
        ],
        scratch_shapes=[
            pltpu.VMEM(w_out_up.shape, SINGLE),
            pltpu.VMEM(w_down.shape, SINGLE),
            pltpu.VMEM((2, width, width), BFLOAT),
            pltpu.SemaphoreType.DMA((2,)),
        ],
        compiler_params=params(),
        cost_estimate=cost(2 * rows * width * (6 * hidden + 3 * width), 14 * rows * width),
    )(tokens, mixture, cotangent, gain.reshape(1, width), w_out_up, w_down)


def unproject_kernel(
    x_ref, gain_ref, dq_ref, dk_ref, dv_ref, dh_ref, w_ref, dx_ref, low_ref, gw_ref, gg_ref, acc
):
    step = pl.program_id(0)
    width = w_ref.shape[0]

    @pl.when(step == 0)
    def _():
        acc[...] = jnp.zeros_like(acc)
        gg_ref[...] = jnp.zeros_like(gg_ref)

    values = x_ref[...].astype(SINGLE)
    gain = gain_ref[...]
    scale = scale_of(values)
    normed = (values * scale * gain).astype(BFLOAT)
    grad = jnp.zeros_like(values)
    for number, ref in enumerate((dq_ref, dk_ref, dv_ref)):
        span = slice(number * width, (number + 1) * width)
        part = ref[...]
        acc[:, span] += tn(normed, part)
        grad = grad + nt(part, w_ref[:, span])
    gg_ref[...] += jnp.sum(grad * values * scale, axis=0, keepdims=True)
    dx = dh_ref[...] + norm_back(values, scale, grad * gain)
    dx_ref[...] = dx
    low_ref[...] = dx.astype(BFLOAT)

    @pl.when(step == pl.num_programs(0) - 1)
    def _():
        gw_ref[...] = acc[...].astype(BFLOAT)


def unproject(tokens, gain, dq, dk, dv, grad_res, w_qkv):
    rows, width = tokens.shape
    block = math.gcd(rows, 256)
    along = pl.BlockSpec((block, width), lambda i: (i, 0))
    return pl.pallas_call(
        unproject_kernel,
        grid=(rows // block,),
        in_specs=[along, whole((1, width)), along, along, along, along, whole(w_qkv.shape)],
        out_specs=[along, along, whole(w_qkv.shape), whole((1, width))],
        out_shape=[
            jax.ShapeDtypeStruct((rows, width), SINGLE),
            jax.ShapeDtypeStruct((rows, width), BFLOAT),
            jax.ShapeDtypeStruct(w_qkv.shape, BFLOAT),
            jax.ShapeDtypeStruct((1, width), SINGLE),
        ],
        scratch_shapes=[pltpu.VMEM(w_qkv.shape, SINGLE)],
        compiler_params=params(),
        cost_estimate=cost(12 * rows * width * width, 18 * rows * width),
    )(tokens, gain.reshape(1, width), dq, dk, dv, grad_res, w_qkv)


def bits_of(count):
    return [1 << place for place in reversed(range(count.bit_length() - 1))]


def axis_bits():
    dp_bits = [("dp", bit) for bit in bits_of(lax.axis_size("dp"))]
    seq_bits = [("seq", bit) for bit in bits_of(lax.axis_size("seq"))]
    return dp_bits, seq_bits


def gather_orders():
    dp_bits, seq_bits = axis_bits()
    far = (len(dp_bits) + 1) // 2
    z_bits, x_bits = dp_bits[:far], dp_bits[far:]
    y_bits, core_bits = seq_bits[:-1], seq_bits[-1:]
    return [z_bits + y_bits + x_bits + core_bits, z_bits + x_bits + y_bits + core_bits]


def swap(values, name, bit):
    count = lax.axis_size(name)
    return lax.ppermute(values, name, [(i, i ^ bit) for i in range(count)])


def is_high(name, bit):
    return (lax.axis_index(name) & bit) != 0


def gather_rows(shard, order):
    dp_bits, seq_bits = axis_bits()
    everything = dp_bits + seq_bits
    done = []
    held = shard
    for item in order:
        other = swap(held, *item)
        done.append(item)
        place = sorted(everything.index(one) for one in done).index(everything.index(item))
        high = is_high(*item)
        held = jnp.where(
            high, jnp.stack([other, held], place), jnp.stack([held, other], place)
        )
    return held.reshape(-1, shard.shape[1])


def scatter_rows(values, order):
    dp_bits, seq_bits = axis_bits()
    left = dp_bits + seq_bits
    rows = values.shape[0] >> len(left)
    held = values.reshape((2,) * len(left) + (rows, values.shape[1]))
    for item in order:
        place = left.index(item)
        mine = is_high(*item).astype(jnp.int32)
        away = lax.dynamic_index_in_dim(held, 1 - mine, place, keepdims=False)
        kept = lax.dynamic_index_in_dim(held, mine, place, keepdims=False)
        other = swap(away, *item)
        held = kept.astype(SINGLE) + other.astype(SINGLE)
        left.remove(item)
        if left:
            held = held.astype(BFLOAT)
    return held


def scatter_columns(values, parts):
    orders = [order[::-1] for order in gather_orders()]
    columns = values.shape[1] // parts
    return jnp.concatenate(
        [
            scatter_rows(values[:, p * columns : (p + 1) * columns], orders[p % len(orders)])
            for p in range(parts)
        ],
        1,
    )


def sum_all(values):
    dp_bits, seq_bits = axis_bits()
    for item in seq_bits[::-1] + dp_bits[::-1]:
        values = values + swap(values, *item)
    return values


def own_document(shard):
    count = lax.axis_size("seq")
    n_docs = shard.shape[0]
    me = lax.axis_index("seq")
    if n_docs >= count:
        per = n_docs // count
        blocks = shard.reshape((count, per) + shard.shape[1:])
        sets, group = count, 1
    else:
        blocks = shard[:, None]
        sets, group = n_docs, count // n_docs
    got = []
    for r in range(sets):
        piece = lax.dynamic_index_in_dim(blocks, (me % sets) ^ r, 0, keepdims=False)
        route = [
            (u * sets + i, (i ^ r) * group + u) for u in range(group) for i in range(sets)
        ]
        if any(a != b for a, b in route):
            piece = lax.ppermute(piece, "seq", route)
        got.append(piece)
    stacked = jnp.stack(got, 0)
    mine = me // group
    ordered = [lax.dynamic_index_in_dim(stacked, mine ^ i, 0, keepdims=False) for i in range(sets)]
    return jnp.concatenate(ordered, 1).reshape(-1, shard.shape[-1])


def spread_document(rows, like):
    count = lax.axis_size("seq")
    n_docs, shard_rows, width = like.shape
    me = lax.axis_index("seq")
    if n_docs >= count:
        per = n_docs // count
        sets, group = count, 1
    else:
        per = 1
        sets, group = n_docs, count // n_docs
    blocks = rows.reshape(per, sets, shard_rows, width)
    mine = me // group
    got = []
    for r in range(sets):
        piece = lax.dynamic_index_in_dim(blocks, mine ^ r, 1, keepdims=False)
        route = [
            ((i ^ r) * group + u, u * sets + i) for u in range(group) for i in range(sets)
        ]
        if any(a != b for a, b in route):
            piece = lax.ppermute(piece, "seq", route)
        got.append(piece)
    stacked = jnp.stack(got, 0)
    ordered = [
        lax.dynamic_index_in_dim(stacked, (me % sets) ^ i, 0, keepdims=False) for i in range(sets)
    ]
    return jnp.concatenate(ordered, 0)


def gather_positions(shard):
    seq_bits = axis_bits()[1]
    done = []
    held = shard
    for item in seq_bits:
        other = swap(held, *item)
        high = is_high(*item)
        place = len(done)
        held = jnp.where(
            high, jnp.stack([other, held], place), jnp.stack([held, other], place)
        )
        done.append(item)
    return held.reshape(-1, shard.shape[1])


class Spot:
    def __init__(self):
        self.dp = lax.axis_index("dp")
        self.seq = lax.axis_index("seq")
        self.core = self.seq % 2
        self.y = self.seq // 2
        self.x = self.dp % 2
        self.z = self.dp // 2

    def partner(self, z=0, x=0, y=0, core=0):
        dp = self.flip(self.z, z) * 2 + self.flip(self.x, x)
        seq = self.flip(self.y, y) * 2 + self.flip(self.core, core)
        return (dp, seq)

    @staticmethod
    def flip(value, bits):
        if bits == 0:
            return value
        if bits == 1:
            return value + 1 - 2 * (value % 2)
        if bits == 2:
            return (value + 2) % 4
        return 3 - value

    def chip(self, z=0, x=0, y=0):
        return (self.flip(self.z, z) * 2 + self.flip(self.x, x)) * 2 + self.flip(self.y, y)


def send(source, target, sems, number, device):
    return pltpu.make_async_remote_copy(
        src_ref=source,
        dst_ref=target,
        send_sem=sems.at[0, number],
        recv_sem=sems.at[1, number],
        device_id=device,
        device_id_type=pl.DeviceIdType.MESH,
    )


def greet(partners):
    barrier = pltpu.get_barrier_semaphore()
    for device in partners:
        pl.semaphore_signal(barrier, inc=1, device_id=device, device_id_type=pl.DeviceIdType.MESH)
    pl.semaphore_wait(barrier, len(partners))


COPIES = 17
GATHER_COPIES = 24


class Gather:
    def __init__(self, spot, shard, whole_ref, theirs, block, sems, local):
        self.spot, self.shard, self.whole = spot, shard, whole_ref
        self.theirs, self.block, self.sems, self.local = theirs, block, sems, local
        self.rows, self.half = block.shape

    def columns(self, core):
        return pl.ds(pl.multiple_of(core * self.half, 128), self.half)

    def area(self, count=1, **bits):
        chip = self.spot.chip(**bits)
        if count == 2:
            chip = chip - chip % 2
        row = pl.multiple_of(chip * self.rows, 16)
        return self.whole.at[pl.ds(row, count * self.rows), self.columns(self.spot.core)]

    def copy(self, number):
        spot = self.spot
        if number == 0:
            source, target = self.shard.at[:, self.columns(1 - spot.core)], self.theirs
            device = spot.partner(core=1)
        elif number < 4:
            source, target, device = self.block, self.area(), spot.partner(z=number)
        elif number < 8:
            target, device = self.area(z=number - 4), spot.partner(y=1)
            source = self.block if number == 4 else target
        elif number < 16:
            target = self.area(z=(number - 8) % 4, y=(number - 8) // 4)
            source, device = self.block if number == 8 else target, spot.partner(x=1)
        else:
            source = target = self.area(2, z=number % 4, x=(number - 16) // 4)
            device = spot.partner(core=1)
        return send(source, target, self.sems, number, device)

    def here(self):
        return pltpu.make_async_copy(self.block, self.area(), self.local)

    def join_end(self):
        self.copy(0).wait_recv()
        part = self.rows // 2
        low = self.spot.core == 0
        mine = self.shard[:, self.columns(self.spot.core)].astype(SINGLE)
        theirs = self.theirs[...].astype(SINGLE)
        self.block[:part, :] = jnp.where(low, mine, theirs).astype(BFLOAT)
        self.block[part:, :] = jnp.where(low, theirs, mine).astype(BFLOAT)
        self.here().start()

    def start(self, *numbers):
        for number in numbers:
            self.copy(number).start()

    def z_got(self, k):
        self.copy(k).wait_recv()
        self.start(4 + k, 8 + k)

    def y_got(self, k):
        self.copy(4 + k).wait_recv()
        if k == 0:
            self.here().wait()
        self.start(12 + k, 16 + k)

    def x_got(self, k):
        self.copy(8 + k).wait_recv()
        self.copy(12 + k).wait_recv()
        self.start(20 + k)

    def finish(self):
        for number in range(16, GATHER_COPIES):
            self.copy(number).wait_recv()
        for number in range(GATHER_COPIES):
            self.copy(number).wait_send()


class Move:
    PARTNERS = ((1, 0), (1, 1), (0, 1))

    def __init__(self, spot, source, target, own_target, sems, local):
        self.spot, self.source, self.target = spot, source, target
        self.own_target, self.sems, self.local = own_target, sems, local

    def own(self):
        return pltpu.make_async_copy(
            self.source(self.spot.seq), self.own_target(self.spot.seq), self.local
        )

    def copy(self, number):
        y, core = self.PARTNERS[number]
        device = self.spot.partner(y=y, core=core)
        return send(self.source(device[1]), self.target(self.spot.seq), self.sems, number, device)

    def start(self):
        self.own().start()
        for number in range(3):
            self.copy(number).start()

    def finish(self):
        self.own().wait()
        for number in range(3):
            self.copy(number).wait()


def all_partners(spot):
    return [
        spot.partner(core=1),
        spot.partner(z=1),
        spot.partner(z=2),
        spot.partner(z=3),
        spot.partner(x=1),
        spot.partner(y=1),
        spot.partner(y=1, core=1),
    ]


def row_block(ref, rows):
    return lambda number: ref.at[pl.ds(pl.multiple_of(number * rows, 16), rows), :]


def front_kernel(
    docs_ref,
    queries_ref,
    doc_cot_ref,
    query_cot_ref,
    q_shard,
    kv_shard,
    out_shard,
    up_shard,
    down_shard,
    bucket_shard,
    gain_ref,
    table_ref,
    small_bucket_ref,
    tokens_out,
    cots_out,
    w_out,
    ou_out,
    down_out,
    bucket_out,
    qkv_out,
    mix_ref,
    prob_ref,
    query_prob_ref,
    query_bucket_ref,
    x_v,
    w_v,
    qkv_v,
    bucket_v,
    bucket_in,
    qkv_own,
    qkv_theirs,
    qkv_block,
    ou_own,
    ou_theirs,
    ou_block,
    down_own,
    down_theirs,
    down_block,
    gather_sems,
    move_sems,
    local,
):
    step = pl.program_id(0)
    last = pl.num_programs(0) - 1
    spot = Spot()
    n_docs, shard_rows, width = docs_ref.shape
    doc_rows = n_docs * shard_rows
    query_rows = queries_ref.shape[0]
    heads = prob_ref.shape[0]
    head_dim = width // heads
    pairs = heads // 2
    block = prob_ref.shape[1]

    gathers = []
    for number, parts in enumerate(
        (
            (qkv_own, w_v, qkv_theirs, qkv_block),
            (ou_own, ou_out, ou_theirs, ou_block),
            (down_own, down_out, down_theirs, down_block),
        )
    ):
        gathers.append(Gather(spot, *parts, gather_sems.at[number], local.at[number]))
    g_qkv, *feeds = gathers
    token_move = Move(
        spot,
        lambda number: docs_ref.at[number],
        row_block(x_v, shard_rows),
        row_block(x_v, shard_rows),
        move_sems.at[0],
        local.at[3],
    )
    cot_move = Move(
        spot,
        lambda number: doc_cot_ref.at[number],
        row_block(cots_out, shard_rows),
        row_block(cots_out, shard_rows),
        move_sems.at[1],
        local.at[4],
    )
    query_load = pltpu.make_async_copy(
        queries_ref, x_v.at[pl.ds(doc_rows, query_rows), :], local.at[5]
    )
    cot_copy = pltpu.make_async_copy(
        query_cot_ref, cots_out.at[pl.ds(doc_rows, query_rows), :], local.at[6]
    )
    bucket_rows = row_block(bucket_v, shard_rows)
    bucket_load = pltpu.make_async_copy(bucket_shard, bucket_in, local.at[7])
    near = bucket_rows(spot.seq)
    far = bucket_rows(spot.partner(y=1)[1])
    bucket_y = send(near, near, move_sems.at[2], 0, spot.partner(y=1))
    bucket_near = send(near, near, move_sems.at[2], 1, spot.partner(core=1))
    bucket_far = send(far, far, move_sems.at[2], 2, spot.partner(core=1))
    saves = [
        pltpu.make_async_copy(x_v, tokens_out, local.at[8]),
        pltpu.make_async_copy(w_v, w_out, local.at[9]),
        pltpu.make_async_copy(qkv_v, qkv_out, local.at[10]),
        pltpu.make_async_copy(bucket_v, bucket_out, local.at[11]),
    ]
    loads = [
        pltpu.make_async_copy(q_shard, qkv_own.at[:, pl.ds(0, width)], local.at[12]),
        pltpu.make_async_copy(kv_shard, qkv_own.at[:, pl.ds(width, 2 * width)], local.at[13]),
        pltpu.make_async_copy(out_shard, ou_own.at[:, pl.ds(0, width)], local.at[14]),
        pltpu.make_async_copy(
            up_shard, ou_own.at[:, pl.ds(width, up_shard.shape[1])], local.at[15]
        ),
        pltpu.make_async_copy(down_shard, down_own, local.at[16]),
    ]

    @pl.when(step == 0)
    def _():
        for load in loads:
            load.start()
        bucket_load.start()
        query_load.start()
        token_move.own().start()
        greet(all_partners(spot))
        token_move.copy(0).start()
        for load in loads[:2]:
            load.wait()
        g_qkv.start(0)
        for load in loads[2:]:
            load.wait()
        for gather in feeds:
            gather.start(0)
        token_move.copy(2).start()
        g_qkv.join_end()
        g_qkv.start(1, 2, 3, 4, 8)
        for gather in feeds:
            gather.join_end()
        bucket_load.wait()
        bucket_v[pl.ds(pl.multiple_of(spot.seq * shard_rows, 16), shard_rows), :] = bucket_in[
            ...
        ].astype(jnp.int16)
        size = small_bucket_ref.shape[0]
        shape = (128, size)
        picks = (
            lax.broadcasted_iota(jnp.int32, shape, 0) % size
            == lax.broadcasted_iota(jnp.int32, shape, 1)
        )
        picks = jnp.where(picks, 1.0, 0.0).astype(BFLOAT)
        numbers = small_bucket_ref[...].astype(SINGLE).astype(BFLOAT)
        spread = nt(nn(picks, numbers).astype(BFLOAT), picks).astype(jnp.int32)
        square = (128, 128)
        same = (
            lax.broadcasted_iota(jnp.int32, square, 0) // size
            == lax.broadcasted_iota(jnp.int32, square, 1) // size
        )
        query_bucket_ref[...] = jnp.where(same, spread, table_ref.shape[1] - 1)
        for k in (1, 2, 3):
            g_qkv.z_got(k)
        for gather in feeds:
            gather.start(1, 2, 3)
        token_move.copy(1).start()
        bucket_y.start()
        bucket_near.start()
        for gather in feeds:
            gather.start(4)
        for k in (0, 1, 2, 3):
            g_qkv.y_got(k)
        for gather in feeds:
            gather.start(8)
        for k in (0, 1, 2, 3):
            g_qkv.x_got(k)
        query_load.wait()
        g_qkv.finish()
        saves[1].start()
        token_move.finish()
        saves[0].start()

        def project_block(number, carry):
            span = pl.ds(pl.multiple_of(number * block, 16), block)
            values = x_v[span, :].astype(SINGLE)
            normed = (values * scale_of(values) * gain_ref[...][None, :]).astype(BFLOAT)
            for part in range(3):
                lanes = slice(part * width, (part + 1) * width)
                qkv_v[span, lanes] = nn(normed, w_v[:, lanes]).astype(BFLOAT)
            return carry

        blocks = (doc_rows + query_rows) // block
        third = blocks // 3
        lax.fori_loop(0, third, project_block, 0)
        for gather in feeds:
            gather.z_got(1)
        lax.fori_loop(third, 2 * third, project_block, 0)
        for gather in feeds:
            gather.z_got(2)
        lax.fori_loop(2 * third, blocks, project_block, 0)
        for gather in feeds:
            gather.z_got(3)
        saves[2].start()
        cot_move.start()
        cot_copy.start()
        bucket_y.wait_recv()
        bucket_far.start()

        def query_step(number, carry):
            span = pl.ds(pl.multiple_of(doc_rows + number * 128, 16), 128)
            softs, mixed = query_block(
                qkv_v[span, :width],
                qkv_v[span, width : 2 * width],
                qkv_v[span, 2 * width :],
                table_ref,
                query_bucket_ref[...],
                heads,
            )
            mix_ref[span, :] = mixed
            for head, soft in enumerate(softs):
                query_prob_ref[head, pl.ds(pl.multiple_of(number * 128, 16), 128), :] = soft
            return carry

        lax.fori_loop(0, query_rows // 128, query_step, 0)
        for gather in feeds:
            gather.y_got(0)
        bucket_near.wait()
        bucket_far.wait()
        bucket_y.wait_send()
        saves[3].start()

    def tick(when, name, k):
        @pl.when(step == when)
        def _():
            for gather in feeds:
                getattr(gather, name)(k)

    tick(1, "y_got", 1)
    tick(2, "y_got", 2)
    tick(2, "y_got", 3)
    tick(3, "x_got", 0)
    tick(4, "x_got", 1)
    tick(4, "x_got", 2)

    @pl.when(step > 0)
    def _():
        span = pl.ds(pl.multiple_of((step - 1) * block, 16), block)

        def pair(number, carry):
            lanes = pair_lanes(number, head_dim)
            mix_ref[span, lanes] = attend_pair(
                qkv_v[span, lanes],
                qkv_v[:doc_rows, pair_lanes(number, head_dim, width)],
                qkv_v[:doc_rows, pair_lanes(number, head_dim, 2 * width)],
                table_ref,
                bucket_v,
                pl.multiple_of((step - 1) * block, 16),
                prob_ref,
                number,
                head_dim,
            )
            return carry

        lax.fori_loop(0, pairs, pair, 0, unroll=True)

    @pl.when(step == last)
    def _():
        for gather in feeds:
            gather.x_got(3)
        for gather in feeds:
            gather.finish()
        cot_move.finish()
        cot_copy.wait()
        for save in saves:
            save.wait()


def gather_scratch(rows, columns):
    return [
        pltpu.VMEM((rows, columns), BFLOAT),
        pltpu.VMEM((rows, columns // 2), BFLOAT),
        pltpu.VMEM((2 * rows, columns // 2), BFLOAT),
    ]


def front(docs, queries, doc_cot, query_cot, weights, buckets, gain, table, query_buckets, heads):
    n_docs, shard_rows, width = docs.shape
    doc_rows = n_docs * shard_rows
    query_rows = queries.shape[0]
    rows = doc_rows + query_rows
    keys = buckets.shape[1]
    block = 256
    steps = doc_rows // block
    anywhere = pl.BlockSpec(memory_space=pl.ANY)
    w_q, w_kv, w_out, w_up, w_down = (weight.shape for weight in weights)
    shards = [
        (w_q[0], w_q[1] + w_kv[1]),
        (w_out[0], w_out[1] + w_up[1]),
        w_down,
    ]
    scratch = []
    for shard in shards:
        scratch += gather_scratch(*shard)
    return pl.pallas_call(
        front_kernel,
        grid=(steps + 1,),
        in_specs=[anywhere] * 10 + [whole((width,)), whole(table.shape), whole(query_buckets.shape)],
        out_specs=[anywhere] * 7
        + [
            whole((rows, width)),
            pl.BlockSpec((heads, block, keys), lambda i: (0, jnp.maximum(i - 1, 0), 0)),
            whole((heads, query_rows, 128)),
            whole((128, 128)),
        ],
        out_shape=[
            jax.ShapeDtypeStruct((rows, width), BFLOAT),
            jax.ShapeDtypeStruct((rows, width), BFLOAT),
            *[jax.ShapeDtypeStruct((shard[0] * 32, shard[1]), BFLOAT) for shard in shards],
            jax.ShapeDtypeStruct((keys, keys), jnp.int16),
            jax.ShapeDtypeStruct((rows, 3 * width), BFLOAT),
            jax.ShapeDtypeStruct((rows, width), BFLOAT),
            jax.ShapeDtypeStruct((heads, doc_rows, keys), BFLOAT),
            jax.ShapeDtypeStruct((heads, query_rows, 128), BFLOAT),
            jax.ShapeDtypeStruct((128, 128), jnp.int32),
        ],
        scratch_shapes=[
            pltpu.VMEM((rows, width), BFLOAT),
            pltpu.VMEM((width, 3 * width), BFLOAT),
            pltpu.VMEM((rows, 3 * width), BFLOAT),
            pltpu.VMEM((keys, keys), jnp.int16),
            pltpu.VMEM(buckets.shape, jnp.int32),
            *scratch,
            pltpu.SemaphoreType.DMA((3, 2, GATHER_COPIES)),
            pltpu.SemaphoreType.DMA((3, 2, 3)),
            pltpu.SemaphoreType.DMA((20,)),
        ],
        compiler_params=pltpu.CompilerParams(
            collective_id=0, has_side_effects=True, vmem_limit_bytes=VMEM_LIMIT
        ),
        cost_estimate=cost(6 * rows * width * width, 100 << 20),
    )(docs, queries, doc_cot, query_cot, *weights, buckets, gain, table, query_buckets)


class Scatter:
    Z_ORDER = (3, 2, 1, 0)

    def __init__(self, spot, away, buffers, sems):
        self.spot, self.away, self.sems = spot, away, sems
        self.held, self.core_in, self.x_in, self.y_in, self.z_in, self.tail, self.tail_in = buffers
        self.half = self.held.shape[1]
        self.rows = self.held.shape[0] // 16

    def span(self, **bits):
        return pl.ds(pl.multiple_of(self.spot.chip(**bits) * self.rows, 16), self.rows)

    def slot(self, number):
        return pl.ds(number * self.rows, self.rows)

    def copy(self, number):
        spot = self.spot
        if number == 0:
            source, target, device = self.away, self.core_in, spot.partner(core=1)
        elif number < 9:
            index = number - 1
            source = self.held.at[self.span(z=self.Z_ORDER[index // 2], x=1, y=1 - index % 2), :]
            target, device = self.x_in.at[self.slot(index), :], spot.partner(x=1)
        elif number < 13:
            index = number - 9
            source = self.held.at[self.span(z=self.Z_ORDER[index], y=1), :]
            target, device = self.y_in.at[self.slot(index), :], spot.partner(y=1)
        elif number < 16:
            index = number - 13
            source = self.held.at[self.span(z=self.Z_ORDER[index]), :]
            target = self.z_in.at[self.slot(index), :]
            device = spot.partner(z=self.Z_ORDER[index])
        else:
            part = self.rows // 2
            theirs = pl.ds(pl.multiple_of((1 - spot.core) * part, 8), part)
            source, target, device = self.tail.at[theirs, :], self.tail_in, spot.partner(core=1)
        return send(source, target, self.sems, number, device)

    def add(self, span, others):
        total = self.held[span, :].astype(SINGLE) + self.core_in[span, :].astype(SINGLE)
        for ref, place in others:
            total = total + ref[place, :].astype(SINGLE)
        return total

    def core_end(self):
        self.copy(0).wait_recv()

    def x_step(self, index):
        span = self.span(z=self.Z_ORDER[index // 2], x=1, y=1 - index % 2)
        self.held[span, :] = self.add(span, []).astype(BFLOAT)
        self.copy(1 + index).start()

    def y_step(self, index):
        self.copy(1 + 2 * index).wait_recv()
        span = self.span(z=self.Z_ORDER[index], y=1)
        total = self.add(span, [(self.x_in, self.slot(2 * index))])
        self.held[span, :] = total.astype(BFLOAT)
        self.copy(9 + index).start()

    def here(self, index):
        self.copy(2 + 2 * index).wait_recv()
        self.copy(9 + index).wait_recv()
        span = self.span(z=self.Z_ORDER[index])
        others = [(self.x_in, self.slot(2 * index + 1)), (self.y_in, self.slot(index))]
        return span, self.add(span, others)

    def z_step(self, index):
        span, total = self.here(index)
        self.held[span, :] = total.astype(BFLOAT)
        self.copy(13 + index).start()

    def tail_start(self):
        _, total = self.here(3)
        for index in range(3):
            self.copy(13 + index).wait_recv()
            total = total + self.z_in[self.slot(index), :].astype(SINGLE)
        self.tail[...] = total
        self.copy(16).start()

    def finish(self):
        part = self.rows // 2
        low = self.spot.core == 0
        mine = jnp.where(low, self.tail[:part, :], self.tail[part:, :])
        self.copy(16).wait_recv()
        other = self.tail_in[...]
        for number in range(COPIES):
            self.copy(number).wait_send()
        return jnp.where(low, mine, other), jnp.where(low, other, mine)


def scatter_scratch(rows, columns):
    half, part = columns // 2, rows // 16
    return [
        pltpu.VMEM((rows, half), BFLOAT),
        pltpu.VMEM((rows, half), BFLOAT),
        pltpu.VMEM((8 * part, half), BFLOAT),
        pltpu.VMEM((4 * part, half), BFLOAT),
        pltpu.VMEM((3 * part, half), BFLOAT),
        pltpu.VMEM((part, half), SINGLE),
        pltpu.VMEM((part // 2, half), SINGLE),
    ]


def half_of(ref, core):
    half = ref.shape[1] // 2
    return ref.at[:, pl.ds(pl.multiple_of(core * half, 128), half)]


def middle_kernel(
    x_ref,
    mix_ref,
    dy_ref,
    gain_ref,
    wo_ref,
    wu_ref,
    wd_ref,
    y_out,
    dh_out,
    da_out,
    rest_ref,
    down_ref,
    near_ref,
    gg_ref,
    h1,
    n2,
    y_acc,
    act_v,
    du_v,
    dh_ref,
    *rest,
):
    fulls, downs, rest = rest[0], rest[1], rest[2:]
    step = pl.program_id(0)
    last = pl.num_programs(0) - 1
    spot = Spot()
    rows, width = x_ref.shape
    gain = gain_ref[...][None, :]
    block = 512 if rows % 512 == 0 else 256
    spans = [slice(start, start + block) for start in range(0, rows, block)]
    sems, local = rest[-2:]
    pieces = []
    for number in range(3):
        full, core = fulls.at[number], spot.core
        buffers = [half_of(full, core), *rest[6 * number : 6 * number + 6]]
        pieces.append(Scatter(spot, half_of(full, 1 - core), buffers, sems.at[number]))

    save_out = pltpu.make_async_copy(downs.at[0], rest_ref.at[:, pl.ds(0, width)], local.at[0])
    save_up = pltpu.make_async_copy(
        fulls.at[3], rest_ref.at[:, pl.ds(width, width)], local.at[3]
    )

    def save_down(chunk):
        target = down_ref.at[pl.ds(chunk * width, width), :]
        return pltpu.make_async_copy(downs.at[chunk % 2], target, local.at[1 + chunk % 2])

    leaving = [
        pltpu.make_async_copy(du_v, y_out, local.at[4]),
        pltpu.make_async_copy(dh_ref, dh_out, local.at[5]),
        pltpu.make_async_copy(n2, da_out, local.at[6]),
    ]

    def at(when, chunk, action, also=True):
        piece = pieces[chunk]

        @pl.when((step == when) & also)
        def _():
            if action == "x":
                piece.core_end()
                for index in range(8):
                    piece.x_step(index)
            elif action == "y":
                for index in range(4):
                    piece.y_step(index)
            elif action == "z":
                for index in range(3):
                    piece.z_step(index)
            else:
                piece.tail_start()

    @pl.when(step == 0)
    def _():
        greet(all_partners(spot))
        for span in spans:
            residual = x_ref[span, :].astype(SINGLE) + nn(mix_ref[span, :], wo_ref[...])
            h1[span, :] = residual
            y_acc[span, :] = residual
            n2[span, :] = (residual * scale_of(residual) * gain).astype(BFLOAT)
            dh_ref[span, :] = jnp.zeros_like(residual)

    def part(number, carry):
        then = number == 1
        for chunk in range(3):
            at(chunk + 1, chunk, "x", also=then)
        for chunk in range(2):
            at(chunk + 2, chunk, "tail", also=then)
        span = pl.ds(pl.multiple_of(number * block, 16), block)
        pre = nn(n2[span, :], wu_ref[...])
        grad_hidden = nt(dy_ref[span, :], wd_ref[...])
        square = pre * pre
        tanh = jnp.tanh(pre * (GELU_A + (GELU_A * GELU_B) * square))
        half = 0.5 + 0.5 * tanh
        act = pre * half
        slope = half + act * (1.0 - tanh) * (GELU_A + (3.0 * GELU_A * GELU_B) * square)
        act_low = act.astype(BFLOAT)
        grad_pre = (grad_hidden * slope).astype(BFLOAT)
        act_v[span, :] = act_low
        du_v[span, :] = grad_pre
        y_acc[span, :] += nn(act_low, wd_ref[...])
        dh_ref[span, :] += nt(grad_pre, wu_ref[...])
        return carry

    lax.fori_loop(0, rows // block, part, 0)
    for chunk in range(3):
        at(chunk + 1, chunk, "y")

    for chunk in (2, 3):

        @pl.when(step == chunk)
        def _():
            save_down(chunk - 2).wait()

    fulls[step] = tn(n2[...], du_v[...]).astype(BFLOAT)
    downs[step % 2] = tn(act_v[...], dy_ref[...]).astype(BFLOAT)
    for chunk in range(4):

        @pl.when(step == chunk)
        def _():
            save_down(chunk).start()
            if chunk < 3:
                pieces[chunk].copy(0).start()

    for chunk in range(3):
        at(chunk + 1, chunk, "z")

    @pl.when(step == last)
    def _():
        save_up.start()
        total = jnp.zeros_like(gain)
        for span in spans:
            du_v[span, :] = y_acc[span, :].astype(BFLOAT)
        leaving[0].start()
        for span in spans:
            residual = h1[span, :]
            scale = scale_of(residual)
            grad_second = dh_ref[span, :]
            total = total + jnp.sum(grad_second * residual * scale, axis=0, keepdims=True)
            grad_res = dy_ref[span, :].astype(SINGLE) + norm_back(
                residual, scale, grad_second * gain
            )
            dh_ref[span, :] = grad_res
            grad_low = grad_res.astype(BFLOAT)
            act_v[span, :] = grad_low
            n2[span, :] = nt(grad_low, wo_ref[...]).astype(BFLOAT)
        gg_ref[...] = total
        leaving[1].start()
        leaving[2].start()
        save_down(2).wait()
        downs[0] = tn(mix_ref[...], act_v[...]).astype(BFLOAT)
        save_out.start()
        pieces[2].tail_start()
        for number, piece in enumerate(pieces):
            left, right = piece.finish()
            base = number * width
            near_ref[:, base : base + width // 2] = left
            near_ref[:, base + width // 2 : base + width] = right
        save_out.wait()
        save_up.wait()
        save_down(3).wait()
        for copy in leaving:
            copy.wait()


def middle(tokens, mixture, cotangent, gain, w_out_up, w_down):
    rows, width = tokens.shape
    hidden = w_down.shape[0]
    chunks = hidden // width
    anywhere = pl.BlockSpec(memory_space=pl.ANY)
    square = (width, width)
    scratch = []
    for _ in range(3):
        scratch += scatter_scratch(*square)[1:]
    return pl.pallas_call(
        middle_kernel,
        grid=(chunks,),
        in_specs=[
            whole((rows, width)),
            whole((rows, width)),
            whole((rows, width)),
            whole((width,)),
            whole(square),
            pl.BlockSpec(square, lambda i: (0, 1 + i)),
            pl.BlockSpec(square, lambda i: (i, 0)),
        ],
        out_specs=[
            anywhere,
            anywhere,
            anywhere,
            anywhere,
            anywhere,
            whole((width // 32, 3 * width)),
            whole((1, width)),
        ],
        out_shape=[
            jax.ShapeDtypeStruct((rows, width), BFLOAT),
            jax.ShapeDtypeStruct((rows, width), SINGLE),
            jax.ShapeDtypeStruct((rows, width), BFLOAT),
            jax.ShapeDtypeStruct((width, 2 * width), BFLOAT),
            jax.ShapeDtypeStruct((hidden, width), BFLOAT),
            jax.ShapeDtypeStruct((width // 32, 3 * width), SINGLE),
            jax.ShapeDtypeStruct((1, width), SINGLE),
        ],
        scratch_shapes=[
            pltpu.VMEM((rows, width), SINGLE),
            pltpu.VMEM((rows, width), BFLOAT),
            pltpu.VMEM((rows, width), SINGLE),
            pltpu.VMEM((rows, width), BFLOAT),
            pltpu.VMEM((rows, width), BFLOAT),
            pltpu.VMEM((rows, width), SINGLE),
            pltpu.VMEM((chunks, *square), BFLOAT),
            pltpu.VMEM((2, *square), BFLOAT),
            *scratch,
            pltpu.SemaphoreType.DMA((3, 2, COPIES)),
            pltpu.SemaphoreType.DMA((7,)),
        ],
        compiler_params=pltpu.CompilerParams(
            collective_id=3, has_side_effects=True, vmem_limit_bytes=VMEM_LIMIT
        ),
        cost_estimate=cost(2 * rows * width * (6 * hidden + 3 * width), 100 << 20),
    )(tokens, mixture, cotangent, gain, w_out_up, w_out_up, w_down)


def back_kernel(
    labels,
    doc_steps,
    q_ref,
    k_ref,
    v_ref,
    query_k_ref,
    query_v_ref,
    da_ref,
    mix_ref,
    prob_ref,
    query_prob_ref,
    query_bucket_ref,
    grad_ref,
    grad_down_ref,
    y_ref,
    dq_ref,
    dkv_ref,
    ds_ref,
    sums_ref,
    shard_ref,
    down_ref,
    docs_ref,
    dk_acc,
    dv_acc,
    ds_keep,
    *rest,
):
    sems, move_sems, local = rest[14:]
    step = pl.program_id(0)
    last = pl.num_programs(0) - 1
    spot = Spot()
    rows, width = q_ref.shape
    pairs = prob_ref.shape[0] // 2
    keys = k_ref.shape[0]
    heads = query_prob_ref.shape[0]
    head_dim = width // heads
    grads, shards = (grad_ref, grad_down_ref), (shard_ref, down_ref)
    scatters = [
        Scatter(spot, half_of(grad, 1 - spot.core), rest[7 * i : 7 * i + 7], sems.at[i])
        for i, grad in enumerate(grads)
    ]
    loads = [
        pltpu.make_async_copy(half_of(grad, spot.core), scatter.held, local.at[i])
        for i, (grad, scatter) in enumerate(zip(grads, scatters))
    ]
    move = Move(
        spot,
        row_block(y_ref, docs_ref.shape[1]),
        lambda number: docs_ref.at[number],
        lambda number: docs_ref.at[number],
        move_sems,
        local.at[2],
    )

    @pl.when(step == 0)
    def _():
        greet(all_partners(spot))
        for scatter, load in zip(scatters, loads):
            scatter.copy(0).start()
            load.start()
        move.start()
        dk_acc[...] = jnp.zeros_like(dk_acc)
        dv_acc[...] = jnp.zeros_like(dv_acc)
        ds_keep[...] = jnp.zeros_like(ds_keep)

    @pl.when(step == 1)
    def _():
        for scatter, load in zip(scatters, loads):
            load.wait()
            scatter.core_end()
        for index in range(8):
            for scatter in scatters:
                scatter.x_step(index)

    def at(when, *actions):
        @pl.when(step == when)
        def _():
            for name, index in actions:
                for scatter in scatters:
                    getattr(scatter, name)(index)

    at(3, ("y_step", 0))
    at(5, ("z_step", 0), ("y_step", 1))
    at(7, ("z_step", 1), ("y_step", 2))
    at(8, ("z_step", 2), ("y_step", 3))

    @pl.when(step == last)
    def _():
        for scatter in scatters:
            scatter.tail_start()

    @pl.when(step < doc_steps)
    def _():
        def pair(number, carry):
            spread = (step % 2) * pairs + number
            lanes = pair_lanes(spread, head_dim)
            dq, dk, dv, kept = attend_back(
                q_ref[:, lanes],
                k_ref[:, lanes],
                v_ref[:, lanes],
                da_ref[:, lanes],
                mix_ref[:, lanes],
                [prob_ref[2 * number], prob_ref[2 * number + 1]],
                head_dim,
            )
            ds_ref[2 * number] = kept[0]
            ds_ref[2 * number + 1] = kept[1]
            dq_ref[:, lanes] = dq.astype(BFLOAT)
            dk_acc[:, lanes] += dk
            dv_acc[:, lanes] += dv
            return carry

        lax.fori_loop(0, pairs, pair, 0, unroll=True)

    @pl.when(step == doc_steps - 1)
    def _():
        dkv_ref[:keys, :width] = dk_acc[...].astype(BFLOAT)
        dkv_ref[:keys, width:] = dv_acc[...].astype(BFLOAT)

    @pl.when(step >= doc_steps)
    def _():
        def part(number, carry):
            span = pl.ds(pl.multiple_of(number * 128, 128), 128)
            place = pl.ds(pl.multiple_of(keys + (step - doc_steps) * rows + number * 128, 16), 128)
            dq, dk, dv, kept = query_back_block(
                q_ref[span, :],
                query_k_ref[span, :],
                query_v_ref[span, :],
                da_ref[span, :],
                mix_ref[span, :],
                [query_prob_ref[head, span, :] for head in range(heads)],
                head_dim,
            )
            for head in range(heads):
                ds_keep[head] += kept[head].astype(SINGLE)
            for pair in range(heads // 2):
                lanes = slice(pair * 2 * head_dim, (pair + 1) * 2 * head_dim)
                dq_ref[span, lanes] = dq[pair]
                dkv_ref[place, lanes] = dk[pair]
                dkv_ref[place, width + lanes.start : width + lanes.stop] = dv[pair]
            return carry

        lax.fori_loop(0, rows // 128, part, 0)

    @pl.when(step == last)
    def _():
        total = jnp.zeros_like(sums_ref)
        for index in range(8):
            some = slice(index * 16, (index + 1) * 16)
            terms = ds_keep[:, some, :].reshape(heads * 16, 128)
            high = terms.astype(BFLOAT)
            low = (terms - high.astype(SINGLE)).astype(BFLOAT)
            onehot = bucket_onehot(query_bucket_ref[some, :], labels)
            total = total + nt(onehot, high) + nt(onehot, low)
        sums_ref[...] = total

    @pl.when(step == last)
    def _():
        for scatter, shard in zip(scatters, shards):
            left, right = scatter.finish()
            shard[:, : scatter.half] = left
            shard[:, scatter.half :] = right
        move.finish()


def back(qkv, da_rows, mixture, probs, query_probs, query_buckets, grads, outputs, n_docs, labels):
    rows, width = da_rows.shape
    heads, doc_rows, keys = probs.shape
    block = 256
    doc_steps = 2 * doc_rows // block
    doc_blocks = doc_rows // block
    steps = doc_steps + (rows - doc_rows) // block
    half = heads // 2

    def row(i):
        return jnp.where(i < doc_steps, i // 2, i - doc_steps + doc_blocks)

    def doc(i):
        clipped = jnp.minimum(i, doc_steps - 1)
        return (clipped % 2, clipped // 2, 0)

    def query(i):
        return jnp.maximum(i, doc_steps) - doc_steps

    anywhere = pl.BlockSpec(memory_space=pl.ANY)
    along = pl.BlockSpec((block, width), lambda i: (row(i), 0))
    once = pl.Buffered(1)
    return pl.pallas_call(
        functools.partial(back_kernel, labels, doc_steps),
        grid=(steps,),
        in_specs=[
            along,
            pl.BlockSpec((keys, width), lambda i: (0, 1), pipeline_mode=once),
            pl.BlockSpec((keys, width), lambda i: (0, 2), pipeline_mode=once),
            pl.BlockSpec((block, width), lambda i: (query(i) + doc_blocks, 1)),
            pl.BlockSpec((block, width), lambda i: (query(i) + doc_blocks, 2)),
            along,
            along,
            pl.BlockSpec((half, block, keys), doc),
            pl.BlockSpec((heads, block, 128), lambda i: (0, query(i), 0)),
            whole(query_buckets.shape),
            anywhere,
            anywhere,
            anywhere,
        ],
        out_specs=[
            along,
            whole((rows, 2 * width)),
            pl.BlockSpec((half, block, keys), doc),
            whole((16 * labels, heads * 16)),
            *[whole((grad.shape[0] // 32, grad.shape[1])) for grad in grads],
            anywhere,
        ],
        out_shape=[
            jax.ShapeDtypeStruct((rows, width), BFLOAT),
            jax.ShapeDtypeStruct((rows, 2 * width), BFLOAT),
            jax.ShapeDtypeStruct(probs.shape, BFLOAT),
            jax.ShapeDtypeStruct((16 * labels, heads * 16), SINGLE),
            *[
                jax.ShapeDtypeStruct((grad.shape[0] // 32, grad.shape[1]), SINGLE)
                for grad in grads
            ],
            jax.ShapeDtypeStruct((n_docs, doc_rows // n_docs, width), BFLOAT),
        ],
        scratch_shapes=[
            pltpu.VMEM((keys, width), SINGLE),
            pltpu.VMEM((keys, width), SINGLE),
            pltpu.VMEM((heads, 128, 128), SINGLE),
            *scatter_scratch(*grads[0].shape),
            *scatter_scratch(*grads[1].shape),
            pltpu.SemaphoreType.DMA((2, 2, COPIES)),
            pltpu.SemaphoreType.DMA((2, 3)),
            pltpu.SemaphoreType.DMA((3,)),
        ],
        compiler_params=pltpu.CompilerParams(
            collective_id=1, has_side_effects=True, vmem_limit_bytes=VMEM_LIMIT
        ),
        cost_estimate=cost(70 * doc_rows * keys * width, 100 << 20),
    )(
        qkv,
        qkv,
        qkv,
        qkv,
        qkv,
        da_rows,
        mixture,
        probs,
        query_probs,
        query_buckets,
        *grads,
        outputs,
    )


class Total:
    def __init__(self, spot, slots, sems):
        self.spot, self.slots, self.sems = spot, slots, sems

    def rounds(self):
        spot = self.spot
        return (
            (spot.core, 2, [(1, spot.partner(core=1))]),
            (
                spot.x * 2 + spot.y,
                4,
                [(1, spot.partner(y=1)), (2, spot.partner(x=1)), (3, spot.partner(x=1, y=1))],
            ),
            (spot.z, 4, [(k, spot.partner(z=k)) for k in (1, 2, 3)]),
        )

    def run(self, values):
        base = 0
        for index, (place, count, partners) in enumerate(self.rounds()):
            mine = self.slots.at[base + place]
            mine[...] = values
            copies = [send(mine, mine, self.sems.at[index], k - 1, device) for k, device in partners]
            for copy in copies:
                copy.start()
            for copy in copies:
                copy.wait_recv()
            values = self.slots[base]
            for other in range(1, count):
                values = values + self.slots[base + other]
            for copy in copies:
                copy.wait_send()
            base += count
        return values


def leave_kernel(
    labels,
    x_ref,
    gain_ref,
    dq_ref,
    dkv_ref,
    dh_in,
    w_in,
    ds_ref,
    bucket_ref,
    query_sums_ref,
    ff_ref,
    found_ref,
    out_ref,
    docs_ref,
    query_dx_ref,
    total_ref,
    normed,
    away,
    low,
    high,
    sums,
    gain_sum,
    slots,
    dh_ref,
    w_ref,
    *rest,
):
    buffers, (sems, move_sems, total_sems, local) = rest[:7], rest[7:]
    step = pl.program_id(0)
    last = pl.num_programs(0) - 1
    spot = Spot()
    rows, width = x_ref.shape
    heads = ds_ref.shape[0]
    doc_rows = low.shape[0]
    block = doc_rows // 4
    scatter = Scatter(spot, away, buffers, sems)
    half = scatter.half
    move = Move(
        spot,
        row_block(low, block),
        lambda number: docs_ref.at[number],
        lambda number: docs_ref.at[number],
        move_sems,
        local.at[0],
    )
    query_copy = pltpu.make_async_copy(high, query_dx_ref, local.at[1])
    late = [
        pltpu.make_async_copy(dh_in, dh_ref, local.at[2]),
        pltpu.make_async_copy(w_in, w_ref, local.at[3]),
    ]

    @pl.when(step == 0)
    def _():
        for copy in late:
            copy.start()
        greet(all_partners(spot) + [spot.partner(x=1, y=1)])
        gain = gain_ref[...]
        sums[...] = query_sums_ref[...]
        gain_sum[...] = jnp.zeros_like(gain_sum)

        def norm_block(number, carry):
            span = pl.ds(pl.multiple_of(number * block, 16), block)
            values = x_ref[span, :].astype(SINGLE)
            normed[span, :] = (values * scale_of(values) * gain).astype(BFLOAT)
            return carry

        lax.fori_loop(0, rows // block, norm_block, 0)

        def product(core, into):
            part = half // 3

            for number in range(3):
                spot_out = slice(number * part, (number + 1) * part)
                start = core * half + number * part

                def from_q():
                    lanes = pl.ds(pl.multiple_of(start, 128), part)
                    into[:, spot_out] = tn(normed[...], dq_ref[:, lanes]).astype(BFLOAT)

                def from_kv():
                    lanes = pl.ds(pl.multiple_of(start - width, 128), part)
                    into[:, spot_out] = tn(normed[...], dkv_ref[:, lanes]).astype(BFLOAT)

                pl.when(start < width)(from_q)
                pl.when(start >= width)(from_kv)

        product(1 - spot.core, away)
        scatter.copy(0).start()
        product(spot.core, scatter.held)
        scatter.core_end()
        for index in range(8):
            scatter.x_step(index)

        def grad_block(start, into, place):
            span = pl.ds(pl.multiple_of(start, 16), block)
            values = x_ref[span, :].astype(SINGLE)
            scale = scale_of(values)
            grad = nt(dq_ref[span, :], w_ref[:, :width])
            grad = grad + nt(dkv_ref[span, :width], w_ref[:, width : 2 * width])
            grad = grad + nt(dkv_ref[span, width:], w_ref[:, 2 * width :])
            gain_sum[...] += jnp.sum(grad * values * scale, axis=0, keepdims=True)
            dx = dh_ref[span, :] + norm_back(values, scale, grad * gain)
            into[place, :] = dx.astype(into.dtype)

        for copy in late:
            copy.wait()
        for number in range(3):
            y, core = Move.PARTNERS[number]
            start = spot.partner(y=y, core=core)[1] * block
            grad_block(start, low, pl.ds(pl.multiple_of(start, 16), block))
            move.copy(number).start()
        start = spot.seq * block
        grad_block(start, low, pl.ds(pl.multiple_of(start, 16), block))
        move.own().start()
        for number in range((rows - doc_rows) // block):
            grad_block(
                doc_rows + number * block, high, pl.ds(number * block, block)
            )
        query_copy.start()

    def at(when, name, index):
        @pl.when(step == when)
        def _():
            getattr(scatter, name)(index)

    at(1, "y_step", 0)
    at(2, "y_step", 1)
    at(3, "z_step", 0)
    at(3, "y_step", 2)
    at(4, "z_step", 1)
    at(4, "y_step", 3)
    at(5, "z_step", 2)

    @pl.when(step == 7)
    def _():
        scatter.tail_start()

    @pl.when(step > 0)
    def _():
        total = sums[...]
        for number in range(ds_ref.shape[1] // 16):
            span = slice(number * 16, (number + 1) * 16)
            grad_rows = ds_ref[:, span, :].reshape(heads * 16, ds_ref.shape[2])
            total = total + bucket_products(bucket_ref[span, :], grad_rows, labels)
        sums[...] = total

    @pl.when(step == last)
    def _():
        shape = sums.shape
        same = (
            lax.broadcasted_iota(jnp.int32, shape, 0) // labels
            == lax.broadcasted_iota(jnp.int32, shape, 1) % 16
        )
        kept = jnp.where(same, sums[...], 0.0)
        folded = kept[:labels]
        for index in range(1, 16):
            folded = folded + kept[index * labels : (index + 1) * labels]
        pick_shape = (heads * 16, 128)
        pick = (
            lax.broadcasted_iota(jnp.int32, pick_shape, 0) // 16
            == lax.broadcasted_iota(jnp.int32, pick_shape, 1)
        )
        bias = jnp.dot(
            folded,
            jnp.where(pick, 1.0, 0.0),
            preferred_element_type=SINGLE,
            precision=lax.Precision.HIGHEST,
        )
        wide = width // 128
        lines = [gain_sum[:, r * 128 : (r + 1) * 128] for r in range(wide)]
        lines += [ff_ref[:, r * 128 : (r + 1) * 128] for r in range(wide)]
        lines += [found_ref[...]] * (slots.shape[1] - labels - 2 * wide)
        total_ref[...] = Total(spot, slots, total_sems).run(jnp.concatenate(lines + [bias], 0))
        left, right = scatter.finish()
        out_ref[:, :half] = left
        out_ref[:, half:] = right
        move.finish()
        query_copy.wait()


def leave(
    tokens, gain, dq, dkv, grad_res, w_qkv, ds, buckets, query_sums, grad_ff, found, n_docs, labels
):
    rows, width = tokens.shape
    heads, doc_rows, keys = ds.shape
    columns = 3 * width
    block = 128
    lines = -(-(2 * width // 128 + 1) // 8) * 8 + labels
    anywhere = pl.BlockSpec(memory_space=pl.ANY)
    return pl.pallas_call(
        functools.partial(leave_kernel, labels),
        grid=(1 + doc_rows // block,),
        in_specs=[
            whole((rows, width)),
            whole((1, width)),
            whole((rows, width)),
            whole((rows, 2 * width)),
            anywhere,
            anywhere,
            pl.BlockSpec((heads, block, keys), lambda i: (0, jnp.maximum(i - 1, 0), 0)),
            pl.BlockSpec((block, keys), lambda i: (jnp.maximum(i - 1, 0), 0)),
            whole(query_sums.shape),
            whole((1, width)),
            whole((1, 128)),
        ],
        out_specs=[whole((width // 32, columns)), anywhere, anywhere, whole((lines, 128))],
        out_shape=[
            jax.ShapeDtypeStruct((width // 32, columns), SINGLE),
            jax.ShapeDtypeStruct((n_docs, doc_rows // n_docs, width), BFLOAT),
            jax.ShapeDtypeStruct((rows - doc_rows, width), SINGLE),
            jax.ShapeDtypeStruct((lines, 128), SINGLE),
        ],
        scratch_shapes=[
            pltpu.VMEM((rows, width), BFLOAT),
            pltpu.VMEM((width, columns // 2), BFLOAT),
            pltpu.VMEM((doc_rows, width), BFLOAT),
            pltpu.VMEM((rows - doc_rows, width), SINGLE),
            pltpu.VMEM(query_sums.shape, SINGLE),
            pltpu.VMEM((1, width), SINGLE),
            pltpu.VMEM((10, lines, 128), SINGLE),
            pltpu.VMEM((rows, width), SINGLE),
            pltpu.VMEM(w_qkv.shape, BFLOAT),
            *scatter_scratch(width, columns),
            pltpu.SemaphoreType.DMA((2, COPIES)),
            pltpu.SemaphoreType.DMA((2, 3)),
            pltpu.SemaphoreType.DMA((3, 2, 3)),
            pltpu.SemaphoreType.DMA((4,)),
        ],
        compiler_params=pltpu.CompilerParams(
            collective_id=2, has_side_effects=True, vmem_limit_bytes=VMEM_LIMIT
        ),
        cost_estimate=cost(12 * rows * width * width, 100 << 20),
    )(
        tokens,
        gain.reshape(1, width),
        dq,
        dkv,
        grad_res,
        w_qkv,
        ds,
        buckets,
        query_sums,
        grad_ff,
        found,
    )


def on_device(
    doc_tokens,
    queries,
    doc_cot,
    query_cot,
    q_weight,
    kv_weight,
    out_weight,
    up_weight,
    down_weight,
    attn_gain,
    ff_gain,
    rel_bias,
    doc_buckets,
    query_buckets,
    topk_mask,
    positives,
    pos_count,
):
    n_docs, shard_rows, width = doc_tokens.shape
    n_query, query_len, _ = queries.shape
    bucket_count, heads = rel_bias.shape
    doc_len = doc_buckets.shape[1]
    doc_rows = n_docs * shard_rows
    query_total = n_query * query_len
    seq_size = lax.axis_size("seq")
    group = max(1, seq_size // n_docs)
    local_docs = max(1, n_docs // seq_size)
    local_rows = doc_len // group
    dp_size = lax.axis_size("dp")
    small = (dp_size, seq_size, n_docs) == (8, 4, 4) and width % 256 == 0 and shard_rows % 256 == 0
    small = small and down_weight.shape[0] * 32 == 4 * width and query_total % 256 == 0

    flat_queries = queries.reshape(query_total, width)
    flat_query_cot = query_cot.reshape(query_total, width)

    table = jnp.pad(rel_bias.T, ((0, 16 - heads), (0, 127 - bucket_count)))
    table = jnp.pad(table, ((0, 0), (0, 1)), constant_values=-1e30)

    if small:
        tokens, cotangent, w_qkv, w_out_up, w_down, buckets, qkv, mixture, doc_probs, query_probs, tiled = front(
            doc_tokens,
            flat_queries,
            doc_cot,
            flat_query_cot,
            (q_weight, kv_weight, out_weight, up_weight, down_weight),
            doc_buckets,
            attn_gain,
            table,
            query_buckets,
            heads,
        )
    else:
        order = gather_orders()[0]
        w_qkv = gather_rows(jnp.concatenate([q_weight, kv_weight], 1), order)
        w_out_up = gather_rows(jnp.concatenate([out_weight, up_weight], 1), order)
        w_down = gather_rows(down_weight, order)
        tokens = jnp.concatenate([own_document(doc_tokens), flat_queries], 0)
        cotangent = jnp.concatenate([own_document(doc_cot), flat_query_cot], 0)
        buckets = gather_positions(doc_buckets.astype(jnp.int16))
        repeats = 128 // query_len
        same = jnp.kron(jnp.eye(repeats, dtype=jnp.int32), jnp.ones_like(query_buckets))
        tiled = jnp.where(same == 1, jnp.tile(query_buckets, (repeats, repeats)), 127)
        if group > 1:
            part = lax.axis_index("seq") % group
            buckets = lax.dynamic_slice_in_dim(buckets, part * local_rows, local_rows, 0)
        q_rows, kv_rows = project(tokens, attn_gain, w_qkv)
        kv_docs = kv_rows
        if group > 1:
            teams = [list(range(t * group, (t + 1) * group)) for t in range(seq_size // group)]
            kv_docs = lax.all_gather(
                kv_rows[:doc_rows], "seq", axis=0, tiled=True, axis_index_groups=teams
            )
        doc_mix, doc_probs = doc_forward(
            q_rows, kv_docs, table, buckets, local_docs, local_rows, heads
        )
        query_mix, query_probs = query_forward(
            q_rows, kv_rows, table, tiled, doc_rows, query_total, heads
        )
        mixture = jnp.concatenate([doc_mix, query_mix], 0)
    if small:
        outputs, grad_res, grad_mix, grad_rest, grad_down, grad_near, grad_ff = middle(
            tokens, mixture, cotangent, ff_gain, w_out_up, w_down
        )
    else:
        outputs, grad_res, grad_mix, grad_out_up, grad_down, grad_ff = feed(
            tokens, mixture, cotangent, ff_gain, w_out_up, w_down
        )
    query_out = outputs[doc_rows:].reshape(queries.shape)
    matches = positives[:, :, None] == jnp.arange(doc_len, dtype=jnp.int32)[None, None, :]
    counted = jnp.arange(positives.shape[1], dtype=jnp.int32)[None, :] < pos_count[:, None]
    retrieved = jnp.sum(
        jnp.where(matches & counted[:, :, None], topk_mask[:, None, :].astype(SINGLE), 0.0)
    )

    if small:
        dq, dkv, ds, query_sums, grad_far, grad_down_shard, doc_out = back(
            qkv,
            grad_mix,
            mixture,
            doc_probs,
            query_probs,
            tiled,
            (grad_rest, grad_down),
            outputs,
            n_docs,
            bucket_count,
        )
        grad_out_shard = grad_far[:, :width]
        grad_up_shard = jnp.concatenate([grad_near, grad_far[:, width:]], 1)
        grad_qkv_shard, doc_dx, query_dx, total = leave(
            tokens,
            attn_gain,
            dq,
            dkv,
            grad_res,
            w_qkv,
            ds,
            buckets,
            query_sums,
            grad_ff,
            jnp.full((1, 128), retrieved),
            n_docs,
            bucket_count,
        )
        lines = width // 128
        total_attn = total[:lines].reshape(-1)
        total_ff = total[lines : 2 * lines].reshape(-1)
        total_found = total[2 * lines, 0]
        total_bias = total[-bucket_count:, :heads]
        query_dx = query_dx.reshape(queries.shape)
    else:
        grad_down_shard = scatter_columns(grad_down, 2)
        grad_out_up_shard = scatter_columns(grad_out_up, 2)
        grad_out_shard = grad_out_up_shard[:, :width]
        grad_up_shard = grad_out_up_shard[:, width:]
        doc_out = spread_document(outputs[:doc_rows], doc_tokens)
        doc_dq, doc_dk, doc_dv, doc_sums = doc_backward(
            q_rows,
            kv_docs,
            grad_mix,
            doc_mix,
            doc_probs,
            buckets,
            local_docs,
            local_rows,
            bucket_count,
        )
        if group > 1:
            both = jnp.concatenate([doc_dk, doc_dv], 1)
            both = lax.psum_scatter(
                both, "seq", scatter_dimension=0, tiled=True, axis_index_groups=teams
            )
            doc_dk, doc_dv = both[:, :width], both[:, width:]
        query_dq, query_dkv, query_sums = query_backward(
            q_rows, kv_rows, grad_mix, mixture, query_probs, tiled, doc_rows, bucket_count
        )
        grad_tokens, grad_low, grad_qkv, grad_attn = unproject(
            tokens,
            attn_gain,
            jnp.concatenate([doc_dq, query_dq], 0),
            jnp.concatenate([doc_dk, query_dkv[:, :width]], 0),
            jnp.concatenate([doc_dv, query_dkv[:, width:]], 0),
            grad_res,
            w_qkv,
        )
        grad_qkv_shard = scatter_columns(grad_qkv, 2)
        doc_dx = spread_document(grad_low[:doc_rows], doc_tokens)
        query_dx = grad_tokens[doc_rows:].reshape(queries.shape)
        sums = (doc_sums + query_sums).reshape(16, bucket_count, heads, 16)
        keep = jnp.eye(16, dtype=SINGLE)[:, None, None, :]
        bias_local = jnp.sum(sums * keep, axis=(0, 3))
        flat = jnp.concatenate(
            [grad_attn[0], grad_ff[0], bias_local.reshape(-1), jnp.full((128,), retrieved)]
        )
        total = sum_all(flat)
        total_attn, total_ff = total[:width], total[width : 2 * width]
        total_bias = total[2 * width : 2 * width + bucket_count * heads]
        total_bias = total_bias.reshape(bucket_count, heads)
        total_found = total[-1]
    slots = float(n_query * dp_size * seq_size * positives.shape[1])
    return (
        doc_out,
        query_out,
        doc_dx.astype(SINGLE),
        query_dx,
        grad_qkv_shard[:, :width],
        grad_qkv_shard[:, width:],
        grad_out_shard,
        grad_up_shard,
        grad_down_shard,
        total_attn,
        total_ff,
        total_bias,
        total_found / slots,
    )


def solution(mesh):
    rows_all = P(("dp", "seq"), None)
    return jax.shard_map(
        on_device,
        mesh=mesh,
        in_specs=(
            P("dp", "seq", None),
            P(("dp", "seq"), None, None),
            P("dp", "seq", None),
            P(("dp", "seq"), None, None),
            rows_all,
            rows_all,
            rows_all,
            rows_all,
            rows_all,
            P(),
            P(),
            P(),
            P("seq", None),
            P(),
            rows_all,
            rows_all,
            P(("dp", "seq")),
        ),
        out_specs=(
            P("dp", "seq", None),
            P(("dp", "seq"), None, None),
            P("dp", "seq", None),
            P(("dp", "seq"), None, None),
            rows_all,
            rows_all,
            rows_all,
            rows_all,
            rows_all,
            P(),
            P(),
            P(),
            P(),
        ),
        check_vma=False,
    )
```

```python
import functools
import math

import jax
import jax.numpy as jnp
from jax import lax
from jax.experimental import pallas as pl
from jax.experimental.pallas import tpu as pltpu
from jax.sharding import PartitionSpec as P

EPSILON = 1e-06
BFLOAT = jnp.bfloat16
SINGLE = jnp.float32
FIXED = 8191.0
GELU_A = math.sqrt(2.0 / math.pi)
GELU_B = 0.044715
VMEM_LIMIT = 63 << 20


def nn(left, right):
    return jnp.dot(left, right, preferred_element_type=SINGLE)


def nt(left, right):
    return lax.dot_general(left, right, (((1,), (1,)), ((), ())), preferred_element_type=SINGLE)


def tn(left, right):
    return lax.dot_general(left, right, (((0,), (0,)), ((), ())), preferred_element_type=SINGLE)


def whole(shape):
    zeros = (0,) * len(shape)
    return pl.BlockSpec(shape, lambda *_: zeros, pipeline_mode=pl.Buffered(1))


def params():
    return pltpu.CompilerParams(vmem_limit_bytes=VMEM_LIMIT)


def cost(flops, moved):
    return pl.CostEstimate(flops=int(flops), bytes_accessed=int(moved), transcendentals=0)


def scale_of(values):
    return lax.rsqrt(jnp.mean(values * values, axis=-1, keepdims=True) + EPSILON)


def norm_back(values, scale, scaled_grad):
    dot = jnp.mean(values * scaled_grad, axis=-1, keepdims=True)
    return scale * (scaled_grad - values * (scale * scale * dot))


def first_lanes(shape, head_dim):
    return lax.broadcasted_iota(jnp.int32, shape, 1) < head_dim


def project_kernel(x_ref, gain_ref, w_ref, q_ref, kv_ref):
    values = x_ref[...].astype(SINGLE)
    normed = (values * scale_of(values) * gain_ref[...]).astype(BFLOAT)
    width = values.shape[1]
    q_ref[...] = nn(normed, w_ref[:, :width]).astype(BFLOAT)
    kv_ref[...] = nn(normed, w_ref[:, width:]).astype(BFLOAT)


def project(tokens, gain, w_qkv):
    rows, width = tokens.shape
    block = math.gcd(rows, 256)
    return pl.pallas_call(
        project_kernel,
        grid=(rows // block,),
        in_specs=[
            pl.BlockSpec((block, width), lambda i: (i, 0)),
            whole((1, width)),
            whole(w_qkv.shape),
        ],
        out_specs=[
            pl.BlockSpec((block, width), lambda i: (i, 0)),
            pl.BlockSpec((block, 2 * width), lambda i: (i, 0)),
        ],
        out_shape=[
            jax.ShapeDtypeStruct((rows, width), BFLOAT),
            jax.ShapeDtypeStruct((rows, 2 * width), BFLOAT),
        ],
        compiler_params=params(),
        cost_estimate=cost(6 * rows * width * width, 12 * rows * width),
    )(tokens, gain.reshape(1, width), w_qkv)


def attend_pair(q_pair, k_pair, v_pair, table_ref, bucket_ref, start, prob_ref, step, head_dim):
    rows, keys = q_pair.shape[0], k_pair.shape[0]
    wide = first_lanes(q_pair.shape, head_dim)
    tall = first_lanes(v_pair.shape, head_dim)
    coded_rows = jnp.round(table_ref[pl.ds(2 * step, 2), :] * FIXED).astype(jnp.int32)
    table = (coded_rows[0:1, :] << 16) | (coded_rows[1:2, :] & 0xFFFF)
    table = jnp.broadcast_to(table, (rows, 128))
    span = pl.ds(start, rows)
    packed = jnp.concatenate(
        [
            jnp.take_along_axis(
                table,
                bucket_ref[span, part * 128 : part * 128 + 128].astype(jnp.int32),
                axis=1,
                mode="promise_in_bounds",
            )
            for part in range(keys // 128)
        ],
        1,
    )
    total = None
    for side in range(2):
        mine = wide if side == 0 else ~wide
        mine_tall = tall if side == 0 else ~tall
        coded = (packed >> 16) if side == 0 else ((packed << 16) >> 16)
        scores = nt(jnp.where(mine, q_pair, 0), k_pair)
        scores = scores + coded.astype(SINGLE) * (1.0 / FIXED)
        shifted = jnp.exp(scores - jnp.max(scores, axis=-1, keepdims=True))
        inverse = 1.0 / jnp.sum(shifted, axis=-1, keepdims=True)
        soft = (shifted * inverse).astype(BFLOAT)
        prob_ref[2 * step + side] = soft
        term = nn(soft, jnp.where(mine_tall, v_pair, 0))
        total = term if total is None else total + term
    return total.astype(BFLOAT)


def pair_lanes(step, head_dim, offset=0):
    return pl.ds(pl.multiple_of(offset + step * 2 * head_dim, 128), 2 * head_dim)


def doc_forward_kernel(q_ref, k_ref, v_ref, table_ref, bucket_ref, mix_ref, prob_ref):
    heads = prob_ref.shape[0]
    head_dim = q_ref.shape[1] // heads

    def pair(step, carry):
        lanes = pair_lanes(step, head_dim)
        mix_ref[:, lanes] = attend_pair(
            q_ref[:, lanes],
            k_ref[:, lanes],
            v_ref[:, lanes],
            table_ref,
            bucket_ref,
            0,
            prob_ref,
            step,
            head_dim,
        )
        return carry

    lax.fori_loop(0, heads // 2, pair, 0)


def doc_forward(q_rows, kv_rows, table, buckets, n_docs, rows, heads):
    width = q_rows.shape[1]
    keys = buckets.shape[1]
    block = math.gcd(rows, 256)
    steps = rows // block
    return pl.pallas_call(
        doc_forward_kernel,
        grid=(n_docs, steps),
        in_specs=[
            pl.BlockSpec((block, width), lambda d, i: (d * steps + i, 0)),
            pl.BlockSpec((keys, width), lambda d, i: (d, 0)),
            pl.BlockSpec((keys, width), lambda d, i: (d, 1)),
            whole(table.shape),
            pl.BlockSpec((block, keys), lambda d, i: (i, 0)),
        ],
        out_specs=[
            pl.BlockSpec((block, width), lambda d, i: (d * steps + i, 0)),
            pl.BlockSpec((heads, block, keys), lambda d, i: (0, d * steps + i, 0)),
        ],
        out_shape=[
            jax.ShapeDtypeStruct((n_docs * rows, width), BFLOAT),
            jax.ShapeDtypeStruct((heads, n_docs * rows, keys), BFLOAT),
        ],
        compiler_params=params(),
        cost_estimate=cost(30 * n_docs * rows * keys * width, 2 * heads * n_docs * rows * keys),
    )(q_rows, kv_rows, kv_rows, table, buckets)


def bucket_onehot(bucket_rows, labels):
    rows, keys = bucket_rows.shape
    numbers = bucket_rows.astype(jnp.int32)
    names = lax.broadcasted_iota(jnp.int32, (labels, keys), 0)
    parts = [
        jnp.where(jnp.broadcast_to(numbers[r : r + 1, :], (labels, keys)) == names, 1.0, 0.0).astype(
            BFLOAT
        )
        for r in range(rows)
    ]
    return jnp.concatenate(parts, 0)


def bucket_products(bucket_rows, grad_rows, labels):
    return nt(bucket_onehot(bucket_rows, labels), grad_rows)


def attend_back(q_pair, k_pair, v_pair, da_pair, mix_pair, probs, head_dim):
    wide = first_lanes(q_pair.shape, head_dim)
    tall = first_lanes(k_pair.shape, head_dim)
    product = da_pair.astype(SINGLE) * mix_pair.astype(SINGLE)
    dq = dk = dv = None
    kept = []
    for side in range(2):
        mine = wide if side == 0 else ~wide
        mine_tall = tall if side == 0 else ~tall
        da_mine = jnp.where(mine, da_pair, 0)
        correction = jnp.sum(jnp.where(mine, product, 0.0), axis=-1, keepdims=True)
        grad_soft = nt(da_mine, v_pair)
        soft = probs[side]
        grad_scores = (soft.astype(SINGLE) * (grad_soft - correction)).astype(BFLOAT)
        kept.append(grad_scores)
        dq_term = nn(grad_scores, jnp.where(mine_tall, k_pair, 0))
        dk_term = tn(grad_scores, jnp.where(mine, q_pair, 0))
        dv_term = tn(soft, da_mine)
        dq = dq_term if dq is None else dq + dq_term
        dk = dk_term if dk is None else dk + dk_term
        dv = dv_term if dv is None else dv + dv_term
    return dq, dk, dv, kept


def query_back_block(q_rows, k_rows, v_rows, da_rows, mix_rows, probs, head_dim):
    rows, width = q_rows.shape
    heads = len(probs)
    wide = first_lanes((rows, 2 * head_dim), head_dim)

    def pair(values, step):
        return values[:, step * 2 * head_dim : (step + 1) * 2 * head_dim]

    def halves(values, step):
        return jnp.where(wide, pair(values, step), 0), jnp.where(wide, 0, pair(values, step))

    das, corrections, grads = [], [], []
    for step in range(heads // 2):
        das += halves(da_rows, step)
    for head in range(heads):
        grads.append(nt(das[head], pair(v_rows, head // 2)))
    for head in range(heads):
        product = das[head].astype(SINGLE) * pair(mix_rows, head // 2).astype(SINGLE)
        corrections.append(jnp.sum(product, axis=-1, keepdims=True))
    kept = [
        (prob.astype(SINGLE) * (grad - correction)).astype(BFLOAT)
        for prob, grad, correction in zip(probs, grads, corrections)
    ]
    dq, dk, dv = [], [], []
    for step in range(heads // 2):
        left, right = kept[2 * step], kept[2 * step + 1]
        k_left, k_right = halves(k_rows, step)
        dq.append((nn(left, k_left) + nn(right, k_right)).astype(BFLOAT))
    for step in range(heads // 2):
        left, right = kept[2 * step], kept[2 * step + 1]
        q_left, q_right = halves(q_rows, step)
        dk.append((tn(left, q_left) + tn(right, q_right)).astype(BFLOAT))
    for step in range(heads // 2):
        terms = tn(probs[2 * step], das[2 * step]) + tn(probs[2 * step + 1], das[2 * step + 1])
        dv.append(terms.astype(BFLOAT))
    return dq, dk, dv, kept


def doc_backward_kernel(
    labels,
    q_ref,
    k_ref,
    v_ref,
    da_ref,
    mix_ref,
    prob_ref,
    bucket_ref,
    dq_ref,
    dk_ref,
    dv_ref,
    sums_ref,
    dk_acc,
    dv_acc,
    ds_keep,
):
    rows, width = q_ref.shape
    heads = prob_ref.shape[0]
    keys = k_ref.shape[0]
    head_dim = width // heads
    doc, step_i = pl.program_id(0), pl.program_id(1)

    @pl.when(step_i == 0)
    def _():
        dk_acc[...] = jnp.zeros_like(dk_acc)
        dv_acc[...] = jnp.zeros_like(dv_acc)

    @pl.when((step_i == 0) & (doc == 0))
    def _():
        sums_ref[...] = jnp.zeros_like(sums_ref)

    def pair(step, carry):
        lanes = pl.ds(pl.multiple_of(step * 2 * head_dim, 128), 2 * head_dim)
        dq, dk, dv, kept = attend_back(
            q_ref[:, lanes],
            k_ref[:, lanes],
            v_ref[:, lanes],
            da_ref[:, lanes],
            mix_ref[:, lanes],
            [prob_ref[2 * step], prob_ref[2 * step + 1]],
            head_dim,
        )
        ds_keep[2 * step] = kept[0]
        ds_keep[2 * step + 1] = kept[1]
        dq_ref[:, lanes] = dq.astype(BFLOAT)
        dk_acc[:, lanes] += dk
        dv_acc[:, lanes] += dv
        return carry

    lax.fori_loop(0, heads // 2, pair, 0)

    def group(number, carry):
        span = pl.ds(pl.multiple_of(number * 16, 16), 16)
        sums_ref[...] += bucket_products(
            bucket_ref[span, :], ds_keep[:, span, :].reshape(heads * 16, keys), labels
        )
        return carry

    lax.fori_loop(0, rows // 16, group, 0)

    @pl.when(step_i == pl.num_programs(1) - 1)
    def _():
        dk_ref[...] = dk_acc[...].astype(BFLOAT)
        dv_ref[...] = dv_acc[...].astype(BFLOAT)


def doc_backward(q_rows, kv_rows, da_rows, mixture, probs, buckets, n_docs, rows, labels):
    width = q_rows.shape[1]
    heads = probs.shape[0]
    keys = buckets.shape[1]
    block = math.gcd(rows, 256)
    steps = rows // block
    along = pl.BlockSpec((block, width), lambda d, i: (d * steps + i, 0))
    per_doc = pl.BlockSpec((keys, width), lambda d, i: (d, 0))
    return pl.pallas_call(
        functools.partial(doc_backward_kernel, labels),
        grid=(n_docs, steps),
        in_specs=[
            along,
            per_doc,
            pl.BlockSpec((keys, width), lambda d, i: (d, 1)),
            along,
            along,
            pl.BlockSpec((heads, block, keys), lambda d, i: (0, d * steps + i, 0)),
            pl.BlockSpec((block, keys), lambda d, i: (i, 0)),
        ],
        out_specs=[along, per_doc, per_doc, whole((16 * labels, heads * 16))],
        out_shape=[
            jax.ShapeDtypeStruct((n_docs * rows, width), BFLOAT),
            jax.ShapeDtypeStruct((n_docs * keys, width), BFLOAT),
            jax.ShapeDtypeStruct((n_docs * keys, width), BFLOAT),
            jax.ShapeDtypeStruct((16 * labels, heads * 16), SINGLE),
        ],
        scratch_shapes=[
            pltpu.VMEM((keys, width), SINGLE),
            pltpu.VMEM((keys, width), SINGLE),
            pltpu.VMEM((heads, block, keys), BFLOAT),
        ],
        compiler_params=params(),
        cost_estimate=cost(70 * n_docs * rows * keys * width, 2 * heads * n_docs * rows * keys),
    )(q_rows, kv_rows, kv_rows, da_rows, mixture, probs, buckets)


def query_block(q_rows, k_rows, v_rows, table_ref, index, heads):
    rows, width = q_rows.shape
    head_dim = width // heads
    wide = first_lanes((rows, 2 * head_dim), head_dim)

    def halves(values, step):
        pair = values[:, step * 2 * head_dim : (step + 1) * 2 * head_dim]
        return jnp.where(wide, pair, 0), jnp.where(wide, 0, pair), pair

    scores = []
    for step in range(heads // 2):
        left, right, _ = halves(q_rows, step)
        keys = halves(k_rows, step)[2]
        scores += [nt(left, keys), nt(right, keys)]
    for head in range(heads):
        table = jnp.broadcast_to(table_ref[head : head + 1, :], (rows, 128))
        bias = jnp.take_along_axis(table, index, axis=1, mode="promise_in_bounds")
        scores[head] = scores[head] + bias
    tops = [jnp.max(score, axis=-1, keepdims=True) for score in scores]
    shifted = [jnp.exp(score - top) for score, top in zip(scores, tops)]
    inverse = [1.0 / jnp.sum(shift, axis=-1, keepdims=True) for shift in shifted]
    softs = [(shift * inv).astype(BFLOAT) for shift, inv in zip(shifted, inverse)]
    outs = []
    for step in range(heads // 2):
        left, right, _ = halves(v_rows, step)
        outs.append((nn(softs[2 * step], left) + nn(softs[2 * step + 1], right)).astype(BFLOAT))
    return softs, jnp.concatenate(outs, 1)


def query_forward_kernel(q_ref, kv_ref, table_ref, bucket_ref, mix_ref, prob_ref):
    width = q_ref.shape[1]
    softs, mix_ref[...] = query_block(
        q_ref[...], kv_ref[:, :width], kv_ref[:, width:], table_ref, bucket_ref[...], prob_ref.shape[0]
    )
    for head, soft in enumerate(softs):
        prob_ref[head] = soft


def query_forward(q_rows, kv_rows, table, buckets, start, count, heads):
    width = q_rows.shape[1]
    offset = start // 128
    return pl.pallas_call(
        query_forward_kernel,
        grid=(count // 128,),
        in_specs=[
            pl.BlockSpec((128, width), lambda i: (offset + i, 0)),
            pl.BlockSpec((128, 2 * width), lambda i: (offset + i, 0)),
            whole(table.shape),
            whole(buckets.shape),
        ],
        out_specs=[
            pl.BlockSpec((128, width), lambda i: (i, 0)),
            pl.BlockSpec((heads, 128, 128), lambda i: (0, i, 0)),
        ],
        out_shape=[
            jax.ShapeDtypeStruct((count, width), BFLOAT),
            jax.ShapeDtypeStruct((heads, count, 128), BFLOAT),
        ],
        compiler_params=params(),
        cost_estimate=cost(4 * count * 128 * width * 4, 10 * count * width),
    )(q_rows, kv_rows, table, buckets)


def query_backward_kernel(
    labels, q_ref, kv_ref, da_ref, mix_ref, prob_ref, bucket_ref, dq_ref, dkv_ref, sums_ref, ds_keep
):
    rows, width = q_ref.shape
    heads = prob_ref.shape[0]
    head_dim = width // heads

    @pl.when(pl.program_id(0) == 0)
    def _():
        sums_ref[...] = jnp.zeros_like(sums_ref)

    for step in range(heads // 2):
        lanes = slice(step * 2 * head_dim, (step + 1) * 2 * head_dim)
        right = slice(width + lanes.start, width + lanes.stop)
        dq, dk, dv, kept = attend_back(
            q_ref[:, lanes],
            kv_ref[:, lanes],
            kv_ref[:, right],
            da_ref[:, lanes],
            mix_ref[:, lanes],
            [prob_ref[2 * step], prob_ref[2 * step + 1]],
            head_dim,
        )
        ds_keep[2 * step] = kept[0]
        ds_keep[2 * step + 1] = kept[1]
        dq_ref[:, lanes] = dq.astype(BFLOAT)
        dkv_ref[:, lanes] = dk.astype(BFLOAT)
        dkv_ref[:, right] = dv.astype(BFLOAT)

    def group(number, carry):
        span = pl.ds(pl.multiple_of(number * 16, 16), 16)
        sums_ref[...] += bucket_products(
            bucket_ref[span, :], ds_keep[:, span, :].reshape(heads * 16, rows), labels
        )
        return carry

    lax.fori_loop(0, rows // 16, group, 0)


def query_backward(q_rows, kv_rows, da_rows, mixture, probs, buckets, start, labels):
    width = q_rows.shape[1]
    heads, count, _ = probs.shape
    offset = start // 128
    return pl.pallas_call(
        functools.partial(query_backward_kernel, labels),
        grid=(count // 128,),
        in_specs=[
            pl.BlockSpec((128, width), lambda i: (offset + i, 0)),
            pl.BlockSpec((128, 2 * width), lambda i: (offset + i, 0)),
            pl.BlockSpec((128, width), lambda i: (offset + i, 0)),
            pl.BlockSpec((128, width), lambda i: (offset + i, 0)),
            pl.BlockSpec((heads, 128, 128), lambda i: (0, i, 0)),
            whole(buckets.shape),
        ],
        out_specs=[
            pl.BlockSpec((128, width), lambda i: (i, 0)),
            pl.BlockSpec((128, 2 * width), lambda i: (i, 0)),
            whole((16 * labels, heads * 16)),
        ],
        out_shape=[
            jax.ShapeDtypeStruct((count, width), BFLOAT),
            jax.ShapeDtypeStruct((count, 2 * width), BFLOAT),
            jax.ShapeDtypeStruct((16 * labels, heads * 16), SINGLE),
        ],
        scratch_shapes=[pltpu.VMEM((heads, 128, 128), BFLOAT)],
        compiler_params=params(),
        cost_estimate=cost(8 * count * 128 * width * 4, 14 * count * width),
    )(q_rows, kv_rows, da_rows, mixture, probs, buckets)


def feed_kernel(
    chunk,
    x_ref,
    mix_ref,
    dy_ref,
    gain_ref,
    wou_ref,
    wd_ref,
    y_ref,
    dh_ref,
    da_ref,
    gou_ref,
    gd_ref,
    gg_ref,
    gou_acc,
    gd_acc,
    stage,
    sems,
):
    step = pl.program_id(0)
    hidden, width = wd_ref.shape

    @pl.when(step == 0)
    def _():
        gou_acc[...] = jnp.zeros_like(gou_acc)
        gd_acc[...] = jnp.zeros_like(gd_acc)
        gg_ref[...] = jnp.zeros_like(gg_ref)

    mixture = mix_ref[...]
    dy = dy_ref[...]
    gain = gain_ref[...]
    residual = x_ref[...].astype(SINGLE) + nn(mixture, wou_ref[:, :width])
    scale = scale_of(residual)
    second = (residual * scale * gain).astype(BFLOAT)
    y = residual
    grad_second = jnp.zeros_like(residual)
    for part in range(hidden // chunk):
        span = slice(part * chunk, (part + 1) * chunk)
        past = slice(width + part * chunk, width + (part + 1) * chunk)
        pre = nn(second, wou_ref[:, past])
        grad_hidden = nt(dy, wd_ref[span, :])
        square = pre * pre
        tanh = jnp.tanh(pre * (GELU_A + (GELU_A * GELU_B) * square))
        half = 0.5 + 0.5 * tanh
        act = pre * half
        slope = half + act * (1.0 - tanh) * (GELU_A + (3.0 * GELU_A * GELU_B) * square)
        act_low = act.astype(BFLOAT)
        grad_pre = (grad_hidden * slope).astype(BFLOAT)
        y = y + nn(act_low, wd_ref[span, :])
        grad_second = grad_second + nt(grad_pre, wou_ref[:, past])
        gd_acc[span, :] += tn(act_low, dy)
        gou_acc[:, past] += tn(second, grad_pre)
    y_ref[...] = y.astype(BFLOAT)
    gg_ref[...] += jnp.sum(grad_second * residual * scale, axis=0, keepdims=True)
    grad_res = dy.astype(SINGLE) + norm_back(residual, scale, grad_second * gain)
    dh_ref[...] = grad_res
    grad_low = grad_res.astype(BFLOAT)
    da_ref[...] = nt(grad_low, wou_ref[:, :width]).astype(BFLOAT)
    gou_acc[:, :width] += tn(mixture, grad_low)

    @pl.when(step == pl.num_programs(0) - 1)
    def _():
        pieces = []
        rows, columns = stage.shape[1:]
        for acc, out in ((gd_acc, gd_ref), (gou_acc, gou_ref)):
            for r in range(acc.shape[0] // rows):
                for c in range(acc.shape[1] // columns):
                    spot = (pl.ds(r * rows, rows), pl.ds(c * columns, columns))
                    pieces.append((acc, out, spot))
        flying = [None, None]
        for number, (acc, out, spot) in enumerate(pieces):
            slot = number % 2
            if flying[slot] is not None:
                flying[slot].wait()
            stage[slot] = acc[spot].astype(BFLOAT)
            flying[slot] = pltpu.make_async_copy(stage.at[slot], out.at[spot], sems.at[slot])
            flying[slot].start()
        for copy in flying:
            if copy is not None:
                copy.wait()


def feed(tokens, mixture, cotangent, gain, w_out_up, w_down):
    rows, width = tokens.shape
    hidden = w_down.shape[0]
    block = math.gcd(rows, 256)
    along = pl.BlockSpec((block, width), lambda i: (i, 0))
    anywhere = pl.BlockSpec(memory_space=pl.ANY)
    return pl.pallas_call(
        functools.partial(feed_kernel, math.gcd(hidden, 768)),
        grid=(rows // block,),
        in_specs=[
            along,
            along,
            along,
            whole((1, width)),
            whole(w_out_up.shape),
            whole(w_down.shape),
        ],
        out_specs=[along, along, along, anywhere, anywhere, whole((1, width))],
        out_shape=[
            jax.ShapeDtypeStruct((rows, width), BFLOAT),
            jax.ShapeDtypeStruct((rows, width), SINGLE),
            jax.ShapeDtypeStruct((rows, width), BFLOAT),
            jax.ShapeDtypeStruct(w_out_up.shape, BFLOAT),
            jax.ShapeDtypeStruct(w_down.shape, BFLOAT),
            jax.ShapeDtypeStruct((1, width), SINGLE),
        ],
        scratch_shapes=[
            pltpu.VMEM(w_out_up.shape, SINGLE),
            pltpu.VMEM(w_down.shape, SINGLE),
            pltpu.VMEM((2, width, width), BFLOAT),
            pltpu.SemaphoreType.DMA((2,)),
        ],
        compiler_params=params(),
        cost_estimate=cost(2 * rows * width * (6 * hidden + 3 * width), 14 * rows * width),
    )(tokens, mixture, cotangent, gain.reshape(1, width), w_out_up, w_down)


def unproject_kernel(
    x_ref, gain_ref, dq_ref, dk_ref, dv_ref, dh_ref, w_ref, dx_ref, low_ref, gw_ref, gg_ref, acc
):
    step = pl.program_id(0)
    width = w_ref.shape[0]

    @pl.when(step == 0)
    def _():
        acc[...] = jnp.zeros_like(acc)
        gg_ref[...] = jnp.zeros_like(gg_ref)

    values = x_ref[...].astype(SINGLE)
    gain = gain_ref[...]
    scale = scale_of(values)
    normed = (values * scale * gain).astype(BFLOAT)
    grad = jnp.zeros_like(values)
    for number, ref in enumerate((dq_ref, dk_ref, dv_ref)):
        span = slice(number * width, (number + 1) * width)
        part = ref[...]
        acc[:, span] += tn(normed, part)
        grad = grad + nt(part, w_ref[:, span])
    gg_ref[...] += jnp.sum(grad * values * scale, axis=0, keepdims=True)
    dx = dh_ref[...] + norm_back(values, scale, grad * gain)
    dx_ref[...] = dx
    low_ref[...] = dx.astype(BFLOAT)

    @pl.when(step == pl.num_programs(0) - 1)
    def _():
        gw_ref[...] = acc[...].astype(BFLOAT)


def unproject(tokens, gain, dq, dk, dv, grad_res, w_qkv):
    rows, width = tokens.shape
    block = math.gcd(rows, 256)
    along = pl.BlockSpec((block, width), lambda i: (i, 0))
    return pl.pallas_call(
        unproject_kernel,
        grid=(rows // block,),
        in_specs=[along, whole((1, width)), along, along, along, along, whole(w_qkv.shape)],
        out_specs=[along, along, whole(w_qkv.shape), whole((1, width))],
        out_shape=[
            jax.ShapeDtypeStruct((rows, width), SINGLE),
            jax.ShapeDtypeStruct((rows, width), BFLOAT),
            jax.ShapeDtypeStruct(w_qkv.shape, BFLOAT),
            jax.ShapeDtypeStruct((1, width), SINGLE),
        ],
        scratch_shapes=[pltpu.VMEM(w_qkv.shape, SINGLE)],
        compiler_params=params(),
        cost_estimate=cost(12 * rows * width * width, 18 * rows * width),
    )(tokens, gain.reshape(1, width), dq, dk, dv, grad_res, w_qkv)


def bits_of(count):
    return [1 << place for place in reversed(range(count.bit_length() - 1))]


def axis_bits():
    dp_bits = [("dp", bit) for bit in bits_of(lax.axis_size("dp"))]
    seq_bits = [("seq", bit) for bit in bits_of(lax.axis_size("seq"))]
    return dp_bits, seq_bits


def gather_orders():
    dp_bits, seq_bits = axis_bits()
    far = (len(dp_bits) + 1) // 2
    z_bits, x_bits = dp_bits[:far], dp_bits[far:]
    y_bits, core_bits = seq_bits[:-1], seq_bits[-1:]
    return [z_bits + y_bits + x_bits + core_bits, z_bits + x_bits + y_bits + core_bits]


def swap(values, name, bit):
    count = lax.axis_size(name)
    return lax.ppermute(values, name, [(i, i ^ bit) for i in range(count)])


def is_high(name, bit):
    return (lax.axis_index(name) & bit) != 0


def gather_rows(shard, order):
    dp_bits, seq_bits = axis_bits()
    everything = dp_bits + seq_bits
    done = []
    held = shard
    for item in order:
        other = swap(held, *item)
        done.append(item)
        place = sorted(everything.index(one) for one in done).index(everything.index(item))
        high = is_high(*item)
        held = jnp.where(
            high, jnp.stack([other, held], place), jnp.stack([held, other], place)
        )
    return held.reshape(-1, shard.shape[1])


def scatter_rows(values, order):
    dp_bits, seq_bits = axis_bits()
    left = dp_bits + seq_bits
    rows = values.shape[0] >> len(left)
    held = values.reshape((2,) * len(left) + (rows, values.shape[1]))
    for item in order:
        place = left.index(item)
        mine = is_high(*item).astype(jnp.int32)
        away = lax.dynamic_index_in_dim(held, 1 - mine, place, keepdims=False)
        kept = lax.dynamic_index_in_dim(held, mine, place, keepdims=False)
        other = swap(away, *item)
        held = kept.astype(SINGLE) + other.astype(SINGLE)
        left.remove(item)
        if left:
            held = held.astype(BFLOAT)
    return held


def scatter_columns(values, parts):
    orders = [order[::-1] for order in gather_orders()]
    columns = values.shape[1] // parts
    return jnp.concatenate(
        [
            scatter_rows(values[:, p * columns : (p + 1) * columns], orders[p % len(orders)])
            for p in range(parts)
        ],
        1,
    )


def sum_all(values):
    dp_bits, seq_bits = axis_bits()
    for item in seq_bits[::-1] + dp_bits[::-1]:
        values = values + swap(values, *item)
    return values


def own_document(shard):
    count = lax.axis_size("seq")
    n_docs = shard.shape[0]
    me = lax.axis_index("seq")
    if n_docs >= count:
        per = n_docs // count
        blocks = shard.reshape((count, per) + shard.shape[1:])
        sets, group = count, 1
    else:
        blocks = shard[:, None]
        sets, group = n_docs, count // n_docs
    got = []
    for r in range(sets):
        piece = lax.dynamic_index_in_dim(blocks, (me % sets) ^ r, 0, keepdims=False)
        route = [
            (u * sets + i, (i ^ r) * group + u) for u in range(group) for i in range(sets)
        ]
        if any(a != b for a, b in route):
            piece = lax.ppermute(piece, "seq", route)
        got.append(piece)
    stacked = jnp.stack(got, 0)
    mine = me // group
    ordered = [lax.dynamic_index_in_dim(stacked, mine ^ i, 0, keepdims=False) for i in range(sets)]
    return jnp.concatenate(ordered, 1).reshape(-1, shard.shape[-1])


def spread_document(rows, like):
    count = lax.axis_size("seq")
    n_docs, shard_rows, width = like.shape
    me = lax.axis_index("seq")
    if n_docs >= count:
        per = n_docs // count
        sets, group = count, 1
    else:
        per = 1
        sets, group = n_docs, count // n_docs
    blocks = rows.reshape(per, sets, shard_rows, width)
    mine = me // group
    got = []
    for r in range(sets):
        piece = lax.dynamic_index_in_dim(blocks, mine ^ r, 1, keepdims=False)
        route = [
            ((i ^ r) * group + u, u * sets + i) for u in range(group) for i in range(sets)
        ]
        if any(a != b for a, b in route):
            piece = lax.ppermute(piece, "seq", route)
        got.append(piece)
    stacked = jnp.stack(got, 0)
    ordered = [
        lax.dynamic_index_in_dim(stacked, (me % sets) ^ i, 0, keepdims=False) for i in range(sets)
    ]
    return jnp.concatenate(ordered, 0)


def gather_positions(shard):
    seq_bits = axis_bits()[1]
    done = []
    held = shard
    for item in seq_bits:
        other = swap(held, *item)
        high = is_high(*item)
        place = len(done)
        held = jnp.where(
            high, jnp.stack([other, held], place), jnp.stack([held, other], place)
        )
        done.append(item)
    return held.reshape(-1, shard.shape[1])


class Spot:
    def __init__(self):
        self.dp = lax.axis_index("dp")
        self.seq = lax.axis_index("seq")
        self.core = self.seq % 2
        self.y = self.seq // 2
        self.x = self.dp % 2
        self.z = self.dp // 2

    def partner(self, z=0, x=0, y=0, core=0):
        dp = self.flip(self.z, z) * 2 + self.flip(self.x, x)
        seq = self.flip(self.y, y) * 2 + self.flip(self.core, core)
        return (dp, seq)

    @staticmethod
    def flip(value, bits):
        if bits == 0:
            return value
        if bits == 1:
            return value + 1 - 2 * (value % 2)
        if bits == 2:
            return (value + 2) % 4
        return 3 - value

    def chip(self, z=0, x=0, y=0):
        return (self.flip(self.z, z) * 2 + self.flip(self.x, x)) * 2 + self.flip(self.y, y)


def send(source, target, sems, number, device):
    return pltpu.make_async_remote_copy(
        src_ref=source,
        dst_ref=target,
        send_sem=sems.at[0, number],
        recv_sem=sems.at[1, number],
        device_id=device,
        device_id_type=pl.DeviceIdType.MESH,
    )


def greet(partners):
    barrier = pltpu.get_barrier_semaphore()
    for device in partners:
        pl.semaphore_signal(barrier, inc=1, device_id=device, device_id_type=pl.DeviceIdType.MESH)
    pl.semaphore_wait(barrier, len(partners))


COPIES = 17
GATHER_COPIES = 24


class Gather:
    def __init__(self, spot, shard, whole_ref, theirs, block, sems, local):
        self.spot, self.shard, self.whole = spot, shard, whole_ref
        self.theirs, self.block, self.sems, self.local = theirs, block, sems, local
        self.rows, self.half = block.shape

    def columns(self, core):
        return pl.ds(pl.multiple_of(core * self.half, 128), self.half)

    def area(self, count=1, **bits):
        chip = self.spot.chip(**bits)
        if count == 2:
            chip = chip - chip % 2
        row = pl.multiple_of(chip * self.rows, 16)
        return self.whole.at[pl.ds(row, count * self.rows), self.columns(self.spot.core)]

    def copy(self, number):
        spot = self.spot
        if number == 0:
            source, target = self.shard.at[:, self.columns(1 - spot.core)], self.theirs
            device = spot.partner(core=1)
        elif number < 4:
            source, target, device = self.block, self.area(), spot.partner(z=number)
        elif number < 8:
            target, device = self.area(z=number - 4), spot.partner(y=1)
            source = self.block if number == 4 else target
        elif number < 16:
            target = self.area(z=(number - 8) % 4, y=(number - 8) // 4)
            source, device = self.block if number == 8 else target, spot.partner(x=1)
        else:
            source = target = self.area(2, z=number % 4, x=(number - 16) // 4)
            device = spot.partner(core=1)
        return send(source, target, self.sems, number, device)

    def here(self):
        return pltpu.make_async_copy(self.block, self.area(), self.local)

    def join_end(self):
        self.copy(0).wait_recv()
        part = self.rows // 2
        low = self.spot.core == 0
        mine = self.shard[:, self.columns(self.spot.core)].astype(SINGLE)
        theirs = self.theirs[...].astype(SINGLE)
        self.block[:part, :] = jnp.where(low, mine, theirs).astype(BFLOAT)
        self.block[part:, :] = jnp.where(low, theirs, mine).astype(BFLOAT)
        self.here().start()

    def start(self, *numbers):
        for number in numbers:
            self.copy(number).start()

    def z_got(self, k):
        self.copy(k).wait_recv()
        self.start(4 + k, 8 + k)

    def y_got(self, k):
        self.copy(4 + k).wait_recv()
        if k == 0:
            self.here().wait()
        self.start(12 + k, 16 + k)

    def x_got(self, k):
        self.copy(8 + k).wait_recv()
        self.copy(12 + k).wait_recv()
        self.start(20 + k)

    def finish(self):
        for number in range(16, GATHER_COPIES):
            self.copy(number).wait_recv()
        for number in range(GATHER_COPIES):
            self.copy(number).wait_send()


class PlaneGather(Gather):
    def copy(self, number):
        spot = self.spot
        if number == 0:
            return Gather.copy(self, 0)
        if number == 1:
            source, target, device = self.block, self.area(), spot.partner(y=1)
        elif number == 2:
            source, target, device = self.block, self.area(), spot.partner(x=1)
        elif number == 3:
            source = target = self.area(y=1)
            device = spot.partner(x=1)
        elif number < 10:
            source = target = self.area(2, x=(number - 4) // 3)
            device = spot.partner(z=(number - 4) % 3 + 1)
        else:
            kind = number - 10
            z, x = (0, kind) if kind < 2 else ((kind - 2) % 3 + 1, (kind - 2) // 3)
            source = target = self.area(2, z=z, x=x)
            device = spot.partner(core=1)
        return send(source, target, self.sems, number, device)

    def y_got(self):
        self.copy(1).wait_recv()
        self.here().wait()
        self.start(3, 4, 5, 6, 10)

    def x_got(self):
        self.copy(2).wait_recv()
        self.copy(3).wait_recv()
        self.start(7, 8, 9, 11)

    def z_got(self, x):
        for k in range(3):
            self.copy(4 + 3 * x + k).wait_recv()
            self.start(12 + 3 * x + k)

    def finish(self):
        for number in range(10, 18):
            self.copy(number).wait_recv()
        for number in range(18):
            self.copy(number).wait_send()


class Move:
    PARTNERS = ((1, 0), (1, 1), (0, 1))

    def __init__(self, spot, source, target, own_target, sems, local):
        self.spot, self.source, self.target = spot, source, target
        self.own_target, self.sems, self.local = own_target, sems, local

    def own(self):
        return pltpu.make_async_copy(
            self.source(self.spot.seq), self.own_target(self.spot.seq), self.local
        )

    def copy(self, number):
        y, core = self.PARTNERS[number]
        device = self.spot.partner(y=y, core=core)
        return send(self.source(device[1]), self.target(self.spot.seq), self.sems, number, device)

    def start(self):
        self.own().start()
        for number in range(3):
            self.copy(number).start()

    def finish(self):
        self.own().wait()
        for number in range(3):
            self.copy(number).wait()


def all_partners(spot):
    return [
        spot.partner(core=1),
        spot.partner(z=1),
        spot.partner(z=2),
        spot.partner(z=3),
        spot.partner(x=1),
        spot.partner(y=1),
        spot.partner(y=1, core=1),
    ]


def row_block(ref, rows):
    return lambda number: ref.at[pl.ds(pl.multiple_of(number * rows, 16), rows), :]


def front_kernel(
    docs_ref,
    queries_ref,
    doc_cot_ref,
    query_cot_ref,
    q_shard,
    kv_shard,
    out_shard,
    up_shard,
    down_shard,
    bucket_shard,
    gain_ref,
    table_ref,
    small_bucket_ref,
    tokens_out,
    cots_out,
    w_out,
    ou_out,
    down_out,
    bucket_out,
    qkv_out,
    mix_ref,
    prob_ref,
    query_prob_ref,
    query_bucket_ref,
    x_v,
    w_v,
    qkv_v,
    bucket_v,
    bucket_in,
    qkv_own,
    qkv_theirs,
    qkv_block,
    ou_own,
    ou_theirs,
    ou_block,
    down_own,
    down_theirs,
    down_block,
    gather_sems,
    move_sems,
    local,
):
    step = pl.program_id(0)
    last = pl.num_programs(0) - 1
    spot = Spot()
    n_docs, shard_rows, width = docs_ref.shape
    doc_rows = n_docs * shard_rows
    query_rows = queries_ref.shape[0]
    heads = prob_ref.shape[0]
    head_dim = width // heads
    pairs = heads // 2
    block = prob_ref.shape[1]

    gathers = []
    for number, parts in enumerate(
        (
            (qkv_own, w_v, qkv_theirs, qkv_block),
            (ou_own, ou_out, ou_theirs, ou_block),
            (down_own, down_out, down_theirs, down_block),
        )
    ):
        kind = PlaneGather if number == 2 else Gather
        gathers.append(kind(spot, *parts, gather_sems.at[number], local.at[number]))
    g_qkv, g_ou, g_down = gathers
    token_move = Move(
        spot,
        lambda number: docs_ref.at[number],
        row_block(x_v, shard_rows),
        row_block(x_v, shard_rows),
        move_sems.at[0],
        local.at[3],
    )
    cot_move = Move(
        spot,
        lambda number: doc_cot_ref.at[number],
        row_block(cots_out, shard_rows),
        row_block(cots_out, shard_rows),
        move_sems.at[1],
        local.at[4],
    )
    query_load = pltpu.make_async_copy(
        queries_ref, x_v.at[pl.ds(doc_rows, query_rows), :], local.at[5]
    )
    cot_copy = pltpu.make_async_copy(
        query_cot_ref, cots_out.at[pl.ds(doc_rows, query_rows), :], local.at[6]
    )
    bucket_rows = row_block(bucket_v, shard_rows)
    bucket_load = pltpu.make_async_copy(bucket_shard, bucket_in, local.at[7])
    near = bucket_rows(spot.seq)
    far = bucket_rows(spot.partner(y=1)[1])
    bucket_y = send(near, near, move_sems.at[2], 0, spot.partner(y=1))
    bucket_near = send(near, near, move_sems.at[2], 1, spot.partner(core=1))
    bucket_far = send(far, far, move_sems.at[2], 2, spot.partner(core=1))
    saves = [
        pltpu.make_async_copy(x_v, tokens_out, local.at[8]),
        pltpu.make_async_copy(w_v, w_out, local.at[9]),
        pltpu.make_async_copy(qkv_v, qkv_out, local.at[10]),
        pltpu.make_async_copy(bucket_v, bucket_out, local.at[11]),
    ]
    loads = [
        pltpu.make_async_copy(q_shard, qkv_own.at[:, pl.ds(0, width)], local.at[12]),
        pltpu.make_async_copy(kv_shard, qkv_own.at[:, pl.ds(width, 2 * width)], local.at[13]),
        pltpu.make_async_copy(out_shard, ou_own.at[:, pl.ds(0, width)], local.at[14]),
        pltpu.make_async_copy(
            up_shard, ou_own.at[:, pl.ds(width, up_shard.shape[1])], local.at[15]
        ),
        pltpu.make_async_copy(down_shard, down_own, local.at[16]),
    ]

    @pl.when(step == 0)
    def _():
        for load in loads:
            load.start()
        bucket_load.start()
        query_load.start()
        token_move.own().start()
        greet(all_partners(spot))
        token_move.copy(0).start()
        for load in loads[:2]:
            load.wait()
        g_qkv.start(0)
        for load in loads[2:]:
            load.wait()
        g_ou.start(0)
        g_down.start(0)
        token_move.copy(2).start()
        g_qkv.join_end()
        g_qkv.start(1, 2, 3, 4, 8)
        g_ou.join_end()
        g_down.join_end()
        g_down.start(1, 2)
        bucket_load.wait()
        bucket_v[pl.ds(pl.multiple_of(spot.seq * shard_rows, 16), shard_rows), :] = bucket_in[
            ...
        ].astype(jnp.int16)
        size = small_bucket_ref.shape[0]
        shape = (128, size)
        picks = (
            lax.broadcasted_iota(jnp.int32, shape, 0) % size
            == lax.broadcasted_iota(jnp.int32, shape, 1)
        )
        picks = jnp.where(picks, 1.0, 0.0).astype(BFLOAT)
        numbers = small_bucket_ref[...].astype(SINGLE).astype(BFLOAT)
        spread = nt(nn(picks, numbers).astype(BFLOAT), picks).astype(jnp.int32)
        square = (128, 128)
        same = (
            lax.broadcasted_iota(jnp.int32, square, 0) // size
            == lax.broadcasted_iota(jnp.int32, square, 1) // size
        )
        query_bucket_ref[...] = jnp.where(same, spread, table_ref.shape[1] - 1)
        for k in (1, 2, 3):
            g_qkv.z_got(k)
        g_ou.start(1, 2, 3)
        token_move.copy(1).start()
        bucket_y.start()
        bucket_near.start()
        g_ou.start(4)
        for k in (0, 1, 2, 3):
            g_qkv.y_got(k)
        g_ou.start(8)
        g_down.y_got()
        g_down.x_got()
        for k in (0, 1, 2, 3):
            g_qkv.x_got(k)
        query_load.wait()
        g_qkv.finish()
        saves[1].start()
        token_move.finish()
        saves[0].start()

        def project_block(number, carry):
            span = pl.ds(pl.multiple_of(number * block, 16), block)
            values = x_v[span, :].astype(SINGLE)
            normed = (values * scale_of(values) * gain_ref[...][None, :]).astype(BFLOAT)
            for part in range(3):
                lanes = slice(part * width, (part + 1) * width)
                qkv_v[span, lanes] = nn(normed, w_v[:, lanes]).astype(BFLOAT)
            return carry

        blocks = (doc_rows + query_rows) // block
        third = blocks // 3
        lax.fori_loop(0, third, project_block, 0)
        g_ou.z_got(1)
        lax.fori_loop(third, 2 * third, project_block, 0)
        g_ou.z_got(2)
        lax.fori_loop(2 * third, blocks, project_block, 0)
        g_ou.z_got(3)
        saves[2].start()
        cot_move.start()
        cot_copy.start()
        bucket_y.wait_recv()
        bucket_far.start()

        def query_step(number, carry):
            span = pl.ds(pl.multiple_of(doc_rows + number * 128, 16), 128)
            softs, mixed = query_block(
                qkv_v[span, :width],
                qkv_v[span, width : 2 * width],
                qkv_v[span, 2 * width :],
                table_ref,
                query_bucket_ref[...],
                heads,
            )
            mix_ref[span, :] = mixed
            for head, soft in enumerate(softs):
                query_prob_ref[head, pl.ds(pl.multiple_of(number * 128, 16), 128), :] = soft
            return carry

        lax.fori_loop(0, query_rows // 128, query_step, 0)
        g_ou.y_got(0)
        bucket_near.wait()
        bucket_far.wait()
        bucket_y.wait_send()
        saves[3].start()

    def tick(when, name, k):
        @pl.when(step == when)
        def _():
            getattr(g_ou, name)(k)

    tick(1, "y_got", 1)
    tick(2, "y_got", 2)
    tick(2, "y_got", 3)
    tick(3, "x_got", 0)
    tick(4, "x_got", 1)
    tick(4, "x_got", 2)

    @pl.when(step == last)
    def _():
        g_down.z_got(0)

    @pl.when(step > 0)
    def _():
        span = pl.ds(pl.multiple_of((step - 1) * block, 16), block)

        def pair(number, carry):
            lanes = pair_lanes(number, head_dim)
            mix_ref[span, lanes] = attend_pair(
                qkv_v[span, lanes],
                qkv_v[:doc_rows, pair_lanes(number, head_dim, width)],
                qkv_v[:doc_rows, pair_lanes(number, head_dim, 2 * width)],
                table_ref,
                bucket_v,
                pl.multiple_of((step - 1) * block, 16),
                prob_ref,
                number,
                head_dim,
            )
            return carry

        lax.fori_loop(0, pairs, pair, 0, unroll=True)

    @pl.when(step == last)
    def _():
        g_ou.x_got(3)
        g_down.z_got(1)
        g_ou.finish()
        g_down.finish()
        cot_move.finish()
        cot_copy.wait()
        for save in saves:
            save.wait()


def gather_scratch(rows, columns):
    return [
        pltpu.VMEM((rows, columns), BFLOAT),
        pltpu.VMEM((rows, columns // 2), BFLOAT),
        pltpu.VMEM((2 * rows, columns // 2), BFLOAT),
    ]


def front(docs, queries, doc_cot, query_cot, weights, buckets, gain, table, query_buckets, heads):
    n_docs, shard_rows, width = docs.shape
    doc_rows = n_docs * shard_rows
    query_rows = queries.shape[0]
    rows = doc_rows + query_rows
    keys = buckets.shape[1]
    block = 256
    steps = doc_rows // block
    anywhere = pl.BlockSpec(memory_space=pl.ANY)
    w_q, w_kv, w_out, w_up, w_down = (weight.shape for weight in weights)
    shards = [
        (w_q[0], w_q[1] + w_kv[1]),
        (w_out[0], w_out[1] + w_up[1]),
        w_down,
    ]
    scratch = []
    for shard in shards:
        scratch += gather_scratch(*shard)
    return pl.pallas_call(
        front_kernel,
        grid=(steps + 1,),
        in_specs=[anywhere] * 10 + [whole((width,)), whole(table.shape), whole(query_buckets.shape)],
        out_specs=[anywhere] * 7
        + [
            whole((rows, width)),
            pl.BlockSpec((heads, block, keys), lambda i: (0, jnp.maximum(i - 1, 0), 0)),
            whole((heads, query_rows, 128)),
            whole((128, 128)),
        ],
        out_shape=[
            jax.ShapeDtypeStruct((rows, width), BFLOAT),
            jax.ShapeDtypeStruct((rows, width), BFLOAT),
            *[jax.ShapeDtypeStruct((shard[0] * 32, shard[1]), BFLOAT) for shard in shards],
            jax.ShapeDtypeStruct((keys, keys), jnp.int16),
            jax.ShapeDtypeStruct((rows, 3 * width), BFLOAT),
            jax.ShapeDtypeStruct((rows, width), BFLOAT),
            jax.ShapeDtypeStruct((heads, doc_rows, keys), BFLOAT),
            jax.ShapeDtypeStruct((heads, query_rows, 128), BFLOAT),
            jax.ShapeDtypeStruct((128, 128), jnp.int32),
        ],
        scratch_shapes=[
            pltpu.VMEM((rows, width), BFLOAT),
            pltpu.VMEM((width, 3 * width), BFLOAT),
            pltpu.VMEM((rows, 3 * width), BFLOAT),
            pltpu.VMEM((keys, keys), jnp.int16),
            pltpu.VMEM(buckets.shape, jnp.int32),
            *scratch,
            pltpu.SemaphoreType.DMA((3, 2, GATHER_COPIES)),
            pltpu.SemaphoreType.DMA((3, 2, 3)),
            pltpu.SemaphoreType.DMA((20,)),
        ],
        compiler_params=pltpu.CompilerParams(
            collective_id=0, has_side_effects=True, vmem_limit_bytes=VMEM_LIMIT
        ),
        cost_estimate=cost(6 * rows * width * width, 100 << 20),
    )(docs, queries, doc_cot, query_cot, *weights, buckets, gain, table, query_buckets)


class Scatter:
    Z_ORDER = (3, 2, 1, 0)

    def __init__(self, spot, away, buffers, sems):
        self.spot, self.away, self.sems = spot, away, sems
        self.held, self.core_in, self.x_in, self.y_in, self.z_in, self.tail, self.tail_in = buffers
        self.half = self.held.shape[1]
        self.rows = self.held.shape[0] // 16

    def span(self, **bits):
        return pl.ds(pl.multiple_of(self.spot.chip(**bits) * self.rows, 16), self.rows)

    def slot(self, number):
        return pl.ds(number * self.rows, self.rows)

    def copy(self, number):
        spot = self.spot
        if number == 0:
            source, target, device = self.away, self.core_in, spot.partner(core=1)
        elif number < 9:
            index = number - 1
            source = self.held.at[self.span(z=self.Z_ORDER[index // 2], x=1, y=1 - index % 2), :]
            target, device = self.x_in.at[self.slot(index), :], spot.partner(x=1)
        elif number < 13:
            index = number - 9
            source = self.held.at[self.span(z=self.Z_ORDER[index], y=1), :]
            target, device = self.y_in.at[self.slot(index), :], spot.partner(y=1)
        elif number < 16:
            index = number - 13
            source = self.held.at[self.span(z=self.Z_ORDER[index]), :]
            target = self.z_in.at[self.slot(index), :]
            device = spot.partner(z=self.Z_ORDER[index])
        else:
            part = self.rows // 2
            theirs = pl.ds(pl.multiple_of((1 - spot.core) * part, 8), part)
            source, target, device = self.tail.at[theirs, :], self.tail_in, spot.partner(core=1)
        return send(source, target, self.sems, number, device)

    def add(self, span, others):
        total = self.held[span, :].astype(SINGLE) + self.core_in[span, :].astype(SINGLE)
        for ref, place in others:
            total = total + ref[place, :].astype(SINGLE)
        return total

    def core_end(self):
        self.copy(0).wait_recv()

    def x_step(self, index):
        span = self.span(z=self.Z_ORDER[index // 2], x=1, y=1 - index % 2)
        self.held[span, :] = self.add(span, []).astype(BFLOAT)
        self.copy(1 + index).start()

    def y_step(self, index):
        self.copy(1 + 2 * index).wait_recv()
        span = self.span(z=self.Z_ORDER[index], y=1)
        total = self.add(span, [(self.x_in, self.slot(2 * index))])
        self.held[span, :] = total.astype(BFLOAT)
        self.copy(9 + index).start()

    def here(self, index):
        self.copy(2 + 2 * index).wait_recv()
        self.copy(9 + index).wait_recv()
        span = self.span(z=self.Z_ORDER[index])
        others = [(self.x_in, self.slot(2 * index + 1)), (self.y_in, self.slot(index))]
        return span, self.add(span, others)

    def z_step(self, index):
        span, total = self.here(index)
        self.held[span, :] = total.astype(BFLOAT)
        self.copy(13 + index).start()

    def tail_start(self):
        _, total = self.here(3)
        for index in range(3):
            self.copy(13 + index).wait_recv()
            total = total + self.z_in[self.slot(index), :].astype(SINGLE)
        self.tail[...] = total
        self.copy(16).start()

    def finish(self):
        part = self.rows // 2
        low = self.spot.core == 0
        mine = jnp.where(low, self.tail[:part, :], self.tail[part:, :])
        self.copy(16).wait_recv()
        other = self.tail_in[...]
        for number in range(COPIES):
            self.copy(number).wait_send()
        return jnp.where(low, mine, other), jnp.where(low, other, mine)


def scatter_scratch(rows, columns):
    half, part = columns // 2, rows // 16
    return [
        pltpu.VMEM((rows, half), BFLOAT),
        pltpu.VMEM((rows, half), BFLOAT),
        pltpu.VMEM((8 * part, half), BFLOAT),
        pltpu.VMEM((4 * part, half), BFLOAT),
        pltpu.VMEM((3 * part, half), BFLOAT),
        pltpu.VMEM((part, half), SINGLE),
        pltpu.VMEM((part // 2, half), SINGLE),
    ]


def half_of(ref, core):
    half = ref.shape[1] // 2
    return ref.at[:, pl.ds(pl.multiple_of(core * half, 128), half)]


def middle_kernel(
    x_ref,
    mix_ref,
    dy_ref,
    gain_ref,
    wo_ref,
    wu_ref,
    wd_ref,
    y_out,
    dh_out,
    da_out,
    rest_ref,
    down_ref,
    near_ref,
    gg_ref,
    h1,
    n2,
    y_acc,
    act_v,
    du_v,
    dh_ref,
    *rest,
):
    fulls, downs, rest = rest[0], rest[1], rest[2:]
    step = pl.program_id(0)
    last = pl.num_programs(0) - 1
    spot = Spot()
    rows, width = x_ref.shape
    gain = gain_ref[...][None, :]
    block = 512 if rows % 512 == 0 else 256
    spans = [slice(start, start + block) for start in range(0, rows, block)]
    sems, local = rest[-2:]
    pieces = []
    for number in range(3):
        full, core = fulls.at[number], spot.core
        buffers = [half_of(full, core), *rest[6 * number : 6 * number + 6]]
        pieces.append(Scatter(spot, half_of(full, 1 - core), buffers, sems.at[number]))

    save_out = pltpu.make_async_copy(downs.at[0], rest_ref.at[:, pl.ds(0, width)], local.at[0])
    save_up = pltpu.make_async_copy(
        fulls.at[3], rest_ref.at[:, pl.ds(width, width)], local.at[3]
    )

    def save_down(chunk):
        target = down_ref.at[pl.ds(chunk * width, width), :]
        return pltpu.make_async_copy(downs.at[chunk % 2], target, local.at[1 + chunk % 2])

    leaving = [
        pltpu.make_async_copy(du_v, y_out, local.at[4]),
        pltpu.make_async_copy(dh_ref, dh_out, local.at[5]),
        pltpu.make_async_copy(n2, da_out, local.at[6]),
    ]

    def at(when, chunk, action, also=True):
        piece = pieces[chunk]

        @pl.when((step == when) & also)
        def _():
            if action == "x":
                piece.core_end()
                for index in range(8):
                    piece.x_step(index)
            elif action == "y":
                for index in range(4):
                    piece.y_step(index)
            elif action == "z":
                for index in range(3):
                    piece.z_step(index)
            else:
                piece.tail_start()

    @pl.when(step == 0)
    def _():
        greet(all_partners(spot))
        for span in spans:
            residual = x_ref[span, :].astype(SINGLE) + nn(mix_ref[span, :], wo_ref[...])
            h1[span, :] = residual
            y_acc[span, :] = residual
            n2[span, :] = (residual * scale_of(residual) * gain).astype(BFLOAT)
            dh_ref[span, :] = jnp.zeros_like(residual)

    def part(number, carry):
        then = number == 1
        for chunk in range(3):
            at(chunk + 1, chunk, "x", also=then)
        for chunk in range(2):
            at(chunk + 2, chunk, "tail", also=then)
        span = pl.ds(pl.multiple_of(number * block, 16), block)
        pre = nn(n2[span, :], wu_ref[...])
        grad_hidden = nt(dy_ref[span, :], wd_ref[...])
        square = pre * pre
        tanh = jnp.tanh(pre * (GELU_A + (GELU_A * GELU_B) * square))
        half = 0.5 + 0.5 * tanh
        act = pre * half
        slope = half + act * (1.0 - tanh) * (GELU_A + (3.0 * GELU_A * GELU_B) * square)
        act_low = act.astype(BFLOAT)
        grad_pre = (grad_hidden * slope).astype(BFLOAT)
        act_v[span, :] = act_low
        du_v[span, :] = grad_pre
        y_acc[span, :] += nn(act_low, wd_ref[...])
        dh_ref[span, :] += nt(grad_pre, wu_ref[...])
        return carry

    lax.fori_loop(0, rows // block, part, 0)
    for chunk in range(3):
        at(chunk + 1, chunk, "y")

    for chunk in (2, 3):

        @pl.when(step == chunk)
        def _():
            save_down(chunk - 2).wait()

    fulls[step] = tn(n2[...], du_v[...]).astype(BFLOAT)
    downs[step % 2] = tn(act_v[...], dy_ref[...]).astype(BFLOAT)
    for chunk in range(4):

        @pl.when(step == chunk)
        def _():
            save_down(chunk).start()
            if chunk < 3:
                pieces[chunk].copy(0).start()

    for chunk in range(3):
        at(chunk + 1, chunk, "z")

    @pl.when(step == last)
    def _():
        save_up.start()
        total = jnp.zeros_like(gain)
        for span in spans:
            du_v[span, :] = y_acc[span, :].astype(BFLOAT)
        leaving[0].start()
        for span in spans:
            residual = h1[span, :]
            scale = scale_of(residual)
            grad_second = dh_ref[span, :]
            total = total + jnp.sum(grad_second * residual * scale, axis=0, keepdims=True)
            grad_res = dy_ref[span, :].astype(SINGLE) + norm_back(
                residual, scale, grad_second * gain
            )
            dh_ref[span, :] = grad_res
            grad_low = grad_res.astype(BFLOAT)
            act_v[span, :] = grad_low
            n2[span, :] = nt(grad_low, wo_ref[...]).astype(BFLOAT)
        gg_ref[...] = total
        leaving[1].start()
        leaving[2].start()
        save_down(2).wait()
        downs[0] = tn(mix_ref[...], act_v[...]).astype(BFLOAT)
        save_out.start()
        pieces[2].tail_start()
        for number, piece in enumerate(pieces):
            left, right = piece.finish()
            base = number * width
            near_ref[:, base : base + width // 2] = left
            near_ref[:, base + width // 2 : base + width] = right
        save_out.wait()
        save_up.wait()
        save_down(3).wait()
        for copy in leaving:
            copy.wait()


def middle(tokens, mixture, cotangent, gain, w_out_up, w_down):
    rows, width = tokens.shape
    hidden = w_down.shape[0]
    chunks = hidden // width
    anywhere = pl.BlockSpec(memory_space=pl.ANY)
    square = (width, width)
    scratch = []
    for _ in range(3):
        scratch += scatter_scratch(*square)[1:]
    return pl.pallas_call(
        middle_kernel,
        grid=(chunks,),
        in_specs=[
            whole((rows, width)),
            whole((rows, width)),
            whole((rows, width)),
            whole((width,)),
            whole(square),
            pl.BlockSpec(square, lambda i: (0, 1 + i)),
            pl.BlockSpec(square, lambda i: (i, 0)),
        ],
        out_specs=[
            anywhere,
            anywhere,
            anywhere,
            anywhere,
            anywhere,
            whole((width // 32, 3 * width)),
            whole((1, width)),
        ],
        out_shape=[
            jax.ShapeDtypeStruct((rows, width), BFLOAT),
            jax.ShapeDtypeStruct((rows, width), SINGLE),
            jax.ShapeDtypeStruct((rows, width), BFLOAT),
            jax.ShapeDtypeStruct((width, 2 * width), BFLOAT),
            jax.ShapeDtypeStruct((hidden, width), BFLOAT),
            jax.ShapeDtypeStruct((width // 32, 3 * width), SINGLE),
            jax.ShapeDtypeStruct((1, width), SINGLE),
        ],
        scratch_shapes=[
            pltpu.VMEM((rows, width), SINGLE),
            pltpu.VMEM((rows, width), BFLOAT),
            pltpu.VMEM((rows, width), SINGLE),
            pltpu.VMEM((rows, width), BFLOAT),
            pltpu.VMEM((rows, width), BFLOAT),
            pltpu.VMEM((rows, width), SINGLE),
            pltpu.VMEM((chunks, *square), BFLOAT),
            pltpu.VMEM((2, *square), BFLOAT),
            *scratch,
            pltpu.SemaphoreType.DMA((3, 2, COPIES)),
            pltpu.SemaphoreType.DMA((7,)),
        ],
        compiler_params=pltpu.CompilerParams(
            collective_id=3, has_side_effects=True, vmem_limit_bytes=VMEM_LIMIT
        ),
        cost_estimate=cost(2 * rows * width * (6 * hidden + 3 * width), 100 << 20),
    )(tokens, mixture, cotangent, gain, w_out_up, w_out_up, w_down)


def back_kernel(
    labels,
    doc_steps,
    q_ref,
    k_ref,
    v_ref,
    query_k_ref,
    query_v_ref,
    da_ref,
    mix_ref,
    prob_ref,
    query_prob_ref,
    query_bucket_ref,
    grad_ref,
    grad_down_ref,
    y_ref,
    dq_ref,
    dkv_ref,
    ds_ref,
    sums_ref,
    shard_ref,
    down_ref,
    docs_ref,
    dk_acc,
    dv_acc,
    ds_keep,
    *rest,
):
    sems, move_sems, local = rest[14:]
    step = pl.program_id(0)
    last = pl.num_programs(0) - 1
    spot = Spot()
    rows, width = q_ref.shape
    pairs = prob_ref.shape[0] // 2
    keys = k_ref.shape[0]
    heads = query_prob_ref.shape[0]
    head_dim = width // heads
    grads, shards = (grad_ref, grad_down_ref), (shard_ref, down_ref)
    scatters = [
        Scatter(spot, half_of(grad, 1 - spot.core), rest[7 * i : 7 * i + 7], sems.at[i])
        for i, grad in enumerate(grads)
    ]
    loads = [
        pltpu.make_async_copy(half_of(grad, spot.core), scatter.held, local.at[i])
        for i, (grad, scatter) in enumerate(zip(grads, scatters))
    ]
    move = Move(
        spot,
        row_block(y_ref, docs_ref.shape[1]),
        lambda number: docs_ref.at[number],
        lambda number: docs_ref.at[number],
        move_sems,
        local.at[2],
    )

    @pl.when(step == 0)
    def _():
        greet(all_partners(spot))
        for scatter, load in zip(scatters, loads):
            scatter.copy(0).start()
            load.start()
        move.start()
        dk_acc[...] = jnp.zeros_like(dk_acc)
        dv_acc[...] = jnp.zeros_like(dv_acc)
        ds_keep[...] = jnp.zeros_like(ds_keep)

    @pl.when(step == 1)
    def _():
        for scatter, load in zip(scatters, loads):
            load.wait()
            scatter.core_end()
        for index in range(8):
            for scatter in scatters:
                scatter.x_step(index)

    def at(when, *actions):
        @pl.when(step == when)
        def _():
            for name, index in actions:
                for scatter in scatters:
                    getattr(scatter, name)(index)

    at(3, ("y_step", 0))
    at(5, ("z_step", 0), ("y_step", 1))
    at(7, ("z_step", 1), ("y_step", 2))
    at(8, ("z_step", 2), ("y_step", 3))

    @pl.when(step == last)
    def _():
        for scatter in scatters:
            scatter.tail_start()

    @pl.when(step < doc_steps)
    def _():
        def pair(number, carry):
            spread = (step % 2) * pairs + number
            lanes = pair_lanes(spread, head_dim)
            dq, dk, dv, kept = attend_back(
                q_ref[:, lanes],
                k_ref[:, lanes],
                v_ref[:, lanes],
                da_ref[:, lanes],
                mix_ref[:, lanes],
                [prob_ref[2 * number], prob_ref[2 * number + 1]],
                head_dim,
            )
            ds_ref[2 * number] = kept[0]
            ds_ref[2 * number + 1] = kept[1]
            dq_ref[:, lanes] = dq.astype(BFLOAT)
            dk_acc[:, lanes] += dk
            dv_acc[:, lanes] += dv
            return carry

        lax.fori_loop(0, pairs, pair, 0, unroll=True)

    @pl.when(step == doc_steps - 1)
    def _():
        dkv_ref[:keys, :width] = dk_acc[...].astype(BFLOAT)
        dkv_ref[:keys, width:] = dv_acc[...].astype(BFLOAT)

    @pl.when(step >= doc_steps)
    def _():
        def part(number, carry):
            span = pl.ds(pl.multiple_of(number * 128, 128), 128)
            place = pl.ds(pl.multiple_of(keys + (step - doc_steps) * rows + number * 128, 16), 128)
            dq, dk, dv, kept = query_back_block(
                q_ref[span, :],
                query_k_ref[span, :],
                query_v_ref[span, :],
                da_ref[span, :],
                mix_ref[span, :],
                [query_prob_ref[head, span, :] for head in range(heads)],
                head_dim,
            )
            for head in range(heads):
                ds_keep[head] += kept[head].astype(SINGLE)
            for pair in range(heads // 2):
                lanes = slice(pair * 2 * head_dim, (pair + 1) * 2 * head_dim)
                dq_ref[span, lanes] = dq[pair]
                dkv_ref[place, lanes] = dk[pair]
                dkv_ref[place, width + lanes.start : width + lanes.stop] = dv[pair]
            return carry

        lax.fori_loop(0, rows // 128, part, 0)

    @pl.when(step == last)
    def _():
        total = jnp.zeros_like(sums_ref)
        for index in range(8):
            some = slice(index * 16, (index + 1) * 16)
            terms = ds_keep[:, some, :].reshape(heads * 16, 128)
            high = terms.astype(BFLOAT)
            low = (terms - high.astype(SINGLE)).astype(BFLOAT)
            onehot = bucket_onehot(query_bucket_ref[some, :], labels)
            total = total + nt(onehot, high) + nt(onehot, low)
        sums_ref[...] = total

    @pl.when(step == last)
    def _():
        for scatter, shard in zip(scatters, shards):
            left, right = scatter.finish()
            shard[:, : scatter.half] = left
            shard[:, scatter.half :] = right
        move.finish()


def back(qkv, da_rows, mixture, probs, query_probs, query_buckets, grads, outputs, n_docs, labels):
    rows, width = da_rows.shape
    heads, doc_rows, keys = probs.shape
    block = 256
    doc_steps = 2 * doc_rows // block
    doc_blocks = doc_rows // block
    steps = doc_steps + (rows - doc_rows) // block
    half = heads // 2

    def row(i):
        return jnp.where(i < doc_steps, i // 2, i - doc_steps + doc_blocks)

    def doc(i):
        clipped = jnp.minimum(i, doc_steps - 1)
        return (clipped % 2, clipped // 2, 0)

    def query(i):
        return jnp.maximum(i, doc_steps) - doc_steps

    anywhere = pl.BlockSpec(memory_space=pl.ANY)
    along = pl.BlockSpec((block, width), lambda i: (row(i), 0))
    once = pl.Buffered(1)
    return pl.pallas_call(
        functools.partial(back_kernel, labels, doc_steps),
        grid=(steps,),
        in_specs=[
            along,
            pl.BlockSpec((keys, width), lambda i: (0, 1), pipeline_mode=once),
            pl.BlockSpec((keys, width), lambda i: (0, 2), pipeline_mode=once),
            pl.BlockSpec((block, width), lambda i: (query(i) + doc_blocks, 1)),
            pl.BlockSpec((block, width), lambda i: (query(i) + doc_blocks, 2)),
            along,
            along,
            pl.BlockSpec((half, block, keys), doc),
            pl.BlockSpec((heads, block, 128), lambda i: (0, query(i), 0)),
            whole(query_buckets.shape),
            anywhere,
            anywhere,
            anywhere,
        ],
        out_specs=[
            along,
            whole((rows, 2 * width)),
            pl.BlockSpec((half, block, keys), doc),
            whole((16 * labels, heads * 16)),
            *[whole((grad.shape[0] // 32, grad.shape[1])) for grad in grads],
            anywhere,
        ],
        out_shape=[
            jax.ShapeDtypeStruct((rows, width), BFLOAT),
            jax.ShapeDtypeStruct((rows, 2 * width), BFLOAT),
            jax.ShapeDtypeStruct(probs.shape, BFLOAT),
            jax.ShapeDtypeStruct((16 * labels, heads * 16), SINGLE),
            *[
                jax.ShapeDtypeStruct((grad.shape[0] // 32, grad.shape[1]), SINGLE)
                for grad in grads
            ],
            jax.ShapeDtypeStruct((n_docs, doc_rows // n_docs, width), BFLOAT),
        ],
        scratch_shapes=[
            pltpu.VMEM((keys, width), SINGLE),
            pltpu.VMEM((keys, width), SINGLE),
            pltpu.VMEM((heads, 128, 128), SINGLE),
            *scatter_scratch(*grads[0].shape),
            *scatter_scratch(*grads[1].shape),
            pltpu.SemaphoreType.DMA((2, 2, COPIES)),
            pltpu.SemaphoreType.DMA((2, 3)),
            pltpu.SemaphoreType.DMA((3,)),
        ],
        compiler_params=pltpu.CompilerParams(
            collective_id=1, has_side_effects=True, vmem_limit_bytes=VMEM_LIMIT
        ),
        cost_estimate=cost(70 * doc_rows * keys * width, 100 << 20),
    )(
        qkv,
        qkv,
        qkv,
        qkv,
        qkv,
        da_rows,
        mixture,
        probs,
        query_probs,
        query_buckets,
        *grads,
        outputs,
    )


class Total:
    def __init__(self, spot, slots, sems):
        self.spot, self.slots, self.sems = spot, slots, sems

    def rounds(self):
        spot = self.spot
        near = [(x, y, core) for x in (0, 1) for y in (0, 1) for core in (0, 1)][1:]
        return (
            (
                (spot.x * 2 + spot.y) * 2 + spot.core,
                8,
                [spot.partner(x=x, y=y, core=core) for x, y, core in near],
            ),
            (spot.z, 4, [spot.partner(z=k) for k in (1, 2, 3)]),
        )

    def copies(self, index):
        base = 8 * index
        place, count, partners = self.rounds()[index]
        mine = self.slots.at[base + place]
        return [
            send(mine, mine, self.sems.at[index], number, device)
            for number, device in enumerate(partners)
        ]

    def begin(self, index, values):
        self.slots[8 * index + self.rounds()[index][0]] = values
        for copy in self.copies(index):
            copy.start()

    def end(self, index):
        for copy in self.copies(index):
            copy.wait_recv()
        values = self.slots[8 * index]
        for other in range(1, self.rounds()[index][1]):
            values = values + self.slots[8 * index + other]
        for copy in self.copies(index):
            copy.wait_send()
        return values


def leave_kernel(
    labels,
    x_ref,
    gain_ref,
    dq_ref,
    dkv_ref,
    dh_in,
    w_in,
    ds_ref,
    bucket_ref,
    query_sums_ref,
    ff_ref,
    found_ref,
    out_ref,
    docs_ref,
    query_dx_ref,
    total_ref,
    normed,
    away,
    low,
    high,
    sums,
    gain_sum,
    slots,
    dh_ref,
    w_ref,
    *rest,
):
    buffers, (sems, move_sems, total_sems, local) = rest[:7], rest[7:]
    step = pl.program_id(0)
    last = pl.num_programs(0) - 1
    spot = Spot()
    rows, width = x_ref.shape
    heads = ds_ref.shape[0]
    doc_rows = low.shape[0]
    block = doc_rows // 4
    scatter = Scatter(spot, away, buffers, sems)
    half = scatter.half
    move = Move(
        spot,
        row_block(low, block),
        lambda number: docs_ref.at[number],
        lambda number: docs_ref.at[number],
        move_sems,
        local.at[0],
    )
    query_copy = pltpu.make_async_copy(high, query_dx_ref, local.at[1])

    def quarter(number):
        device, rows = spot.partner(y=1, core=1), block // 4
        start = pl.multiple_of(device[1] * block + number * rows, 16)
        return send(
            low.at[pl.ds(start, rows), :],
            docs_ref.at[spot.seq, pl.ds(number * rows, rows), :],
            move_sems,
            3 + number,
            device,
        )

    late = [
        pltpu.make_async_copy(dh_in, dh_ref, local.at[2]),
        pltpu.make_async_copy(w_in, w_ref, local.at[3]),
    ]

    @pl.when(step == 0)
    def _():
        for copy in late:
            copy.start()
        more = [spot.partner(x=1, y=y, core=core) for y, core in ((0, 1), (1, 0), (1, 1))]
        greet(all_partners(spot) + more)
        gain = gain_ref[...]
        sums[...] = query_sums_ref[...]
        gain_sum[...] = jnp.zeros_like(gain_sum)

        def norm_block(number, carry):
            span = pl.ds(pl.multiple_of(number * block, 16), block)
            values = x_ref[span, :].astype(SINGLE)
            normed[span, :] = (values * scale_of(values) * gain).astype(BFLOAT)
            return carry

        lax.fori_loop(0, rows // block, norm_block, 0)

        def product(core, into):
            part = half // 3

            for number in range(3):
                spot_out = slice(number * part, (number + 1) * part)
                start = core * half + number * part

                def from_q():
                    lanes = pl.ds(pl.multiple_of(start, 128), part)
                    into[:, spot_out] = tn(normed[...], dq_ref[:, lanes]).astype(BFLOAT)

                def from_kv():
                    lanes = pl.ds(pl.multiple_of(start - width, 128), part)
                    into[:, spot_out] = tn(normed[...], dkv_ref[:, lanes]).astype(BFLOAT)

                pl.when(start < width)(from_q)
                pl.when(start >= width)(from_kv)

        product(1 - spot.core, away)
        scatter.copy(0).start()
        product(spot.core, scatter.held)
        scatter.core_end()
        for index in range(8):
            scatter.x_step(index)

        def grad_block(start, into, place):
            span = pl.ds(pl.multiple_of(start, 16), block)
            values = x_ref[span, :].astype(SINGLE)
            scale = scale_of(values)
            grad = nt(dq_ref[span, :], w_ref[:, :width])
            grad = grad + nt(dkv_ref[span, :width], w_ref[:, width : 2 * width])
            grad = grad + nt(dkv_ref[span, width:], w_ref[:, 2 * width :])
            gain_sum[...] += jnp.sum(grad * values * scale, axis=0, keepdims=True)
            dx = dh_ref[span, :] + norm_back(values, scale, grad * gain)
            into[place, :] = dx.astype(into.dtype)

        for copy in late:
            copy.wait()
        for number in range(3):
            y, core = Move.PARTNERS[number]
            start = spot.partner(y=y, core=core)[1] * block
            grad_block(start, low, pl.ds(pl.multiple_of(start, 16), block))
            if number != 1:
                move.copy(number).start()
        start = spot.seq * block
        grad_block(start, low, pl.ds(pl.multiple_of(start, 16), block))
        move.own().start()
        for number in range((rows - doc_rows) // block):
            grad_block(
                doc_rows + number * block, high, pl.ds(number * block, block)
            )
        query_copy.start()

    def at(when, name, index):
        @pl.when(step == when)
        def _():
            getattr(scatter, name)(index)

    at(1, "y_step", 0)
    at(2, "y_step", 1)
    at(3, "z_step", 0)
    at(3, "y_step", 2)
    at(4, "z_step", 1)
    at(4, "y_step", 3)
    at(5, "z_step", 2)

    for number in range(4):

        @pl.when(step == number + 2)
        def _():
            quarter(number).start()

    @pl.when(step > 0)
    def _():
        total = sums[...]
        for number in range(ds_ref.shape[1] // 16):
            span = slice(number * 16, (number + 1) * 16)
            grad_rows = ds_ref[:, span, :].reshape(heads * 16, ds_ref.shape[2])
            total = total + bucket_products(bucket_ref[span, :], grad_rows, labels)
        sums[...] = total

    @pl.when(step == last)
    def _():
        shape = sums.shape
        same = (
            lax.broadcasted_iota(jnp.int32, shape, 0) // labels
            == lax.broadcasted_iota(jnp.int32, shape, 1) % 16
        )
        kept = jnp.where(same, sums[...], 0.0)
        folded = kept[:labels]
        for index in range(1, 16):
            folded = folded + kept[index * labels : (index + 1) * labels]
        pick_shape = (heads * 16, 128)
        pick = (
            lax.broadcasted_iota(jnp.int32, pick_shape, 0) // 16
            == lax.broadcasted_iota(jnp.int32, pick_shape, 1)
        )
        bias = jnp.dot(
            folded,
            jnp.where(pick, 1.0, 0.0),
            preferred_element_type=SINGLE,
            precision=lax.Precision.HIGHEST,
        )
        wide = width // 128
        lines = [gain_sum[:, r * 128 : (r + 1) * 128] for r in range(wide)]
        lines += [ff_ref[:, r * 128 : (r + 1) * 128] for r in range(wide)]
        lines += [found_ref[...]] * (slots.shape[1] - labels - 2 * wide)
        total = Total(spot, slots, total_sems)
        total.begin(0, jnp.concatenate(lines + [bias], 0))
        scatter.tail_start()
        total.begin(1, total.end(0))
        left, right = scatter.finish()
        out_ref[:, :half] = left
        out_ref[:, half:] = right
        move.own().wait()
        move.copy(0).wait()
        move.copy(2).wait()
        for number in range(4):
            quarter(number).wait()
        query_copy.wait()
        total_ref[...] = total.end(1)


def leave(
    tokens, gain, dq, dkv, grad_res, w_qkv, ds, buckets, query_sums, grad_ff, found, n_docs, labels
):
    rows, width = tokens.shape
    heads, doc_rows, keys = ds.shape
    columns = 3 * width
    block = 128
    lines = -(-(2 * width // 128 + 1) // 8) * 8 + labels
    anywhere = pl.BlockSpec(memory_space=pl.ANY)
    return pl.pallas_call(
        functools.partial(leave_kernel, labels),
        grid=(1 + doc_rows // block,),
        in_specs=[
            whole((rows, width)),
            whole((1, width)),
            whole((rows, width)),
            whole((rows, 2 * width)),
            anywhere,
            anywhere,
            pl.BlockSpec((heads, block, keys), lambda i: (0, jnp.maximum(i - 1, 0), 0)),
            pl.BlockSpec((block, keys), lambda i: (jnp.maximum(i - 1, 0), 0)),
            whole(query_sums.shape),
            whole((1, width)),
            whole((1, 128)),
        ],
        out_specs=[whole((width // 32, columns)), anywhere, anywhere, whole((lines, 128))],
        out_shape=[
            jax.ShapeDtypeStruct((width // 32, columns), SINGLE),
            jax.ShapeDtypeStruct((n_docs, doc_rows // n_docs, width), BFLOAT),
            jax.ShapeDtypeStruct((rows - doc_rows, width), SINGLE),
            jax.ShapeDtypeStruct((lines, 128), SINGLE),
        ],
        scratch_shapes=[
            pltpu.VMEM((rows, width), BFLOAT),
            pltpu.VMEM((width, columns // 2), BFLOAT),
            pltpu.VMEM((doc_rows, width), BFLOAT),
            pltpu.VMEM((rows - doc_rows, width), SINGLE),
            pltpu.VMEM(query_sums.shape, SINGLE),
            pltpu.VMEM((1, width), SINGLE),
            pltpu.VMEM((12, lines, 128), SINGLE),
            pltpu.VMEM((rows, width), SINGLE),
            pltpu.VMEM(w_qkv.shape, BFLOAT),
            *scatter_scratch(width, columns),
            pltpu.SemaphoreType.DMA((2, COPIES)),
            pltpu.SemaphoreType.DMA((2, 7)),
            pltpu.SemaphoreType.DMA((2, 2, 7)),
            pltpu.SemaphoreType.DMA((4,)),
        ],
        compiler_params=pltpu.CompilerParams(
            collective_id=2, has_side_effects=True, vmem_limit_bytes=VMEM_LIMIT
        ),
        cost_estimate=cost(12 * rows * width * width, 100 << 20),
    )(
        tokens,
        gain.reshape(1, width),
        dq,
        dkv,
        grad_res,
        w_qkv,
        ds,
        buckets,
        query_sums,
        grad_ff,
        found,
    )


def on_device(
    doc_tokens,
    queries,
    doc_cot,
    query_cot,
    q_weight,
    kv_weight,
    out_weight,
    up_weight,
    down_weight,
    attn_gain,
    ff_gain,
    rel_bias,
    doc_buckets,
    query_buckets,
    topk_mask,
    positives,
    pos_count,
):
    n_docs, shard_rows, width = doc_tokens.shape
    n_query, query_len, _ = queries.shape
    bucket_count, heads = rel_bias.shape
    doc_len = doc_buckets.shape[1]
    doc_rows = n_docs * shard_rows
    query_total = n_query * query_len
    seq_size = lax.axis_size("seq")
    group = max(1, seq_size // n_docs)
    local_docs = max(1, n_docs // seq_size)
    local_rows = doc_len // group
    dp_size = lax.axis_size("dp")
    small = (dp_size, seq_size, n_docs) == (8, 4, 4) and width % 256 == 0 and shard_rows % 256 == 0
    small = small and down_weight.shape[0] * 32 == 4 * width and query_total % 256 == 0

    flat_queries = queries.reshape(query_total, width)
    flat_query_cot = query_cot.reshape(query_total, width)

    table = jnp.pad(rel_bias.T, ((0, 16 - heads), (0, 127 - bucket_count)))
    table = jnp.pad(table, ((0, 0), (0, 1)), constant_values=-1e30)

    if small:
        tokens, cotangent, w_qkv, w_out_up, w_down, buckets, qkv, mixture, doc_probs, query_probs, tiled = front(
            doc_tokens,
            flat_queries,
            doc_cot,
            flat_query_cot,
            (q_weight, kv_weight, out_weight, up_weight, down_weight),
            doc_buckets,
            attn_gain,
            table,
            query_buckets,
            heads,
        )
    else:
        order = gather_orders()[0]
        w_qkv = gather_rows(jnp.concatenate([q_weight, kv_weight], 1), order)
        w_out_up = gather_rows(jnp.concatenate([out_weight, up_weight], 1), order)
        w_down = gather_rows(down_weight, order)
        tokens = jnp.concatenate([own_document(doc_tokens), flat_queries], 0)
        cotangent = jnp.concatenate([own_document(doc_cot), flat_query_cot], 0)
        buckets = gather_positions(doc_buckets.astype(jnp.int16))
        repeats = 128 // query_len
        same = jnp.kron(jnp.eye(repeats, dtype=jnp.int32), jnp.ones_like(query_buckets))
        tiled = jnp.where(same == 1, jnp.tile(query_buckets, (repeats, repeats)), 127)
        if group > 1:
            part = lax.axis_index("seq") % group
            buckets = lax.dynamic_slice_in_dim(buckets, part * local_rows, local_rows, 0)
        q_rows, kv_rows = project(tokens, attn_gain, w_qkv)
        kv_docs = kv_rows
        if group > 1:
            teams = [list(range(t * group, (t + 1) * group)) for t in range(seq_size // group)]
            kv_docs = lax.all_gather(
                kv_rows[:doc_rows], "seq", axis=0, tiled=True, axis_index_groups=teams
            )
        doc_mix, doc_probs = doc_forward(
            q_rows, kv_docs, table, buckets, local_docs, local_rows, heads
        )
        query_mix, query_probs = query_forward(
            q_rows, kv_rows, table, tiled, doc_rows, query_total, heads
        )
        mixture = jnp.concatenate([doc_mix, query_mix], 0)
    if small:
        outputs, grad_res, grad_mix, grad_rest, grad_down, grad_near, grad_ff = middle(
            tokens, mixture, cotangent, ff_gain, w_out_up, w_down
        )
    else:
        outputs, grad_res, grad_mix, grad_out_up, grad_down, grad_ff = feed(
            tokens, mixture, cotangent, ff_gain, w_out_up, w_down
        )
    query_out = outputs[doc_rows:].reshape(queries.shape)
    matches = positives[:, :, None] == jnp.arange(doc_len, dtype=jnp.int32)[None, None, :]
    counted = jnp.arange(positives.shape[1], dtype=jnp.int32)[None, :] < pos_count[:, None]
    retrieved = jnp.sum(
        jnp.where(matches & counted[:, :, None], topk_mask[:, None, :].astype(SINGLE), 0.0)
    )

    if small:
        dq, dkv, ds, query_sums, grad_far, grad_down_shard, doc_out = back(
            qkv,
            grad_mix,
            mixture,
            doc_probs,
            query_probs,
            tiled,
            (grad_rest, grad_down),
            outputs,
            n_docs,
            bucket_count,
        )
        grad_out_shard = grad_far[:, :width]
        grad_up_shard = jnp.concatenate([grad_near, grad_far[:, width:]], 1)
        grad_qkv_shard, doc_dx, query_dx, total = leave(
            tokens,
            attn_gain,
            dq,
            dkv,
            grad_res,
            w_qkv,
            ds,
            buckets,
            query_sums,
            grad_ff,
            jnp.full((1, 128), retrieved),
            n_docs,
            bucket_count,
        )
        lines = width // 128
        total_attn = total[:lines].reshape(-1)
        total_ff = total[lines : 2 * lines].reshape(-1)
        total_found = total[2 * lines, 0]
        total_bias = total[-bucket_count:, :heads]
        query_dx = query_dx.reshape(queries.shape)
    else:
        grad_down_shard = scatter_columns(grad_down, 2)
        grad_out_up_shard = scatter_columns(grad_out_up, 2)
        grad_out_shard = grad_out_up_shard[:, :width]
        grad_up_shard = grad_out_up_shard[:, width:]
        doc_out = spread_document(outputs[:doc_rows], doc_tokens)
        doc_dq, doc_dk, doc_dv, doc_sums = doc_backward(
            q_rows,
            kv_docs,
            grad_mix,
            doc_mix,
            doc_probs,
            buckets,
            local_docs,
            local_rows,
            bucket_count,
        )
        if group > 1:
            both = jnp.concatenate([doc_dk, doc_dv], 1)
            both = lax.psum_scatter(
                both, "seq", scatter_dimension=0, tiled=True, axis_index_groups=teams
            )
            doc_dk, doc_dv = both[:, :width], both[:, width:]
        query_dq, query_dkv, query_sums = query_backward(
            q_rows, kv_rows, grad_mix, mixture, query_probs, tiled, doc_rows, bucket_count
        )
        grad_tokens, grad_low, grad_qkv, grad_attn = unproject(
            tokens,
            attn_gain,
            jnp.concatenate([doc_dq, query_dq], 0),
            jnp.concatenate([doc_dk, query_dkv[:, :width]], 0),
            jnp.concatenate([doc_dv, query_dkv[:, width:]], 0),
            grad_res,
            w_qkv,
        )
        grad_qkv_shard = scatter_columns(grad_qkv, 2)
        doc_dx = spread_document(grad_low[:doc_rows], doc_tokens)
        query_dx = grad_tokens[doc_rows:].reshape(queries.shape)
        sums = (doc_sums + query_sums).reshape(16, bucket_count, heads, 16)
        keep = jnp.eye(16, dtype=SINGLE)[:, None, None, :]
        bias_local = jnp.sum(sums * keep, axis=(0, 3))
        flat = jnp.concatenate(
            [grad_attn[0], grad_ff[0], bias_local.reshape(-1), jnp.full((128,), retrieved)]
        )
        total = sum_all(flat)
        total_attn, total_ff = total[:width], total[width : 2 * width]
        total_bias = total[2 * width : 2 * width + bucket_count * heads]
        total_bias = total_bias.reshape(bucket_count, heads)
        total_found = total[-1]
    slots = float(n_query * dp_size * seq_size * positives.shape[1])
    return (
        doc_out,
        query_out,
        doc_dx.astype(SINGLE),
        query_dx,
        grad_qkv_shard[:, :width],
        grad_qkv_shard[:, width:],
        grad_out_shard,
        grad_up_shard,
        grad_down_shard,
        total_attn,
        total_ff,
        total_bias,
        total_found / slots,
    )


def solution(mesh):
    rows_all = P(("dp", "seq"), None)
    return jax.shard_map(
        on_device,
        mesh=mesh,
        in_specs=(
            P("dp", "seq", None),
            P(("dp", "seq"), None, None),
            P("dp", "seq", None),
            P(("dp", "seq"), None, None),
            rows_all,
            rows_all,
            rows_all,
            rows_all,
            rows_all,
            P(),
            P(),
            P(),
            P("seq", None),
            P(),
            rows_all,
            rows_all,
            P(("dp", "seq")),
        ),
        out_specs=(
            P("dp", "seq", None),
            P(("dp", "seq"), None, None),
            P("dp", "seq", None),
            P(("dp", "seq"), None, None),
            rows_all,
            rows_all,
            rows_all,
            rows_all,
            rows_all,
            P(),
            P(),
            P(),
            P(),
        ),
        check_vma=False,
    )
```

```python
import functools
import math

import jax
import jax.numpy as jnp
from jax import lax
from jax.experimental import pallas as pl
from jax.experimental.pallas import tpu as pltpu
from jax.sharding import PartitionSpec as P

EPSILON = 1e-06
BFLOAT = jnp.bfloat16
SINGLE = jnp.float32
FIXED = 8191.0
GELU_A = math.sqrt(2.0 / math.pi)
GELU_B = 0.044715
VMEM_LIMIT = 63 << 20


def nn(left, right):
    return jnp.dot(left, right, preferred_element_type=SINGLE)


def nt(left, right):
    return lax.dot_general(left, right, (((1,), (1,)), ((), ())), preferred_element_type=SINGLE)


def tn(left, right):
    return lax.dot_general(left, right, (((0,), (0,)), ((), ())), preferred_element_type=SINGLE)


def whole(shape):
    zeros = (0,) * len(shape)
    return pl.BlockSpec(shape, lambda *_: zeros, pipeline_mode=pl.Buffered(1))


def params():
    return pltpu.CompilerParams(vmem_limit_bytes=VMEM_LIMIT)


def cost(flops, moved):
    return pl.CostEstimate(flops=int(flops), bytes_accessed=int(moved), transcendentals=0)


def scale_of(values):
    return lax.rsqrt(jnp.mean(values * values, axis=-1, keepdims=True) + EPSILON)


def norm_back(values, scale, scaled_grad):
    dot = jnp.mean(values * scaled_grad, axis=-1, keepdims=True)
    return scale * (scaled_grad - values * (scale * scale * dot))


def first_lanes(shape, head_dim):
    return lax.broadcasted_iota(jnp.int32, shape, 1) < head_dim


def project_kernel(x_ref, gain_ref, w_ref, q_ref, kv_ref):
    values = x_ref[...].astype(SINGLE)
    normed = (values * scale_of(values) * gain_ref[...]).astype(BFLOAT)
    width = values.shape[1]
    q_ref[...] = nn(normed, w_ref[:, :width]).astype(BFLOAT)
    kv_ref[...] = nn(normed, w_ref[:, width:]).astype(BFLOAT)


def project(tokens, gain, w_qkv):
    rows, width = tokens.shape
    block = math.gcd(rows, 256)
    return pl.pallas_call(
        project_kernel,
        grid=(rows // block,),
        in_specs=[
            pl.BlockSpec((block, width), lambda i: (i, 0)),
            whole((1, width)),
            whole(w_qkv.shape),
        ],
        out_specs=[
            pl.BlockSpec((block, width), lambda i: (i, 0)),
            pl.BlockSpec((block, 2 * width), lambda i: (i, 0)),
        ],
        out_shape=[
            jax.ShapeDtypeStruct((rows, width), BFLOAT),
            jax.ShapeDtypeStruct((rows, 2 * width), BFLOAT),
        ],
        compiler_params=params(),
        cost_estimate=cost(6 * rows * width * width, 12 * rows * width),
    )(tokens, gain.reshape(1, width), w_qkv)


def attend_pair(q_pair, k_pair, v_pair, table_ref, bucket_ref, start, prob_ref, step, head_dim):
    rows, keys = q_pair.shape[0], k_pair.shape[0]
    wide = first_lanes(q_pair.shape, head_dim)
    tall = first_lanes(v_pair.shape, head_dim)
    coded_rows = jnp.round(table_ref[pl.ds(2 * step, 2), :] * FIXED).astype(jnp.int32)
    table = (coded_rows[0:1, :] << 16) | (coded_rows[1:2, :] & 0xFFFF)
    table = jnp.broadcast_to(table, (rows, 128))
    span = pl.ds(start, rows)
    packed = jnp.concatenate(
        [
            jnp.take_along_axis(
                table,
                bucket_ref[span, part * 128 : part * 128 + 128].astype(jnp.int32),
                axis=1,
                mode="promise_in_bounds",
            )
            for part in range(keys // 128)
        ],
        1,
    )
    total = None
    for side in range(2):
        mine = wide if side == 0 else ~wide
        mine_tall = tall if side == 0 else ~tall
        coded = (packed >> 16) if side == 0 else ((packed << 16) >> 16)
        scores = nt(jnp.where(mine, q_pair, 0), k_pair)
        scores = scores + coded.astype(SINGLE) * (1.0 / FIXED)
        shifted = jnp.exp(scores - jnp.max(scores, axis=-1, keepdims=True))
        inverse = 1.0 / jnp.sum(shifted, axis=-1, keepdims=True)
        soft = (shifted * inverse).astype(BFLOAT)
        prob_ref[2 * step + side] = soft
        term = nn(soft, jnp.where(mine_tall, v_pair, 0))
        total = term if total is None else total + term
    return total.astype(BFLOAT)


def pair_lanes(step, head_dim, offset=0):
    return pl.ds(pl.multiple_of(offset + step * 2 * head_dim, 128), 2 * head_dim)


def doc_forward_kernel(q_ref, k_ref, v_ref, table_ref, bucket_ref, mix_ref, prob_ref):
    heads = prob_ref.shape[0]
    head_dim = q_ref.shape[1] // heads

    def pair(step, carry):
        lanes = pair_lanes(step, head_dim)
        mix_ref[:, lanes] = attend_pair(
            q_ref[:, lanes],
            k_ref[:, lanes],
            v_ref[:, lanes],
            table_ref,
            bucket_ref,
            0,
            prob_ref,
            step,
            head_dim,
        )
        return carry

    lax.fori_loop(0, heads // 2, pair, 0)


def doc_forward(q_rows, kv_rows, table, buckets, n_docs, rows, heads):
    width = q_rows.shape[1]
    keys = buckets.shape[1]
    block = math.gcd(rows, 256)
    steps = rows // block
    return pl.pallas_call(
        doc_forward_kernel,
        grid=(n_docs, steps),
        in_specs=[
            pl.BlockSpec((block, width), lambda d, i: (d * steps + i, 0)),
            pl.BlockSpec((keys, width), lambda d, i: (d, 0)),
            pl.BlockSpec((keys, width), lambda d, i: (d, 1)),
            whole(table.shape),
            pl.BlockSpec((block, keys), lambda d, i: (i, 0)),
        ],
        out_specs=[
            pl.BlockSpec((block, width), lambda d, i: (d * steps + i, 0)),
            pl.BlockSpec((heads, block, keys), lambda d, i: (0, d * steps + i, 0)),
        ],
        out_shape=[
            jax.ShapeDtypeStruct((n_docs * rows, width), BFLOAT),
            jax.ShapeDtypeStruct((heads, n_docs * rows, keys), BFLOAT),
        ],
        compiler_params=params(),
        cost_estimate=cost(30 * n_docs * rows * keys * width, 2 * heads * n_docs * rows * keys),
    )(q_rows, kv_rows, kv_rows, table, buckets)


def bucket_onehot(bucket_rows, labels):
    rows, keys = bucket_rows.shape
    numbers = bucket_rows.astype(jnp.int32)
    names = lax.broadcasted_iota(jnp.int32, (labels, keys), 0)
    parts = [
        jnp.where(jnp.broadcast_to(numbers[r : r + 1, :], (labels, keys)) == names, 1.0, 0.0).astype(
            BFLOAT
        )
        for r in range(rows)
    ]
    return jnp.concatenate(parts, 0)


def bucket_products(bucket_rows, grad_rows, labels):
    return nt(bucket_onehot(bucket_rows, labels), grad_rows)


def attend_back(q_pair, k_pair, v_pair, da_pair, mix_pair, probs, head_dim):
    wide = first_lanes(q_pair.shape, head_dim)
    tall = first_lanes(k_pair.shape, head_dim)
    product = da_pair.astype(SINGLE) * mix_pair.astype(SINGLE)
    dq = dk = dv = None
    kept = []
    for side in range(2):
        mine = wide if side == 0 else ~wide
        mine_tall = tall if side == 0 else ~tall
        da_mine = jnp.where(mine, da_pair, 0)
        correction = jnp.sum(jnp.where(mine, product, 0.0), axis=-1, keepdims=True)
        grad_soft = nt(da_mine, v_pair)
        soft = probs[side]
        grad_scores = (soft.astype(SINGLE) * (grad_soft - correction)).astype(BFLOAT)
        kept.append(grad_scores)
        dq_term = nn(grad_scores, jnp.where(mine_tall, k_pair, 0))
        dk_term = tn(grad_scores, jnp.where(mine, q_pair, 0))
        dv_term = tn(soft, da_mine)
        dq = dq_term if dq is None else dq + dq_term
        dk = dk_term if dk is None else dk + dk_term
        dv = dv_term if dv is None else dv + dv_term
    return dq, dk, dv, kept


def query_back_block(q_rows, k_rows, v_rows, da_rows, mix_rows, probs, head_dim):
    rows, width = q_rows.shape
    heads = len(probs)
    wide = first_lanes((rows, 2 * head_dim), head_dim)

    def pair(values, step):
        return values[:, step * 2 * head_dim : (step + 1) * 2 * head_dim]

    def halves(values, step):
        return jnp.where(wide, pair(values, step), 0), jnp.where(wide, 0, pair(values, step))

    das, corrections, grads = [], [], []
    for step in range(heads // 2):
        das += halves(da_rows, step)
    for head in range(heads):
        grads.append(nt(das[head], pair(v_rows, head // 2)))
    for head in range(heads):
        product = das[head].astype(SINGLE) * pair(mix_rows, head // 2).astype(SINGLE)
        corrections.append(jnp.sum(product, axis=-1, keepdims=True))
    kept = [
        (prob.astype(SINGLE) * (grad - correction)).astype(BFLOAT)
        for prob, grad, correction in zip(probs, grads, corrections)
    ]
    dq, dk, dv = [], [], []
    for step in range(heads // 2):
        left, right = kept[2 * step], kept[2 * step + 1]
        k_left, k_right = halves(k_rows, step)
        dq.append((nn(left, k_left) + nn(right, k_right)).astype(BFLOAT))
    for step in range(heads // 2):
        left, right = kept[2 * step], kept[2 * step + 1]
        q_left, q_right = halves(q_rows, step)
        dk.append((tn(left, q_left) + tn(right, q_right)).astype(BFLOAT))
    for step in range(heads // 2):
        terms = tn(probs[2 * step], das[2 * step]) + tn(probs[2 * step + 1], das[2 * step + 1])
        dv.append(terms.astype(BFLOAT))
    return dq, dk, dv, kept


def doc_backward_kernel(
    labels,
    q_ref,
    k_ref,
    v_ref,
    da_ref,
    mix_ref,
    prob_ref,
    bucket_ref,
    dq_ref,
    dk_ref,
    dv_ref,
    sums_ref,
    dk_acc,
    dv_acc,
    ds_keep,
):
    rows, width = q_ref.shape
    heads = prob_ref.shape[0]
    keys = k_ref.shape[0]
    head_dim = width // heads
    doc, step_i = pl.program_id(0), pl.program_id(1)

    @pl.when(step_i == 0)
    def _():
        dk_acc[...] = jnp.zeros_like(dk_acc)
        dv_acc[...] = jnp.zeros_like(dv_acc)

    @pl.when((step_i == 0) & (doc == 0))
    def _():
        sums_ref[...] = jnp.zeros_like(sums_ref)

    def pair(step, carry):
        lanes = pl.ds(pl.multiple_of(step * 2 * head_dim, 128), 2 * head_dim)
        dq, dk, dv, kept = attend_back(
            q_ref[:, lanes],
            k_ref[:, lanes],
            v_ref[:, lanes],
            da_ref[:, lanes],
            mix_ref[:, lanes],
            [prob_ref[2 * step], prob_ref[2 * step + 1]],
            head_dim,
        )
        ds_keep[2 * step] = kept[0]
        ds_keep[2 * step + 1] = kept[1]
        dq_ref[:, lanes] = dq.astype(BFLOAT)
        dk_acc[:, lanes] += dk
        dv_acc[:, lanes] += dv
        return carry

    lax.fori_loop(0, heads // 2, pair, 0)

    def group(number, carry):
        span = pl.ds(pl.multiple_of(number * 16, 16), 16)
        sums_ref[...] += bucket_products(
            bucket_ref[span, :], ds_keep[:, span, :].reshape(heads * 16, keys), labels
        )
        return carry

    lax.fori_loop(0, rows // 16, group, 0)

    @pl.when(step_i == pl.num_programs(1) - 1)
    def _():
        dk_ref[...] = dk_acc[...].astype(BFLOAT)
        dv_ref[...] = dv_acc[...].astype(BFLOAT)


def doc_backward(q_rows, kv_rows, da_rows, mixture, probs, buckets, n_docs, rows, labels):
    width = q_rows.shape[1]
    heads = probs.shape[0]
    keys = buckets.shape[1]
    block = math.gcd(rows, 256)
    steps = rows // block
    along = pl.BlockSpec((block, width), lambda d, i: (d * steps + i, 0))
    per_doc = pl.BlockSpec((keys, width), lambda d, i: (d, 0))
    return pl.pallas_call(
        functools.partial(doc_backward_kernel, labels),
        grid=(n_docs, steps),
        in_specs=[
            along,
            per_doc,
            pl.BlockSpec((keys, width), lambda d, i: (d, 1)),
            along,
            along,
            pl.BlockSpec((heads, block, keys), lambda d, i: (0, d * steps + i, 0)),
            pl.BlockSpec((block, keys), lambda d, i: (i, 0)),
        ],
        out_specs=[along, per_doc, per_doc, whole((16 * labels, heads * 16))],
        out_shape=[
            jax.ShapeDtypeStruct((n_docs * rows, width), BFLOAT),
            jax.ShapeDtypeStruct((n_docs * keys, width), BFLOAT),
            jax.ShapeDtypeStruct((n_docs * keys, width), BFLOAT),
            jax.ShapeDtypeStruct((16 * labels, heads * 16), SINGLE),
        ],
        scratch_shapes=[
            pltpu.VMEM((keys, width), SINGLE),
            pltpu.VMEM((keys, width), SINGLE),
            pltpu.VMEM((heads, block, keys), BFLOAT),
        ],
        compiler_params=params(),
        cost_estimate=cost(70 * n_docs * rows * keys * width, 2 * heads * n_docs * rows * keys),
    )(q_rows, kv_rows, kv_rows, da_rows, mixture, probs, buckets)


def query_block(q_rows, k_rows, v_rows, table_ref, index, heads):
    rows, width = q_rows.shape
    head_dim = width // heads
    wide = first_lanes((rows, 2 * head_dim), head_dim)

    def halves(values, step):
        pair = values[:, step * 2 * head_dim : (step + 1) * 2 * head_dim]
        return jnp.where(wide, pair, 0), jnp.where(wide, 0, pair), pair

    scores = []
    for step in range(heads // 2):
        left, right, _ = halves(q_rows, step)
        keys = halves(k_rows, step)[2]
        scores += [nt(left, keys), nt(right, keys)]
    for head in range(heads):
        table = jnp.broadcast_to(table_ref[head : head + 1, :], (rows, 128))
        bias = jnp.take_along_axis(table, index, axis=1, mode="promise_in_bounds")
        scores[head] = scores[head] + bias
    tops = [jnp.max(score, axis=-1, keepdims=True) for score in scores]
    shifted = [jnp.exp(score - top) for score, top in zip(scores, tops)]
    inverse = [1.0 / jnp.sum(shift, axis=-1, keepdims=True) for shift in shifted]
    softs = [(shift * inv).astype(BFLOAT) for shift, inv in zip(shifted, inverse)]
    outs = []
    for step in range(heads // 2):
        left, right, _ = halves(v_rows, step)
        outs.append((nn(softs[2 * step], left) + nn(softs[2 * step + 1], right)).astype(BFLOAT))
    return softs, jnp.concatenate(outs, 1)


def query_forward_kernel(q_ref, kv_ref, table_ref, bucket_ref, mix_ref, prob_ref):
    width = q_ref.shape[1]
    softs, mix_ref[...] = query_block(
        q_ref[...], kv_ref[:, :width], kv_ref[:, width:], table_ref, bucket_ref[...], prob_ref.shape[0]
    )
    for head, soft in enumerate(softs):
        prob_ref[head] = soft


def query_forward(q_rows, kv_rows, table, buckets, start, count, heads):
    width = q_rows.shape[1]
    offset = start // 128
    return pl.pallas_call(
        query_forward_kernel,
        grid=(count // 128,),
        in_specs=[
            pl.BlockSpec((128, width), lambda i: (offset + i, 0)),
            pl.BlockSpec((128, 2 * width), lambda i: (offset + i, 0)),
            whole(table.shape),
            whole(buckets.shape),
        ],
        out_specs=[
            pl.BlockSpec((128, width), lambda i: (i, 0)),
            pl.BlockSpec((heads, 128, 128), lambda i: (0, i, 0)),
        ],
        out_shape=[
            jax.ShapeDtypeStruct((count, width), BFLOAT),
            jax.ShapeDtypeStruct((heads, count, 128), BFLOAT),
        ],
        compiler_params=params(),
        cost_estimate=cost(4 * count * 128 * width * 4, 10 * count * width),
    )(q_rows, kv_rows, table, buckets)


def query_backward_kernel(
    labels, q_ref, kv_ref, da_ref, mix_ref, prob_ref, bucket_ref, dq_ref, dkv_ref, sums_ref, ds_keep
):
    rows, width = q_ref.shape
    heads = prob_ref.shape[0]
    head_dim = width // heads

    @pl.when(pl.program_id(0) == 0)
    def _():
        sums_ref[...] = jnp.zeros_like(sums_ref)

    for step in range(heads // 2):
        lanes = slice(step * 2 * head_dim, (step + 1) * 2 * head_dim)
        right = slice(width + lanes.start, width + lanes.stop)
        dq, dk, dv, kept = attend_back(
            q_ref[:, lanes],
            kv_ref[:, lanes],
            kv_ref[:, right],
            da_ref[:, lanes],
            mix_ref[:, lanes],
            [prob_ref[2 * step], prob_ref[2 * step + 1]],
            head_dim,
        )
        ds_keep[2 * step] = kept[0]
        ds_keep[2 * step + 1] = kept[1]
        dq_ref[:, lanes] = dq.astype(BFLOAT)
        dkv_ref[:, lanes] = dk.astype(BFLOAT)
        dkv_ref[:, right] = dv.astype(BFLOAT)

    def group(number, carry):
        span = pl.ds(pl.multiple_of(number * 16, 16), 16)
        sums_ref[...] += bucket_products(
            bucket_ref[span, :], ds_keep[:, span, :].reshape(heads * 16, rows), labels
        )
        return carry

    lax.fori_loop(0, rows // 16, group, 0)


def query_backward(q_rows, kv_rows, da_rows, mixture, probs, buckets, start, labels):
    width = q_rows.shape[1]
    heads, count, _ = probs.shape
    offset = start // 128
    return pl.pallas_call(
        functools.partial(query_backward_kernel, labels),
        grid=(count // 128,),
        in_specs=[
            pl.BlockSpec((128, width), lambda i: (offset + i, 0)),
            pl.BlockSpec((128, 2 * width), lambda i: (offset + i, 0)),
            pl.BlockSpec((128, width), lambda i: (offset + i, 0)),
            pl.BlockSpec((128, width), lambda i: (offset + i, 0)),
            pl.BlockSpec((heads, 128, 128), lambda i: (0, i, 0)),
            whole(buckets.shape),
        ],
        out_specs=[
            pl.BlockSpec((128, width), lambda i: (i, 0)),
            pl.BlockSpec((128, 2 * width), lambda i: (i, 0)),
            whole((16 * labels, heads * 16)),
        ],
        out_shape=[
            jax.ShapeDtypeStruct((count, width), BFLOAT),
            jax.ShapeDtypeStruct((count, 2 * width), BFLOAT),
            jax.ShapeDtypeStruct((16 * labels, heads * 16), SINGLE),
        ],
        scratch_shapes=[pltpu.VMEM((heads, 128, 128), BFLOAT)],
        compiler_params=params(),
        cost_estimate=cost(8 * count * 128 * width * 4, 14 * count * width),
    )(q_rows, kv_rows, da_rows, mixture, probs, buckets)


def feed_kernel(
    chunk,
    x_ref,
    mix_ref,
    dy_ref,
    gain_ref,
    wou_ref,
    wd_ref,
    y_ref,
    dh_ref,
    da_ref,
    gou_ref,
    gd_ref,
    gg_ref,
    gou_acc,
    gd_acc,
    stage,
    sems,
):
    step = pl.program_id(0)
    hidden, width = wd_ref.shape

    @pl.when(step == 0)
    def _():
        gou_acc[...] = jnp.zeros_like(gou_acc)
        gd_acc[...] = jnp.zeros_like(gd_acc)
        gg_ref[...] = jnp.zeros_like(gg_ref)

    mixture = mix_ref[...]
    dy = dy_ref[...]
    gain = gain_ref[...]
    residual = x_ref[...].astype(SINGLE) + nn(mixture, wou_ref[:, :width])
    scale = scale_of(residual)
    second = (residual * scale * gain).astype(BFLOAT)
    y = residual
    grad_second = jnp.zeros_like(residual)
    for part in range(hidden // chunk):
        span = slice(part * chunk, (part + 1) * chunk)
        past = slice(width + part * chunk, width + (part + 1) * chunk)
        pre = nn(second, wou_ref[:, past])
        grad_hidden = nt(dy, wd_ref[span, :])
        square = pre * pre
        tanh = jnp.tanh(pre * (GELU_A + (GELU_A * GELU_B) * square))
        half = 0.5 + 0.5 * tanh
        act = pre * half
        slope = half + act * (1.0 - tanh) * (GELU_A + (3.0 * GELU_A * GELU_B) * square)
        act_low = act.astype(BFLOAT)
        grad_pre = (grad_hidden * slope).astype(BFLOAT)
        y = y + nn(act_low, wd_ref[span, :])
        grad_second = grad_second + nt(grad_pre, wou_ref[:, past])
        gd_acc[span, :] += tn(act_low, dy)
        gou_acc[:, past] += tn(second, grad_pre)
    y_ref[...] = y.astype(BFLOAT)
    gg_ref[...] += jnp.sum(grad_second * residual * scale, axis=0, keepdims=True)
    grad_res = dy.astype(SINGLE) + norm_back(residual, scale, grad_second * gain)
    dh_ref[...] = grad_res
    grad_low = grad_res.astype(BFLOAT)
    da_ref[...] = nt(grad_low, wou_ref[:, :width]).astype(BFLOAT)
    gou_acc[:, :width] += tn(mixture, grad_low)

    @pl.when(step == pl.num_programs(0) - 1)
    def _():
        pieces = []
        rows, columns = stage.shape[1:]
        for acc, out in ((gd_acc, gd_ref), (gou_acc, gou_ref)):
            for r in range(acc.shape[0] // rows):
                for c in range(acc.shape[1] // columns):
                    spot = (pl.ds(r * rows, rows), pl.ds(c * columns, columns))
                    pieces.append((acc, out, spot))
        flying = [None, None]
        for number, (acc, out, spot) in enumerate(pieces):
            slot = number % 2
            if flying[slot] is not None:
                flying[slot].wait()
            stage[slot] = acc[spot].astype(BFLOAT)
            flying[slot] = pltpu.make_async_copy(stage.at[slot], out.at[spot], sems.at[slot])
            flying[slot].start()
        for copy in flying:
            if copy is not None:
                copy.wait()


def feed(tokens, mixture, cotangent, gain, w_out_up, w_down):
    rows, width = tokens.shape
    hidden = w_down.shape[0]
    block = math.gcd(rows, 256)
    along = pl.BlockSpec((block, width), lambda i: (i, 0))
    anywhere = pl.BlockSpec(memory_space=pl.ANY)
    return pl.pallas_call(
        functools.partial(feed_kernel, math.gcd(hidden, 768)),
        grid=(rows // block,),
        in_specs=[
            along,
            along,
            along,
            whole((1, width)),
            whole(w_out_up.shape),
            whole(w_down.shape),
        ],
        out_specs=[along, along, along, anywhere, anywhere, whole((1, width))],
        out_shape=[
            jax.ShapeDtypeStruct((rows, width), BFLOAT),
            jax.ShapeDtypeStruct((rows, width), SINGLE),
            jax.ShapeDtypeStruct((rows, width), BFLOAT),
            jax.ShapeDtypeStruct(w_out_up.shape, BFLOAT),
            jax.ShapeDtypeStruct(w_down.shape, BFLOAT),
            jax.ShapeDtypeStruct((1, width), SINGLE),
        ],
        scratch_shapes=[
            pltpu.VMEM(w_out_up.shape, SINGLE),
            pltpu.VMEM(w_down.shape, SINGLE),
            pltpu.VMEM((2, width, width), BFLOAT),
            pltpu.SemaphoreType.DMA((2,)),
        ],
        compiler_params=params(),
        cost_estimate=cost(2 * rows * width * (6 * hidden + 3 * width), 14 * rows * width),
    )(tokens, mixture, cotangent, gain.reshape(1, width), w_out_up, w_down)


def unproject_kernel(
    x_ref, gain_ref, dq_ref, dk_ref, dv_ref, dh_ref, w_ref, dx_ref, low_ref, gw_ref, gg_ref, acc
):
    step = pl.program_id(0)
    width = w_ref.shape[0]

    @pl.when(step == 0)
    def _():
        acc[...] = jnp.zeros_like(acc)
        gg_ref[...] = jnp.zeros_like(gg_ref)

    values = x_ref[...].astype(SINGLE)
    gain = gain_ref[...]
    scale = scale_of(values)
    normed = (values * scale * gain).astype(BFLOAT)
    grad = jnp.zeros_like(values)
    for number, ref in enumerate((dq_ref, dk_ref, dv_ref)):
        span = slice(number * width, (number + 1) * width)
        part = ref[...]
        acc[:, span] += tn(normed, part)
        grad = grad + nt(part, w_ref[:, span])
    gg_ref[...] += jnp.sum(grad * values * scale, axis=0, keepdims=True)
    dx = dh_ref[...] + norm_back(values, scale, grad * gain)
    dx_ref[...] = dx
    low_ref[...] = dx.astype(BFLOAT)

    @pl.when(step == pl.num_programs(0) - 1)
    def _():
        gw_ref[...] = acc[...].astype(BFLOAT)


def unproject(tokens, gain, dq, dk, dv, grad_res, w_qkv):
    rows, width = tokens.shape
    block = math.gcd(rows, 256)
    along = pl.BlockSpec((block, width), lambda i: (i, 0))
    return pl.pallas_call(
        unproject_kernel,
        grid=(rows // block,),
        in_specs=[along, whole((1, width)), along, along, along, along, whole(w_qkv.shape)],
        out_specs=[along, along, whole(w_qkv.shape), whole((1, width))],
        out_shape=[
            jax.ShapeDtypeStruct((rows, width), SINGLE),
            jax.ShapeDtypeStruct((rows, width), BFLOAT),
            jax.ShapeDtypeStruct(w_qkv.shape, BFLOAT),
            jax.ShapeDtypeStruct((1, width), SINGLE),
        ],
        scratch_shapes=[pltpu.VMEM(w_qkv.shape, SINGLE)],
        compiler_params=params(),
        cost_estimate=cost(12 * rows * width * width, 18 * rows * width),
    )(tokens, gain.reshape(1, width), dq, dk, dv, grad_res, w_qkv)


def bits_of(count):
    return [1 << place for place in reversed(range(count.bit_length() - 1))]


def axis_bits():
    dp_bits = [("dp", bit) for bit in bits_of(lax.axis_size("dp"))]
    seq_bits = [("seq", bit) for bit in bits_of(lax.axis_size("seq"))]
    return dp_bits, seq_bits


def gather_orders():
    dp_bits, seq_bits = axis_bits()
    far = (len(dp_bits) + 1) // 2
    z_bits, x_bits = dp_bits[:far], dp_bits[far:]
    y_bits, core_bits = seq_bits[:-1], seq_bits[-1:]
    return [z_bits + y_bits + x_bits + core_bits, z_bits + x_bits + y_bits + core_bits]


def swap(values, name, bit):
    count = lax.axis_size(name)
    return lax.ppermute(values, name, [(i, i ^ bit) for i in range(count)])


def is_high(name, bit):
    return (lax.axis_index(name) & bit) != 0


def gather_rows(shard, order):
    dp_bits, seq_bits = axis_bits()
    everything = dp_bits + seq_bits
    done = []
    held = shard
    for item in order:
        other = swap(held, *item)
        done.append(item)
        place = sorted(everything.index(one) for one in done).index(everything.index(item))
        high = is_high(*item)
        held = jnp.where(
            high, jnp.stack([other, held], place), jnp.stack([held, other], place)
        )
    return held.reshape(-1, shard.shape[1])


def scatter_rows(values, order):
    dp_bits, seq_bits = axis_bits()
    left = dp_bits + seq_bits
    rows = values.shape[0] >> len(left)
    held = values.reshape((2,) * len(left) + (rows, values.shape[1]))
    for item in order:
        place = left.index(item)
        mine = is_high(*item).astype(jnp.int32)
        away = lax.dynamic_index_in_dim(held, 1 - mine, place, keepdims=False)
        kept = lax.dynamic_index_in_dim(held, mine, place, keepdims=False)
        other = swap(away, *item)
        held = kept.astype(SINGLE) + other.astype(SINGLE)
        left.remove(item)
        if left:
            held = held.astype(BFLOAT)
    return held


def scatter_columns(values, parts):
    orders = [order[::-1] for order in gather_orders()]
    columns = values.shape[1] // parts
    return jnp.concatenate(
        [
            scatter_rows(values[:, p * columns : (p + 1) * columns], orders[p % len(orders)])
            for p in range(parts)
        ],
        1,
    )


def sum_all(values):
    dp_bits, seq_bits = axis_bits()
    for item in seq_bits[::-1] + dp_bits[::-1]:
        values = values + swap(values, *item)
    return values


def own_document(shard):
    count = lax.axis_size("seq")
    n_docs = shard.shape[0]
    me = lax.axis_index("seq")
    if n_docs >= count:
        per = n_docs // count
        blocks = shard.reshape((count, per) + shard.shape[1:])
        sets, group = count, 1
    else:
        blocks = shard[:, None]
        sets, group = n_docs, count // n_docs
    got = []
    for r in range(sets):
        piece = lax.dynamic_index_in_dim(blocks, (me % sets) ^ r, 0, keepdims=False)
        route = [
            (u * sets + i, (i ^ r) * group + u) for u in range(group) for i in range(sets)
        ]
        if any(a != b for a, b in route):
            piece = lax.ppermute(piece, "seq", route)
        got.append(piece)
    stacked = jnp.stack(got, 0)
    mine = me // group
    ordered = [lax.dynamic_index_in_dim(stacked, mine ^ i, 0, keepdims=False) for i in range(sets)]
    return jnp.concatenate(ordered, 1).reshape(-1, shard.shape[-1])


def spread_document(rows, like):
    count = lax.axis_size("seq")
    n_docs, shard_rows, width = like.shape
    me = lax.axis_index("seq")
    if n_docs >= count:
        per = n_docs // count
        sets, group = count, 1
    else:
        per = 1
        sets, group = n_docs, count // n_docs
    blocks = rows.reshape(per, sets, shard_rows, width)
    mine = me // group
    got = []
    for r in range(sets):
        piece = lax.dynamic_index_in_dim(blocks, mine ^ r, 1, keepdims=False)
        route = [
            ((i ^ r) * group + u, u * sets + i) for u in range(group) for i in range(sets)
        ]
        if any(a != b for a, b in route):
            piece = lax.ppermute(piece, "seq", route)
        got.append(piece)
    stacked = jnp.stack(got, 0)
    ordered = [
        lax.dynamic_index_in_dim(stacked, (me % sets) ^ i, 0, keepdims=False) for i in range(sets)
    ]
    return jnp.concatenate(ordered, 0)


def gather_positions(shard):
    seq_bits = axis_bits()[1]
    done = []
    held = shard
    for item in seq_bits:
        other = swap(held, *item)
        high = is_high(*item)
        place = len(done)
        held = jnp.where(
            high, jnp.stack([other, held], place), jnp.stack([held, other], place)
        )
        done.append(item)
    return held.reshape(-1, shard.shape[1])


class Spot:
    def __init__(self):
        self.dp = lax.axis_index("dp")
        self.seq = lax.axis_index("seq")
        self.core = self.seq % 2
        self.y = self.seq // 2
        self.x = self.dp % 2
        self.z = self.dp // 2

    def partner(self, z=0, x=0, y=0, core=0):
        dp = self.flip(self.z, z) * 2 + self.flip(self.x, x)
        seq = self.flip(self.y, y) * 2 + self.flip(self.core, core)
        return (dp, seq)

    @staticmethod
    def flip(value, bits):
        if bits == 0:
            return value
        if bits == 1:
            return value + 1 - 2 * (value % 2)
        if bits == 2:
            return (value + 2) % 4
        return 3 - value

    def chip(self, z=0, x=0, y=0):
        return (self.flip(self.z, z) * 2 + self.flip(self.x, x)) * 2 + self.flip(self.y, y)


def send(source, target, sems, number, device):
    return pltpu.make_async_remote_copy(
        src_ref=source,
        dst_ref=target,
        send_sem=sems.at[0, number],
        recv_sem=sems.at[1, number],
        device_id=device,
        device_id_type=pl.DeviceIdType.MESH,
    )


def greet(partners):
    barrier = pltpu.get_barrier_semaphore()
    for device in partners:
        pl.semaphore_signal(barrier, inc=1, device_id=device, device_id_type=pl.DeviceIdType.MESH)
    pl.semaphore_wait(barrier, len(partners))


COPIES = 17
GATHER_COPIES = 24


class Gather:
    def __init__(self, spot, shard, whole_ref, theirs, block, sems, local):
        self.spot, self.shard, self.whole = spot, shard, whole_ref
        self.theirs, self.block, self.sems, self.local = theirs, block, sems, local
        self.rows, self.half = block.shape

    def columns(self, core):
        return pl.ds(pl.multiple_of(core * self.half, 128), self.half)

    def area(self, count=1, **bits):
        chip = self.spot.chip(**bits)
        if count == 2:
            chip = chip - chip % 2
        row = pl.multiple_of(chip * self.rows, 16)
        return self.whole.at[pl.ds(row, count * self.rows), self.columns(self.spot.core)]

    def copy(self, number):
        spot = self.spot
        if number == 0:
            source, target = self.shard.at[:, self.columns(1 - spot.core)], self.theirs
            device = spot.partner(core=1)
        elif number < 4:
            source, target, device = self.block, self.area(), spot.partner(z=number)
        elif number < 8:
            target, device = self.area(z=number - 4), spot.partner(y=1)
            source = self.block if number == 4 else target
        elif number < 16:
            target = self.area(z=(number - 8) % 4, y=(number - 8) // 4)
            source, device = self.block if number == 8 else target, spot.partner(x=1)
        else:
            source = target = self.area(2, z=number % 4, x=(number - 16) // 4)
            device = spot.partner(core=1)
        return send(source, target, self.sems, number, device)

    def here(self):
        return pltpu.make_async_copy(self.block, self.area(), self.local)

    def join_end(self):
        self.copy(0).wait_recv()
        part = self.rows // 2
        low = self.spot.core == 0
        mine = self.shard[:, self.columns(self.spot.core)].astype(SINGLE)
        theirs = self.theirs[...].astype(SINGLE)
        self.block[:part, :] = jnp.where(low, mine, theirs).astype(BFLOAT)
        self.block[part:, :] = jnp.where(low, theirs, mine).astype(BFLOAT)
        self.here().start()

    def start(self, *numbers):
        for number in numbers:
            self.copy(number).start()

    def z_got(self, k):
        self.copy(k).wait_recv()
        self.start(4 + k, 8 + k)

    def y_got(self, k):
        self.copy(4 + k).wait_recv()
        if k == 0:
            self.here().wait()
        self.start(12 + k, 16 + k)

    def x_got(self, k):
        self.copy(8 + k).wait_recv()
        self.copy(12 + k).wait_recv()
        self.start(20 + k)

    def finish(self):
        for number in range(16, GATHER_COPIES):
            self.copy(number).wait_recv()
        for number in range(GATHER_COPIES):
            self.copy(number).wait_send()


class PlaneGather(Gather):
    def copy(self, number):
        spot = self.spot
        if number == 0:
            return Gather.copy(self, 0)
        if number == 1:
            source, target, device = self.block, self.area(), spot.partner(y=1)
        elif number == 2:
            source, target, device = self.block, self.area(), spot.partner(x=1)
        elif number == 3:
            source = target = self.area(y=1)
            device = spot.partner(x=1)
        elif number < 10:
            source = target = self.area(2, x=(number - 4) // 3)
            device = spot.partner(z=(number - 4) % 3 + 1)
        else:
            kind = number - 10
            z, x = (0, kind) if kind < 2 else ((kind - 2) % 3 + 1, (kind - 2) // 3)
            source = target = self.area(2, z=z, x=x)
            device = spot.partner(core=1)
        return send(source, target, self.sems, number, device)

    def y_got(self):
        self.copy(1).wait_recv()
        self.here().wait()
        self.start(3, 4, 5, 6, 10)

    def x_got(self):
        self.copy(2).wait_recv()
        self.copy(3).wait_recv()
        self.start(7, 8, 9, 11)

    def z_got(self, x):
        for k in range(3):
            self.copy(4 + 3 * x + k).wait_recv()
            self.start(12 + 3 * x + k)

    def finish(self):
        for number in range(10, 18):
            self.copy(number).wait_recv()
        for number in range(18):
            self.copy(number).wait_send()


class Move:
    PARTNERS = ((1, 0), (1, 1), (0, 1))

    def __init__(self, spot, source, target, own_target, sems, local):
        self.spot, self.source, self.target = spot, source, target
        self.own_target, self.sems, self.local = own_target, sems, local

    def own(self):
        return pltpu.make_async_copy(
            self.source(self.spot.seq), self.own_target(self.spot.seq), self.local
        )

    def copy(self, number):
        y, core = self.PARTNERS[number]
        device = self.spot.partner(y=y, core=core)
        return send(self.source(device[1]), self.target(self.spot.seq), self.sems, number, device)

    def start(self):
        self.own().start()
        for number in range(3):
            self.copy(number).start()

    def finish(self):
        self.own().wait()
        for number in range(3):
            self.copy(number).wait()


def all_partners(spot):
    return [
        spot.partner(core=1),
        spot.partner(z=1),
        spot.partner(z=2),
        spot.partner(z=3),
        spot.partner(x=1),
        spot.partner(y=1),
        spot.partner(y=1, core=1),
    ]


def row_block(ref, rows):
    return lambda number: ref.at[pl.ds(pl.multiple_of(number * rows, 16), rows), :]


def front_kernel(
    docs_ref,
    queries_ref,
    doc_cot_ref,
    query_cot_ref,
    q_shard,
    kv_shard,
    out_shard,
    up_shard,
    down_shard,
    bucket_shard,
    gain_ref,
    table_ref,
    small_bucket_ref,
    tokens_out,
    cots_out,
    w_out,
    ou_out,
    down_out,
    bucket_out,
    qkv_out,
    mix_ref,
    prob_ref,
    query_prob_ref,
    query_bucket_ref,
    x_v,
    w_v,
    qkv_v,
    bucket_v,
    bucket_in,
    qkv_own,
    qkv_theirs,
    qkv_block,
    ou_own,
    ou_theirs,
    ou_block,
    down_own,
    down_theirs,
    down_block,
    gather_sems,
    move_sems,
    local,
):
    step = pl.program_id(0)
    last = pl.num_programs(0) - 1
    spot = Spot()
    n_docs, shard_rows, width = docs_ref.shape
    doc_rows = n_docs * shard_rows
    query_rows = queries_ref.shape[0]
    heads = prob_ref.shape[0]
    head_dim = width // heads
    pairs = heads // 2
    block = prob_ref.shape[1]

    gathers = []
    for number, parts in enumerate(
        (
            (qkv_own, w_v, qkv_theirs, qkv_block),
            (ou_own, ou_out, ou_theirs, ou_block),
            (down_own, down_out, down_theirs, down_block),
        )
    ):
        kind = PlaneGather if number == 2 else Gather
        gathers.append(kind(spot, *parts, gather_sems.at[number], local.at[number]))
    g_qkv, g_ou, g_down = gathers
    token_move = Move(
        spot,
        lambda number: docs_ref.at[number],
        row_block(x_v, shard_rows),
        row_block(x_v, shard_rows),
        move_sems.at[0],
        local.at[3],
    )
    cot_move = Move(
        spot,
        lambda number: doc_cot_ref.at[number],
        row_block(cots_out, shard_rows),
        row_block(cots_out, shard_rows),
        move_sems.at[1],
        local.at[4],
    )
    query_load = pltpu.make_async_copy(
        queries_ref, x_v.at[pl.ds(doc_rows, query_rows), :], local.at[5]
    )
    cot_copy = pltpu.make_async_copy(
        query_cot_ref, cots_out.at[pl.ds(doc_rows, query_rows), :], local.at[6]
    )
    bucket_rows = row_block(bucket_v, shard_rows)
    bucket_load = pltpu.make_async_copy(bucket_shard, bucket_in, local.at[7])
    near = bucket_rows(spot.seq)
    far = bucket_rows(spot.partner(y=1)[1])
    bucket_y = send(near, near, move_sems.at[2], 0, spot.partner(y=1))
    bucket_near = send(near, near, move_sems.at[2], 1, spot.partner(core=1))
    bucket_far = send(far, far, move_sems.at[2], 2, spot.partner(core=1))
    saves = [
        pltpu.make_async_copy(x_v, tokens_out, local.at[8]),
        pltpu.make_async_copy(w_v, w_out, local.at[9]),
        pltpu.make_async_copy(qkv_v, qkv_out, local.at[10]),
        pltpu.make_async_copy(bucket_v, bucket_out, local.at[11]),
    ]
    loads = [
        pltpu.make_async_copy(q_shard, qkv_own.at[:, pl.ds(0, width)], local.at[12]),
        pltpu.make_async_copy(kv_shard, qkv_own.at[:, pl.ds(width, 2 * width)], local.at[13]),
        pltpu.make_async_copy(out_shard, ou_own.at[:, pl.ds(0, width)], local.at[14]),
        pltpu.make_async_copy(
            up_shard, ou_own.at[:, pl.ds(width, up_shard.shape[1])], local.at[15]
        ),
        pltpu.make_async_copy(down_shard, down_own, local.at[16]),
    ]

    @pl.when(step == 0)
    def _():
        for load in loads:
            load.start()
        bucket_load.start()
        query_load.start()
        token_move.own().start()
        greet(all_partners(spot))
        token_move.copy(0).start()
        for load in loads[:2]:
            load.wait()
        g_qkv.start(0)
        for load in loads[2:]:
            load.wait()
        g_ou.start(0)
        g_down.start(0)
        token_move.copy(2).start()
        g_qkv.join_end()
        g_qkv.start(1, 2, 3, 4, 8)
        g_ou.join_end()
        g_down.join_end()
        g_down.start(1, 2)
        bucket_load.wait()
        bucket_v[pl.ds(pl.multiple_of(spot.seq * shard_rows, 16), shard_rows), :] = bucket_in[
            ...
        ].astype(jnp.int16)
        size = small_bucket_ref.shape[0]
        shape = (128, size)
        picks = (
            lax.broadcasted_iota(jnp.int32, shape, 0) % size
            == lax.broadcasted_iota(jnp.int32, shape, 1)
        )
        picks = jnp.where(picks, 1.0, 0.0).astype(BFLOAT)
        numbers = small_bucket_ref[...].astype(SINGLE).astype(BFLOAT)
        spread = nt(nn(picks, numbers).astype(BFLOAT), picks).astype(jnp.int32)
        square = (128, 128)
        same = (
            lax.broadcasted_iota(jnp.int32, square, 0) // size
            == lax.broadcasted_iota(jnp.int32, square, 1) // size
        )
        query_bucket_ref[...] = jnp.where(same, spread, table_ref.shape[1] - 1)
        for k in (1, 2, 3):
            g_qkv.z_got(k)
        g_ou.start(1, 2, 3)
        token_move.copy(1).start()
        bucket_y.start()
        bucket_near.start()
        g_ou.start(4)
        for k in (0, 1, 2, 3):
            g_qkv.y_got(k)
        g_ou.start(8)
        g_down.y_got()
        for k in (0, 1, 2, 3):
            g_qkv.x_got(k)
        query_load.wait()
        g_qkv.finish()
        saves[1].start()
        token_move.finish()
        saves[0].start()

        def project_block(number, carry):
            span = pl.ds(pl.multiple_of(number * block, 16), block)
            values = x_v[span, :].astype(SINGLE)
            normed = (values * scale_of(values) * gain_ref[...][None, :]).astype(BFLOAT)
            for part in range(3):
                lanes = slice(part * width, (part + 1) * width)
                qkv_v[span, lanes] = nn(normed, w_v[:, lanes]).astype(BFLOAT)
            return carry

        blocks = (doc_rows + query_rows) // block
        third = blocks // 3
        lax.fori_loop(0, third, project_block, 0)
        g_down.x_got()
        g_ou.z_got(1)
        lax.fori_loop(third, 2 * third, project_block, 0)
        g_ou.z_got(2)
        lax.fori_loop(2 * third, blocks, project_block, 0)
        g_ou.z_got(3)
        saves[2].start()
        cot_move.start()
        cot_copy.start()
        bucket_y.wait_recv()
        bucket_far.start()

        def query_step(number, carry):
            span = pl.ds(pl.multiple_of(doc_rows + number * 128, 16), 128)
            softs, mixed = query_block(
                qkv_v[span, :width],
                qkv_v[span, width : 2 * width],
                qkv_v[span, 2 * width :],
                table_ref,
                query_bucket_ref[...],
                heads,
            )
            mix_ref[span, :] = mixed
            for head, soft in enumerate(softs):
                query_prob_ref[head, pl.ds(pl.multiple_of(number * 128, 16), 128), :] = soft
            return carry

        lax.fori_loop(0, query_rows // 128, query_step, 0)
        g_ou.y_got(0)
        bucket_near.wait()
        bucket_far.wait()
        bucket_y.wait_send()
        saves[3].start()

    def tick(when, name, k):
        @pl.when(step == when)
        def _():
            getattr(g_ou, name)(k)

    tick(1, "y_got", 1)
    tick(2, "y_got", 2)
    tick(2, "y_got", 3)
    tick(3, "x_got", 0)
    tick(4, "x_got", 1)
    tick(4, "x_got", 2)

    @pl.when(step == last)
    def _():
        g_down.z_got(0)

    @pl.when(step > 0)
    def _():
        span = pl.ds(pl.multiple_of((step - 1) * block, 16), block)

        def pair(number, carry):
            lanes = pair_lanes(number, head_dim)
            mix_ref[span, lanes] = attend_pair(
                qkv_v[span, lanes],
                qkv_v[:doc_rows, pair_lanes(number, head_dim, width)],
                qkv_v[:doc_rows, pair_lanes(number, head_dim, 2 * width)],
                table_ref,
                bucket_v,
                pl.multiple_of((step - 1) * block, 16),
                prob_ref,
                number,
                head_dim,
            )
            return carry

        lax.fori_loop(0, pairs, pair, 0, unroll=True)

    @pl.when(step == last)
    def _():
        g_ou.x_got(3)
        g_down.z_got(1)
        g_ou.finish()
        g_down.finish()
        cot_move.finish()
        cot_copy.wait()
        for save in saves:
            save.wait()


def gather_scratch(rows, columns):
    return [
        pltpu.VMEM((rows, columns), BFLOAT),
        pltpu.VMEM((rows, columns // 2), BFLOAT),
        pltpu.VMEM((2 * rows, columns // 2), BFLOAT),
    ]


def front(docs, queries, doc_cot, query_cot, weights, buckets, gain, table, query_buckets, heads):
    n_docs, shard_rows, width = docs.shape
    doc_rows = n_docs * shard_rows
    query_rows = queries.shape[0]
    rows = doc_rows + query_rows
    keys = buckets.shape[1]
    block = 256
    steps = doc_rows // block
    anywhere = pl.BlockSpec(memory_space=pl.ANY)
    w_q, w_kv, w_out, w_up, w_down = (weight.shape for weight in weights)
    shards = [
        (w_q[0], w_q[1] + w_kv[1]),
        (w_out[0], w_out[1] + w_up[1]),
        w_down,
    ]
    scratch = []
    for shard in shards:
        scratch += gather_scratch(*shard)
    return pl.pallas_call(
        front_kernel,
        grid=(steps + 1,),
        in_specs=[anywhere] * 10 + [whole((width,)), whole(table.shape), whole(query_buckets.shape)],
        out_specs=[anywhere] * 7
        + [
            whole((rows, width)),
            pl.BlockSpec((heads, block, keys), lambda i: (0, jnp.maximum(i - 1, 0), 0)),
            whole((heads, query_rows, 128)),
            whole((128, 128)),
        ],
        out_shape=[
            jax.ShapeDtypeStruct((rows, width), BFLOAT),
            jax.ShapeDtypeStruct((rows, width), BFLOAT),
            *[jax.ShapeDtypeStruct((shard[0] * 32, shard[1]), BFLOAT) for shard in shards],
            jax.ShapeDtypeStruct((keys, keys), jnp.int16),
            jax.ShapeDtypeStruct((rows, 3 * width), BFLOAT),
            jax.ShapeDtypeStruct((rows, width), BFLOAT),
            jax.ShapeDtypeStruct((heads, doc_rows, keys), BFLOAT),
            jax.ShapeDtypeStruct((heads, query_rows, 128), BFLOAT),
            jax.ShapeDtypeStruct((128, 128), jnp.int32),
        ],
        scratch_shapes=[
            pltpu.VMEM((rows, width), BFLOAT),
            pltpu.VMEM((width, 3 * width), BFLOAT),
            pltpu.VMEM((rows, 3 * width), BFLOAT),
            pltpu.VMEM((keys, keys), jnp.int16),
            pltpu.VMEM(buckets.shape, jnp.int32),
            *scratch,
            pltpu.SemaphoreType.DMA((3, 2, GATHER_COPIES)),
            pltpu.SemaphoreType.DMA((3, 2, 3)),
            pltpu.SemaphoreType.DMA((20,)),
        ],
        compiler_params=pltpu.CompilerParams(
            collective_id=0, has_side_effects=True, vmem_limit_bytes=VMEM_LIMIT
        ),
        cost_estimate=cost(6 * rows * width * width, 100 << 20),
    )(docs, queries, doc_cot, query_cot, *weights, buckets, gain, table, query_buckets)


class Scatter:
    Z_ORDER = (3, 2, 1, 0)

    def __init__(self, spot, away, buffers, sems):
        self.spot, self.away, self.sems = spot, away, sems
        self.held, self.core_in, self.x_in, self.y_in, self.z_in, self.tail, self.tail_in = buffers
        self.half = self.held.shape[1]
        self.rows = self.held.shape[0] // 16

    def span(self, **bits):
        return pl.ds(pl.multiple_of(self.spot.chip(**bits) * self.rows, 16), self.rows)

    def slot(self, number):
        return pl.ds(number * self.rows, self.rows)

    def copy(self, number):
        spot = self.spot
        if number == 0:
            source, target, device = self.away, self.core_in, spot.partner(core=1)
        elif number < 9:
            index = number - 1
            source = self.held.at[self.span(z=self.Z_ORDER[index // 2], x=1, y=1 - index % 2), :]
            target, device = self.x_in.at[self.slot(index), :], spot.partner(x=1)
        elif number < 13:
            index = number - 9
            source = self.held.at[self.span(z=self.Z_ORDER[index], y=1), :]
            target, device = self.y_in.at[self.slot(index), :], spot.partner(y=1)
        elif number < 16:
            index = number - 13
            source = self.held.at[self.span(z=self.Z_ORDER[index]), :]
            target = self.z_in.at[self.slot(index), :]
            device = spot.partner(z=self.Z_ORDER[index])
        else:
            part = self.rows // 2
            theirs = pl.ds(pl.multiple_of((1 - spot.core) * part, 8), part)
            source, target, device = self.tail.at[theirs, :], self.tail_in, spot.partner(core=1)
        return send(source, target, self.sems, number, device)

    def add(self, span, others):
        total = self.held[span, :].astype(SINGLE) + self.core_in[span, :].astype(SINGLE)
        for ref, place in others:
            total = total + ref[place, :].astype(SINGLE)
        return total

    def core_end(self):
        self.copy(0).wait_recv()

    def x_step(self, index):
        span = self.span(z=self.Z_ORDER[index // 2], x=1, y=1 - index % 2)
        self.held[span, :] = self.add(span, []).astype(BFLOAT)
        self.copy(1 + index).start()

    def y_step(self, index):
        self.copy(1 + 2 * index).wait_recv()
        span = self.span(z=self.Z_ORDER[index], y=1)
        total = self.add(span, [(self.x_in, self.slot(2 * index))])
        self.held[span, :] = total.astype(BFLOAT)
        self.copy(9 + index).start()

    def here(self, index):
        self.copy(2 + 2 * index).wait_recv()
        self.copy(9 + index).wait_recv()
        span = self.span(z=self.Z_ORDER[index])
        others = [(self.x_in, self.slot(2 * index + 1)), (self.y_in, self.slot(index))]
        return span, self.add(span, others)

    def z_step(self, index):
        span, total = self.here(index)
        self.held[span, :] = total.astype(BFLOAT)
        self.copy(13 + index).start()

    def tail_start(self):
        _, total = self.here(3)
        for index in range(3):
            self.copy(13 + index).wait_recv()
            total = total + self.z_in[self.slot(index), :].astype(SINGLE)
        self.tail[...] = total
        self.copy(16).start()

    def finish(self):
        part = self.rows // 2
        low = self.spot.core == 0
        mine = jnp.where(low, self.tail[:part, :], self.tail[part:, :])
        self.copy(16).wait_recv()
        other = self.tail_in[...]
        for number in range(COPIES):
            self.copy(number).wait_send()
        return jnp.where(low, mine, other), jnp.where(low, other, mine)


def scatter_scratch(rows, columns):
    half, part = columns // 2, rows // 16
    return [
        pltpu.VMEM((rows, half), BFLOAT),
        pltpu.VMEM((rows, half), BFLOAT),
        pltpu.VMEM((8 * part, half), BFLOAT),
        pltpu.VMEM((4 * part, half), BFLOAT),
        pltpu.VMEM((3 * part, half), BFLOAT),
        pltpu.VMEM((part, half), SINGLE),
        pltpu.VMEM((part // 2, half), SINGLE),
    ]


def half_of(ref, core):
    half = ref.shape[1] // 2
    return ref.at[:, pl.ds(pl.multiple_of(core * half, 128), half)]


def middle_kernel(
    x_in,
    mix_in,
    dy_in,
    gain_ref,
    wo_ref,
    wu_ref,
    wd_ref,
    y_out,
    query_out,
    dh_out,
    da_out,
    rest_ref,
    down_ref,
    near_ref,
    gg_ref,
    h1,
    n2,
    y_acc,
    act_v,
    du_v,
    dh_ref,
    x_ref,
    mix_ref,
    dy_ref,
    *rest,
):
    fulls, downs, rest = rest[0], rest[1], rest[2:]
    step = pl.program_id(0)
    last = pl.num_programs(0) - 1
    spot = Spot()
    rows, width = x_ref.shape
    docs = y_out.shape[0]
    gain = gain_ref[...][None, :]
    block = 512 if rows % 512 == 0 else 256
    spans = [slice(start, start + block) for start in range(0, rows, block)]
    sems, local = rest[-2:]
    pieces = []
    for number in range(3):
        full, core = fulls.at[number], spot.core
        buffers = [half_of(full, core), *rest[6 * number : 6 * number + 6]]
        pieces.append(Scatter(spot, half_of(full, 1 - core), buffers, sems.at[number]))

    loads = [
        pltpu.make_async_copy(source, target, local.at[8 + number])
        for number, (source, target) in enumerate(
            ((x_in, x_ref), (mix_in, mix_ref), (dy_in, dy_ref))
        )
    ]
    save_out = pltpu.make_async_copy(downs.at[0], rest_ref.at[:, pl.ds(0, width)], local.at[0])
    save_up = pltpu.make_async_copy(
        fulls.at[3], rest_ref.at[:, pl.ds(width, width)], local.at[3]
    )

    def save_down(chunk):
        target = down_ref.at[pl.ds(chunk * width, width), :]
        return pltpu.make_async_copy(downs.at[chunk % 2], target, local.at[1 + chunk % 2])

    leaving = [
        pltpu.make_async_copy(du_v.at[pl.ds(0, docs), :], y_out, local.at[4]),
        pltpu.make_async_copy(du_v.at[pl.ds(docs, rows - docs), :], query_out, local.at[7]),
        pltpu.make_async_copy(dh_ref, dh_out, local.at[5]),
        pltpu.make_async_copy(n2, da_out, local.at[6]),
    ]

    def at(when, chunk, action, also=True):
        piece = pieces[chunk]

        @pl.when((step == when) & also)
        def _():
            if action == "x":
                piece.core_end()
                for index in range(8):
                    piece.x_step(index)
            elif action == "y":
                for index in range(4):
                    piece.y_step(index)
            elif action == "z":
                for index in range(3):
                    piece.z_step(index)
            else:
                piece.tail_start()

    @pl.when(step == 0)
    def _():
        for copy in loads:
            copy.start()
        greet(all_partners(spot))
        loads[0].wait()
        loads[1].wait()
        for span in spans:
            residual = x_ref[span, :].astype(SINGLE) + nn(mix_ref[span, :], wo_ref[...])
            h1[span, :] = residual
            y_acc[span, :] = residual
            n2[span, :] = (residual * scale_of(residual) * gain).astype(BFLOAT)
            dh_ref[span, :] = jnp.zeros_like(residual)
        loads[2].wait()

    def part(number, carry):
        then = number == 1
        for chunk in range(3):
            at(chunk + 1, chunk, "x", also=then)
        for chunk in range(2):
            at(chunk + 2, chunk, "tail", also=then)
        span = pl.ds(pl.multiple_of(number * block, 16), block)
        pre = nn(n2[span, :], wu_ref[...])
        grad_hidden = nt(dy_ref[span, :], wd_ref[...])
        square = pre * pre
        tanh = jnp.tanh(pre * (GELU_A + (GELU_A * GELU_B) * square))
        half = 0.5 + 0.5 * tanh
        act = pre * half
        slope = half + act * (1.0 - tanh) * (GELU_A + (3.0 * GELU_A * GELU_B) * square)
        act_low = act.astype(BFLOAT)
        grad_pre = (grad_hidden * slope).astype(BFLOAT)
        act_v[span, :] = act_low
        du_v[span, :] = grad_pre
        y_acc[span, :] += nn(act_low, wd_ref[...])
        dh_ref[span, :] += nt(grad_pre, wu_ref[...])
        return carry

    lax.fori_loop(0, rows // block, part, 0)
    for chunk in range(3):
        at(chunk + 1, chunk, "y")

    for chunk in (2, 3):

        @pl.when(step == chunk)
        def _():
            save_down(chunk - 2).wait()

    fulls[step] = tn(n2[...], du_v[...]).astype(BFLOAT)
    downs[step % 2] = tn(act_v[...], dy_ref[...]).astype(BFLOAT)
    for chunk in range(4):

        @pl.when(step == chunk)
        def _():
            save_down(chunk).start()
            if chunk < 3:
                pieces[chunk].copy(0).start()

    for chunk in range(3):
        at(chunk + 1, chunk, "z")

    @pl.when(step == last)
    def _():
        save_up.start()
        total = jnp.zeros_like(gain)
        for span in spans:
            du_v[span, :] = y_acc[span, :].astype(BFLOAT)
        leaving[0].start()
        leaving[1].start()
        for span in spans:
            residual = h1[span, :]
            scale = scale_of(residual)
            grad_second = dh_ref[span, :]
            total = total + jnp.sum(grad_second * residual * scale, axis=0, keepdims=True)
            grad_res = dy_ref[span, :].astype(SINGLE) + norm_back(
                residual, scale, grad_second * gain
            )
            dh_ref[span, :] = grad_res
            grad_low = grad_res.astype(BFLOAT)
            act_v[span, :] = grad_low
            n2[span, :] = nt(grad_low, wo_ref[...]).astype(BFLOAT)
        gg_ref[...] = total
        leaving[2].start()
        leaving[3].start()
        save_down(2).wait()
        downs[0] = tn(mix_ref[...], act_v[...]).astype(BFLOAT)
        save_out.start()
        pieces[2].tail_start()
        for number, piece in enumerate(pieces):
            left, right = piece.finish()
            base = number * width
            near_ref[:, base : base + width // 2] = left
            near_ref[:, base + width // 2 : base + width] = right
        save_out.wait()
        save_up.wait()
        save_down(3).wait()
        for copy in leaving:
            copy.wait()


def middle(tokens, mixture, cotangent, gain, w_out_up, w_down, doc_rows):
    rows, width = tokens.shape
    hidden = w_down.shape[0]
    chunks = hidden // width
    anywhere = pl.BlockSpec(memory_space=pl.ANY)
    square = (width, width)
    scratch = []
    for _ in range(3):
        scratch += scatter_scratch(*square)[1:]
    return pl.pallas_call(
        middle_kernel,
        grid=(chunks,),
        in_specs=[
            anywhere,
            anywhere,
            anywhere,
            whole((width,)),
            whole(square),
            pl.BlockSpec(square, lambda i: (0, 1 + i)),
            pl.BlockSpec(square, lambda i: (i, 0)),
        ],
        out_specs=[
            anywhere,
            anywhere,
            anywhere,
            anywhere,
            anywhere,
            anywhere,
            whole((width // 32, 3 * width)),
            whole((1, width)),
        ],
        out_shape=[
            jax.ShapeDtypeStruct((doc_rows, width), BFLOAT),
            jax.ShapeDtypeStruct((rows - doc_rows, width), BFLOAT),
            jax.ShapeDtypeStruct((rows, width), SINGLE),
            jax.ShapeDtypeStruct((rows, width), BFLOAT),
            jax.ShapeDtypeStruct((width, 2 * width), BFLOAT),
            jax.ShapeDtypeStruct((hidden, width), BFLOAT),
            jax.ShapeDtypeStruct((width // 32, 3 * width), SINGLE),
            jax.ShapeDtypeStruct((1, width), SINGLE),
        ],
        scratch_shapes=[
            pltpu.VMEM((rows, width), SINGLE),
            pltpu.VMEM((rows, width), BFLOAT),
            pltpu.VMEM((rows, width), SINGLE),
            pltpu.VMEM((rows, width), BFLOAT),
            pltpu.VMEM((rows, width), BFLOAT),
            pltpu.VMEM((rows, width), SINGLE),
            pltpu.VMEM((rows, width), BFLOAT),
            pltpu.VMEM((rows, width), BFLOAT),
            pltpu.VMEM((rows, width), BFLOAT),
            pltpu.VMEM((chunks, *square), BFLOAT),
            pltpu.VMEM((2, *square), BFLOAT),
            *scratch,
            pltpu.SemaphoreType.DMA((3, 2, COPIES)),
            pltpu.SemaphoreType.DMA((11,)),
        ],
        compiler_params=pltpu.CompilerParams(
            collective_id=3, has_side_effects=True, vmem_limit_bytes=VMEM_LIMIT
        ),
        cost_estimate=cost(2 * rows * width * (6 * hidden + 3 * width), 100 << 20),
    )(tokens, mixture, cotangent, gain, w_out_up, w_out_up, w_down)


def back_kernel(
    labels,
    doc_steps,
    q_ref,
    k_ref,
    v_ref,
    query_k_ref,
    query_v_ref,
    da_ref,
    mix_ref,
    prob_ref,
    query_prob_ref,
    query_bucket_ref,
    grad_ref,
    grad_down_ref,
    y_ref,
    near_ref,
    dq_ref,
    dkv_ref,
    ds_ref,
    sums_ref,
    shard_ref,
    down_ref,
    docs_ref,
    dk_acc,
    dv_acc,
    ds_keep,
    *rest,
):
    sems, move_sems, local = rest[14:]
    step = pl.program_id(0)
    last = pl.num_programs(0) - 1
    spot = Spot()
    rows, width = q_ref.shape
    pairs = prob_ref.shape[0] // 2
    keys = k_ref.shape[0]
    heads = query_prob_ref.shape[0]
    head_dim = width // heads
    grads = (grad_ref, grad_down_ref)
    scatters = [
        Scatter(spot, half_of(grad, 1 - spot.core), rest[7 * i : 7 * i + 7], sems.at[i])
        for i, grad in enumerate(grads)
    ]
    loads = [
        pltpu.make_async_copy(half_of(grad, spot.core), scatter.held, local.at[i])
        for i, (grad, scatter) in enumerate(zip(grads, scatters))
    ]
    move = Move(
        spot,
        row_block(y_ref, docs_ref.shape[1]),
        lambda number: docs_ref.at[number],
        lambda number: docs_ref.at[number],
        move_sems,
        local.at[2],
    )

    @pl.when(step == 0)
    def _():
        greet(all_partners(spot))
        for scatter, load in zip(scatters, loads):
            scatter.copy(0).start()
            load.start()
        move.start()
        dk_acc[...] = jnp.zeros_like(dk_acc)
        dv_acc[...] = jnp.zeros_like(dv_acc)
        ds_keep[...] = jnp.zeros_like(ds_keep)

    @pl.when(step == 1)
    def _():
        loads[0].wait()
        scatters[0].core_end()
        for index in range(8):
            scatters[0].x_step(index)

    @pl.when(step == 2)
    def _():
        loads[1].wait()
        scatters[1].core_end()
        for index in range(8):
            scatters[1].x_step(index)

    def at(when, number, *actions):
        @pl.when(step == when)
        def _():
            for name, index in actions:
                getattr(scatters[number], name)(index)

    at(4, 0, *[("y_step", index) for index in range(4)])
    at(6, 0, *[("z_step", index) for index in range(3)])
    at(5, 1, ("y_step", 0))
    at(7, 1, ("z_step", 0), ("y_step", 1))
    at(8, 1, ("z_step", 1), ("y_step", 2))
    at(9, 1, ("z_step", 2), ("y_step", 3))

    @pl.when(step == last)
    def _():
        for scatter in scatters:
            scatter.tail_start()

    @pl.when(step < doc_steps)
    def _():
        def pair(number, carry):
            spread = (step % 2) * pairs + number
            lanes = pair_lanes(spread, head_dim)
            dq, dk, dv, kept = attend_back(
                q_ref[:, lanes],
                k_ref[:, lanes],
                v_ref[:, lanes],
                da_ref[:, lanes],
                mix_ref[:, lanes],
                [prob_ref[2 * number], prob_ref[2 * number + 1]],
                head_dim,
            )
            ds_ref[2 * number] = kept[0]
            ds_ref[2 * number + 1] = kept[1]
            dq_ref[:, lanes] = dq.astype(BFLOAT)
            dk_acc[:, lanes] += dk
            dv_acc[:, lanes] += dv
            return carry

        lax.fori_loop(0, pairs, pair, 0, unroll=True)

    @pl.when(step == doc_steps - 1)
    def _():
        dkv_ref[:keys, :width] = dk_acc[...].astype(BFLOAT)
        dkv_ref[:keys, width:] = dv_acc[...].astype(BFLOAT)

    @pl.when(step >= doc_steps)
    def _():
        def part(number, carry):
            span = pl.ds(pl.multiple_of(number * 128, 128), 128)
            place = pl.ds(pl.multiple_of(keys + (step - doc_steps) * rows + number * 128, 16), 128)
            dq, dk, dv, kept = query_back_block(
                q_ref[span, :],
                query_k_ref[span, :],
                query_v_ref[span, :],
                da_ref[span, :],
                mix_ref[span, :],
                [query_prob_ref[head, span, :] for head in range(heads)],
                head_dim,
            )
            for head in range(heads):
                ds_keep[head] += kept[head].astype(SINGLE)
            for pair in range(heads // 2):
                lanes = slice(pair * 2 * head_dim, (pair + 1) * 2 * head_dim)
                dq_ref[span, lanes] = dq[pair]
                dkv_ref[place, lanes] = dk[pair]
                dkv_ref[place, width + lanes.start : width + lanes.stop] = dv[pair]
            return carry

        lax.fori_loop(0, rows // 128, part, 0)

    @pl.when(step == last)
    def _():
        total = jnp.zeros_like(sums_ref)
        for index in range(8):
            some = slice(index * 16, (index + 1) * 16)
            terms = ds_keep[:, some, :].reshape(heads * 16, 128)
            high = terms.astype(BFLOAT)
            low = (terms - high.astype(SINGLE)).astype(BFLOAT)
            onehot = bucket_onehot(query_bucket_ref[some, :], labels)
            total = total + nt(onehot, high) + nt(onehot, low)
        sums_ref[...] = total

    @pl.when(step == last)
    def _():
        left, right = scatters[0].finish()
        shard_ref[:, :width] = left
        shard_ref[:, width : 4 * width] = near_ref[...]
        shard_ref[:, 4 * width :] = right
        left, right = scatters[1].finish()
        down_ref[:, : width // 2] = left
        down_ref[:, width // 2 :] = right
        move.finish()


def back(qkv, da_rows, mixture, probs, query_probs, query_buckets, grads, outputs, near, n_docs, labels):
    rows, width = da_rows.shape
    heads, doc_rows, keys = probs.shape
    block = 256
    doc_steps = 2 * doc_rows // block
    doc_blocks = doc_rows // block
    steps = doc_steps + (rows - doc_rows) // block
    half = heads // 2

    def row(i):
        return jnp.where(i < doc_steps, i // 2, i - doc_steps + doc_blocks)

    def doc(i):
        clipped = jnp.minimum(i, doc_steps - 1)
        return (clipped % 2, clipped // 2, 0)

    def query(i):
        return jnp.maximum(i, doc_steps) - doc_steps

    anywhere = pl.BlockSpec(memory_space=pl.ANY)
    along = pl.BlockSpec((block, width), lambda i: (row(i), 0))
    once = pl.Buffered(1)
    return pl.pallas_call(
        functools.partial(back_kernel, labels, doc_steps),
        grid=(steps,),
        in_specs=[
            along,
            pl.BlockSpec((keys, width), lambda i: (0, 1), pipeline_mode=once),
            pl.BlockSpec((keys, width), lambda i: (0, 2), pipeline_mode=once),
            pl.BlockSpec((block, width), lambda i: (query(i) + doc_blocks, 1)),
            pl.BlockSpec((block, width), lambda i: (query(i) + doc_blocks, 2)),
            along,
            along,
            pl.BlockSpec((half, block, keys), doc),
            pl.BlockSpec((heads, block, 128), lambda i: (0, query(i), 0)),
            whole(query_buckets.shape),
            anywhere,
            anywhere,
            anywhere,
            whole(near.shape),
        ],
        out_specs=[
            along,
            whole((rows, 2 * width)),
            pl.BlockSpec((half, block, keys), doc),
            whole((16 * labels, heads * 16)),
            whole((near.shape[0], 5 * width)),
            whole((grads[1].shape[0] // 32, width)),
            anywhere,
        ],
        out_shape=[
            jax.ShapeDtypeStruct((rows, width), BFLOAT),
            jax.ShapeDtypeStruct((rows, 2 * width), BFLOAT),
            jax.ShapeDtypeStruct(probs.shape, BFLOAT),
            jax.ShapeDtypeStruct((16 * labels, heads * 16), SINGLE),
            jax.ShapeDtypeStruct((near.shape[0], 5 * width), SINGLE),
            jax.ShapeDtypeStruct((grads[1].shape[0] // 32, width), SINGLE),
            jax.ShapeDtypeStruct((n_docs, doc_rows // n_docs, width), BFLOAT),
        ],
        scratch_shapes=[
            pltpu.VMEM((keys, width), SINGLE),
            pltpu.VMEM((keys, width), SINGLE),
            pltpu.VMEM((heads, 128, 128), SINGLE),
            *scatter_scratch(*grads[0].shape),
            *scatter_scratch(*grads[1].shape),
            pltpu.SemaphoreType.DMA((2, 2, COPIES)),
            pltpu.SemaphoreType.DMA((2, 3)),
            pltpu.SemaphoreType.DMA((3,)),
        ],
        compiler_params=pltpu.CompilerParams(
            collective_id=1, has_side_effects=True, vmem_limit_bytes=VMEM_LIMIT
        ),
        cost_estimate=cost(70 * doc_rows * keys * width, 100 << 20),
    )(
        qkv,
        qkv,
        qkv,
        qkv,
        qkv,
        da_rows,
        mixture,
        probs,
        query_probs,
        query_buckets,
        *grads,
        outputs,
        near,
    )


class Total:
    def __init__(self, spot, slots, sems):
        self.spot, self.slots, self.sems = spot, slots, sems

    def rounds(self):
        spot = self.spot
        near = [(x, y, core) for x in (0, 1) for y in (0, 1) for core in (0, 1)][1:]
        return (
            (
                (spot.x * 2 + spot.y) * 2 + spot.core,
                8,
                [spot.partner(x=x, y=y, core=core) for x, y, core in near],
            ),
            (spot.z, 4, [spot.partner(z=k) for k in (1, 2, 3)]),
        )

    def copies(self, index):
        base = 8 * index
        place, count, partners = self.rounds()[index]
        mine = self.slots.at[base + place]
        return [
            send(mine, mine, self.sems.at[index], number, device)
            for number, device in enumerate(partners)
        ]

    def begin(self, index, values):
        self.slots[8 * index + self.rounds()[index][0]] = values
        for copy in self.copies(index):
            copy.start()

    def end(self, index):
        for copy in self.copies(index):
            copy.wait_recv()
        values = self.slots[8 * index]
        for other in range(1, self.rounds()[index][1]):
            values = values + self.slots[8 * index + other]
        for copy in self.copies(index):
            copy.wait_send()
        return values


def leave_kernel(
    labels,
    x_in,
    gain_ref,
    dq_in,
    dkv_in,
    dh_in,
    w_in,
    ds_ref,
    bucket_ref,
    query_sums_ref,
    ff_ref,
    found_ref,
    out_ref,
    docs_ref,
    query_dx_ref,
    total_ref,
    normed,
    away,
    low,
    high,
    sums,
    gain_sum,
    slots,
    dh_ref,
    w_ref,
    x_ref,
    dq_ref,
    dkv_ref,
    *rest,
):
    buffers, (sems, move_sems, total_sems, local) = rest[:7], rest[7:]
    step = pl.program_id(0)
    last = pl.num_programs(0) - 1
    spot = Spot()
    rows, width = x_ref.shape
    heads = ds_ref.shape[0]
    doc_rows = low.shape[0]
    block = doc_rows // 4
    scatter = Scatter(spot, away, buffers, sems)
    half = scatter.half
    move = Move(
        spot,
        row_block(low, block),
        lambda number: docs_ref.at[number],
        lambda number: docs_ref.at[number],
        move_sems,
        local.at[0],
    )
    query_copy = pltpu.make_async_copy(high, query_dx_ref, local.at[1])

    def quarter(number):
        device, rows = spot.partner(y=1, core=1), block // 4
        start = pl.multiple_of(device[1] * block + number * rows, 16)
        return send(
            low.at[pl.ds(start, rows), :],
            docs_ref.at[spot.seq, pl.ds(number * rows, rows), :],
            move_sems,
            3 + number,
            device,
        )

    soon = [
        pltpu.make_async_copy(x_in, x_ref, local.at[4]),
        pltpu.make_async_copy(dq_in, dq_ref, local.at[5]),
        pltpu.make_async_copy(dkv_in, dkv_ref, local.at[6]),
    ]
    late = [
        pltpu.make_async_copy(dh_in, dh_ref, local.at[2]),
        pltpu.make_async_copy(w_in, w_ref, local.at[3]),
    ]

    @pl.when(step == 0)
    def _():
        for copy in soon + late:
            copy.start()
        more = [spot.partner(x=1, y=y, core=core) for y, core in ((0, 1), (1, 0), (1, 1))]
        greet(all_partners(spot) + more)
        gain = gain_ref[...][None, :]
        sums[...] = query_sums_ref[...]
        gain_sum[...] = jnp.zeros_like(gain_sum)

        def norm_block(number, carry):
            span = pl.ds(pl.multiple_of(number * block, 16), block)
            values = x_ref[span, :].astype(SINGLE)
            normed[span, :] = (values * scale_of(values) * gain).astype(BFLOAT)
            return carry

        soon[0].wait()
        lax.fori_loop(0, rows // block, norm_block, 0)
        soon[1].wait()
        soon[2].wait()

        def product(core, into):
            part = half // 3

            for number in range(3):
                spot_out = slice(number * part, (number + 1) * part)
                start = core * half + number * part

                def from_q():
                    lanes = pl.ds(pl.multiple_of(start, 128), part)
                    into[:, spot_out] = tn(normed[...], dq_ref[:, lanes]).astype(BFLOAT)

                def from_kv():
                    lanes = pl.ds(pl.multiple_of(start - width, 128), part)
                    into[:, spot_out] = tn(normed[...], dkv_ref[:, lanes]).astype(BFLOAT)

                pl.when(start < width)(from_q)
                pl.when(start >= width)(from_kv)

        product(1 - spot.core, away)
        scatter.copy(0).start()
        product(spot.core, scatter.held)
        scatter.core_end()
        for index in range(8):
            scatter.x_step(index)

        def grad_block(start, into, place):
            span = pl.ds(pl.multiple_of(start, 16), block)
            values = x_ref[span, :].astype(SINGLE)
            scale = scale_of(values)
            grad = nt(dq_ref[span, :], w_ref[:, :width])
            grad = grad + nt(dkv_ref[span, :width], w_ref[:, width : 2 * width])
            grad = grad + nt(dkv_ref[span, width:], w_ref[:, 2 * width :])
            gain_sum[...] += jnp.sum(grad * values * scale, axis=0, keepdims=True)
            dx = dh_ref[span, :] + norm_back(values, scale, grad * gain)
            into[place, :] = dx.astype(into.dtype)

        for copy in late:
            copy.wait()
        for number in range(3):
            y, core = Move.PARTNERS[number]
            start = spot.partner(y=y, core=core)[1] * block
            grad_block(start, low, pl.ds(pl.multiple_of(start, 16), block))
            if number != 1:
                move.copy(number).start()
        start = spot.seq * block
        grad_block(start, low, pl.ds(pl.multiple_of(start, 16), block))
        move.own().start()
        for number in range((rows - doc_rows) // block):
            grad_block(
                doc_rows + number * block, high, pl.ds(number * block, block)
            )
        query_copy.start()

    def at(when, name, index):
        @pl.when(step == when)
        def _():
            getattr(scatter, name)(index)

    at(1, "y_step", 0)
    at(2, "y_step", 1)
    at(3, "z_step", 0)
    at(3, "y_step", 2)
    at(4, "z_step", 1)
    at(4, "y_step", 3)
    at(5, "z_step", 2)

    for number in range(4):

        @pl.when(step == number + 2)
        def _():
            quarter(number).start()

    @pl.when(step > 0)
    def _():
        total = sums[...]
        for number in range(ds_ref.shape[1] // 16):
            span = slice(number * 16, (number + 1) * 16)
            grad_rows = ds_ref[:, span, :].reshape(heads * 16, ds_ref.shape[2])
            total = total + bucket_products(bucket_ref[span, :], grad_rows, labels)
        sums[...] = total

    @pl.when(step == last)
    def _():
        shape = sums.shape
        same = (
            lax.broadcasted_iota(jnp.int32, shape, 0) // labels
            == lax.broadcasted_iota(jnp.int32, shape, 1) % 16
        )
        kept = jnp.where(same, sums[...], 0.0)
        folded = kept[:labels]
        for index in range(1, 16):
            folded = folded + kept[index * labels : (index + 1) * labels]
        pick_shape = (heads * 16, 128)
        pick = (
            lax.broadcasted_iota(jnp.int32, pick_shape, 0) // 16
            == lax.broadcasted_iota(jnp.int32, pick_shape, 1)
        )
        bias = jnp.dot(
            folded,
            jnp.where(pick, 1.0, 0.0),
            preferred_element_type=SINGLE,
            precision=lax.Precision.HIGHEST,
        )
        wide = width // 128
        lines = [gain_sum[:, r * 128 : (r + 1) * 128] for r in range(wide)]
        lines += [ff_ref[:, r * 128 : (r + 1) * 128] for r in range(wide)]
        lines += [jnp.full((slots.shape[1] - labels - 2 * wide, 128), found_ref[0, 0])]
        total = Total(spot, slots, total_sems)
        total.begin(0, jnp.concatenate(lines + [bias], 0))
        scatter.tail_start()
        total.begin(1, total.end(0))
        left, right = scatter.finish()
        out_ref[:, :half] = left
        out_ref[:, half:] = right
        move.own().wait()
        move.copy(0).wait()
        move.copy(2).wait()
        for number in range(4):
            quarter(number).wait()
        query_copy.wait()
        total_ref[...] = total.end(1)


def leave(
    tokens, gain, dq, dkv, grad_res, w_qkv, ds, buckets, query_sums, grad_ff, found, n_docs, labels
):
    rows, width = tokens.shape
    heads, doc_rows, keys = ds.shape
    columns = 3 * width
    block = 128
    lines = -(-(2 * width // 128 + 1) // 8) * 8 + labels
    anywhere = pl.BlockSpec(memory_space=pl.ANY)
    return pl.pallas_call(
        functools.partial(leave_kernel, labels),
        grid=(1 + doc_rows // block,),
        in_specs=[
            anywhere,
            whole((width,)),
            anywhere,
            anywhere,
            anywhere,
            anywhere,
            pl.BlockSpec((heads, block, keys), lambda i: (0, jnp.maximum(i - 1, 0), 0)),
            pl.BlockSpec((block, keys), lambda i: (jnp.maximum(i - 1, 0), 0)),
            whole(query_sums.shape),
            whole((1, width)),
            pl.BlockSpec(memory_space=pltpu.SMEM),
        ],
        out_specs=[whole((width // 32, columns)), anywhere, anywhere, whole((lines, 128))],
        out_shape=[
            jax.ShapeDtypeStruct((width // 32, columns), SINGLE),
            jax.ShapeDtypeStruct((n_docs, doc_rows // n_docs, width), BFLOAT),
            jax.ShapeDtypeStruct((rows - doc_rows, width), SINGLE),
            jax.ShapeDtypeStruct((lines, 128), SINGLE),
        ],
        scratch_shapes=[
            pltpu.VMEM((rows, width), BFLOAT),
            pltpu.VMEM((width, columns // 2), BFLOAT),
            pltpu.VMEM((doc_rows, width), BFLOAT),
            pltpu.VMEM((rows - doc_rows, width), SINGLE),
            pltpu.VMEM(query_sums.shape, SINGLE),
            pltpu.VMEM((1, width), SINGLE),
            pltpu.VMEM((12, lines, 128), SINGLE),
            pltpu.VMEM((rows, width), SINGLE),
            pltpu.VMEM(w_qkv.shape, BFLOAT),
            pltpu.VMEM((rows, width), BFLOAT),
            pltpu.VMEM((rows, width), BFLOAT),
            pltpu.VMEM((rows, 2 * width), BFLOAT),
            *scatter_scratch(width, columns),
            pltpu.SemaphoreType.DMA((2, COPIES)),
            pltpu.SemaphoreType.DMA((2, 7)),
            pltpu.SemaphoreType.DMA((2, 2, 7)),
            pltpu.SemaphoreType.DMA((7,)),
        ],
        compiler_params=pltpu.CompilerParams(
            collective_id=2, has_side_effects=True, vmem_limit_bytes=VMEM_LIMIT
        ),
        cost_estimate=cost(12 * rows * width * width, 100 << 20),
    )(
        tokens,
        gain,
        dq,
        dkv,
        grad_res,
        w_qkv,
        ds,
        buckets,
        query_sums,
        grad_ff,
        found,
    )


def on_device(
    doc_tokens,
    queries,
    doc_cot,
    query_cot,
    q_weight,
    kv_weight,
    out_weight,
    up_weight,
    down_weight,
    attn_gain,
    ff_gain,
    rel_bias,
    doc_buckets,
    query_buckets,
    topk_mask,
    positives,
    pos_count,
):
    n_docs, shard_rows, width = doc_tokens.shape
    n_query, query_len, _ = queries.shape
    bucket_count, heads = rel_bias.shape
    doc_len = doc_buckets.shape[1]
    doc_rows = n_docs * shard_rows
    query_total = n_query * query_len
    seq_size = lax.axis_size("seq")
    group = max(1, seq_size // n_docs)
    local_docs = max(1, n_docs // seq_size)
    local_rows = doc_len // group
    dp_size = lax.axis_size("dp")
    small = (dp_size, seq_size, n_docs) == (8, 4, 4) and width % 256 == 0 and shard_rows % 256 == 0
    small = small and down_weight.shape[0] * 32 == 4 * width and query_total % 256 == 0

    flat_queries = queries.reshape(query_total, width)
    flat_query_cot = query_cot.reshape(query_total, width)

    table = jnp.pad(rel_bias.T, ((0, 16 - heads), (0, 127 - bucket_count)))
    table = jnp.pad(table, ((0, 0), (0, 1)), constant_values=-1e30)

    if small:
        tokens, cotangent, w_qkv, w_out_up, w_down, buckets, qkv, mixture, doc_probs, query_probs, tiled = front(
            doc_tokens,
            flat_queries,
            doc_cot,
            flat_query_cot,
            (q_weight, kv_weight, out_weight, up_weight, down_weight),
            doc_buckets,
            attn_gain,
            table,
            query_buckets,
            heads,
        )
    else:
        order = gather_orders()[0]
        w_qkv = gather_rows(jnp.concatenate([q_weight, kv_weight], 1), order)
        w_out_up = gather_rows(jnp.concatenate([out_weight, up_weight], 1), order)
        w_down = gather_rows(down_weight, order)
        tokens = jnp.concatenate([own_document(doc_tokens), flat_queries], 0)
        cotangent = jnp.concatenate([own_document(doc_cot), flat_query_cot], 0)
        buckets = gather_positions(doc_buckets.astype(jnp.int16))
        repeats = 128 // query_len
        same = jnp.kron(jnp.eye(repeats, dtype=jnp.int32), jnp.ones_like(query_buckets))
        tiled = jnp.where(same == 1, jnp.tile(query_buckets, (repeats, repeats)), 127)
        if group > 1:
            part = lax.axis_index("seq") % group
            buckets = lax.dynamic_slice_in_dim(buckets, part * local_rows, local_rows, 0)
        q_rows, kv_rows = project(tokens, attn_gain, w_qkv)
        kv_docs = kv_rows
        if group > 1:
            teams = [list(range(t * group, (t + 1) * group)) for t in range(seq_size // group)]
            kv_docs = lax.all_gather(
                kv_rows[:doc_rows], "seq", axis=0, tiled=True, axis_index_groups=teams
            )
        doc_mix, doc_probs = doc_forward(
            q_rows, kv_docs, table, buckets, local_docs, local_rows, heads
        )
        query_mix, query_probs = query_forward(
            q_rows, kv_rows, table, tiled, doc_rows, query_total, heads
        )
        mixture = jnp.concatenate([doc_mix, query_mix], 0)
    if small:
        outputs, query_out, grad_res, grad_mix, grad_rest, grad_down, grad_near, grad_ff = middle(
            tokens, mixture, cotangent, ff_gain, w_out_up, w_down, doc_rows
        )
        query_out = query_out.reshape(queries.shape)
    else:
        outputs, grad_res, grad_mix, grad_out_up, grad_down, grad_ff = feed(
            tokens, mixture, cotangent, ff_gain, w_out_up, w_down
        )
        query_out = outputs[doc_rows:].reshape(queries.shape)
    matches = positives[:, :, None] == jnp.arange(doc_len, dtype=jnp.int32)[None, None, :]
    counted = jnp.arange(positives.shape[1], dtype=jnp.int32)[None, :] < pos_count[:, None]
    retrieved = jnp.sum(
        jnp.where(matches & counted[:, :, None], topk_mask[:, None, :].astype(SINGLE), 0.0)
    )

    if small:
        dq, dkv, ds, query_sums, grad_far, grad_down_shard, doc_out = back(
            qkv,
            grad_mix,
            mixture,
            doc_probs,
            query_probs,
            tiled,
            (grad_rest, grad_down),
            outputs,
            grad_near,
            n_docs,
            bucket_count,
        )
        grad_out_shard = grad_far[:, :width]
        grad_up_shard = grad_far[:, width:]
        grad_qkv_shard, doc_dx, query_dx, total = leave(
            tokens,
            attn_gain,
            dq,
            dkv,
            grad_res,
            w_qkv,
            ds,
            buckets,
            query_sums,
            grad_ff,
            retrieved.reshape(1, 1),
            n_docs,
            bucket_count,
        )
        lines = width // 128
        total_attn = total[:lines].reshape(-1)
        total_ff = total[lines : 2 * lines].reshape(-1)
        total_found = total[2 * lines, 0]
        total_bias = total[-bucket_count:, :heads]
        query_dx = query_dx.reshape(queries.shape)
    else:
        grad_down_shard = scatter_columns(grad_down, 2)
        grad_out_up_shard = scatter_columns(grad_out_up, 2)
        grad_out_shard = grad_out_up_shard[:, :width]
        grad_up_shard = grad_out_up_shard[:, width:]
        doc_out = spread_document(outputs[:doc_rows], doc_tokens)
        doc_dq, doc_dk, doc_dv, doc_sums = doc_backward(
            q_rows,
            kv_docs,
            grad_mix,
            doc_mix,
            doc_probs,
            buckets,
            local_docs,
            local_rows,
            bucket_count,
        )
        if group > 1:
            both = jnp.concatenate([doc_dk, doc_dv], 1)
            both = lax.psum_scatter(
                both, "seq", scatter_dimension=0, tiled=True, axis_index_groups=teams
            )
            doc_dk, doc_dv = both[:, :width], both[:, width:]
        query_dq, query_dkv, query_sums = query_backward(
            q_rows, kv_rows, grad_mix, mixture, query_probs, tiled, doc_rows, bucket_count
        )
        grad_tokens, grad_low, grad_qkv, grad_attn = unproject(
            tokens,
            attn_gain,
            jnp.concatenate([doc_dq, query_dq], 0),
            jnp.concatenate([doc_dk, query_dkv[:, :width]], 0),
            jnp.concatenate([doc_dv, query_dkv[:, width:]], 0),
            grad_res,
            w_qkv,
        )
        grad_qkv_shard = scatter_columns(grad_qkv, 2)
        doc_dx = spread_document(grad_low[:doc_rows], doc_tokens)
        query_dx = grad_tokens[doc_rows:].reshape(queries.shape)
        sums = (doc_sums + query_sums).reshape(16, bucket_count, heads, 16)
        keep = jnp.eye(16, dtype=SINGLE)[:, None, None, :]
        bias_local = jnp.sum(sums * keep, axis=(0, 3))
        flat = jnp.concatenate(
            [grad_attn[0], grad_ff[0], bias_local.reshape(-1), jnp.full((128,), retrieved)]
        )
        total = sum_all(flat)
        total_attn, total_ff = total[:width], total[width : 2 * width]
        total_bias = total[2 * width : 2 * width + bucket_count * heads]
        total_bias = total_bias.reshape(bucket_count, heads)
        total_found = total[-1]
    slots = float(n_query * dp_size * seq_size * positives.shape[1])
    return (
        doc_out,
        query_out,
        doc_dx.astype(SINGLE),
        query_dx,
        grad_qkv_shard[:, :width],
        grad_qkv_shard[:, width:],
        grad_out_shard,
        grad_up_shard,
        grad_down_shard,
        total_attn,
        total_ff,
        total_bias,
        total_found / slots,
    )


def solution(mesh):
    rows_all = P(("dp", "seq"), None)
    return jax.shard_map(
        on_device,
        mesh=mesh,
        in_specs=(
            P("dp", "seq", None),
            P(("dp", "seq"), None, None),
            P("dp", "seq", None),
            P(("dp", "seq"), None, None),
            rows_all,
            rows_all,
            rows_all,
            rows_all,
            rows_all,
            P(),
            P(),
            P(),
            P("seq", None),
            P(),
            rows_all,
            rows_all,
            P(("dp", "seq")),
        ),
        out_specs=(
            P("dp", "seq", None),
            P(("dp", "seq"), None, None),
            P("dp", "seq", None),
            P(("dp", "seq"), None, None),
            rows_all,
            rows_all,
            rows_all,
            rows_all,
            rows_all,
            P(),
            P(),
            P(),
            P(),
        ),
        check_vma=False,
    )
```

```python
import functools
import math

import jax
import jax.numpy as jnp
from jax import lax
from jax.experimental import pallas as pl
from jax.experimental.pallas import tpu as pltpu
from jax.sharding import PartitionSpec as P

EPSILON = 1e-06
BFLOAT = jnp.bfloat16
SINGLE = jnp.float32
FIXED = 8191.0
GELU_A = math.sqrt(2.0 / math.pi)
GELU_B = 0.044715
VMEM_LIMIT = 63 << 20


def nn(left, right):
    return jnp.dot(left, right, preferred_element_type=SINGLE)


def nt(left, right):
    return lax.dot_general(left, right, (((1,), (1,)), ((), ())), preferred_element_type=SINGLE)


def tn(left, right):
    return lax.dot_general(left, right, (((0,), (0,)), ((), ())), preferred_element_type=SINGLE)


def whole(shape):
    zeros = (0,) * len(shape)
    return pl.BlockSpec(shape, lambda *_: zeros, pipeline_mode=pl.Buffered(1))


def params():
    return pltpu.CompilerParams(vmem_limit_bytes=VMEM_LIMIT)


def cost(flops, moved):
    return pl.CostEstimate(flops=int(flops), bytes_accessed=int(moved), transcendentals=0)


def scale_of(values):
    return lax.rsqrt(jnp.mean(values * values, axis=-1, keepdims=True) + EPSILON)


def norm_back(values, scale, scaled_grad):
    dot = jnp.mean(values * scaled_grad, axis=-1, keepdims=True)
    return scale * (scaled_grad - values * (scale * scale * dot))


def first_lanes(shape, head_dim):
    return lax.broadcasted_iota(jnp.int32, shape, 1) < head_dim


def project_kernel(x_ref, gain_ref, w_ref, q_ref, kv_ref):
    values = x_ref[...].astype(SINGLE)
    normed = (values * scale_of(values) * gain_ref[...]).astype(BFLOAT)
    width = values.shape[1]
    q_ref[...] = nn(normed, w_ref[:, :width]).astype(BFLOAT)
    kv_ref[...] = nn(normed, w_ref[:, width:]).astype(BFLOAT)


def project(tokens, gain, w_qkv):
    rows, width = tokens.shape
    block = math.gcd(rows, 256)
    return pl.pallas_call(
        project_kernel,
        grid=(rows // block,),
        in_specs=[
            pl.BlockSpec((block, width), lambda i: (i, 0)),
            whole((1, width)),
            whole(w_qkv.shape),
        ],
        out_specs=[
            pl.BlockSpec((block, width), lambda i: (i, 0)),
            pl.BlockSpec((block, 2 * width), lambda i: (i, 0)),
        ],
        out_shape=[
            jax.ShapeDtypeStruct((rows, width), BFLOAT),
            jax.ShapeDtypeStruct((rows, 2 * width), BFLOAT),
        ],
        compiler_params=params(),
        cost_estimate=cost(6 * rows * width * width, 12 * rows * width),
    )(tokens, gain.reshape(1, width), w_qkv)


def attend_pair(q_pair, k_pair, v_pair, table_ref, bucket_ref, start, prob_ref, step, head_dim):
    rows, keys = q_pair.shape[0], k_pair.shape[0]
    wide = first_lanes(q_pair.shape, head_dim)
    tall = first_lanes(v_pair.shape, head_dim)
    coded_rows = jnp.round(table_ref[pl.ds(2 * step, 2), :] * FIXED).astype(jnp.int32)
    table = (coded_rows[0:1, :] << 16) | (coded_rows[1:2, :] & 0xFFFF)
    table = jnp.broadcast_to(table, (rows, 128))
    span = pl.ds(start, rows)
    packed = jnp.concatenate(
        [
            jnp.take_along_axis(
                table,
                bucket_ref[span, part * 128 : part * 128 + 128].astype(jnp.int32),
                axis=1,
                mode="promise_in_bounds",
            )
            for part in range(keys // 128)
        ],
        1,
    )
    total = None
    for side in range(2):
        mine = wide if side == 0 else ~wide
        mine_tall = tall if side == 0 else ~tall
        coded = (packed >> 16) if side == 0 else ((packed << 16) >> 16)
        scores = nt(jnp.where(mine, q_pair, 0), k_pair)
        scores = scores + coded.astype(SINGLE) * (1.0 / FIXED)
        shifted = jnp.exp(scores - jnp.max(scores, axis=-1, keepdims=True))
        inverse = 1.0 / jnp.sum(shifted, axis=-1, keepdims=True)
        soft = (shifted * inverse).astype(BFLOAT)
        prob_ref[2 * step + side] = soft
        term = nn(soft, jnp.where(mine_tall, v_pair, 0))
        total = term if total is None else total + term
    return total.astype(BFLOAT)


def pair_lanes(step, head_dim, offset=0):
    return pl.ds(pl.multiple_of(offset + step * 2 * head_dim, 128), 2 * head_dim)


def doc_forward_kernel(q_ref, k_ref, v_ref, table_ref, bucket_ref, mix_ref, prob_ref):
    heads = prob_ref.shape[0]
    head_dim = q_ref.shape[1] // heads

    def pair(step, carry):
        lanes = pair_lanes(step, head_dim)
        mix_ref[:, lanes] = attend_pair(
            q_ref[:, lanes],
            k_ref[:, lanes],
            v_ref[:, lanes],
            table_ref,
            bucket_ref,
            0,
            prob_ref,
            step,
            head_dim,
        )
        return carry

    lax.fori_loop(0, heads // 2, pair, 0)


def doc_forward(q_rows, kv_rows, table, buckets, n_docs, rows, heads):
    width = q_rows.shape[1]
    keys = buckets.shape[1]
    block = math.gcd(rows, 256)
    steps = rows // block
    return pl.pallas_call(
        doc_forward_kernel,
        grid=(n_docs, steps),
        in_specs=[
            pl.BlockSpec((block, width), lambda d, i: (d * steps + i, 0)),
            pl.BlockSpec((keys, width), lambda d, i: (d, 0)),
            pl.BlockSpec((keys, width), lambda d, i: (d, 1)),
            whole(table.shape),
            pl.BlockSpec((block, keys), lambda d, i: (i, 0)),
        ],
        out_specs=[
            pl.BlockSpec((block, width), lambda d, i: (d * steps + i, 0)),
            pl.BlockSpec((heads, block, keys), lambda d, i: (0, d * steps + i, 0)),
        ],
        out_shape=[
            jax.ShapeDtypeStruct((n_docs * rows, width), BFLOAT),
            jax.ShapeDtypeStruct((heads, n_docs * rows, keys), BFLOAT),
        ],
        compiler_params=params(),
        cost_estimate=cost(30 * n_docs * rows * keys * width, 2 * heads * n_docs * rows * keys),
    )(q_rows, kv_rows, kv_rows, table, buckets)


def bucket_onehot(bucket_rows, labels):
    rows, keys = bucket_rows.shape
    numbers = bucket_rows.astype(jnp.int32)
    names = lax.broadcasted_iota(jnp.int32, (labels, keys), 0)
    parts = [
        jnp.where(jnp.broadcast_to(numbers[r : r + 1, :], (labels, keys)) == names, 1.0, 0.0).astype(
            BFLOAT
        )
        for r in range(rows)
    ]
    return jnp.concatenate(parts, 0)


def bucket_products(bucket_rows, grad_rows, labels):
    return nt(bucket_onehot(bucket_rows, labels), grad_rows)


def attend_back(q_pair, k_pair, v_pair, da_pair, mix_pair, probs, head_dim):
    wide = first_lanes(q_pair.shape, head_dim)
    tall = first_lanes(k_pair.shape, head_dim)
    product = da_pair.astype(SINGLE) * mix_pair.astype(SINGLE)
    dq = dk = dv = None
    kept = []
    for side in range(2):
        mine = wide if side == 0 else ~wide
        mine_tall = tall if side == 0 else ~tall
        da_mine = jnp.where(mine, da_pair, 0)
        correction = jnp.sum(jnp.where(mine, product, 0.0), axis=-1, keepdims=True)
        grad_soft = nt(da_mine, v_pair)
        soft = probs[side]
        grad_scores = (soft.astype(SINGLE) * (grad_soft - correction)).astype(BFLOAT)
        kept.append(grad_scores)
        dq_term = nn(grad_scores, jnp.where(mine_tall, k_pair, 0))
        dk_term = tn(grad_scores, jnp.where(mine, q_pair, 0))
        dv_term = tn(soft, da_mine)
        dq = dq_term if dq is None else dq + dq_term
        dk = dk_term if dk is None else dk + dk_term
        dv = dv_term if dv is None else dv + dv_term
    return dq, dk, dv, kept


def query_back_block(q_rows, k_rows, v_rows, da_rows, mix_rows, probs, head_dim):
    rows, width = q_rows.shape
    heads = len(probs)
    wide = first_lanes((rows, 2 * head_dim), head_dim)

    def pair(values, step):
        return values[:, step * 2 * head_dim : (step + 1) * 2 * head_dim]

    def halves(values, step):
        return jnp.where(wide, pair(values, step), 0), jnp.where(wide, 0, pair(values, step))

    das, corrections, grads = [], [], []
    for step in range(heads // 2):
        das += halves(da_rows, step)
    for head in range(heads):
        grads.append(nt(das[head], pair(v_rows, head // 2)))
    for head in range(heads):
        product = das[head].astype(SINGLE) * pair(mix_rows, head // 2).astype(SINGLE)
        corrections.append(jnp.sum(product, axis=-1, keepdims=True))
    kept = [
        (prob.astype(SINGLE) * (grad - correction)).astype(BFLOAT)
        for prob, grad, correction in zip(probs, grads, corrections)
    ]
    dq, dk, dv = [], [], []
    for step in range(heads // 2):
        left, right = kept[2 * step], kept[2 * step + 1]
        k_left, k_right = halves(k_rows, step)
        dq.append((nn(left, k_left) + nn(right, k_right)).astype(BFLOAT))
    for step in range(heads // 2):
        left, right = kept[2 * step], kept[2 * step + 1]
        q_left, q_right = halves(q_rows, step)
        dk.append((tn(left, q_left) + tn(right, q_right)).astype(BFLOAT))
    for step in range(heads // 2):
        terms = tn(probs[2 * step], das[2 * step]) + tn(probs[2 * step + 1], das[2 * step + 1])
        dv.append(terms.astype(BFLOAT))
    return dq, dk, dv, kept


def doc_backward_kernel(
    labels,
    q_ref,
    k_ref,
    v_ref,
    da_ref,
    mix_ref,
    prob_ref,
    bucket_ref,
    dq_ref,
    dk_ref,
    dv_ref,
    sums_ref,
    dk_acc,
    dv_acc,
    ds_keep,
):
    rows, width = q_ref.shape
    heads = prob_ref.shape[0]
    keys = k_ref.shape[0]
    head_dim = width // heads
    doc, step_i = pl.program_id(0), pl.program_id(1)

    @pl.when(step_i == 0)
    def _():
        dk_acc[...] = jnp.zeros_like(dk_acc)
        dv_acc[...] = jnp.zeros_like(dv_acc)

    @pl.when((step_i == 0) & (doc == 0))
    def _():
        sums_ref[...] = jnp.zeros_like(sums_ref)

    def pair(step, carry):
        lanes = pl.ds(pl.multiple_of(step * 2 * head_dim, 128), 2 * head_dim)
        dq, dk, dv, kept = attend_back(
            q_ref[:, lanes],
            k_ref[:, lanes],
            v_ref[:, lanes],
            da_ref[:, lanes],
            mix_ref[:, lanes],
            [prob_ref[2 * step], prob_ref[2 * step + 1]],
            head_dim,
        )
        ds_keep[2 * step] = kept[0]
        ds_keep[2 * step + 1] = kept[1]
        dq_ref[:, lanes] = dq.astype(BFLOAT)
        dk_acc[:, lanes] += dk
        dv_acc[:, lanes] += dv
        return carry

    lax.fori_loop(0, heads // 2, pair, 0)

    def group(number, carry):
        span = pl.ds(pl.multiple_of(number * 16, 16), 16)
        sums_ref[...] += bucket_products(
            bucket_ref[span, :], ds_keep[:, span, :].reshape(heads * 16, keys), labels
        )
        return carry

    lax.fori_loop(0, rows // 16, group, 0)

    @pl.when(step_i == pl.num_programs(1) - 1)
    def _():
        dk_ref[...] = dk_acc[...].astype(BFLOAT)
        dv_ref[...] = dv_acc[...].astype(BFLOAT)


def doc_backward(q_rows, kv_rows, da_rows, mixture, probs, buckets, n_docs, rows, labels):
    width = q_rows.shape[1]
    heads = probs.shape[0]
    keys = buckets.shape[1]
    block = math.gcd(rows, 256)
    steps = rows // block
    along = pl.BlockSpec((block, width), lambda d, i: (d * steps + i, 0))
    per_doc = pl.BlockSpec((keys, width), lambda d, i: (d, 0))
    return pl.pallas_call(
        functools.partial(doc_backward_kernel, labels),
        grid=(n_docs, steps),
        in_specs=[
            along,
            per_doc,
            pl.BlockSpec((keys, width), lambda d, i: (d, 1)),
            along,
            along,
            pl.BlockSpec((heads, block, keys), lambda d, i: (0, d * steps + i, 0)),
            pl.BlockSpec((block, keys), lambda d, i: (i, 0)),
        ],
        out_specs=[along, per_doc, per_doc, whole((16 * labels, heads * 16))],
        out_shape=[
            jax.ShapeDtypeStruct((n_docs * rows, width), BFLOAT),
            jax.ShapeDtypeStruct((n_docs * keys, width), BFLOAT),
            jax.ShapeDtypeStruct((n_docs * keys, width), BFLOAT),
            jax.ShapeDtypeStruct((16 * labels, heads * 16), SINGLE),
        ],
        scratch_shapes=[
            pltpu.VMEM((keys, width), SINGLE),
            pltpu.VMEM((keys, width), SINGLE),
            pltpu.VMEM((heads, block, keys), BFLOAT),
        ],
        compiler_params=params(),
        cost_estimate=cost(70 * n_docs * rows * keys * width, 2 * heads * n_docs * rows * keys),
    )(q_rows, kv_rows, kv_rows, da_rows, mixture, probs, buckets)


def query_block(q_rows, k_rows, v_rows, table_ref, index, heads):
    rows, width = q_rows.shape
    head_dim = width // heads
    wide = first_lanes((rows, 2 * head_dim), head_dim)

    def halves(values, step):
        pair = values[:, step * 2 * head_dim : (step + 1) * 2 * head_dim]
        return jnp.where(wide, pair, 0), jnp.where(wide, 0, pair), pair

    scores = []
    for step in range(heads // 2):
        left, right, _ = halves(q_rows, step)
        keys = halves(k_rows, step)[2]
        scores += [nt(left, keys), nt(right, keys)]
    for head in range(heads):
        table = jnp.broadcast_to(table_ref[head : head + 1, :], (rows, 128))
        bias = jnp.take_along_axis(table, index, axis=1, mode="promise_in_bounds")
        scores[head] = scores[head] + bias
    tops = [jnp.max(score, axis=-1, keepdims=True) for score in scores]
    shifted = [jnp.exp(score - top) for score, top in zip(scores, tops)]
    inverse = [1.0 / jnp.sum(shift, axis=-1, keepdims=True) for shift in shifted]
    softs = [(shift * inv).astype(BFLOAT) for shift, inv in zip(shifted, inverse)]
    outs = []
    for step in range(heads // 2):
        left, right, _ = halves(v_rows, step)
        outs.append((nn(softs[2 * step], left) + nn(softs[2 * step + 1], right)).astype(BFLOAT))
    return softs, jnp.concatenate(outs, 1)


def query_forward_kernel(q_ref, kv_ref, table_ref, bucket_ref, mix_ref, prob_ref):
    width = q_ref.shape[1]
    softs, mix_ref[...] = query_block(
        q_ref[...], kv_ref[:, :width], kv_ref[:, width:], table_ref, bucket_ref[...], prob_ref.shape[0]
    )
    for head, soft in enumerate(softs):
        prob_ref[head] = soft


def query_forward(q_rows, kv_rows, table, buckets, start, count, heads):
    width = q_rows.shape[1]
    offset = start // 128
    return pl.pallas_call(
        query_forward_kernel,
        grid=(count // 128,),
        in_specs=[
            pl.BlockSpec((128, width), lambda i: (offset + i, 0)),
            pl.BlockSpec((128, 2 * width), lambda i: (offset + i, 0)),
            whole(table.shape),
            whole(buckets.shape),
        ],
        out_specs=[
            pl.BlockSpec((128, width), lambda i: (i, 0)),
            pl.BlockSpec((heads, 128, 128), lambda i: (0, i, 0)),
        ],
        out_shape=[
            jax.ShapeDtypeStruct((count, width), BFLOAT),
            jax.ShapeDtypeStruct((heads, count, 128), BFLOAT),
        ],
        compiler_params=params(),
        cost_estimate=cost(4 * count * 128 * width * 4, 10 * count * width),
    )(q_rows, kv_rows, table, buckets)


def query_backward_kernel(
    labels, q_ref, kv_ref, da_ref, mix_ref, prob_ref, bucket_ref, dq_ref, dkv_ref, sums_ref, ds_keep
):
    rows, width = q_ref.shape
    heads = prob_ref.shape[0]
    head_dim = width // heads

    @pl.when(pl.program_id(0) == 0)
    def _():
        sums_ref[...] = jnp.zeros_like(sums_ref)

    for step in range(heads // 2):
        lanes = slice(step * 2 * head_dim, (step + 1) * 2 * head_dim)
        right = slice(width + lanes.start, width + lanes.stop)
        dq, dk, dv, kept = attend_back(
            q_ref[:, lanes],
            kv_ref[:, lanes],
            kv_ref[:, right],
            da_ref[:, lanes],
            mix_ref[:, lanes],
            [prob_ref[2 * step], prob_ref[2 * step + 1]],
            head_dim,
        )
        ds_keep[2 * step] = kept[0]
        ds_keep[2 * step + 1] = kept[1]
        dq_ref[:, lanes] = dq.astype(BFLOAT)
        dkv_ref[:, lanes] = dk.astype(BFLOAT)
        dkv_ref[:, right] = dv.astype(BFLOAT)

    def group(number, carry):
        span = pl.ds(pl.multiple_of(number * 16, 16), 16)
        sums_ref[...] += bucket_products(
            bucket_ref[span, :], ds_keep[:, span, :].reshape(heads * 16, rows), labels
        )
        return carry

    lax.fori_loop(0, rows // 16, group, 0)


def query_backward(q_rows, kv_rows, da_rows, mixture, probs, buckets, start, labels):
    width = q_rows.shape[1]
    heads, count, _ = probs.shape
    offset = start // 128
    return pl.pallas_call(
        functools.partial(query_backward_kernel, labels),
        grid=(count // 128,),
        in_specs=[
            pl.BlockSpec((128, width), lambda i: (offset + i, 0)),
            pl.BlockSpec((128, 2 * width), lambda i: (offset + i, 0)),
            pl.BlockSpec((128, width), lambda i: (offset + i, 0)),
            pl.BlockSpec((128, width), lambda i: (offset + i, 0)),
            pl.BlockSpec((heads, 128, 128), lambda i: (0, i, 0)),
            whole(buckets.shape),
        ],
        out_specs=[
            pl.BlockSpec((128, width), lambda i: (i, 0)),
            pl.BlockSpec((128, 2 * width), lambda i: (i, 0)),
            whole((16 * labels, heads * 16)),
        ],
        out_shape=[
            jax.ShapeDtypeStruct((count, width), BFLOAT),
            jax.ShapeDtypeStruct((count, 2 * width), BFLOAT),
            jax.ShapeDtypeStruct((16 * labels, heads * 16), SINGLE),
        ],
        scratch_shapes=[pltpu.VMEM((heads, 128, 128), BFLOAT)],
        compiler_params=params(),
        cost_estimate=cost(8 * count * 128 * width * 4, 14 * count * width),
    )(q_rows, kv_rows, da_rows, mixture, probs, buckets)


def feed_kernel(
    chunk,
    x_ref,
    mix_ref,
    dy_ref,
    gain_ref,
    wou_ref,
    wd_ref,
    y_ref,
    dh_ref,
    da_ref,
    gou_ref,
    gd_ref,
    gg_ref,
    gou_acc,
    gd_acc,
    stage,
    sems,
):
    step = pl.program_id(0)
    hidden, width = wd_ref.shape

    @pl.when(step == 0)
    def _():
        gou_acc[...] = jnp.zeros_like(gou_acc)
        gd_acc[...] = jnp.zeros_like(gd_acc)
        gg_ref[...] = jnp.zeros_like(gg_ref)

    mixture = mix_ref[...]
    dy = dy_ref[...]
    gain = gain_ref[...]
    residual = x_ref[...].astype(SINGLE) + nn(mixture, wou_ref[:, :width])
    scale = scale_of(residual)
    second = (residual * scale * gain).astype(BFLOAT)
    y = residual
    grad_second = jnp.zeros_like(residual)
    for part in range(hidden // chunk):
        span = slice(part * chunk, (part + 1) * chunk)
        past = slice(width + part * chunk, width + (part + 1) * chunk)
        pre = nn(second, wou_ref[:, past])
        grad_hidden = nt(dy, wd_ref[span, :])
        square = pre * pre
        tanh = jnp.tanh(pre * (GELU_A + (GELU_A * GELU_B) * square))
        half = 0.5 + 0.5 * tanh
        act = pre * half
        slope = half + act * (1.0 - tanh) * (GELU_A + (3.0 * GELU_A * GELU_B) * square)
        act_low = act.astype(BFLOAT)
        grad_pre = (grad_hidden * slope).astype(BFLOAT)
        y = y + nn(act_low, wd_ref[span, :])
        grad_second = grad_second + nt(grad_pre, wou_ref[:, past])
        gd_acc[span, :] += tn(act_low, dy)
        gou_acc[:, past] += tn(second, grad_pre)
    y_ref[...] = y.astype(BFLOAT)
    gg_ref[...] += jnp.sum(grad_second * residual * scale, axis=0, keepdims=True)
    grad_res = dy.astype(SINGLE) + norm_back(residual, scale, grad_second * gain)
    dh_ref[...] = grad_res
    grad_low = grad_res.astype(BFLOAT)
    da_ref[...] = nt(grad_low, wou_ref[:, :width]).astype(BFLOAT)
    gou_acc[:, :width] += tn(mixture, grad_low)

    @pl.when(step == pl.num_programs(0) - 1)
    def _():
        pieces = []
        rows, columns = stage.shape[1:]
        for acc, out in ((gd_acc, gd_ref), (gou_acc, gou_ref)):
            for r in range(acc.shape[0] // rows):
                for c in range(acc.shape[1] // columns):
                    spot = (pl.ds(r * rows, rows), pl.ds(c * columns, columns))
                    pieces.append((acc, out, spot))
        flying = [None, None]
        for number, (acc, out, spot) in enumerate(pieces):
            slot = number % 2
            if flying[slot] is not None:
                flying[slot].wait()
            stage[slot] = acc[spot].astype(BFLOAT)
            flying[slot] = pltpu.make_async_copy(stage.at[slot], out.at[spot], sems.at[slot])
            flying[slot].start()
        for copy in flying:
            if copy is not None:
                copy.wait()


def feed(tokens, mixture, cotangent, gain, w_out_up, w_down):
    rows, width = tokens.shape
    hidden = w_down.shape[0]
    block = math.gcd(rows, 256)
    along = pl.BlockSpec((block, width), lambda i: (i, 0))
    anywhere = pl.BlockSpec(memory_space=pl.ANY)
    return pl.pallas_call(
        functools.partial(feed_kernel, math.gcd(hidden, 768)),
        grid=(rows // block,),
        in_specs=[
            along,
            along,
            along,
            whole((1, width)),
            whole(w_out_up.shape),
            whole(w_down.shape),
        ],
        out_specs=[along, along, along, anywhere, anywhere, whole((1, width))],
        out_shape=[
            jax.ShapeDtypeStruct((rows, width), BFLOAT),
            jax.ShapeDtypeStruct((rows, width), SINGLE),
            jax.ShapeDtypeStruct((rows, width), BFLOAT),
            jax.ShapeDtypeStruct(w_out_up.shape, BFLOAT),
            jax.ShapeDtypeStruct(w_down.shape, BFLOAT),
            jax.ShapeDtypeStruct((1, width), SINGLE),
        ],
        scratch_shapes=[
            pltpu.VMEM(w_out_up.shape, SINGLE),
            pltpu.VMEM(w_down.shape, SINGLE),
            pltpu.VMEM((2, width, width), BFLOAT),
            pltpu.SemaphoreType.DMA((2,)),
        ],
        compiler_params=params(),
        cost_estimate=cost(2 * rows * width * (6 * hidden + 3 * width), 14 * rows * width),
    )(tokens, mixture, cotangent, gain.reshape(1, width), w_out_up, w_down)


def unproject_kernel(
    x_ref, gain_ref, dq_ref, dk_ref, dv_ref, dh_ref, w_ref, dx_ref, low_ref, gw_ref, gg_ref, acc
):
    step = pl.program_id(0)
    width = w_ref.shape[0]

    @pl.when(step == 0)
    def _():
        acc[...] = jnp.zeros_like(acc)
        gg_ref[...] = jnp.zeros_like(gg_ref)

    values = x_ref[...].astype(SINGLE)
    gain = gain_ref[...]
    scale = scale_of(values)
    normed = (values * scale * gain).astype(BFLOAT)
    grad = jnp.zeros_like(values)
    for number, ref in enumerate((dq_ref, dk_ref, dv_ref)):
        span = slice(number * width, (number + 1) * width)
        part = ref[...]
        acc[:, span] += tn(normed, part)
        grad = grad + nt(part, w_ref[:, span])
    gg_ref[...] += jnp.sum(grad * values * scale, axis=0, keepdims=True)
    dx = dh_ref[...] + norm_back(values, scale, grad * gain)
    dx_ref[...] = dx
    low_ref[...] = dx.astype(BFLOAT)

    @pl.when(step == pl.num_programs(0) - 1)
    def _():
        gw_ref[...] = acc[...].astype(BFLOAT)


def unproject(tokens, gain, dq, dk, dv, grad_res, w_qkv):
    rows, width = tokens.shape
    block = math.gcd(rows, 256)
    along = pl.BlockSpec((block, width), lambda i: (i, 0))
    return pl.pallas_call(
        unproject_kernel,
        grid=(rows // block,),
        in_specs=[along, whole((1, width)), along, along, along, along, whole(w_qkv.shape)],
        out_specs=[along, along, whole(w_qkv.shape), whole((1, width))],
        out_shape=[
            jax.ShapeDtypeStruct((rows, width), SINGLE),
            jax.ShapeDtypeStruct((rows, width), BFLOAT),
            jax.ShapeDtypeStruct(w_qkv.shape, BFLOAT),
            jax.ShapeDtypeStruct((1, width), SINGLE),
        ],
        scratch_shapes=[pltpu.VMEM(w_qkv.shape, SINGLE)],
        compiler_params=params(),
        cost_estimate=cost(12 * rows * width * width, 18 * rows * width),
    )(tokens, gain.reshape(1, width), dq, dk, dv, grad_res, w_qkv)


def bits_of(count):
    return [1 << place for place in reversed(range(count.bit_length() - 1))]


def axis_bits():
    dp_bits = [("dp", bit) for bit in bits_of(lax.axis_size("dp"))]
    seq_bits = [("seq", bit) for bit in bits_of(lax.axis_size("seq"))]
    return dp_bits, seq_bits


def gather_orders():
    dp_bits, seq_bits = axis_bits()
    far = (len(dp_bits) + 1) // 2
    z_bits, x_bits = dp_bits[:far], dp_bits[far:]
    y_bits, core_bits = seq_bits[:-1], seq_bits[-1:]
    return [z_bits + y_bits + x_bits + core_bits, z_bits + x_bits + y_bits + core_bits]


def swap(values, name, bit):
    count = lax.axis_size(name)
    return lax.ppermute(values, name, [(i, i ^ bit) for i in range(count)])


def is_high(name, bit):
    return (lax.axis_index(name) & bit) != 0


def gather_rows(shard, order):
    dp_bits, seq_bits = axis_bits()
    everything = dp_bits + seq_bits
    done = []
    held = shard
    for item in order:
        other = swap(held, *item)
        done.append(item)
        place = sorted(everything.index(one) for one in done).index(everything.index(item))
        high = is_high(*item)
        held = jnp.where(
            high, jnp.stack([other, held], place), jnp.stack([held, other], place)
        )
    return held.reshape(-1, shard.shape[1])


def scatter_rows(values, order):
    dp_bits, seq_bits = axis_bits()
    left = dp_bits + seq_bits
    rows = values.shape[0] >> len(left)
    held = values.reshape((2,) * len(left) + (rows, values.shape[1]))
    for item in order:
        place = left.index(item)
        mine = is_high(*item).astype(jnp.int32)
        away = lax.dynamic_index_in_dim(held, 1 - mine, place, keepdims=False)
        kept = lax.dynamic_index_in_dim(held, mine, place, keepdims=False)
        other = swap(away, *item)
        held = kept.astype(SINGLE) + other.astype(SINGLE)
        left.remove(item)
        if left:
            held = held.astype(BFLOAT)
    return held


def scatter_columns(values, parts):
    orders = [order[::-1] for order in gather_orders()]
    columns = values.shape[1] // parts
    return jnp.concatenate(
        [
            scatter_rows(values[:, p * columns : (p + 1) * columns], orders[p % len(orders)])
            for p in range(parts)
        ],
        1,
    )


def sum_all(values):
    dp_bits, seq_bits = axis_bits()
    for item in seq_bits[::-1] + dp_bits[::-1]:
        values = values + swap(values, *item)
    return values


def own_document(shard):
    count = lax.axis_size("seq")
    n_docs = shard.shape[0]
    me = lax.axis_index("seq")
    if n_docs >= count:
        per = n_docs // count
        blocks = shard.reshape((count, per) + shard.shape[1:])
        sets, group = count, 1
    else:
        blocks = shard[:, None]
        sets, group = n_docs, count // n_docs
    got = []
    for r in range(sets):
        piece = lax.dynamic_index_in_dim(blocks, (me % sets) ^ r, 0, keepdims=False)
        route = [
            (u * sets + i, (i ^ r) * group + u) for u in range(group) for i in range(sets)
        ]
        if any(a != b for a, b in route):
            piece = lax.ppermute(piece, "seq", route)
        got.append(piece)
    stacked = jnp.stack(got, 0)
    mine = me // group
    ordered = [lax.dynamic_index_in_dim(stacked, mine ^ i, 0, keepdims=False) for i in range(sets)]
    return jnp.concatenate(ordered, 1).reshape(-1, shard.shape[-1])


def spread_document(rows, like):
    count = lax.axis_size("seq")
    n_docs, shard_rows, width = like.shape
    me = lax.axis_index("seq")
    if n_docs >= count:
        per = n_docs // count
        sets, group = count, 1
    else:
        per = 1
        sets, group = n_docs, count // n_docs
    blocks = rows.reshape(per, sets, shard_rows, width)
    mine = me // group
    got = []
    for r in range(sets):
        piece = lax.dynamic_index_in_dim(blocks, mine ^ r, 1, keepdims=False)
        route = [
            ((i ^ r) * group + u, u * sets + i) for u in range(group) for i in range(sets)
        ]
        if any(a != b for a, b in route):
            piece = lax.ppermute(piece, "seq", route)
        got.append(piece)
    stacked = jnp.stack(got, 0)
    ordered = [
        lax.dynamic_index_in_dim(stacked, (me % sets) ^ i, 0, keepdims=False) for i in range(sets)
    ]
    return jnp.concatenate(ordered, 0)


def gather_positions(shard):
    seq_bits = axis_bits()[1]
    done = []
    held = shard
    for item in seq_bits:
        other = swap(held, *item)
        high = is_high(*item)
        place = len(done)
        held = jnp.where(
            high, jnp.stack([other, held], place), jnp.stack([held, other], place)
        )
        done.append(item)
    return held.reshape(-1, shard.shape[1])


class Spot:
    def __init__(self):
        self.dp = lax.axis_index("dp")
        self.seq = lax.axis_index("seq")
        self.core = self.seq % 2
        self.y = self.seq // 2
        self.x = self.dp % 2
        self.z = self.dp // 2

    def partner(self, z=0, x=0, y=0, core=0):
        dp = self.flip(self.z, z) * 2 + self.flip(self.x, x)
        seq = self.flip(self.y, y) * 2 + self.flip(self.core, core)
        return (dp, seq)

    @staticmethod
    def flip(value, bits):
        if bits == 0:
            return value
        if bits == 1:
            return value + 1 - 2 * (value % 2)
        if bits == 2:
            return (value + 2) % 4
        return 3 - value

    def chip(self, z=0, x=0, y=0):
        return (self.flip(self.z, z) * 2 + self.flip(self.x, x)) * 2 + self.flip(self.y, y)


def send(source, target, sems, number, device):
    return pltpu.make_async_remote_copy(
        src_ref=source,
        dst_ref=target,
        send_sem=sems.at[0, number],
        recv_sem=sems.at[1, number],
        device_id=device,
        device_id_type=pl.DeviceIdType.MESH,
    )


def greet(partners):
    barrier = pltpu.get_barrier_semaphore()
    for device in partners:
        pl.semaphore_signal(barrier, inc=1, device_id=device, device_id_type=pl.DeviceIdType.MESH)
    pl.semaphore_wait(barrier, len(partners))


COPIES = 17
GATHER_COPIES = 24


class Gather:
    def __init__(self, spot, shard, whole_ref, theirs, block, sems, local):
        self.spot, self.shard, self.whole = spot, shard, whole_ref
        self.theirs, self.block, self.sems, self.local = theirs, block, sems, local
        self.rows, self.half = block.shape

    def columns(self, core):
        return pl.ds(pl.multiple_of(core * self.half, 128), self.half)

    def area(self, count=1, **bits):
        chip = self.spot.chip(**bits)
        if count == 2:
            chip = chip - chip % 2
        row = pl.multiple_of(chip * self.rows, 16)
        return self.whole.at[pl.ds(row, count * self.rows), self.columns(self.spot.core)]

    def copy(self, number):
        spot = self.spot
        if number == 0:
            source, target = self.shard.at[:, self.columns(1 - spot.core)], self.theirs
            device = spot.partner(core=1)
        elif number < 4:
            source, target, device = self.block, self.area(), spot.partner(z=number)
        elif number < 8:
            target, device = self.area(z=number - 4), spot.partner(y=1)
            source = self.block if number == 4 else target
        elif number < 16:
            target = self.area(z=(number - 8) % 4, y=(number - 8) // 4)
            source, device = self.block if number == 8 else target, spot.partner(x=1)
        else:
            source = target = self.area(2, z=number % 4, x=(number - 16) // 4)
            device = spot.partner(core=1)
        return send(source, target, self.sems, number, device)

    def here(self):
        return pltpu.make_async_copy(self.block, self.area(), self.local)

    def join_end(self):
        self.copy(0).wait_recv()
        part = self.rows // 2
        low = self.spot.core == 0
        mine = self.shard[:, self.columns(self.spot.core)].astype(SINGLE)
        theirs = self.theirs[...].astype(SINGLE)
        self.block[:part, :] = jnp.where(low, mine, theirs).astype(BFLOAT)
        self.block[part:, :] = jnp.where(low, theirs, mine).astype(BFLOAT)
        self.here().start()

    def start(self, *numbers):
        for number in numbers:
            self.copy(number).start()

    def z_got(self, k):
        self.copy(k).wait_recv()
        self.start(4 + k, 8 + k)

    def y_got(self, k):
        self.copy(4 + k).wait_recv()
        if k == 0:
            self.here().wait()
        self.start(12 + k, 16 + k)

    def x_got(self, k):
        self.copy(8 + k).wait_recv()
        self.copy(12 + k).wait_recv()
        self.start(20 + k)

    def finish(self):
        for number in range(16, GATHER_COPIES):
            self.copy(number).wait_recv()
        for number in range(GATHER_COPIES):
            self.copy(number).wait_send()


class PlaneGather(Gather):
    def copy(self, number):
        spot = self.spot
        if number == 0:
            return Gather.copy(self, 0)
        if number == 1:
            source, target, device = self.block, self.area(), spot.partner(y=1)
        elif number == 2:
            source, target, device = self.block, self.area(), spot.partner(x=1)
        elif number == 3:
            source = target = self.area(y=1)
            device = spot.partner(x=1)
        elif number < 10:
            source = target = self.area(2, x=(number - 4) // 3)
            device = spot.partner(z=(number - 4) % 3 + 1)
        else:
            kind = number - 10
            z, x = (0, kind) if kind < 2 else ((kind - 2) % 3 + 1, (kind - 2) // 3)
            source = target = self.area(2, z=z, x=x)
            device = spot.partner(core=1)
        return send(source, target, self.sems, number, device)

    def y_got(self):
        self.copy(1).wait_recv()
        self.here().wait()
        self.start(3, 4, 5, 6, 10)

    def x_got(self):
        self.copy(2).wait_recv()
        self.copy(3).wait_recv()
        self.start(7, 8, 9, 11)

    def z_got(self, x):
        for k in range(3):
            self.copy(4 + 3 * x + k).wait_recv()
            self.start(12 + 3 * x + k)

    def finish(self):
        for number in range(10, 18):
            self.copy(number).wait_recv()
        for number in range(18):
            self.copy(number).wait_send()


class Move:
    PARTNERS = ((1, 0), (1, 1), (0, 1))

    def __init__(self, spot, source, target, own_target, sems, local):
        self.spot, self.source, self.target = spot, source, target
        self.own_target, self.sems, self.local = own_target, sems, local

    def own(self):
        return pltpu.make_async_copy(
            self.source(self.spot.seq), self.own_target(self.spot.seq), self.local
        )

    def copy(self, number):
        y, core = self.PARTNERS[number]
        device = self.spot.partner(y=y, core=core)
        return send(self.source(device[1]), self.target(self.spot.seq), self.sems, number, device)

    def start(self):
        self.own().start()
        for number in range(3):
            self.copy(number).start()

    def finish(self):
        self.own().wait()
        for number in range(3):
            self.copy(number).wait()


def all_partners(spot):
    return [
        spot.partner(core=1),
        spot.partner(z=1),
        spot.partner(z=2),
        spot.partner(z=3),
        spot.partner(x=1),
        spot.partner(y=1),
        spot.partner(y=1, core=1),
    ]


def row_block(ref, rows):
    return lambda number: ref.at[pl.ds(pl.multiple_of(number * rows, 16), rows), :]


def front_kernel(
    docs_ref,
    queries_ref,
    doc_cot_ref,
    query_cot_ref,
    q_shard,
    kv_shard,
    out_shard,
    up_shard,
    down_shard,
    bucket_shard,
    gain_ref,
    table_ref,
    small_bucket_ref,
    tokens_out,
    cots_out,
    w_out,
    ou_out,
    down_out,
    bucket_out,
    qkv_out,
    mix_ref,
    prob_ref,
    query_prob_ref,
    query_bucket_ref,
    x_v,
    w_v,
    qkv_v,
    bucket_v,
    bucket_in,
    qkv_own,
    qkv_theirs,
    qkv_block,
    ou_own,
    ou_theirs,
    ou_block,
    down_own,
    down_theirs,
    down_block,
    gather_sems,
    move_sems,
    local,
):
    step = pl.program_id(0)
    last = pl.num_programs(0) - 1
    spot = Spot()
    n_docs, shard_rows, width = docs_ref.shape
    doc_rows = n_docs * shard_rows
    query_rows = queries_ref.shape[0]
    heads = prob_ref.shape[0]
    head_dim = width // heads
    pairs = heads // 2
    block = prob_ref.shape[1]

    gathers = []
    for number, parts in enumerate(
        (
            (qkv_own, w_v, qkv_theirs, qkv_block),
            (ou_own, ou_out, ou_theirs, ou_block),
            (down_own, down_out, down_theirs, down_block),
        )
    ):
        kind = PlaneGather if number == 2 else Gather
        gathers.append(kind(spot, *parts, gather_sems.at[number], local.at[number]))
    g_qkv, g_ou, g_down = gathers
    token_move = Move(
        spot,
        lambda number: docs_ref.at[number],
        row_block(x_v, shard_rows),
        row_block(x_v, shard_rows),
        move_sems.at[0],
        local.at[3],
    )
    cot_move = Move(
        spot,
        lambda number: doc_cot_ref.at[number],
        row_block(cots_out, shard_rows),
        row_block(cots_out, shard_rows),
        move_sems.at[1],
        local.at[4],
    )
    query_load = pltpu.make_async_copy(
        queries_ref, x_v.at[pl.ds(doc_rows, query_rows), :], local.at[5]
    )
    cot_copy = pltpu.make_async_copy(
        query_cot_ref, cots_out.at[pl.ds(doc_rows, query_rows), :], local.at[6]
    )
    bucket_rows = row_block(bucket_v, shard_rows)
    bucket_load = pltpu.make_async_copy(bucket_shard, bucket_in, local.at[7])
    near = bucket_rows(spot.seq)
    far = bucket_rows(spot.partner(y=1)[1])
    bucket_y = send(near, near, move_sems.at[2], 0, spot.partner(y=1))
    bucket_near = send(near, near, move_sems.at[2], 1, spot.partner(core=1))
    bucket_far = send(far, far, move_sems.at[2], 2, spot.partner(core=1))
    saves = [
        pltpu.make_async_copy(x_v, tokens_out, local.at[8]),
        pltpu.make_async_copy(w_v, w_out, local.at[9]),
        pltpu.make_async_copy(qkv_v, qkv_out, local.at[10]),
        pltpu.make_async_copy(bucket_v, bucket_out, local.at[11]),
    ]
    loads = [
        pltpu.make_async_copy(q_shard, qkv_own.at[:, pl.ds(0, width)], local.at[12]),
        pltpu.make_async_copy(kv_shard, qkv_own.at[:, pl.ds(width, 2 * width)], local.at[13]),
        pltpu.make_async_copy(out_shard, ou_own.at[:, pl.ds(0, width)], local.at[14]),
        pltpu.make_async_copy(
            up_shard, ou_own.at[:, pl.ds(width, up_shard.shape[1])], local.at[15]
        ),
        pltpu.make_async_copy(down_shard, down_own, local.at[16]),
    ]

    @pl.when(step == 0)
    def _():
        for load in loads:
            load.start()
        bucket_load.start()
        query_load.start()
        token_move.own().start()
        greet(all_partners(spot))
        token_move.copy(0).start()
        for load in loads[:2]:
            load.wait()
        g_qkv.start(0)
        for load in loads[2:]:
            load.wait()
        g_ou.start(0)
        g_down.start(0)
        token_move.copy(2).start()
        g_qkv.join_end()
        g_qkv.start(1, 2, 3, 4, 8)
        g_ou.join_end()
        g_down.join_end()
        g_down.start(1, 2)
        bucket_load.wait()
        bucket_v[pl.ds(pl.multiple_of(spot.seq * shard_rows, 16), shard_rows), :] = bucket_in[
            ...
        ].astype(jnp.int16)
        size = small_bucket_ref.shape[0]
        shape = (128, size)
        picks = (
            lax.broadcasted_iota(jnp.int32, shape, 0) % size
            == lax.broadcasted_iota(jnp.int32, shape, 1)
        )
        picks = jnp.where(picks, 1.0, 0.0).astype(BFLOAT)
        numbers = small_bucket_ref[...].astype(SINGLE).astype(BFLOAT)
        spread = nt(nn(picks, numbers).astype(BFLOAT), picks).astype(jnp.int32)
        square = (128, 128)
        same = (
            lax.broadcasted_iota(jnp.int32, square, 0) // size
            == lax.broadcasted_iota(jnp.int32, square, 1) // size
        )
        query_bucket_ref[...] = jnp.where(same, spread, table_ref.shape[1] - 1)
        for k in (1, 2, 3):
            g_qkv.z_got(k)
        g_ou.start(1, 2, 3)
        token_move.copy(1).start()
        bucket_y.start()
        bucket_near.start()
        g_ou.start(4)
        for k in (0, 1, 2, 3):
            g_qkv.y_got(k)
        g_ou.start(8)
        g_down.y_got()
        for k in (0, 1, 2, 3):
            g_qkv.x_got(k)
        query_load.wait()
        g_qkv.finish()
        saves[1].start()
        token_move.finish()
        saves[0].start()

        tall = (doc_rows + query_rows) // 3

        def project_block(number, carry):
            span = pl.ds(pl.multiple_of(number * tall, 16), tall)
            values = x_v[span, :].astype(SINGLE)
            normed = (values * scale_of(values) * gain_ref[...][None, :]).astype(BFLOAT)
            for part in range(3):
                lanes = slice(part * width, (part + 1) * width)
                qkv_v[span, lanes] = nn(normed, w_v[:, lanes]).astype(BFLOAT)
            return carry

        project_block(0, 0)
        g_down.x_got()
        g_ou.z_got(1)
        project_block(1, 0)
        g_ou.z_got(2)
        project_block(2, 0)
        g_ou.z_got(3)
        saves[2].start()
        cot_move.start()
        cot_copy.start()
        bucket_y.wait_recv()
        bucket_far.start()

        def query_step(number, carry):
            span = pl.ds(pl.multiple_of(doc_rows + number * 128, 16), 128)
            softs, mixed = query_block(
                qkv_v[span, :width],
                qkv_v[span, width : 2 * width],
                qkv_v[span, 2 * width :],
                table_ref,
                query_bucket_ref[...],
                heads,
            )
            mix_ref[span, :] = mixed
            for head, soft in enumerate(softs):
                query_prob_ref[head, pl.ds(pl.multiple_of(number * 128, 16), 128), :] = soft
            return carry

        lax.fori_loop(0, query_rows // 128, query_step, 0)
        g_ou.y_got(0)
        bucket_near.wait()
        bucket_far.wait()
        bucket_y.wait_send()
        saves[3].start()

    def tick(when, name, k):
        @pl.when(step == when)
        def _():
            getattr(g_ou, name)(k)

    tick(1, "y_got", 1)
    tick(2, "y_got", 2)
    tick(2, "y_got", 3)
    tick(3, "x_got", 0)
    tick(4, "x_got", 1)
    tick(4, "x_got", 2)

    @pl.when(step == last)
    def _():
        g_down.z_got(0)

    @pl.when(step > 0)
    def _():
        span = pl.ds(pl.multiple_of((step - 1) * block, 16), block)

        def pair(number, carry):
            lanes = pair_lanes(number, head_dim)
            mix_ref[span, lanes] = attend_pair(
                qkv_v[span, lanes],
                qkv_v[:doc_rows, pair_lanes(number, head_dim, width)],
                qkv_v[:doc_rows, pair_lanes(number, head_dim, 2 * width)],
                table_ref,
                bucket_v,
                pl.multiple_of((step - 1) * block, 16),
                prob_ref,
                number,
                head_dim,
            )
            return carry

        lax.fori_loop(0, pairs, pair, 0, unroll=True)

    @pl.when(step == last)
    def _():
        g_ou.x_got(3)
        g_down.z_got(1)
        g_ou.finish()
        g_down.finish()
        cot_move.finish()
        cot_copy.wait()
        for save in saves:
            save.wait()


def gather_scratch(rows, columns):
    return [
        pltpu.VMEM((rows, columns), BFLOAT),
        pltpu.VMEM((rows, columns // 2), BFLOAT),
        pltpu.VMEM((2 * rows, columns // 2), BFLOAT),
    ]


def front(docs, queries, doc_cot, query_cot, weights, buckets, gain, table, query_buckets, heads):
    n_docs, shard_rows, width = docs.shape
    doc_rows = n_docs * shard_rows
    query_rows = queries.shape[0]
    rows = doc_rows + query_rows
    keys = buckets.shape[1]
    block = 256
    steps = doc_rows // block
    anywhere = pl.BlockSpec(memory_space=pl.ANY)
    w_q, w_kv, w_out, w_up, w_down = (weight.shape for weight in weights)
    shards = [
        (w_q[0], w_q[1] + w_kv[1]),
        (w_out[0], w_out[1] + w_up[1]),
        w_down,
    ]
    scratch = []
    for shard in shards:
        scratch += gather_scratch(*shard)
    return pl.pallas_call(
        front_kernel,
        grid=(steps + 1,),
        in_specs=[anywhere] * 10 + [whole((width,)), whole(table.shape), whole(query_buckets.shape)],
        out_specs=[anywhere] * 7
        + [
            whole((rows, width)),
            pl.BlockSpec((heads, block, keys), lambda i: (0, jnp.maximum(i - 1, 0), 0)),
            whole((heads, query_rows, 128)),
            whole((128, 128)),
        ],
        out_shape=[
            jax.ShapeDtypeStruct((rows, width), BFLOAT),
            jax.ShapeDtypeStruct((rows, width), BFLOAT),
            *[jax.ShapeDtypeStruct((shard[0] * 32, shard[1]), BFLOAT) for shard in shards],
            jax.ShapeDtypeStruct((keys, keys), jnp.int16),
            jax.ShapeDtypeStruct((rows, 3 * width), BFLOAT),
            jax.ShapeDtypeStruct((rows, width), BFLOAT),
            jax.ShapeDtypeStruct((heads, doc_rows, keys), BFLOAT),
            jax.ShapeDtypeStruct((heads, query_rows, 128), BFLOAT),
            jax.ShapeDtypeStruct((128, 128), jnp.int32),
        ],
        scratch_shapes=[
            pltpu.VMEM((rows, width), BFLOAT),
            pltpu.VMEM((width, 3 * width), BFLOAT),
            pltpu.VMEM((rows, 3 * width), BFLOAT),
            pltpu.VMEM((keys, keys), jnp.int16),
            pltpu.VMEM(buckets.shape, jnp.int32),
            *scratch,
            pltpu.SemaphoreType.DMA((3, 2, GATHER_COPIES)),
            pltpu.SemaphoreType.DMA((3, 2, 3)),
            pltpu.SemaphoreType.DMA((20,)),
        ],
        compiler_params=pltpu.CompilerParams(
            collective_id=0, has_side_effects=True, vmem_limit_bytes=VMEM_LIMIT
        ),
        cost_estimate=cost(6 * rows * width * width, 100 << 20),
    )(docs, queries, doc_cot, query_cot, *weights, buckets, gain, table, query_buckets)


class Scatter:
    Z_ORDER = (3, 2, 1, 0)

    def __init__(self, spot, away, buffers, sems):
        self.spot, self.away, self.sems = spot, away, sems
        self.held, self.core_in, self.x_in, self.y_in, self.z_in, self.tail, self.tail_in = buffers
        self.half = self.held.shape[1]
        self.rows = self.held.shape[0] // 16

    def span(self, **bits):
        return pl.ds(pl.multiple_of(self.spot.chip(**bits) * self.rows, 16), self.rows)

    def slot(self, number):
        return pl.ds(number * self.rows, self.rows)

    def copy(self, number):
        spot = self.spot
        if number == 0:
            source, target, device = self.away, self.core_in, spot.partner(core=1)
        elif number < 9:
            index = number - 1
            source = self.held.at[self.span(z=self.Z_ORDER[index // 2], x=1, y=1 - index % 2), :]
            target, device = self.x_in.at[self.slot(index), :], spot.partner(x=1)
        elif number < 13:
            index = number - 9
            source = self.held.at[self.span(z=self.Z_ORDER[index], y=1), :]
            target, device = self.y_in.at[self.slot(index), :], spot.partner(y=1)
        elif number < 16:
            index = number - 13
            source = self.held.at[self.span(z=self.Z_ORDER[index]), :]
            target = self.z_in.at[self.slot(index), :]
            device = spot.partner(z=self.Z_ORDER[index])
        else:
            part = self.rows // 2
            theirs = pl.ds(pl.multiple_of((1 - spot.core) * part, 8), part)
            source, target, device = self.tail.at[theirs, :], self.tail_in, spot.partner(core=1)
        return send(source, target, self.sems, number, device)

    def add(self, span, others):
        total = self.held[span, :].astype(SINGLE) + self.core_in[span, :].astype(SINGLE)
        for ref, place in others:
            total = total + ref[place, :].astype(SINGLE)
        return total

    def core_end(self):
        self.copy(0).wait_recv()

    def x_step(self, index):
        span = self.span(z=self.Z_ORDER[index // 2], x=1, y=1 - index % 2)
        self.held[span, :] = self.add(span, []).astype(BFLOAT)
        self.copy(1 + index).start()

    def y_step(self, index):
        self.copy(1 + 2 * index).wait_recv()
        span = self.span(z=self.Z_ORDER[index], y=1)
        total = self.add(span, [(self.x_in, self.slot(2 * index))])
        self.held[span, :] = total.astype(BFLOAT)
        self.copy(9 + index).start()

    def here(self, index):
        self.copy(2 + 2 * index).wait_recv()
        self.copy(9 + index).wait_recv()
        span = self.span(z=self.Z_ORDER[index])
        others = [(self.x_in, self.slot(2 * index + 1)), (self.y_in, self.slot(index))]
        return span, self.add(span, others)

    def z_step(self, index):
        span, total = self.here(index)
        self.held[span, :] = total.astype(BFLOAT)
        self.copy(13 + index).start()

    def tail_start(self):
        _, total = self.here(3)
        for index in range(3):
            self.copy(13 + index).wait_recv()
            total = total + self.z_in[self.slot(index), :].astype(SINGLE)
        self.tail[...] = total
        self.copy(16).start()

    def finish(self):
        part = self.rows // 2
        low = self.spot.core == 0
        mine = jnp.where(low, self.tail[:part, :], self.tail[part:, :])
        self.copy(16).wait_recv()
        other = self.tail_in[...]
        for number in range(COPIES):
            self.copy(number).wait_send()
        return jnp.where(low, mine, other), jnp.where(low, other, mine)


def scatter_scratch(rows, columns):
    half, part = columns // 2, rows // 16
    return [
        pltpu.VMEM((rows, half), BFLOAT),
        pltpu.VMEM((rows, half), BFLOAT),
        pltpu.VMEM((8 * part, half), BFLOAT),
        pltpu.VMEM((4 * part, half), BFLOAT),
        pltpu.VMEM((3 * part, half), BFLOAT),
        pltpu.VMEM((part, half), SINGLE),
        pltpu.VMEM((part // 2, half), SINGLE),
    ]


def half_of(ref, core):
    half = ref.shape[1] // 2
    return ref.at[:, pl.ds(pl.multiple_of(core * half, 128), half)]


def middle_kernel(
    x_in,
    mix_in,
    dy_in,
    gain_ref,
    wo_ref,
    wu_ref,
    wd_ref,
    y_out,
    query_out,
    dh_out,
    da_out,
    rest_ref,
    down_ref,
    near_ref,
    gg_ref,
    h1,
    n2,
    y_acc,
    act_v,
    du_v,
    dh_ref,
    x_ref,
    mix_ref,
    dy_ref,
    *rest,
):
    fulls, downs, rest = rest[0], rest[1], rest[2:]
    step = pl.program_id(0)
    last = pl.num_programs(0) - 1
    spot = Spot()
    rows, width = x_ref.shape
    docs = y_out.shape[0]
    gain = gain_ref[...][None, :]
    block = 512 if rows % 512 == 0 else 256
    spans = [slice(start, start + block) for start in range(0, rows, block)]
    sems, local = rest[-2:]
    pieces = []
    for number in range(3):
        full, core = fulls.at[number], spot.core
        buffers = [half_of(full, core), *rest[6 * number : 6 * number + 6]]
        pieces.append(Scatter(spot, half_of(full, 1 - core), buffers, sems.at[number]))

    loads = [
        pltpu.make_async_copy(source, target, local.at[8 + number])
        for number, (source, target) in enumerate(
            ((x_in, x_ref), (mix_in, mix_ref), (dy_in, dy_ref))
        )
    ]
    save_out = pltpu.make_async_copy(downs.at[0], rest_ref.at[:, pl.ds(0, width)], local.at[0])
    save_up = pltpu.make_async_copy(
        fulls.at[3], rest_ref.at[:, pl.ds(width, width)], local.at[3]
    )

    def save_down(chunk):
        target = down_ref.at[pl.ds(chunk * width, width), :]
        return pltpu.make_async_copy(downs.at[chunk % 2], target, local.at[1 + chunk % 2])

    leaving = [
        pltpu.make_async_copy(du_v.at[pl.ds(0, docs), :], y_out, local.at[4]),
        pltpu.make_async_copy(du_v.at[pl.ds(docs, rows - docs), :], query_out, local.at[7]),
        pltpu.make_async_copy(dh_ref, dh_out, local.at[5]),
        pltpu.make_async_copy(n2, da_out, local.at[6]),
    ]

    def at(when, chunk, action, also=True):
        piece = pieces[chunk]

        @pl.when((step == when) & also)
        def _():
            if action == "x":
                piece.core_end()
                for index in range(8):
                    piece.x_step(index)
            elif action == "y":
                for index in range(4):
                    piece.y_step(index)
            elif action == "z":
                for index in range(3):
                    piece.z_step(index)
            else:
                piece.tail_start()

    @pl.when(step == 0)
    def _():
        for copy in loads:
            copy.start()
        greet(all_partners(spot))
        loads[0].wait()
        loads[1].wait()
        for span in spans:
            residual = x_ref[span, :].astype(SINGLE) + nn(mix_ref[span, :], wo_ref[...])
            h1[span, :] = residual
            y_acc[span, :] = residual
            n2[span, :] = (residual * scale_of(residual) * gain).astype(BFLOAT)
            dh_ref[span, :] = jnp.zeros_like(residual)
        loads[2].wait()

    def part(number, carry):
        then = number == 1
        for chunk in range(3):
            at(chunk + 1, chunk, "x", also=then)
        for chunk in range(2):
            at(chunk + 2, chunk, "tail", also=then)
        span = pl.ds(pl.multiple_of(number * block, 16), block)
        pre = nn(n2[span, :], wu_ref[...])
        grad_hidden = nt(dy_ref[span, :], wd_ref[...])
        square = pre * pre
        tanh = jnp.tanh(pre * (GELU_A + (GELU_A * GELU_B) * square))
        half = 0.5 + 0.5 * tanh
        act = pre * half
        slope = half + act * (1.0 - tanh) * (GELU_A + (3.0 * GELU_A * GELU_B) * square)
        act_low = act.astype(BFLOAT)
        grad_pre = (grad_hidden * slope).astype(BFLOAT)
        act_v[span, :] = act_low
        du_v[span, :] = grad_pre
        y_acc[span, :] += nn(act_low, wd_ref[...])
        dh_ref[span, :] += nt(grad_pre, wu_ref[...])
        return carry

    lax.fori_loop(0, rows // block, part, 0)
    for chunk in range(3):
        at(chunk + 1, chunk, "y")

    for chunk in (2, 3):

        @pl.when(step == chunk)
        def _():
            save_down(chunk - 2).wait()

    fulls[step] = tn(n2[...], du_v[...]).astype(BFLOAT)
    downs[step % 2] = tn(act_v[...], dy_ref[...]).astype(BFLOAT)
    for chunk in range(4):

        @pl.when(step == chunk)
        def _():
            save_down(chunk).start()
            if chunk < 3:
                pieces[chunk].copy(0).start()

    for chunk in range(3):
        at(chunk + 1, chunk, "z")

    @pl.when(step == last)
    def _():
        save_up.start()
        total = jnp.zeros_like(gain)
        for span in spans:
            du_v[span, :] = y_acc[span, :].astype(BFLOAT)
        leaving[0].start()
        leaving[1].start()
        for span in spans:
            residual = h1[span, :]
            scale = scale_of(residual)
            grad_second = dh_ref[span, :]
            total = total + jnp.sum(grad_second * residual * scale, axis=0, keepdims=True)
            grad_res = dy_ref[span, :].astype(SINGLE) + norm_back(
                residual, scale, grad_second * gain
            )
            dh_ref[span, :] = grad_res
            grad_low = grad_res.astype(BFLOAT)
            act_v[span, :] = grad_low
            n2[span, :] = nt(grad_low, wo_ref[...]).astype(BFLOAT)
        gg_ref[...] = total
        leaving[2].start()
        leaving[3].start()
        save_down(2).wait()
        downs[0] = tn(mix_ref[...], act_v[...]).astype(BFLOAT)
        save_out.start()
        pieces[2].tail_start()
        for number, piece in enumerate(pieces):
            left, right = piece.finish()
            base = number * width
            near_ref[:, base : base + width // 2] = left
            near_ref[:, base + width // 2 : base + width] = right
        save_out.wait()
        save_up.wait()
        save_down(3).wait()
        for copy in leaving:
            copy.wait()


def middle(tokens, mixture, cotangent, gain, w_out_up, w_down, doc_rows):
    rows, width = tokens.shape
    hidden = w_down.shape[0]
    chunks = hidden // width
    anywhere = pl.BlockSpec(memory_space=pl.ANY)
    square = (width, width)
    scratch = []
    for _ in range(3):
        scratch += scatter_scratch(*square)[1:]
    return pl.pallas_call(
        middle_kernel,
        grid=(chunks,),
        in_specs=[
            anywhere,
            anywhere,
            anywhere,
            whole((width,)),
            whole(square),
            pl.BlockSpec(square, lambda i: (0, 1 + i)),
            pl.BlockSpec(square, lambda i: (i, 0)),
        ],
        out_specs=[
            anywhere,
            anywhere,
            anywhere,
            anywhere,
            anywhere,
            anywhere,
            whole((width // 32, 3 * width)),
            whole((1, width)),
        ],
        out_shape=[
            jax.ShapeDtypeStruct((doc_rows, width), BFLOAT),
            jax.ShapeDtypeStruct((rows - doc_rows, width), BFLOAT),
            jax.ShapeDtypeStruct((rows, width), SINGLE),
            jax.ShapeDtypeStruct((rows, width), BFLOAT),
            jax.ShapeDtypeStruct((width, 2 * width), BFLOAT),
            jax.ShapeDtypeStruct((hidden, width), BFLOAT),
            jax.ShapeDtypeStruct((width // 32, 3 * width), SINGLE),
            jax.ShapeDtypeStruct((1, width), SINGLE),
        ],
        scratch_shapes=[
            pltpu.VMEM((rows, width), SINGLE),
            pltpu.VMEM((rows, width), BFLOAT),
            pltpu.VMEM((rows, width), SINGLE),
            pltpu.VMEM((rows, width), BFLOAT),
            pltpu.VMEM((rows, width), BFLOAT),
            pltpu.VMEM((rows, width), SINGLE),
            pltpu.VMEM((rows, width), BFLOAT),
            pltpu.VMEM((rows, width), BFLOAT),
            pltpu.VMEM((rows, width), BFLOAT),
            pltpu.VMEM((chunks, *square), BFLOAT),
            pltpu.VMEM((2, *square), BFLOAT),
            *scratch,
            pltpu.SemaphoreType.DMA((3, 2, COPIES)),
            pltpu.SemaphoreType.DMA((11,)),
        ],
        compiler_params=pltpu.CompilerParams(
            collective_id=3, has_side_effects=True, vmem_limit_bytes=VMEM_LIMIT
        ),
        cost_estimate=cost(2 * rows * width * (6 * hidden + 3 * width), 100 << 20),
    )(tokens, mixture, cotangent, gain, w_out_up, w_out_up, w_down)


def back_kernel(
    labels,
    doc_steps,
    q_ref,
    k_ref,
    v_ref,
    query_k_ref,
    query_v_ref,
    da_ref,
    mix_ref,
    prob_ref,
    query_prob_ref,
    query_bucket_ref,
    grad_ref,
    grad_down_ref,
    y_ref,
    near_ref,
    dq_ref,
    dkv_ref,
    ds_ref,
    sums_ref,
    shard_ref,
    down_ref,
    docs_ref,
    dk_acc,
    dv_acc,
    ds_keep,
    *rest,
):
    sems, move_sems, local = rest[14:]
    step = pl.program_id(0)
    last = pl.num_programs(0) - 1
    spot = Spot()
    rows, width = q_ref.shape
    pairs = prob_ref.shape[0] // 2
    keys = k_ref.shape[0]
    heads = query_prob_ref.shape[0]
    head_dim = width // heads
    grads = (grad_ref, grad_down_ref)
    scatters = [
        Scatter(spot, half_of(grad, 1 - spot.core), rest[7 * i : 7 * i + 7], sems.at[i])
        for i, grad in enumerate(grads)
    ]
    loads = [
        pltpu.make_async_copy(half_of(grad, spot.core), scatter.held, local.at[i])
        for i, (grad, scatter) in enumerate(zip(grads, scatters))
    ]
    move = Move(
        spot,
        row_block(y_ref, docs_ref.shape[1]),
        lambda number: docs_ref.at[number],
        lambda number: docs_ref.at[number],
        move_sems,
        local.at[2],
    )

    @pl.when(step == 0)
    def _():
        greet(all_partners(spot))
        for scatter, load in zip(scatters, loads):
            scatter.copy(0).start()
            load.start()
        move.start()
        dk_acc[...] = jnp.zeros_like(dk_acc)
        dv_acc[...] = jnp.zeros_like(dv_acc)
        ds_keep[...] = jnp.zeros_like(ds_keep)

    @pl.when(step == 1)
    def _():
        loads[0].wait()
        scatters[0].core_end()
        for index in range(8):
            scatters[0].x_step(index)

    @pl.when(step == 2)
    def _():
        loads[1].wait()
        scatters[1].core_end()
        for index in range(8):
            scatters[1].x_step(index)

    def at(when, number, *actions):
        @pl.when(step == when)
        def _():
            for name, *index in actions:
                getattr(scatters[number], name)(*index)

    at(4, 0, *[("y_step", index) for index in range(4)])
    at(6, 0, *[("z_step", index) for index in range(3)])
    at(5, 1, ("y_step", 0))
    at(7, 1, ("z_step", 0), ("y_step", 1))
    at(8, 1, ("z_step", 1), ("y_step", 2))
    at(9, 1, ("z_step", 2), ("y_step", 3))

    at(8, 0, ("tail_start",))

    @pl.when(step == last)
    def _():
        scatters[1].tail_start()

    @pl.when(step < doc_steps)
    def _():
        def pair(number, carry):
            spread = (step % 2) * pairs + number
            lanes = pair_lanes(spread, head_dim)
            dq, dk, dv, kept = attend_back(
                q_ref[:, lanes],
                k_ref[:, lanes],
                v_ref[:, lanes],
                da_ref[:, lanes],
                mix_ref[:, lanes],
                [prob_ref[2 * number], prob_ref[2 * number + 1]],
                head_dim,
            )
            ds_ref[2 * number] = kept[0]
            ds_ref[2 * number + 1] = kept[1]
            dq_ref[:, lanes] = dq.astype(BFLOAT)
            dk_acc[:, lanes] += dk
            dv_acc[:, lanes] += dv
            return carry

        lax.fori_loop(0, pairs, pair, 0, unroll=True)

    @pl.when(step == doc_steps - 1)
    def _():
        dkv_ref[:keys, :width] = dk_acc[...].astype(BFLOAT)
        dkv_ref[:keys, width:] = dv_acc[...].astype(BFLOAT)

    @pl.when(step >= doc_steps)
    def _():
        def part(number, carry):
            span = pl.ds(pl.multiple_of(number * 128, 128), 128)
            place = pl.ds(pl.multiple_of(keys + (step - doc_steps) * rows + number * 128, 16), 128)
            dq, dk, dv, kept = query_back_block(
                q_ref[span, :],
                query_k_ref[span, :],
                query_v_ref[span, :],
                da_ref[span, :],
                mix_ref[span, :],
                [query_prob_ref[head, span, :] for head in range(heads)],
                head_dim,
            )
            for head in range(heads):
                ds_keep[head] += kept[head].astype(SINGLE)
            for pair in range(heads // 2):
                lanes = slice(pair * 2 * head_dim, (pair + 1) * 2 * head_dim)
                dq_ref[span, lanes] = dq[pair]
                dkv_ref[place, lanes] = dk[pair]
                dkv_ref[place, width + lanes.start : width + lanes.stop] = dv[pair]
            return carry

        lax.fori_loop(0, rows // 128, part, 0, unroll=True)

    @pl.when(step == last)
    def _():
        total = jnp.zeros_like(sums_ref)
        for index in range(8):
            some = slice(index * 16, (index + 1) * 16)
            terms = ds_keep[:, some, :].reshape(heads * 16, 128)
            high = terms.astype(BFLOAT)
            low = (terms - high.astype(SINGLE)).astype(BFLOAT)
            onehot = bucket_onehot(query_bucket_ref[some, :], labels)
            total = total + nt(onehot, high) + nt(onehot, low)
        sums_ref[...] = total

    @pl.when(step == last)
    def _():
        left, right = scatters[0].finish()
        shard_ref[:, :width] = left
        shard_ref[:, width : 4 * width] = near_ref[...]
        shard_ref[:, 4 * width :] = right
        left, right = scatters[1].finish()
        down_ref[:, : width // 2] = left
        down_ref[:, width // 2 :] = right
        move.finish()


def back(qkv, da_rows, mixture, probs, query_probs, query_buckets, grads, outputs, near, n_docs, labels):
    rows, width = da_rows.shape
    heads, doc_rows, keys = probs.shape
    block = 256
    doc_steps = 2 * doc_rows // block
    doc_blocks = doc_rows // block
    steps = doc_steps + (rows - doc_rows) // block
    half = heads // 2

    def row(i):
        return jnp.where(i < doc_steps, i // 2, i - doc_steps + doc_blocks)

    def doc(i):
        clipped = jnp.minimum(i, doc_steps - 1)
        return (clipped % 2, clipped // 2, 0)

    def query(i):
        return jnp.maximum(i, doc_steps) - doc_steps

    anywhere = pl.BlockSpec(memory_space=pl.ANY)
    along = pl.BlockSpec((block, width), lambda i: (row(i), 0))
    once = pl.Buffered(1)
    return pl.pallas_call(
        functools.partial(back_kernel, labels, doc_steps),
        grid=(steps,),
        in_specs=[
            along,
            pl.BlockSpec((keys, width), lambda i: (0, 1), pipeline_mode=once),
            pl.BlockSpec((keys, width), lambda i: (0, 2), pipeline_mode=once),
            pl.BlockSpec((block, width), lambda i: (query(i) + doc_blocks, 1)),
            pl.BlockSpec((block, width), lambda i: (query(i) + doc_blocks, 2)),
            along,
            along,
            pl.BlockSpec((half, block, keys), doc),
            pl.BlockSpec((heads, block, 128), lambda i: (0, query(i), 0)),
            whole(query_buckets.shape),
            anywhere,
            anywhere,
            anywhere,
            whole(near.shape),
        ],
        out_specs=[
            along,
            whole((rows, 2 * width)),
            pl.BlockSpec((half, block, keys), doc),
            whole((16 * labels, heads * 16)),
            whole((near.shape[0], 5 * width)),
            whole((grads[1].shape[0] // 32, width)),
            anywhere,
        ],
        out_shape=[
            jax.ShapeDtypeStruct((rows, width), BFLOAT),
            jax.ShapeDtypeStruct((rows, 2 * width), BFLOAT),
            jax.ShapeDtypeStruct(probs.shape, BFLOAT),
            jax.ShapeDtypeStruct((16 * labels, heads * 16), SINGLE),
            jax.ShapeDtypeStruct((near.shape[0], 5 * width), SINGLE),
            jax.ShapeDtypeStruct((grads[1].shape[0] // 32, width), SINGLE),
            jax.ShapeDtypeStruct((n_docs, doc_rows // n_docs, width), BFLOAT),
        ],
        scratch_shapes=[
            pltpu.VMEM((keys, width), SINGLE),
            pltpu.VMEM((keys, width), SINGLE),
            pltpu.VMEM((heads, 128, 128), SINGLE),
            *scatter_scratch(*grads[0].shape),
            *scatter_scratch(*grads[1].shape),
            pltpu.SemaphoreType.DMA((2, 2, COPIES)),
            pltpu.SemaphoreType.DMA((2, 3)),
            pltpu.SemaphoreType.DMA((3,)),
        ],
        compiler_params=pltpu.CompilerParams(
            collective_id=1, has_side_effects=True, vmem_limit_bytes=VMEM_LIMIT
        ),
        cost_estimate=cost(70 * doc_rows * keys * width, 100 << 20),
    )(
        qkv,
        qkv,
        qkv,
        qkv,
        qkv,
        da_rows,
        mixture,
        probs,
        query_probs,
        query_buckets,
        *grads,
        outputs,
        near,
    )


class Total:
    def __init__(self, spot, slots, sems):
        self.spot, self.slots, self.sems = spot, slots, sems

    def rounds(self):
        spot = self.spot
        near = [(x, y, core) for x in (0, 1) for y in (0, 1) for core in (0, 1)][1:]
        return (
            (
                (spot.x * 2 + spot.y) * 2 + spot.core,
                8,
                [spot.partner(x=x, y=y, core=core) for x, y, core in near],
            ),
            (spot.z, 4, [spot.partner(z=k) for k in (1, 2, 3)]),
        )

    def copies(self, index):
        base = 8 * index
        place, count, partners = self.rounds()[index]
        mine = self.slots.at[base + place]
        return [
            send(mine, mine, self.sems.at[index], number, device)
            for number, device in enumerate(partners)
        ]

    def begin(self, index, values):
        self.slots[8 * index + self.rounds()[index][0]] = values
        for copy in self.copies(index):
            copy.start()

    def end(self, index):
        for copy in self.copies(index):
            copy.wait_recv()
        values = self.slots[8 * index]
        for other in range(1, self.rounds()[index][1]):
            values = values + self.slots[8 * index + other]
        for copy in self.copies(index):
            copy.wait_send()
        return values


def leave_kernel(
    labels,
    x_in,
    gain_ref,
    dq_in,
    dkv_in,
    dh_in,
    w_in,
    ds_ref,
    bucket_ref,
    query_sums_ref,
    ff_ref,
    found_ref,
    out_ref,
    docs_ref,
    query_dx_ref,
    total_ref,
    normed,
    away,
    low,
    high,
    sums,
    gain_sum,
    slots,
    dh_ref,
    w_ref,
    x_ref,
    dq_ref,
    dkv_ref,
    *rest,
):
    buffers, (sems, move_sems, total_sems, local) = rest[:7], rest[7:]
    step = pl.program_id(0)
    last = pl.num_programs(0) - 1
    spot = Spot()
    rows, width = x_ref.shape
    heads = ds_ref.shape[0]
    doc_rows = low.shape[0]
    block = doc_rows // 4
    scatter = Scatter(spot, away, buffers, sems)
    half = scatter.half
    move = Move(
        spot,
        row_block(low, block),
        lambda number: docs_ref.at[number],
        lambda number: docs_ref.at[number],
        move_sems,
        local.at[0],
    )
    query_copy = pltpu.make_async_copy(high, query_dx_ref, local.at[1])

    def quarter(number):
        device, rows = spot.partner(y=1, core=1), block // 4
        start = pl.multiple_of(device[1] * block + number * rows, 16)
        return send(
            low.at[pl.ds(start, rows), :],
            docs_ref.at[spot.seq, pl.ds(number * rows, rows), :],
            move_sems,
            3 + number,
            device,
        )

    soon = [
        pltpu.make_async_copy(x_in, x_ref, local.at[4]),
        pltpu.make_async_copy(dq_in, dq_ref, local.at[5]),
        pltpu.make_async_copy(dkv_in, dkv_ref, local.at[6]),
    ]
    late = [
        pltpu.make_async_copy(dh_in, dh_ref, local.at[2]),
        pltpu.make_async_copy(w_in, w_ref, local.at[3]),
    ]

    @pl.when(step == 0)
    def _():
        for copy in soon + late:
            copy.start()
        more = [spot.partner(x=1, y=y, core=core) for y, core in ((0, 1), (1, 0), (1, 1))]
        greet(all_partners(spot) + more)
        gain = gain_ref[...][None, :]
        sums[...] = query_sums_ref[...]
        gain_sum[...] = jnp.zeros_like(gain_sum)

        def norm_block(number, carry):
            span = pl.ds(pl.multiple_of(number * block, 16), block)
            values = x_ref[span, :].astype(SINGLE)
            normed[span, :] = (values * scale_of(values) * gain).astype(BFLOAT)
            return carry

        soon[0].wait()
        lax.fori_loop(0, rows // block, norm_block, 0)
        soon[1].wait()
        soon[2].wait()

        def product(core, into):
            part = half // 3

            for number in range(3):
                spot_out = slice(number * part, (number + 1) * part)
                start = core * half + number * part

                def from_q():
                    lanes = pl.ds(pl.multiple_of(start, 128), part)
                    into[:, spot_out] = tn(normed[...], dq_ref[:, lanes]).astype(BFLOAT)

                def from_kv():
                    lanes = pl.ds(pl.multiple_of(start - width, 128), part)
                    into[:, spot_out] = tn(normed[...], dkv_ref[:, lanes]).astype(BFLOAT)

                pl.when(start < width)(from_q)
                pl.when(start >= width)(from_kv)

        product(1 - spot.core, away)
        scatter.copy(0).start()
        product(spot.core, scatter.held)
        scatter.core_end()
        for index in range(8):
            scatter.x_step(index)

        def grad_block(start, into, place):
            span = pl.ds(pl.multiple_of(start, 16), block)
            values = x_ref[span, :].astype(SINGLE)
            scale = scale_of(values)
            grad = nt(dq_ref[span, :], w_ref[:, :width])
            grad = grad + nt(dkv_ref[span, :width], w_ref[:, width : 2 * width])
            grad = grad + nt(dkv_ref[span, width:], w_ref[:, 2 * width :])
            gain_sum[...] += jnp.sum(grad * values * scale, axis=0, keepdims=True)
            dx = dh_ref[span, :] + norm_back(values, scale, grad * gain)
            into[place, :] = dx.astype(into.dtype)

        for copy in late:
            copy.wait()
        for number in range(3):
            y, core = Move.PARTNERS[number]
            start = spot.partner(y=y, core=core)[1] * block
            grad_block(start, low, pl.ds(pl.multiple_of(start, 16), block))
            if number != 1:
                move.copy(number).start()
        start = spot.seq * block
        grad_block(start, low, pl.ds(pl.multiple_of(start, 16), block))
        move.own().start()
        for number in range((rows - doc_rows) // block):
            grad_block(
                doc_rows + number * block, high, pl.ds(number * block, block)
            )
        query_copy.start()

    def at(when, name, index):
        @pl.when(step == when)
        def _():
            getattr(scatter, name)(index)

    at(1, "y_step", 0)
    at(2, "y_step", 1)
    at(3, "z_step", 0)
    at(3, "y_step", 2)
    at(4, "z_step", 1)
    at(4, "y_step", 3)
    at(5, "z_step", 2)

    for number in range(4):

        @pl.when(step == number + 2)
        def _():
            quarter(number).start()

    @pl.when(step > 0)
    def _():
        total = sums[...]
        for number in range(ds_ref.shape[1] // 16):
            span = slice(number * 16, (number + 1) * 16)
            grad_rows = ds_ref[:, span, :].reshape(heads * 16, ds_ref.shape[2])
            total = total + bucket_products(bucket_ref[span, :], grad_rows, labels)
        sums[...] = total

    @pl.when(step == last)
    def _():
        shape = sums.shape
        same = (
            lax.broadcasted_iota(jnp.int32, shape, 0) // labels
            == lax.broadcasted_iota(jnp.int32, shape, 1) % 16
        )
        kept = jnp.where(same, sums[...], 0.0)
        folded = kept[:labels]
        for index in range(1, 16):
            folded = folded + kept[index * labels : (index + 1) * labels]
        pick_shape = (heads * 16, 128)
        pick = (
            lax.broadcasted_iota(jnp.int32, pick_shape, 0) // 16
            == lax.broadcasted_iota(jnp.int32, pick_shape, 1)
        )
        bias = jnp.dot(
            folded,
            jnp.where(pick, 1.0, 0.0),
            preferred_element_type=SINGLE,
            precision=lax.Precision.HIGHEST,
        )
        wide = width // 128
        lines = [gain_sum[:, r * 128 : (r + 1) * 128] for r in range(wide)]
        lines += [ff_ref[:, r * 128 : (r + 1) * 128] for r in range(wide)]
        lines += [jnp.full((slots.shape[1] - labels - 2 * wide, 128), found_ref[0, 0])]
        total = Total(spot, slots, total_sems)
        total.begin(0, jnp.concatenate(lines + [bias], 0))
        scatter.tail_start()
        total.begin(1, total.end(0))
        left, right = scatter.finish()
        out_ref[:, :half] = left
        out_ref[:, half:] = right
        move.own().wait()
        move.copy(0).wait()
        move.copy(2).wait()
        for number in range(4):
            quarter(number).wait()
        query_copy.wait()
        total_ref[...] = total.end(1)


def leave(
    tokens, gain, dq, dkv, grad_res, w_qkv, ds, buckets, query_sums, grad_ff, found, n_docs, labels
):
    rows, width = tokens.shape
    heads, doc_rows, keys = ds.shape
    columns = 3 * width
    block = 128
    lines = -(-(2 * width // 128 + 1) // 8) * 8 + labels
    anywhere = pl.BlockSpec(memory_space=pl.ANY)
    return pl.pallas_call(
        functools.partial(leave_kernel, labels),
        grid=(1 + doc_rows // block,),
        in_specs=[
            anywhere,
            whole((width,)),
            anywhere,
            anywhere,
            anywhere,
            anywhere,
            pl.BlockSpec((heads, block, keys), lambda i: (0, jnp.maximum(i - 1, 0), 0)),
            pl.BlockSpec((block, keys), lambda i: (jnp.maximum(i - 1, 0), 0)),
            whole(query_sums.shape),
            whole((1, width)),
            pl.BlockSpec(memory_space=pltpu.SMEM),
        ],
        out_specs=[whole((width // 32, columns)), anywhere, anywhere, whole((lines, 128))],
        out_shape=[
            jax.ShapeDtypeStruct((width // 32, columns), SINGLE),
            jax.ShapeDtypeStruct((n_docs, doc_rows // n_docs, width), BFLOAT),
            jax.ShapeDtypeStruct((rows - doc_rows, width), SINGLE),
            jax.ShapeDtypeStruct((lines, 128), SINGLE),
        ],
        scratch_shapes=[
            pltpu.VMEM((rows, width), BFLOAT),
            pltpu.VMEM((width, columns // 2), BFLOAT),
            pltpu.VMEM((doc_rows, width), BFLOAT),
            pltpu.VMEM((rows - doc_rows, width), SINGLE),
            pltpu.VMEM(query_sums.shape, SINGLE),
            pltpu.VMEM((1, width), SINGLE),
            pltpu.VMEM((12, lines, 128), SINGLE),
            pltpu.VMEM((rows, width), SINGLE),
            pltpu.VMEM(w_qkv.shape, BFLOAT),
            pltpu.VMEM((rows, width), BFLOAT),
            pltpu.VMEM((rows, width), BFLOAT),
            pltpu.VMEM((rows, 2 * width), BFLOAT),
            *scatter_scratch(width, columns),
            pltpu.SemaphoreType.DMA((2, COPIES)),
            pltpu.SemaphoreType.DMA((2, 7)),
            pltpu.SemaphoreType.DMA((2, 2, 7)),
            pltpu.SemaphoreType.DMA((7,)),
        ],
        compiler_params=pltpu.CompilerParams(
            collective_id=2, has_side_effects=True, vmem_limit_bytes=VMEM_LIMIT
        ),
        cost_estimate=cost(12 * rows * width * width, 100 << 20),
    )(
        tokens,
        gain,
        dq,
        dkv,
        grad_res,
        w_qkv,
        ds,
        buckets,
        query_sums,
        grad_ff,
        found,
    )


def on_device(
    doc_tokens,
    queries,
    doc_cot,
    query_cot,
    q_weight,
    kv_weight,
    out_weight,
    up_weight,
    down_weight,
    attn_gain,
    ff_gain,
    rel_bias,
    doc_buckets,
    query_buckets,
    topk_mask,
    positives,
    pos_count,
):
    n_docs, shard_rows, width = doc_tokens.shape
    n_query, query_len, _ = queries.shape
    bucket_count, heads = rel_bias.shape
    doc_len = doc_buckets.shape[1]
    doc_rows = n_docs * shard_rows
    query_total = n_query * query_len
    seq_size = lax.axis_size("seq")
    group = max(1, seq_size // n_docs)
    local_docs = max(1, n_docs // seq_size)
    local_rows = doc_len // group
    dp_size = lax.axis_size("dp")
    small = (dp_size, seq_size, n_docs) == (8, 4, 4) and width % 256 == 0 and shard_rows % 256 == 0
    small = small and down_weight.shape[0] * 32 == 4 * width and query_total % 256 == 0

    flat_queries = queries.reshape(query_total, width)
    flat_query_cot = query_cot.reshape(query_total, width)

    table = jnp.pad(rel_bias.T, ((0, 16 - heads), (0, 127 - bucket_count)))
    table = jnp.pad(table, ((0, 0), (0, 1)), constant_values=-1e30)

    if small:
        tokens, cotangent, w_qkv, w_out_up, w_down, buckets, qkv, mixture, doc_probs, query_probs, tiled = front(
            doc_tokens,
            flat_queries,
            doc_cot,
            flat_query_cot,
            (q_weight, kv_weight, out_weight, up_weight, down_weight),
            doc_buckets,
            attn_gain,
            table,
            query_buckets,
            heads,
        )
    else:
        order = gather_orders()[0]
        w_qkv = gather_rows(jnp.concatenate([q_weight, kv_weight], 1), order)
        w_out_up = gather_rows(jnp.concatenate([out_weight, up_weight], 1), order)
        w_down = gather_rows(down_weight, order)
        tokens = jnp.concatenate([own_document(doc_tokens), flat_queries], 0)
        cotangent = jnp.concatenate([own_document(doc_cot), flat_query_cot], 0)
        buckets = gather_positions(doc_buckets.astype(jnp.int16))
        repeats = 128 // query_len
        same = jnp.kron(jnp.eye(repeats, dtype=jnp.int32), jnp.ones_like(query_buckets))
        tiled = jnp.where(same == 1, jnp.tile(query_buckets, (repeats, repeats)), 127)
        if group > 1:
            part = lax.axis_index("seq") % group
            buckets = lax.dynamic_slice_in_dim(buckets, part * local_rows, local_rows, 0)
        q_rows, kv_rows = project(tokens, attn_gain, w_qkv)
        kv_docs = kv_rows
        if group > 1:
            teams = [list(range(t * group, (t + 1) * group)) for t in range(seq_size // group)]
            kv_docs = lax.all_gather(
                kv_rows[:doc_rows], "seq", axis=0, tiled=True, axis_index_groups=teams
            )
        doc_mix, doc_probs = doc_forward(
            q_rows, kv_docs, table, buckets, local_docs, local_rows, heads
        )
        query_mix, query_probs = query_forward(
            q_rows, kv_rows, table, tiled, doc_rows, query_total, heads
        )
        mixture = jnp.concatenate([doc_mix, query_mix], 0)
    if small:
        outputs, query_out, grad_res, grad_mix, grad_rest, grad_down, grad_near, grad_ff = middle(
            tokens, mixture, cotangent, ff_gain, w_out_up, w_down, doc_rows
        )
        query_out = query_out.reshape(queries.shape)
    else:
        outputs, grad_res, grad_mix, grad_out_up, grad_down, grad_ff = feed(
            tokens, mixture, cotangent, ff_gain, w_out_up, w_down
        )
        query_out = outputs[doc_rows:].reshape(queries.shape)
    matches = positives[:, :, None] == jnp.arange(doc_len, dtype=jnp.int32)[None, None, :]
    counted = jnp.arange(positives.shape[1], dtype=jnp.int32)[None, :] < pos_count[:, None]
    retrieved = jnp.sum(
        jnp.where(matches & counted[:, :, None], topk_mask[:, None, :].astype(SINGLE), 0.0)
    )

    if small:
        dq, dkv, ds, query_sums, grad_far, grad_down_shard, doc_out = back(
            qkv,
            grad_mix,
            mixture,
            doc_probs,
            query_probs,
            tiled,
            (grad_rest, grad_down),
            outputs,
            grad_near,
            n_docs,
            bucket_count,
        )
        grad_out_shard = grad_far[:, :width]
        grad_up_shard = grad_far[:, width:]
        grad_qkv_shard, doc_dx, query_dx, total = leave(
            tokens,
            attn_gain,
            dq,
            dkv,
            grad_res,
            w_qkv,
            ds,
            buckets,
            query_sums,
            grad_ff,
            retrieved.reshape(1, 1),
            n_docs,
            bucket_count,
        )
        lines = width // 128
        total_attn = total[:lines].reshape(-1)
        total_ff = total[lines : 2 * lines].reshape(-1)
        total_found = total[2 * lines, 0]
        total_bias = total[-bucket_count:, :heads]
        query_dx = query_dx.reshape(queries.shape)
    else:
        grad_down_shard = scatter_columns(grad_down, 2)
        grad_out_up_shard = scatter_columns(grad_out_up, 2)
        grad_out_shard = grad_out_up_shard[:, :width]
        grad_up_shard = grad_out_up_shard[:, width:]
        doc_out = spread_document(outputs[:doc_rows], doc_tokens)
        doc_dq, doc_dk, doc_dv, doc_sums = doc_backward(
            q_rows,
            kv_docs,
            grad_mix,
            doc_mix,
            doc_probs,
            buckets,
            local_docs,
            local_rows,
            bucket_count,
        )
        if group > 1:
            both = jnp.concatenate([doc_dk, doc_dv], 1)
            both = lax.psum_scatter(
                both, "seq", scatter_dimension=0, tiled=True, axis_index_groups=teams
            )
            doc_dk, doc_dv = both[:, :width], both[:, width:]
        query_dq, query_dkv, query_sums = query_backward(
            q_rows, kv_rows, grad_mix, mixture, query_probs, tiled, doc_rows, bucket_count
        )
        grad_tokens, grad_low, grad_qkv, grad_attn = unproject(
            tokens,
            attn_gain,
            jnp.concatenate([doc_dq, query_dq], 0),
            jnp.concatenate([doc_dk, query_dkv[:, :width]], 0),
            jnp.concatenate([doc_dv, query_dkv[:, width:]], 0),
            grad_res,
            w_qkv,
        )
        grad_qkv_shard = scatter_columns(grad_qkv, 2)
        doc_dx = spread_document(grad_low[:doc_rows], doc_tokens)
        query_dx = grad_tokens[doc_rows:].reshape(queries.shape)
        sums = (doc_sums + query_sums).reshape(16, bucket_count, heads, 16)
        keep = jnp.eye(16, dtype=SINGLE)[:, None, None, :]
        bias_local = jnp.sum(sums * keep, axis=(0, 3))
        flat = jnp.concatenate(
            [grad_attn[0], grad_ff[0], bias_local.reshape(-1), jnp.full((128,), retrieved)]
        )
        total = sum_all(flat)
        total_attn, total_ff = total[:width], total[width : 2 * width]
        total_bias = total[2 * width : 2 * width + bucket_count * heads]
        total_bias = total_bias.reshape(bucket_count, heads)
        total_found = total[-1]
    slots = float(n_query * dp_size * seq_size * positives.shape[1])
    return (
        doc_out,
        query_out,
        doc_dx.astype(SINGLE),
        query_dx,
        grad_qkv_shard[:, :width],
        grad_qkv_shard[:, width:],
        grad_out_shard,
        grad_up_shard,
        grad_down_shard,
        total_attn,
        total_ff,
        total_bias,
        total_found / slots,
    )


def solution(mesh):
    rows_all = P(("dp", "seq"), None)
    return jax.shard_map(
        on_device,
        mesh=mesh,
        in_specs=(
            P("dp", "seq", None),
            P(("dp", "seq"), None, None),
            P("dp", "seq", None),
            P(("dp", "seq"), None, None),
            rows_all,
            rows_all,
            rows_all,
            rows_all,
            rows_all,
            P(),
            P(),
            P(),
            P("seq", None),
            P(),
            rows_all,
            rows_all,
            P(("dp", "seq")),
        ),
        out_specs=(
            P("dp", "seq", None),
            P(("dp", "seq"), None, None),
            P("dp", "seq", None),
            P(("dp", "seq"), None, None),
            rows_all,
            rows_all,
            rows_all,
            rows_all,
            rows_all,
            P(),
            P(),
            P(),
            P(),
        ),
        check_vma=False,
    )
```
